128 devices in a mesh: seq: 32 (over z, y, core), tensor: 4 (over x).
Axes of the slice: x: 4, y: 4, z: 4, core: 2. Of those that a mesh axis runs over, the one named last changes fastest.
Arguments:
- layer_input: bfloat16 [8192, 1152], P('seq'), may hold values from -6 to 6
- segment_ids: int32 [8192], P('seq'), may hold values from 0 to 4, as said below
- out_cotangent: bfloat16 [8192, 1152], P('seq'), may hold values from -16 to 16
- attn_norm_gain: float32 [1152], replicated, may hold values from 0.1 to 1.9
- query_weight: bfloat16 [1152, 1024], P(None, 'tensor'), may hold values from -0.1875 to 0.1875
- key_weight: bfloat16 [1152, 256], replicated, may hold values from -0.1875 to 0.1875
- value_weight: bfloat16 [1152, 256], replicated, may hold values from -0.1875 to 0.1875
- query_gain: float32 [256], replicated, may hold values from 0.1 to 1.9
- key_gain: float32 [256], replicated, may hold values from 0.1 to 1.9
- output_weight: bfloat16 [1024, 1152], P('tensor'), may hold values from -0.1875 to 0.1875
- attn_post_gain: float32 [1152], replicated, may hold values from 0.1 to 1.9
- ffw_norm_gain: float32 [1152], replicated, may hold values from 0.1 to 1.9
- gate_weight: bfloat16 [1152, 6912], P(None, 'tensor'), may hold values from -0.1875 to 0.1875
- up_weight: bfloat16 [1152, 6912], P(None, 'tensor'), may hold values from -0.1875 to 0.1875
- down_weight: bfloat16 [6912, 1152], P('tensor'), may hold values from -0.078125 to 0.078125
- ffw_post_gain: float32 [1152], replicated, may hold values from 0.1 to 1.9
Outputs:
- layer_output: bfloat16 [8192, 1152], P('seq')
- input_grad: bfloat16 [8192, 1152], P('seq')
- attn_norm_gain_grad: float32 [1152], replicated
- query_weight_grad: float32 [1152, 1024], P(None, 'tensor')
- key_weight_grad: float32 [1152, 256], replicated
- value_weight_grad: float32 [1152, 256], replicated
- query_gain_grad: float32 [256], replicated
- key_gain_grad: float32 [256], replicated
- output_weight_grad: float32 [1024, 1152], P('tensor')
- attn_post_gain_grad: float32 [1152], replicated
- ffw_norm_gain_grad: float32 [1152], replicated
- gate_weight_grad: float32 [1152, 6912], P(None, 'tensor')
- up_weight_grad: float32 [1152, 6912], P(None, 'tensor')
- down_weight_grad: float32 [6912, 1152], P('tensor')
- ffw_post_gain_grad: float32 [1152], replicated
The draws below stay inside these ranges and needn't reach their ends.
Inputs may be any that keep to these rules, and one draw needn't show every extreme that they name: `segment_ids`: ids never fall, every one of the 5 values occurs, and one document runs from within the first 256 tokens into the last 256 tokens.
All inputs are finite; a program needn't handle non-finite values.
Results may differ from the reference program's by a relative error of at most 0.03.
Values may be sent and summed in bfloat16 or wider, within the bound.
No kernel may reach another device: no remote copies, remote signals or barrier semaphores. Data moves between devices by JAX's collectives and lax.ppermute only.
A program may use at most 192 MiB of HBM per device.

```python
import jax
import jax.numpy as jnp
from jax import lax

D = 1152
HEADS = 4
HD = 256
FF = 6912
WINDOW = 512
TOK_DEV = 256
TOKENS = 8192


def draw_segment_ids(key, part):
    key = jax.random.fold_in(key, 11)
    keys = jax.random.split(key, 4)
    half = TOK_DEV // 2
    first = jax.random.randint(keys[0], (), 2, half + 1)
    inner = jax.random.randint(keys[1], (), 1, first)
    last = jax.random.randint(keys[2], (), TOKENS - half, TOKENS - 1)
    tail = jax.random.randint(keys[3], (), last + 1, TOKENS)
    index = jnp.arange(TOKENS, dtype=jnp.int32)
    ids = (index >= inner).astype(jnp.int32) + (index >= first).astype(jnp.int32)
    ids = ids + (index >= last).astype(jnp.int32) + (index >= tail).astype(jnp.int32)
    return ids


def draw_out_cotangent(key, part):
    key = jax.random.fold_in(key, 23)
    rows = jnp.arange(TOKENS, dtype=jnp.float32) / TOKENS
    base = jnp.clip(jax.random.normal(key, (TOKENS, D), jnp.float32), -4.0, 4.0)
    rise = jnp.exp(jnp.log(3.0) * rows)
    return (base * rise[:, None]).astype(jnp.bfloat16)


def block_levels(own_key, dims, shards, low, largest):
    level = 1.0
    for axis_at, parts in shards:
        heights = jax.random.uniform(jax.random.fold_in(jax.random.fold_in(own_key, 6), axis_at), (parts,), jnp.float32, low / len(shards), largest / len(shards))
        level = level * jnp.repeat(jnp.exp(heights), dims[axis_at] // parts).reshape((-1,) + (1,) * (len(dims) - 1 - axis_at))
    return level


def normal_values(own_key, dims, scale, limit, cuts=(), kind=jnp.bfloat16):
    entries = jax.random.normal(own_key, dims, jnp.float32) * scale
    if len(cuts) > 0:
        entries = block_levels(own_key, dims, cuts, -0.22, 0.18) * entries
    return jnp.clip(entries, min=-limit, max=limit).astype(kind)


def setup_inputs(seed: int = 0) -> dict:
    arg_keys = jax.random.split(jax.random.key(seed), 17)
    return {
        "layer_input": normal_values(arg_keys[0], (TOKENS, D), 1.0, 6.0, ((0, 32),)),
        "segment_ids": draw_segment_ids(jax.random.fold_in(arg_keys[16], 71), 0),
        "out_cotangent": draw_out_cotangent(jax.random.fold_in(arg_keys[16], 71), 0),
        "attn_norm_gain": jnp.clip(1.0 + 0.18 * jax.random.normal(arg_keys[3], (D,), jnp.float32), 0.1, 1.9),
        "query_weight": normal_values(arg_keys[4], (D, HEADS * HD), D ** -0.5, 0.1875, ((1, 4),)),
        "key_weight": normal_values(arg_keys[5], (D, HD), D ** -0.5, 0.1875),
        "value_weight": normal_values(arg_keys[6], (D, HD), D ** -0.5, 0.1875),
        "query_gain": jnp.clip(1.0 + 0.18 * jax.random.normal(arg_keys[7], (HD,), jnp.float32), 0.1, 1.9),
        "key_gain": jnp.clip(1.0 + 0.18 * jax.random.normal(arg_keys[8], (HD,), jnp.float32), 0.1, 1.9),
        "output_weight": normal_values(arg_keys[9], (HEADS * HD, D), (HEADS * HD) ** -0.5, 0.1875, ((0, 4),)),
        "attn_post_gain": jnp.clip(1.0 + 0.18 * jax.random.normal(arg_keys[10], (D,), jnp.float32), 0.1, 1.9),
        "ffw_norm_gain": jnp.clip(1.0 + 0.18 * jax.random.normal(arg_keys[11], (D,), jnp.float32), 0.1, 1.9),
        "gate_weight": normal_values(arg_keys[12], (D, FF), D ** -0.5, 0.1875, ((1, 4),)),
        "up_weight": normal_values(arg_keys[13], (D, FF), D ** -0.5, 0.1875, ((1, 4),)),
        "down_weight": normal_values(arg_keys[14], (FF, D), FF ** -0.5, 0.078125, ((0, 4),)),
        "ffw_post_gain": jnp.clip(1.0 + 0.18 * jax.random.normal(arg_keys[15], (D,), jnp.float32), 0.1, 1.9),
    }


eps = 1e-06
rope_base = 10000.0

@jax.custom_vjp
def low(v):
    return lax.optimization_barrier(v.astype(jnp.bfloat16)).astype(jnp.float32)

@jax.custom_vjp
def low_back(v):
    return v

def low_keep(v):
    return (low(v), None)

def low_pass(kept, grad):
    return (grad,)

def back_keep(v):
    return (v, None)

def back_low(kept, grad):
    return (low(grad),)
low.defvjp(low_keep, low_pass)
low_back.defvjp(back_keep, back_low)

def matmul(a, b):
    return jnp.dot(a, b, precision=lax.Precision.HIGHEST, preferred_element_type=jnp.float32)

def norm_rows(values, gain):
    return values * lax.rsqrt(lax.optimization_barrier(jnp.mean(values * values, axis=-1, keepdims=True)) + eps) * gain

def rotate(values, cosine, sine):
    half = values.shape[-1] // 2
    first = values[..., :half]
    second = values[..., half:]
    return jnp.concatenate([first * cosine - second * sine, second * cosine + first * sine], axis=-1)

def positions(segment_ids):
    index = jnp.arange(TOKENS, dtype=jnp.int32)
    fresh = jnp.concatenate([jnp.ones((1,), dtype=bool), segment_ids[1:] != segment_ids[:-1]])
    begin = lax.cummax(jnp.where(fresh, index, 0), axis=0)
    return index - begin

def attention(queries, keys, values, segment_ids):
    span = max(1, WINDOW // TOK_DEV) * TOK_DEV
    keys_pad = jnp.concatenate([jnp.zeros((span, HD), keys.dtype), keys])
    values_pad = jnp.concatenate([jnp.zeros((span, HD), values.dtype), values])
    segment_pad = jnp.concatenate([jnp.full((span,), -1, jnp.int32), segment_ids])
    width = span + TOK_DEV

    def block(index):
        start = index * TOK_DEV
        query_block = lax.dynamic_slice_in_dim(queries, start, TOK_DEV, 0)
        key_block = lax.dynamic_slice_in_dim(keys_pad, start, width, 0)
        value_block = lax.dynamic_slice_in_dim(values_pad, start, width, 0)
        query_segment = lax.dynamic_slice_in_dim(segment_ids, start, TOK_DEV, 0)
        key_segment = lax.dynamic_slice_in_dim(segment_pad, start, width, 0)
        distance = span + jnp.arange(TOK_DEV, dtype=jnp.int32)[:, None] - jnp.arange(width, dtype=jnp.int32)[None, :]
        allowed = (query_segment[:, None] == key_segment[None, :]) & (distance >= 0) & (distance < WINDOW)
        scores = low_back(jnp.einsum('qhd,kd->hqk', query_block, key_block, precision=lax.Precision.HIGHEST))
        scores = jnp.where(allowed[None], scores, -1e+30)
        top = lax.optimization_barrier(jnp.max(scores, axis=-1, keepdims=True))
        weights = jnp.exp(scores - top)
        probs = low(weights / lax.optimization_barrier(jnp.sum(weights, axis=-1, keepdims=True)))
        return jnp.einsum('hqk,kd->qhd', probs, value_block, precision=lax.Precision.HIGHEST)
    blocks = lax.map(jax.checkpoint(block), jnp.arange(TOKENS // TOK_DEV, dtype=jnp.int32))
    return blocks.reshape(TOKENS, HEADS * HD)

def layer(params, x, segment_ids, cosine, sine):
    g_attn, w_query, w_key, w_value, g_query, g_key, w_out, g_post, g_ffw, w_gate, w_up, w_down, g_final = params
    normed = low(norm_rows(x, g_attn))
    q_raw = low_back(matmul(normed, w_query)).reshape(TOKENS, HEADS, HD)
    k_raw = low_back(matmul(normed, w_key))
    values = low(low_back(matmul(normed, w_value)))
    queries = low(rotate(norm_rows(q_raw, g_query), cosine[:, None, :], sine[:, None, :]) * HD ** (-0.5))
    keys = low(rotate(norm_rows(k_raw, g_key), cosine, sine))
    context = low_back(low(attention(queries, keys, values, segment_ids)))
    branch = low_back(matmul(context, w_out))
    middle = x + norm_rows(branch, g_post)
    normed_two = low(norm_rows(middle, g_ffw))
    gate = low_back(matmul(normed_two, w_gate))
    up_val = low_back(matmul(normed_two, w_up))
    hidden = low(jax.nn.gelu(gate, approximate=True) * up_val)
    branch_two = low_back(matmul(hidden, w_down))
    return middle + norm_rows(branch_two, g_final)

def reference(layer_input, segment_ids, out_cotangent, attn_norm_gain, query_weight, key_weight, value_weight, query_gain, key_gain, output_weight, attn_post_gain, ffw_norm_gain, gate_weight, up_weight, down_weight, ffw_post_gain):
    place = positions(segment_ids).astype(jnp.float32)
    freq = rope_base ** (-2.0 * jnp.arange(HD // 2, dtype=jnp.float32) / HD)
    theta = place[:, None] * freq[None, :]
    cosine = jnp.cos(theta)
    sine = jnp.sin(theta)
    params = tuple((w.astype(jnp.float32) for w in (attn_norm_gain, query_weight, key_weight, value_weight, query_gain, key_gain, output_weight, attn_post_gain, ffw_norm_gain, gate_weight, up_weight, down_weight, ffw_post_gain)))
    start_x = layer_input.astype(jnp.float32)

    def forward(weights, x):
        return layer(weights, x, segment_ids, cosine, sine)
    result, pull = jax.vjp(forward, params, start_x)
    grads, input_grad = pull(out_cotangent.astype(jnp.float32))
    return (result.astype(jnp.bfloat16), input_grad.astype(jnp.bfloat16), grads[0], grads[1], grads[2], grads[3], grads[4], grads[5], grads[6], grads[7], grads[8], grads[9], grads[10], grads[11], grads[12])
```

```python
import jax
import jax.numpy as jnp
from jax import lax
from jax.experimental import pallas as pl
from jax.experimental.pallas import tpu as pltpu
from jax.sharding import PartitionSpec as P

WINDOW = 512

eps = 1e-06
rope_base = 10000.0
f32 = jnp.float32
bf16 = jnp.bfloat16
BOTH = ("seq", "tensor")


def places():
    return [(z, y, c, x) for z in range(4) for y in range(4) for c in range(2) for x in range(4)]


def number(z, y, c, x):
    return ((z * 4 + y) * 2 + c) * 4 + x


def route(move):
    return [(number(*p), number(*move(*p))) for p in places()]


def round_x(by):
    return route(lambda z, y, c, x: (z, y, c, (x + by) % 4))


def swap_cores():
    return route(lambda z, y, c, x: (z, y, 1 - c, x))


def along_first(flip):
    return route(lambda z, y, c, x: (z, y ^ flip, c, x) if c == 0 else (z ^ flip, y, c, x))


def round_first(by):
    return route(
        lambda z, y, c, x: (z, (y + by) % 4, c, x) if c == 0 else ((z + by) % 4, y, c, x)
    )


def round_second(by):
    return route(
        lambda z, y, c, x: ((z + by) % 4, y, c, x) if c == 0 else (z, (y + by) % 4, c, x)
    )


def send(value, pairs):
    return lax.ppermute(value, BOTH, pairs)


def shifted(value, by):
    pairs = [
        (i * 4 + x, (i + by) * 4 + x) for i in range(32) if 0 <= i + by < 32 for x in range(4)
    ]
    return send(value, pairs)


def pick(parts, index):
    return lax.dynamic_index_in_dim(parts, index, 0, keepdims=False)


def dot(first, second, over):
    return lax.dot_general(
        first, second, (((over[0],), (over[1],)), ((), ())), preferred_element_type=f32
    )


def scatter_sum(parts, index, turn):
    total = pick(parts, index).astype(f32)
    for by in (1, 2, 3):
        total = total + send(pick(parts, (index + by) % 4), turn(by)).astype(f32)
    return total


def gather(part, index, turn):
    whole = jnp.zeros((4, *part.shape), part.dtype)
    whole = lax.dynamic_update_index_in_dim(whole, part, index, 0)
    for by in (1, 2, 3):
        whole = lax.dynamic_update_index_in_dim(
            whole, send(part, turn(by)), (index + 4 - by) % 4, 0
        )
    return whole


def inv_scale(values):
    return lax.rsqrt(jnp.mean(values * values, axis=-1, keepdims=True) + eps)


def norm_back(values, scale, gain, grad):
    unit = values * scale
    weighted = grad * gain
    d_values = scale * (weighted - unit * jnp.mean(weighted * unit, axis=-1, keepdims=True))
    return (d_values, jnp.sum(grad * unit, axis=0))


def rotate(values, cosine, sine):
    half = values.shape[-1] // 2
    first = values[..., :half]
    second = values[..., half:]
    return jnp.concatenate(
        [first * cosine - second * sine, second * cosine + first * sine], axis=-1
    )


def padded(values, rows):
    return jnp.pad(values, ((0, rows - values.shape[0]), (0, 0)))


def tied(*values):
    return lax.optimization_barrier(values)


def weight_kernel(
    hid_own, hid_got, gate_own, gate_got, up_own, up_got, dy_own, dy_got, xn_own, xn_got, *outs
):
    mats = (
        (hid_own, hid_got, dy_own, dy_got),
        (gate_own, gate_got, xn_own, xn_got),
        (up_own, up_got, xn_own, xn_got),
    )
    for group, out in enumerate(outs):
        for index, (left_own, left_got, right_own, right_got) in enumerate(mats):
            total = jnp.dot(left_own[group], right_own[...], preferred_element_type=f32)
            total += jnp.dot(left_got[group], right_got[...], preferred_element_type=f32)
            total = total.astype(bf16)
            out[112 * index : 112 * index + 112] = total[:112]
            out[336 + 112 * index : 448 + 112 * index] = total[112:]


def weight_parts(*arrays):
    width = arrays[-1].shape[1]
    return pl.pallas_call(
        weight_kernel,
        out_shape=[jax.ShapeDtypeStruct((672, width), bf16)] * 4,
        in_specs=[pl.BlockSpec(memory_space=pltpu.VMEM)] * len(arrays),
        out_specs=[pl.BlockSpec(memory_space=pltpu.VMEM)] * 4,
        compiler_params=pltpu.CompilerParams(vmem_limit_bytes=40 * 1024 * 1024),
        cost_estimate=pl.CostEstimate(
            flops=2 * 2688 * 512 * width, bytes_accessed=12_000_000, transcendentals=0
        ),
    )(*arrays)


def local(
    layer_input,
    segment_ids,
    out_cotangent,
    attn_norm_gain,
    query_weight,
    key_weight,
    value_weight,
    query_gain,
    key_gain,
    output_weight,
    attn_post_gain,
    ffw_norm_gain,
    gate_weight,
    up_weight,
    down_weight,
    ffw_post_gain,
):
    tok, width = layer_input.shape
    head_dim = key_weight.shape[1]
    units = down_weight.shape[0]
    block = lax.axis_index("seq")
    lane = lax.axis_index("tensor")
    core = block % 2
    row = (block // 2) % 4
    plane = block // 8
    first = jnp.where(core == 0, row, plane)
    second = jnp.where(core == 0, plane, row)
    quarter_tok = tok // 4

    local_index = jnp.arange(tok, dtype=jnp.int32)
    here = block * tok + local_index
    freq = rope_base ** (-2.0 * jnp.arange(head_dim // 2, dtype=f32) / head_dim)
    theta = here.astype(f32)[:, None] * freq[None, :]
    cosine = jnp.cos(theta)
    sine = jnp.sin(theta)
    scale = head_dim ** (-0.5)

    x_full = layer_input.astype(f32)
    scale_in = inv_scale(x_full)
    normed = (x_full * scale_in * attn_norm_gain).astype(bf16)
    k_raw = jnp.dot(normed, key_weight, preferred_element_type=f32)
    values = jnp.dot(normed, value_weight, preferred_element_type=f32).astype(bf16)
    k_scale = inv_scale(k_raw)
    keys = rotate(k_raw * k_scale * key_gain, cosine, sine).astype(bf16)
    marks = jnp.broadcast_to(segment_ids.astype(bf16)[None, :], (16, tok))
    own_pair = jnp.concatenate([keys, values, marks])
    left_one = shifted(own_pair, 1)
    left_two = shifted(own_pair, 2)
    q_raw = jnp.dot(normed, query_weight, preferred_element_type=f32)
    q_scale = inv_scale(q_raw)
    queries = (rotate(q_raw * q_scale * query_gain, cosine, sine) * scale).astype(bf16)

    weight_half = tok // 2
    own_weight = pick(output_weight.reshape(2, weight_half, width), core)
    got_weight = jnp.stack([send(own_weight, round_x(by)) for by in (1, 2, 3)])
    other_weight = send(got_weight, swap_cores())

    pairs = (left_two, left_one, own_pair)
    keys_all = jnp.concatenate([p[:tok] for p in pairs])
    values_all = jnp.concatenate([p[tok : 2 * tok] for p in pairs])
    key_segment = jnp.concatenate([p[2 * tok] for p in pairs]).astype(jnp.int32)
    key_index = (block - 2) * tok + jnp.arange(3 * tok, dtype=jnp.int32)
    distance = here[:, None] - key_index[None, :]
    allowed = (
        (segment_ids[:, None] == key_segment[None, :])
        & (distance >= 0)
        & (distance < WINDOW)
        & (key_index[None, :] >= 0)
    )
    scores = jnp.where(allowed, dot(queries, keys_all, (1, 1)), -1e30)
    top = jnp.max(scores, axis=-1, keepdims=True)
    weights = jnp.exp(scores - top)
    total = jnp.sum(weights, axis=-1, keepdims=True)
    log_total = top + jnp.log(total)
    probs_low = (weights / total).astype(bf16)
    context = dot(probs_low, values_all, (1, 0)).astype(bf16)

    branch = dot(context, output_weight, (1, 0))
    for by in (1, 2, 3):
        got = send(context, round_x(by))
        mine, theirs = got_weight[by - 1], other_weight[by - 1]
        low = jnp.where(core == 0, mine, theirs)
        high = jnp.where(core == 0, theirs, mine)
        branch = branch + dot(got[:, :weight_half], low, (1, 0))
        branch = branch + dot(got[:, weight_half:], high, (1, 0))
    middle = x_full + branch * inv_scale(branch) * attn_post_gain
    normed_two = (middle * inv_scale(middle) * ffw_norm_gain).astype(bf16)

    gate = dot(gate_weight, normed_two, (0, 1))
    up_val = dot(up_weight, normed_two, (0, 1))
    active, gelu_back = jax.vjp(lambda val: jax.nn.gelu(val, approximate=True), gate)
    hidden = (active * up_val).astype(bf16)

    def halves(values):
        groups = values.reshape(8, units // 8, tok)
        groups = jnp.concatenate([groups[:, :56], groups[:, 48:]], axis=1)
        pieces = groups.reshape(4, 4, 2, 56, tok)
        return (
            lax.dynamic_index_in_dim(pieces, core, 2, keepdims=False),
            lax.dynamic_index_in_dim(pieces, 1 - core, 2, keepdims=False),
        )

    def arranged(values):
        values = jnp.where(core == 0, values.swapaxes(0, 1), values)
        by_first = [pick(values, first ^ flip) for flip in range(4)]
        groups = [
            jnp.stack([by_first[i][2 * stream : 2 * stream + 2] for i in order])
            for stream, order in ((0, (0, 3)), (0, (1, 2)), (1, (0, 1)), (1, (3, 2)))
        ]
        return jnp.stack(groups).reshape(4, 224, tok)

    hidden_own, hidden_give = halves(hidden)
    hidden_got = send(hidden_give, swap_cores())
    normed_two_got = send(normed_two, swap_cores())

    down_part = dot(hidden, down_weight, (0, 0)).astype(bf16).reshape(4, quarter_tok, width)
    branch_two = scatter_sum(down_part, lane, round_x)
    cot = pick(out_cotangent.reshape(4, quarter_tok, width), lane).astype(f32)
    final_scale = inv_scale(branch_two)
    d_branch_two, final_part = norm_back(branch_two, final_scale, ffw_post_gain, cot)
    d_branch_two = gather(d_branch_two.astype(bf16), lane, round_x).reshape(tok, width)
    d_branch_two_got = send(d_branch_two, swap_cores())

    branch_own = pick(branch.reshape(4, quarter_tok, width), lane)
    middle_own = pick(middle.reshape(4, quarter_tok, width), lane)
    out_own = (middle_own + branch_two * final_scale * ffw_post_gain).astype(bf16)

    d_hidden = dot(down_weight, d_branch_two, (1, 1))
    d_gate = gelu_back(d_hidden * up_val)[0].astype(bf16)
    d_up = (d_hidden * active).astype(bf16)
    d_gate_own, d_gate_give = halves(d_gate)
    d_up_own, d_up_give = halves(d_up)
    d_pair_got = send(jnp.stack([d_gate_give, d_up_give]), swap_cores())

    keep_a, give_a, keep_b, give_b = weight_parts(
        *(
            arranged(v)
            for v in (hidden_own, hidden_got, d_gate_own, d_pair_got[0], d_up_own, d_pair_got[1])
        ),
        d_branch_two,
        d_branch_two_got,
        normed_two,
        normed_two_got,
    )
    d_normed_two = (dot(d_gate, gate_weight, (0, 1)) + dot(d_up, up_weight, (0, 1))).astype(bf16)
    d_normed_two, give_a, give_b = tied(d_normed_two, give_a, give_b)
    got_a = send(give_a, along_first(1))
    got_b = send(give_b, along_first(3))

    d_normed_two = scatter_sum(d_normed_two.reshape(4, quarter_tok, width), lane, round_x)
    d_middle, ffw_gain_part = norm_back(
        middle_own, inv_scale(middle_own), ffw_norm_gain, d_normed_two
    )
    d_middle = cot + d_middle
    d_branch, post_part = norm_back(branch_own, inv_scale(branch_own), attn_post_gain, d_middle)
    spread = gather(jnp.stack([d_branch.astype(bf16), out_own]), lane, round_x)
    both_a = keep_a.astype(f32) + got_a.astype(f32)
    both_b = keep_b.astype(f32) + got_b.astype(f32)
    keep_a, give_a = both_a[:336], both_a[336:].astype(bf16)
    keep_b, give_b = both_b[:336], both_b[336:].astype(bf16)
    spread, give_a, give_b, keep_a, keep_b = tied(spread, give_a, give_b, keep_a, keep_b)
    got_a = send(give_a, along_first(3))
    got_b = send(give_b, along_first(1))
    d_branch = spread[:, 0].reshape(tok, width)
    layer_output = spread[:, 1].reshape(tok, width)
    out_grad = dot(context, d_branch, (0, 0)).astype(bf16)
    d_context = dot(d_branch, output_weight, (1, 1)).astype(bf16)
    probs = jnp.exp(jnp.where(allowed, dot(queries, keys_all, (1, 1)), -1e30) - log_total)
    d_probs = dot(d_context, values_all, (1, 1))
    d_scores = (probs * (d_probs - jnp.sum(probs * d_probs, axis=-1, keepdims=True))).astype(bf16)
    d_queries = dot(d_scores, keys_all, (1, 0))
    d_pair = jnp.concatenate(
        [dot(d_scores, queries, (0, 0)), dot(probs_low, d_context, (0, 0))], axis=1
    ).reshape(3, tok, 2 * head_dim)
    d_left = d_pair[:2].astype(bf16)
    fours = jnp.stack([keep_a + got_a.astype(f32), keep_b + got_b.astype(f32)]).astype(bf16)
    fours = fours.reshape(2, 3, 2, 56, width).swapaxes(1, 2).reshape(4, 168, width)
    d_left, fours = tied(d_left, fours)
    mine = scatter_sum(fours, second, round_second).astype(bf16)
    summed = d_pair[2] + shifted(d_left[1], -1).astype(f32) + shifted(d_left[0], -2).astype(f32)

    summed, mine = tied(summed, mine)
    everyone = lax.all_gather(mine, "seq")

    d_q_raw, q_gain_part = norm_back(
        q_raw, q_scale, query_gain, rotate(d_queries * scale, cosine, -sine)
    )
    d_q_raw = d_q_raw.astype(bf16)
    d_k_raw, k_gain_part = norm_back(
        k_raw, k_scale, key_gain, rotate(summed[:, :head_dim], cosine, -sine)
    )
    d_k_raw = d_k_raw.astype(bf16)
    d_values = summed[:, head_dim:].astype(bf16)
    query_part = dot(d_q_raw, normed, (0, 0)).astype(bf16)
    d_normed = (
        dot(d_q_raw, query_weight, (1, 1))
        + dot(d_k_raw, key_weight, (1, 1))
        + dot(d_values, value_weight, (1, 1))
    ).astype(bf16)
    d_kv = jnp.concatenate([d_k_raw, d_values], axis=1).T.reshape(2, 4, head_dim // 4, tok)
    d_kv = d_kv.transpose(1, 2, 0, 3).reshape(4, head_dim // 4, 2 * tok)
    d_both = jnp.concatenate([d_normed.reshape(4, quarter_tok, width), d_kv], axis=2)
    d_both = scatter_sum(d_both, lane, round_x)
    d_normed = d_both[:, :width]
    x_own = pick(x_full.reshape(4, quarter_tok, width), lane)
    d_input, attn_gain_part = norm_back(x_own, inv_scale(x_own), attn_norm_gain, d_normed)
    input_grad = gather((d_middle + d_input).astype(bf16), lane, round_x).reshape(tok, width)

    d_kv = d_both[:, width:].astype(bf16)
    kv_part = jnp.concatenate(
        [dot(d_kv[:, :tok], normed, (1, 0)), dot(d_kv[:, tok:], normed, (1, 0))]
    ).astype(bf16)
    gains = jnp.stack(
        [
            attn_gain_part,
            post_part,
            ffw_gain_part,
            final_part,
            jnp.pad(jnp.concatenate([q_gain_part, k_gain_part]), (0, width - 2 * head_dim)),
        ]
    )
    pack = jnp.concatenate([out_grad, query_part, kv_part, padded(gains, 8).astype(bf16)])
    pack = pack.reshape(2, 324, width)
    pack = pick(pack, core).astype(f32) + send(pick(pack, 1 - core), swap_cores()).astype(f32)
    pack = padded(pack.astype(bf16), 352).reshape(4, 88, width)
    pack = scatter_sum(pack, first, round_first).astype(bf16).reshape(4, 22, width)
    pack = scatter_sum(pack, second, round_second).astype(bf16)
    pack = gather(pack, second, round_second).reshape(88, width)
    pack = gather(pack, first, round_first).reshape(352, width)[:324]
    pack_got = send(pack, swap_cores())
    pack = jnp.concatenate(
        [jnp.where(core == 0, pack, pack_got), jnp.where(core == 0, pack_got, pack)]
    )
    rest = gather(pack[512:], lane, round_x)
    query_grad = pack[256:512].T.astype(f32)
    out_grad = pack[:256].astype(f32)
    key_grad = rest[:, :64].reshape(head_dim, width).T.astype(f32)
    value_grad = rest[:, 64:128].reshape(head_dim, width).T.astype(f32)
    gains = jnp.sum(rest[:, 128:].astype(f32), axis=0)

    everyone = everyone.reshape(8, 4, 3, 56, width)

    def assembled(index):
        rows = everyone[:, :, index].reshape(8, 224, width)
        rows = jnp.concatenate([rows[:, :48], rows[:, 56:]], axis=1)
        return rows.reshape(units, width).astype(f32)

    down_grad, gate_grad, up_grad = (assembled(i) for i in range(3))
    return (
        layer_output,
        input_grad,
        gains[0],
        query_grad,
        key_grad,
        value_grad,
        gains[4, :head_dim],
        gains[4, head_dim : 2 * head_dim],
        out_grad,
        gains[1],
        gains[2],
        gate_grad.T,
        up_grad.T,
        down_grad,
        gains[3],
    )


def solution(mesh):
    rows = P("seq", None)
    return jax.shard_map(
        local,
        mesh=mesh,
        in_specs=(
            rows,
            P("seq"),
            rows,
            P(),
            P(None, "tensor"),
            P(),
            P(),
            P(),
            P(),
            P("tensor", None),
            P(),
            P(),
            P(None, "tensor"),
            P(None, "tensor"),
            P("tensor", None),
            P(),
        ),
        out_specs=(
            rows,
            rows,
            P(),
            P(None, "tensor"),
            P(),
            P(),
            P(),
            P(),
            P("tensor", None),
            P(),
            P(),
            P(None, "tensor"),
            P(None, "tensor"),
            P("tensor", None),
            P(),
        ),
        check_vma=False,
    )
```

```python
import functools

import jax
import jax.numpy as jnp
from jax import lax
from jax.experimental import pallas as pl
from jax.experimental.pallas import tpu as pltpu
from jax.sharding import PartitionSpec as P

WINDOW = 512

eps = 1e-06
rope_base = 10000.0
f32 = jnp.float32
bf16 = jnp.bfloat16
BOTH = ("seq", "tensor")


def places():
    return [(z, y, c, x) for z in range(4) for y in range(4) for c in range(2) for x in range(4)]


def number(z, y, c, x):
    return ((z * 4 + y) * 2 + c) * 4 + x


def route(move):
    return [(number(*p), number(*move(*p))) for p in places()]


def round_x(by):
    return route(lambda z, y, c, x: (z, y, c, (x + by) % 4))


def swap_cores():
    return route(lambda z, y, c, x: (z, y, 1 - c, x))


def along_first(flip):
    return route(lambda z, y, c, x: (z, y ^ flip, c, x) if c == 0 else (z ^ flip, y, c, x))


def round_first(by):
    return route(
        lambda z, y, c, x: (z, (y + by) % 4, c, x) if c == 0 else ((z + by) % 4, y, c, x)
    )


def round_second(by):
    return route(
        lambda z, y, c, x: ((z + by) % 4, y, c, x) if c == 0 else (z, (y + by) % 4, c, x)
    )


def send(value, pairs):
    return lax.ppermute(value, BOTH, pairs)


def shifted(value, by):
    pairs = [
        (i * 4 + x, (i + by) * 4 + x) for i in range(32) if 0 <= i + by < 32 for x in range(4)
    ]
    return send(value, pairs)


def pick(parts, index):
    return lax.dynamic_index_in_dim(parts, index, 0, keepdims=False)


def dot(first, second, over):
    return lax.dot_general(
        first, second, (((over[0],), (over[1],)), ((), ())), preferred_element_type=f32
    )


def scatter_sum(parts, index, turn):
    total = pick(parts, index).astype(f32)
    for by in (1, 2, 3):
        total = total + send(pick(parts, (index + by) % 4), turn(by)).astype(f32)
    return total


def all_sum(part, turn):
    far = part.astype(f32) + send(part, turn(2)).astype(f32)
    return far + (send(part, turn(1)).astype(f32) + send(part, turn(3)).astype(f32))


def gather(part, index, turn):
    whole = jnp.zeros((4, *part.shape), part.dtype)
    whole = lax.dynamic_update_index_in_dim(whole, part, index, 0)
    for by in (1, 2, 3):
        whole = lax.dynamic_update_index_in_dim(
            whole, send(part, turn(by)), (index + 4 - by) % 4, 0
        )
    return whole


def inv_scale(values):
    return lax.rsqrt(jnp.mean(values * values, axis=-1, keepdims=True) + eps)


def norm_back(values, scale, gain, grad):
    unit = values * scale
    weighted = grad * gain
    d_values = scale * (weighted - unit * jnp.mean(weighted * unit, axis=-1, keepdims=True))
    return (d_values, jnp.sum(grad * unit, axis=0))


def rotate(values, cosine, sine):
    half = values.shape[-1] // 2
    first = values[..., :half]
    second = values[..., half:]
    return jnp.concatenate(
        [first * cosine - second * sine, second * cosine + first * sine], axis=-1
    )


def padded(values, rows):
    return jnp.pad(values, ((0, rows - values.shape[0]), (0, 0)))


def tied(*values):
    return lax.optimization_barrier(values)


def weight_kernel(
    hid_own, hid_got, gate_own, gate_got, up_own, up_got, dy_own, dy_got, xn_own, xn_got, *outs
):
    mats = (
        (hid_own, hid_got, dy_own, dy_got),
        (gate_own, gate_got, xn_own, xn_got),
        (up_own, up_got, xn_own, xn_got),
    )
    for group, out in enumerate(outs):
        for index, (left_own, left_got, right_own, right_got) in enumerate(mats):
            total = jnp.dot(left_own[group], right_own[...], preferred_element_type=f32)
            total += jnp.dot(left_got[group], right_got[...], preferred_element_type=f32)
            total = total.astype(bf16)
            out[112 * index : 112 * index + 112] = total[:112]
            out[336 + 112 * index : 448 + 112 * index] = total[112:]


def weight_parts(*arrays):
    width = arrays[-1].shape[1]
    return pl.pallas_call(
        weight_kernel,
        out_shape=[jax.ShapeDtypeStruct((672, width), bf16)] * 4,
        in_specs=[pl.BlockSpec(memory_space=pltpu.VMEM)] * len(arrays),
        out_specs=[pl.BlockSpec(memory_space=pltpu.VMEM)] * 4,
        compiler_params=pltpu.CompilerParams(vmem_limit_bytes=40 * 1024 * 1024),
        cost_estimate=pl.CostEstimate(
            flops=2 * 2688 * 512 * width, bytes_accessed=12_000_000, transcendentals=0
        ),
    )(*arrays)


def place_kernel(rows_ref, *refs, counts, held):
    n = len(counts)
    parts, outs = refs[:n], refs[n + held : n + held + 3]
    stage, sems, tail_sems = refs[-3:]
    slots = stage.shape[0]
    chunks = [(ref, i) for ref, count in zip(parts, counts, strict=True) for i in range(count)]

    def copies(index):
        slot = index % slots
        row = pl.multiple_of(rows_ref[index, 0], 8)
        for mat, out in enumerate(outs):
            yield (
                pltpu.make_async_copy(
                    stage.at[slot, mat, pl.ds(0, 48)],
                    out.at[pl.ds(row, 48)],
                    sems.at[slot, mat],
                ),
                pltpu.make_async_copy(
                    stage.at[slot, mat, pl.ds(48, 8)],
                    out.at[pl.ds(pl.multiple_of(row + 48, 8), 8)],
                    tail_sems.at[slot, mat],
                ),
            )

    def finish(index):
        for most, tail in copies(index):
            most.wait()
            pl.when(rows_ref[index, 1] == 1)(tail.wait)

    for index, (ref, i) in enumerate(chunks):
        if index >= slots:
            finish(index - slots)
        stage[index % slots] = ref[i].astype(f32)
        for most, tail in copies(index):
            most.start()
            pl.when(rows_ref[index, 1] == 1)(tail.start)
    for index in range(max(0, len(chunks) - slots), len(chunks)):
        finish(index)


def placed(rows, parts, outs, units):
    width = parts[0].shape[-1]
    parts = [p.reshape(-1, 3, 56, width) for p in parts]
    slots = 4
    return pl.pallas_call(
        functools.partial(
            place_kernel, counts=tuple(p.shape[0] for p in parts), held=len(outs)
        ),
        out_shape=[jax.ShapeDtypeStruct((units, width), f32)] * 3,
        in_specs=[pl.BlockSpec(memory_space=pltpu.SMEM)]
        + [pl.BlockSpec(memory_space=pltpu.VMEM)] * len(parts)
        + [pl.BlockSpec(memory_space=pl.ANY)] * len(outs),
        out_specs=[pl.BlockSpec(memory_space=pl.ANY)] * 3,
        scratch_shapes=[
            pltpu.VMEM((slots, 3, 56, width), f32),
            pltpu.SemaphoreType.DMA((slots, 3)),
            pltpu.SemaphoreType.DMA((slots, 3)),
        ],
        input_output_aliases={1 + len(parts) + i: i for i in range(len(outs))},
        compiler_params=pltpu.CompilerParams(vmem_limit_bytes=40 * 1024 * 1024),
        cost_estimate=pl.CostEstimate(
            flops=0, bytes_accessed=sum(p.size for p in parts) * 6, transcendentals=0
        ),
    )(rows, *parts, *outs)


def local(
    layer_input,
    segment_ids,
    out_cotangent,
    attn_norm_gain,
    query_weight,
    key_weight,
    value_weight,
    query_gain,
    key_gain,
    output_weight,
    attn_post_gain,
    ffw_norm_gain,
    gate_weight,
    up_weight,
    down_weight,
    ffw_post_gain,
):
    tok, width = layer_input.shape
    head_dim = key_weight.shape[1]
    units = down_weight.shape[0]
    block = lax.axis_index("seq")
    lane = lax.axis_index("tensor")
    core = block % 2
    row = (block // 2) % 4
    plane = block // 8
    first = jnp.where(core == 0, row, plane)
    second = jnp.where(core == 0, plane, row)
    quarter_tok = tok // 4

    local_index = jnp.arange(tok, dtype=jnp.int32)
    here = block * tok + local_index
    freq = rope_base ** (-2.0 * jnp.arange(head_dim // 2, dtype=f32) / head_dim)
    theta = here.astype(f32)[:, None] * freq[None, :]
    cosine = jnp.cos(theta)
    sine = jnp.sin(theta)
    scale = head_dim ** (-0.5)

    x_full = layer_input.astype(f32)
    scale_in = inv_scale(x_full)
    normed = (x_full * scale_in * attn_norm_gain).astype(bf16)
    k_raw = jnp.dot(normed, key_weight, preferred_element_type=f32)
    values = jnp.dot(normed, value_weight, preferred_element_type=f32).astype(bf16)
    k_scale = inv_scale(k_raw)
    keys = rotate(k_raw * k_scale * key_gain, cosine, sine).astype(bf16)
    marks = jnp.broadcast_to(segment_ids.astype(bf16)[None, :], (16, tok))
    own_pair = jnp.concatenate([keys, values, marks])
    left_one = shifted(own_pair, 1)
    left_two = shifted(own_pair, 2)
    q_raw = jnp.dot(normed, query_weight, preferred_element_type=f32)
    q_scale = inv_scale(q_raw)
    queries = (rotate(q_raw * q_scale * query_gain, cosine, sine) * scale).astype(bf16)

    weight_half = tok // 2
    own_weight = pick(output_weight.reshape(2, weight_half, width), core)
    got_weight = [send(own_weight, round_x(by)) for by in (1, 2, 3)]

    pairs = (left_two, left_one, own_pair)
    keys_all = jnp.concatenate([p[:tok] for p in pairs])
    values_all = jnp.concatenate([p[tok : 2 * tok] for p in pairs])
    key_segment = jnp.concatenate([p[2 * tok] for p in pairs]).astype(jnp.int32)
    key_index = (block - 2) * tok + jnp.arange(3 * tok, dtype=jnp.int32)
    distance = here[:, None] - key_index[None, :]
    allowed = (
        (segment_ids[:, None] == key_segment[None, :])
        & (distance >= 0)
        & (distance < WINDOW)
        & (key_index[None, :] >= 0)
    )
    scores = jnp.where(allowed, dot(queries, keys_all, (1, 1)), -1e30)
    top = jnp.max(scores, axis=-1, keepdims=True)
    weights = jnp.exp(scores - top)
    total = jnp.sum(weights, axis=-1, keepdims=True)
    log_total = top + jnp.log(total)
    probs_low = (weights / total).astype(bf16)
    context = dot(probs_low, values_all, (1, 0)).astype(bf16)

    context, *got_weight = tied(context, *got_weight)
    got_context = [send(context, round_x(by)) for by in (1, 2, 3)]
    branch = dot(context, output_weight, (1, 0))
    for got, mine in zip(got_context, got_weight, strict=True):
        theirs = send(mine, swap_cores())
        low = jnp.where(core == 0, mine, theirs)
        high = jnp.where(core == 0, theirs, mine)
        branch = branch + dot(got[:, :weight_half], low, (1, 0))
        branch = branch + dot(got[:, weight_half:], high, (1, 0))
    middle = x_full + branch * inv_scale(branch) * attn_post_gain
    normed_two = (middle * inv_scale(middle) * ffw_norm_gain).astype(bf16)

    gate = dot(gate_weight, normed_two, (0, 1))
    up_val = dot(up_weight, normed_two, (0, 1))
    active, gelu_back = jax.vjp(lambda val: jax.nn.gelu(val, approximate=True), gate)
    hidden = (active * up_val).astype(bf16)

    def halves(values):
        groups = values.reshape(8, units // 8, tok)
        groups = jnp.concatenate([groups[:, :56], groups[:, 48:]], axis=1)
        pieces = groups.reshape(4, 4, 2, 56, tok)
        return (
            lax.dynamic_index_in_dim(pieces, core, 2, keepdims=False),
            lax.dynamic_index_in_dim(pieces, 1 - core, 2, keepdims=False),
        )

    def arranged(values):
        values = jnp.where(core == 0, values.swapaxes(0, 1), values)
        by_first = [pick(values, first ^ flip) for flip in range(4)]
        groups = [
            jnp.stack([by_first[i][2 * stream : 2 * stream + 2] for i in order])
            for stream, order in ((0, (0, 3)), (0, (1, 2)), (1, (0, 1)), (1, (3, 2)))
        ]
        return jnp.stack(groups).reshape(4, 224, tok)

    hidden_own, hidden_give = halves(hidden)
    hidden_got = send(hidden_give, swap_cores())
    normed_two_got = send(normed_two, swap_cores())

    down_part = dot(hidden, down_weight, (0, 0)).astype(bf16).reshape(4, quarter_tok, width)
    branch_two = scatter_sum(down_part, lane, round_x)
    cot = pick(out_cotangent.reshape(4, quarter_tok, width), lane).astype(f32)
    final_scale = inv_scale(branch_two)
    d_branch_two, final_part = norm_back(branch_two, final_scale, ffw_post_gain, cot)
    d_branch_two = gather(d_branch_two.astype(bf16), lane, round_x).reshape(tok, width)
    d_branch_two_got = send(d_branch_two, swap_cores())

    branch_own = pick(branch.reshape(4, quarter_tok, width), lane)
    middle_own = pick(middle.reshape(4, quarter_tok, width), lane)
    out_own = (middle_own + branch_two * final_scale * ffw_post_gain).astype(bf16)

    d_hidden = dot(down_weight, d_branch_two, (1, 1))
    d_gate = gelu_back(d_hidden * up_val)[0].astype(bf16)
    d_up = (d_hidden * active).astype(bf16)
    d_gate_own, d_gate_give = halves(d_gate)
    d_up_own, d_up_give = halves(d_up)
    d_pair_got = send(jnp.stack([d_gate_give, d_up_give]), swap_cores())

    d_normed_two = (dot(d_gate, gate_weight, (0, 1)) + dot(d_up, up_weight, (0, 1))).astype(bf16)
    keep_a, give_a, keep_b, give_b = weight_parts(
        *(
            arranged(v)
            for v in (hidden_own, hidden_got, d_gate_own, d_pair_got[0], d_up_own, d_pair_got[1])
        ),
        d_branch_two,
        d_branch_two_got,
        normed_two,
        normed_two_got,
    )
    got_a = send(give_a, along_first(1))
    got_b = send(give_b, along_first(3))

    d_normed_two = scatter_sum(d_normed_two.reshape(4, quarter_tok, width), lane, round_x)
    d_middle, ffw_gain_part = norm_back(
        middle_own, inv_scale(middle_own), ffw_norm_gain, d_normed_two
    )
    d_middle = cot + d_middle
    d_branch, post_part = norm_back(branch_own, inv_scale(branch_own), attn_post_gain, d_middle)
    d_branch = gather(d_branch.astype(bf16), lane, round_x).reshape(tok, width)

    def added(first, second):
        return (first.astype(f32) + second.astype(f32)).astype(bf16)

    give_a, give_b = added(keep_a[336:], got_a[336:]), added(keep_b[336:], got_b[336:])
    keep_a, keep_b = added(keep_a[:336], got_a[:336]), added(keep_b[:336], got_b[:336])
    d_branch, give_a, give_b = tied(d_branch, give_a, give_b)
    got_a = send(give_a, along_first(3))
    got_b = send(give_b, along_first(1))

    d_context = dot(d_branch, output_weight, (1, 1)).astype(bf16)
    probs = jnp.exp(jnp.where(allowed, dot(queries, keys_all, (1, 1)), -1e30) - log_total)
    d_probs = dot(d_context, values_all, (1, 1))
    d_scores = (probs * (d_probs - jnp.sum(probs * d_probs, axis=-1, keepdims=True))).astype(bf16)
    d_pair = jnp.stack([dot(d_scores, queries, (0, 0)), dot(probs_low, d_context, (0, 0))])
    d_pair = d_pair.reshape(2, 3, tok, head_dim)
    left_near, left_far = d_pair[:, 1].astype(bf16), d_pair[:, 0].astype(bf16)
    fours = jnp.stack([added(keep_a, got_a), added(keep_b, got_b)])
    fours = fours.reshape(2, 3, 2, 56, width).swapaxes(1, 2).reshape(4, 168, width)
    left_near, left_far, fours = tied(left_near, left_far, fours)
    summed = d_pair[:, 2] + shifted(left_near, -1).astype(f32) + shifted(left_far, -2).astype(f32)
    mine = scatter_sum(fours, second, round_second).astype(bf16)
    d_queries = dot(d_scores, keys_all, (1, 0))
    d_q_raw, q_gain_part = norm_back(
        q_raw, q_scale, query_gain, rotate(d_queries * scale, cosine, -sine)
    )
    d_q_raw = d_q_raw.astype(bf16)
    out_part = dot(context, d_branch, (0, 0)).astype(bf16)
    query_part = dot(d_q_raw, normed, (0, 0)).astype(bf16)

    summed, mine = tied(summed, mine)
    quarter = gather(mine, second, round_second)
    d_k_raw, k_gain_part = norm_back(
        k_raw, k_scale, key_gain, rotate(summed[0], cosine, -sine)
    )
    d_k_raw = d_k_raw.astype(bf16)
    d_values = summed[1].astype(bf16)
    d_normed = (
        dot(d_q_raw, query_weight, (1, 1))
        + dot(d_k_raw, key_weight, (1, 1))
        + dot(d_values, value_weight, (1, 1))
    ).astype(bf16)
    d_kv = jnp.concatenate([d_k_raw, d_values], axis=1).T.reshape(2, 4, head_dim // 4, tok)
    d_kv = d_kv.transpose(1, 2, 0, 3).reshape(4, head_dim // 4, 2 * tok)
    d_both = jnp.concatenate([d_normed.reshape(4, quarter_tok, width), d_kv], axis=2)
    d_both, quarter = tied(d_both, quarter)
    near_a = send(quarter, along_first(1))
    near_b = send(quarter, along_first(3))
    other_own = send(quarter, swap_cores())
    d_both = scatter_sum(d_both, lane, round_x)
    d_normed = d_both[:, :width]
    d_kv = d_both[:, width:].astype(bf16)
    x_own = pick(x_full.reshape(4, quarter_tok, width), lane)
    d_input, attn_gain_part = norm_back(x_own, inv_scale(x_own), attn_norm_gain, d_normed)
    ends = gather(jnp.stack([out_own, (d_middle + d_input).astype(bf16)]), lane, round_x)

    kv_part = jnp.concatenate(
        [dot(d_kv[:, :tok], normed, (1, 0)), dot(d_kv[:, tok:], normed, (1, 0))]
    ).astype(bf16)
    gains = jnp.stack(
        [
            attn_gain_part,
            post_part,
            ffw_gain_part,
            final_part,
            jnp.pad(jnp.concatenate([q_gain_part, k_gain_part]), (0, width - 2 * head_dim)),
        ]
    ).astype(bf16)
    rest_part = jnp.concatenate(
        [kv_part.reshape(32, 4, width), jnp.pad(gains[:, None], ((0, 27), (0, 3), (0, 0)))], axis=1
    )
    pack = jnp.stack([out_part, query_part, rest_part.reshape(256, width)])
    pack = pack.reshape(3, 4, 4, 2, 8, width)
    pack_got = send(lax.dynamic_index_in_dim(pack, 1 - core, 3, keepdims=False), swap_cores())
    pack = added(lax.dynamic_index_in_dim(pack, core, 3, keepdims=False), pack_got)
    pack = jnp.where(core == 0, pack.transpose(2, 0, 1, 3, 4), pack.transpose(1, 0, 2, 3, 4))
    pack = scatter_sum(pack, first, round_first).astype(bf16)

    pack, near_a, near_b = tied(pack, near_a, near_b)
    far_a = send(near_b[:2], along_first(1))
    far_b = send(near_a[2:], along_first(3))
    other_a = send(near_a, swap_cores())
    other_b = send(near_b, swap_cores())

    def rows_of(which, firsts):
        along = jnp.stack(firsts)[:, None] + jnp.zeros((1, 4), jnp.int32)
        across = jnp.arange(4, dtype=jnp.int32)[None, :] + jnp.zeros((len(firsts), 1), jnp.int32)
        y = jnp.where(which == 0, along, across).reshape(-1)
        z = jnp.where(which == 0, across, along).reshape(-1)
        start = 216 * (2 * z + y // 2) + 104 * (y % 2) + 48 * which + 8 * which * (y % 2)
        whole = jnp.where((which == 0) & (y % 2 == 0), 0, 1)
        return jnp.stack([start, whole], axis=1).astype(jnp.int32)

    near = jnp.concatenate(
        [
            rows_of(core, [first, first ^ 1, first ^ 3]),
            rows_of(1 - core, [second, second ^ 1, second ^ 3]),
        ]
    )
    grads = placed(near, [quarter, near_a, near_b, other_own, other_a, other_b], [], units)

    pack = all_sum(pack, round_second)
    rest = gather(pack[2].astype(bf16), lane, round_x)
    pack, rest, far_a, far_b, *grads = tied(pack.astype(bf16), rest, far_a, far_b, *grads)
    other_far_a = send(far_a, swap_cores())
    other_far_b = send(far_b, swap_cores())
    pack = jnp.concatenate([pack[:2], rest]).reshape(6, 4, 8, width)
    pack = gather(pack, first, round_first)
    far = jnp.concatenate([rows_of(core, [first ^ 2]), rows_of(1 - core, [second ^ 2])])
    down_grad, gate_grad, up_grad = placed(
        far, [far_a, far_b, other_far_a, other_far_b], grads, units
    )
    pack_got = send(pack, swap_cores())
    even = jnp.where(core == 0, pack, pack_got).transpose(1, 2, 0, 3, 4)
    odd = jnp.where(core == 0, pack_got, pack).transpose(1, 0, 2, 3, 4)
    pack = jnp.stack([even, odd], axis=3)
    out_grad = pack[0].reshape(256, width).astype(f32)
    query_grad = pack[1].reshape(256, width).T.astype(f32)
    rest = pack[2:].reshape(4, 32, 8, width)
    key_value = rest[:, :, :4].reshape(4, 2, head_dim // 4, width)
    key_grad = key_value[:, 0].reshape(head_dim, width).T.astype(f32)
    value_grad = key_value[:, 1].reshape(head_dim, width).T.astype(f32)
    gains = jnp.sum(rest[:, :5, 4].astype(f32), axis=0)
    layer_output = ends[:, 0].reshape(tok, width)
    input_grad = ends[:, 1].reshape(tok, width)
    return (
        layer_output,
        input_grad,
        gains[0],
        query_grad,
        key_grad,
        value_grad,
        gains[4, :head_dim],
        gains[4, head_dim : 2 * head_dim],
        out_grad,
        gains[1],
        gains[2],
        gate_grad.T,
        up_grad.T,
        down_grad,
        gains[3],
    )


def solution(mesh):
    rows = P("seq", None)
    return jax.shard_map(
        local,
        mesh=mesh,
        in_specs=(
            rows,
            P("seq"),
            rows,
            P(),
            P(None, "tensor"),
            P(),
            P(),
            P(),
            P(),
            P("tensor", None),
            P(),
            P(),
            P(None, "tensor"),
            P(None, "tensor"),
            P("tensor", None),
            P(),
        ),
        out_specs=(
            rows,
            rows,
            P(),
            P(None, "tensor"),
            P(),
            P(),
            P(),
            P(),
            P("tensor", None),
            P(),
            P(),
            P(None, "tensor"),
            P(None, "tensor"),
            P("tensor", None),
            P(),
        ),
        check_vma=False,
    )
```

```python
import functools

import jax
import jax.numpy as jnp
from jax import lax
from jax.experimental import pallas as pl
from jax.experimental.pallas import tpu as pltpu
from jax.sharding import PartitionSpec as P

WINDOW = 512

eps = 1e-06
rope_base = 10000.0
f32 = jnp.float32
bf16 = jnp.bfloat16
BOTH = ("seq", "tensor")


def places():
    return [(z, y, c, x) for z in range(4) for y in range(4) for c in range(2) for x in range(4)]


def number(z, y, c, x):
    return ((z * 4 + y) * 2 + c) * 4 + x


def route(move):
    return [(number(*p), number(*move(*p))) for p in places()]


def round_x(by):
    return route(lambda z, y, c, x: (z, y, c, (x + by) % 4))


def swap_cores():
    return route(lambda z, y, c, x: (z, y, 1 - c, x))


def round_first(by):
    return route(
        lambda z, y, c, x: (z, (y + by) % 4, c, x) if c == 0 else ((z + by) % 4, y, c, x)
    )


def round_second(by):
    return route(
        lambda z, y, c, x: ((z + by) % 4, y, c, x) if c == 0 else (z, (y + by) % 4, c, x)
    )


def send(value, pairs):
    return lax.ppermute(value, BOTH, pairs)


def shifted(value, by):
    pairs = [
        (i * 4 + x, (i + by) * 4 + x) for i in range(32) if 0 <= i + by < 32 for x in range(4)
    ]
    return send(value, pairs)


def pick(parts, index):
    return lax.dynamic_index_in_dim(parts, index, 0, keepdims=False)


def dot(first, second, over):
    return lax.dot_general(
        first, second, (((over[0],), (over[1],)), ((), ())), preferred_element_type=f32
    )


def scatter_sum(parts, index, turn):
    total = pick(parts, index).astype(f32)
    for by in (1, 2, 3):
        total = total + send(pick(parts, (index + by) % 4), turn(by)).astype(f32)
    return total


def all_sum(part, turn):
    far = part.astype(f32) + send(part, turn(2)).astype(f32)
    return far + (send(part, turn(1)).astype(f32) + send(part, turn(3)).astype(f32))


def gather(part, index, turn):
    whole = jnp.zeros((4, *part.shape), part.dtype)
    whole = lax.dynamic_update_index_in_dim(whole, part, index, 0)
    for by in (1, 2, 3):
        whole = lax.dynamic_update_index_in_dim(
            whole, send(part, turn(by)), (index + 4 - by) % 4, 0
        )
    return whole


def inv_scale(values):
    return lax.rsqrt(jnp.mean(values * values, axis=-1, keepdims=True) + eps)


def norm_back(values, scale, gain, grad):
    unit = values * scale
    weighted = grad * gain
    d_values = scale * (weighted - unit * jnp.mean(weighted * unit, axis=-1, keepdims=True))
    return (d_values, jnp.sum(grad * unit, axis=0))


def rotate(values, cosine, sine):
    half = values.shape[-1] // 2
    first = values[..., :half]
    second = values[..., half:]
    return jnp.concatenate(
        [first * cosine - second * sine, second * cosine + first * sine], axis=-1
    )


def padded(values, rows):
    return jnp.pad(values, ((0, rows - values.shape[0]), (0, 0)))


def tied(*values):
    return lax.optimization_barrier(values)


def weight_kernel(
    hid_own, hid_got, gate_own, gate_got, up_own, up_got, dy_own, dy_got, xn_own, xn_got, *outs
):
    mats = (
        (hid_own, hid_got, dy_own, dy_got),
        (gate_own, gate_got, xn_own, xn_got),
        (up_own, up_got, xn_own, xn_got),
    )
    for group, out in enumerate(outs):
        for index, (left_own, left_got, right_own, right_got) in enumerate(mats):
            total = jnp.dot(left_own[group], right_own[...], preferred_element_type=f32)
            total += jnp.dot(left_got[group], right_got[...], preferred_element_type=f32)
            out[224 * index : 224 * index + 224] = total.astype(bf16)


def weight_parts(*arrays):
    width = arrays[-1].shape[1]
    return pl.pallas_call(
        weight_kernel,
        out_shape=[jax.ShapeDtypeStruct((672, width), bf16)] * 4,
        in_specs=[pl.BlockSpec(memory_space=pltpu.VMEM)] * len(arrays),
        out_specs=[pl.BlockSpec(memory_space=pltpu.VMEM)] * 4,
        compiler_params=pltpu.CompilerParams(vmem_limit_bytes=40 * 1024 * 1024),
        cost_estimate=pl.CostEstimate(
            flops=2 * 2688 * 512 * width, bytes_accessed=12_000_000, transcendentals=0
        ),
    )(*arrays)


def masks(block, segment, pairs):
    tok = segment.shape[0]
    query = lax.broadcasted_iota(jnp.int32, (tok, tok), 0)
    key = lax.broadcasted_iota(jnp.int32, (tok, tok), 1)
    same = [segment == pair[2 * tok : 2 * tok + 16].astype(f32)[:1] for pair in pairs]
    return (
        same[0] & (key > query) & (block >= 2),
        same[1] & (block >= 1),
        same[2] & (key <= query),
    )


def attend_kernel(block, segment, queries, far, near, own, context, log_total):
    pairs = (far, near, own)
    tok = queries.shape[0]
    allowed = masks(block[0], segment[...], pairs)
    scores = [
        jnp.where(ok, dot(queries[...], pair[:tok], (1, 1)), -1e30)
        for ok, pair in zip(allowed, pairs, strict=True)
    ]
    top = functools.reduce(jnp.maximum, [jnp.max(s, axis=1, keepdims=True) for s in scores])
    weights = [jnp.exp(s - top) for s in scores]
    total = sum(jnp.sum(w, axis=1, keepdims=True) for w in weights)
    context[...] = sum(
        dot((w / total).astype(bf16), pair[tok : 2 * tok], (1, 0))
        for w, pair in zip(weights, pairs, strict=True)
    ).astype(bf16)
    log_total[...] = jnp.broadcast_to(top + jnp.log(total), log_total.shape)


def attend(block, segment, queries, pairs):
    tok, head_dim = queries.shape
    vmem = pl.BlockSpec(memory_space=pltpu.VMEM)
    return pl.pallas_call(
        attend_kernel,
        out_shape=[
            jax.ShapeDtypeStruct((tok, head_dim), bf16),
            jax.ShapeDtypeStruct((tok, 128), f32),
        ],
        in_specs=[pl.BlockSpec(memory_space=pltpu.SMEM)] + [vmem] * 5,
        out_specs=[vmem] * 2,
        cost_estimate=pl.CostEstimate(
            flops=12 * tok * tok * head_dim, bytes_accessed=1_500_000, transcendentals=3 * tok * tok
        ),
    )(block, segment, queries, *pairs)


def attend_back_kernel(
    block, segment, log_total, d_branch, weight, queries, far, near, own, d_queries, d_far, d_near, d_own
):
    pairs = (far, near, own)
    tok = queries.shape[0]
    d_context = dot(d_branch[...], weight[...], (1, 1)).astype(bf16)
    allowed = masks(block[0], segment[...], pairs)
    lse = log_total[:, :1]
    probs, d_probs = [], []
    for ok, pair in zip(allowed, pairs, strict=True):
        scores = jnp.where(ok, dot(queries[...], pair[:tok], (1, 1)), -1e30)
        probs.append(jnp.exp(scores - lse))
        d_probs.append(dot(d_context, pair[tok : 2 * tok], (1, 1)))
    mean = sum(
        jnp.sum(p * d, axis=1, keepdims=True) for p, d in zip(probs, d_probs, strict=True)
    )
    total = None
    for p, d, pair, out in zip(probs, d_probs, pairs, (d_far, d_near, d_own), strict=True):
        d_scores = (p * (d - mean)).astype(bf16)
        part = dot(d_scores, pair[:tok], (1, 0))
        total = part if total is None else total + part
        out[:tok] = dot(d_scores, queries[...], (0, 0)).astype(out.dtype)
        out[tok:] = dot(p.astype(bf16), d_context, (0, 0)).astype(out.dtype)
    d_queries[...] = total


def attend_back(block, segment, log_total, d_branch, weight, queries, pairs):
    tok, head_dim = queries.shape
    vmem = pl.BlockSpec(memory_space=pltpu.VMEM)
    return pl.pallas_call(
        attend_back_kernel,
        out_shape=[
            jax.ShapeDtypeStruct((tok, head_dim), f32),
            jax.ShapeDtypeStruct((2 * tok, head_dim), bf16),
            jax.ShapeDtypeStruct((2 * tok, head_dim), bf16),
            jax.ShapeDtypeStruct((2 * tok, head_dim), f32),
        ],
        in_specs=[pl.BlockSpec(memory_space=pltpu.SMEM)] + [vmem] * 8,
        out_specs=[vmem] * 4,
        cost_estimate=pl.CostEstimate(
            flops=30 * tok * tok * head_dim, bytes_accessed=3_500_000, transcendentals=3 * tok * tok
        ),
    )(block, segment, log_total, d_branch, weight, queries, *pairs)


def place_kernel(where_ref, *refs, turns, held):
    n = len(turns)
    parts, outs = refs[:n], refs[n + held : n + held + 3]
    stage, sems, tail_sems = refs[-3:]
    slots = stage.shape[0]
    core, first, second = where_ref[0], where_ref[1], where_ref[2]
    chunks = [
        (ref, i, other, by)
        for ref, (other, by) in zip(parts, turns, strict=True)
        for i in range(ref.shape[0])
    ]

    def place(index):
        _, across, other, by = chunks[index]
        which = 1 - core if other else core
        along = lax.rem((second if other else first) + 4 - by, 4)
        y = jnp.where(which == 0, along, across)
        z = jnp.where(which == 0, across, along)
        odd = lax.rem(y, 2)
        row = 216 * (2 * z + y // 2) + 104 * odd + 48 * which + 8 * which * odd
        return pl.multiple_of(row, 8), (which == 1) | (odd == 1)

    def copies(index):
        slot = index % slots
        row, whole = place(index)
        for mat, out in enumerate(outs):
            yield (
                pltpu.make_async_copy(
                    stage.at[slot, mat, pl.ds(0, 48)],
                    out.at[pl.ds(row, 48)],
                    sems.at[slot, mat],
                ),
                pltpu.make_async_copy(
                    stage.at[slot, mat, pl.ds(48, 8)],
                    out.at[pl.ds(pl.multiple_of(row + 48, 8), 8)],
                    tail_sems.at[slot, mat],
                ),
                whole,
            )

    def finish(index):
        for most, tail, whole in copies(index):
            most.wait()
            pl.when(whole)(tail.wait)

    for index, (ref, i, _, _) in enumerate(chunks):
        if index >= slots:
            finish(index - slots)
        stage[index % slots] = ref[i].astype(f32)
        for most, tail, whole in copies(index):
            most.start()
            pl.when(whole)(tail.start)
    for index in range(max(0, len(chunks) - slots), len(chunks)):
        finish(index)


def placed(where, parts, outs, units):
    arrays = [p.reshape(-1, 3, 56, p.shape[-1]) for p, _, _ in parts]
    width = arrays[0].shape[-1]
    slots = 4
    return pl.pallas_call(
        functools.partial(
            place_kernel, turns=tuple((other, by) for _, other, by in parts), held=len(outs)
        ),
        out_shape=[jax.ShapeDtypeStruct((units, width), f32)] * 3,
        in_specs=[pl.BlockSpec(memory_space=pltpu.SMEM)]
        + [pl.BlockSpec(memory_space=pltpu.VMEM)] * len(arrays)
        + [pl.BlockSpec(memory_space=pl.ANY)] * len(outs),
        out_specs=[pl.BlockSpec(memory_space=pl.ANY)] * 3,
        scratch_shapes=[
            pltpu.VMEM((slots, 3, 56, width), f32),
            pltpu.SemaphoreType.DMA((slots, 3)),
            pltpu.SemaphoreType.DMA((slots, 3)),
        ],
        input_output_aliases={1 + len(arrays) + i: i for i in range(len(outs))},
        compiler_params=pltpu.CompilerParams(vmem_limit_bytes=40 * 1024 * 1024),
        cost_estimate=pl.CostEstimate(
            flops=0, bytes_accessed=sum(p.size for p in arrays) * 6, transcendentals=0
        ),
    )(where, *arrays, *outs)


def local(
    layer_input,
    segment_ids,
    out_cotangent,
    attn_norm_gain,
    query_weight,
    key_weight,
    value_weight,
    query_gain,
    key_gain,
    output_weight,
    attn_post_gain,
    ffw_norm_gain,
    gate_weight,
    up_weight,
    down_weight,
    ffw_post_gain,
):
    tok, width = layer_input.shape
    head_dim = key_weight.shape[1]
    units = down_weight.shape[0]
    block = lax.axis_index("seq")
    lane = lax.axis_index("tensor")
    core = block % 2
    row = (block // 2) % 4
    plane = block // 8
    first = jnp.where(core == 0, row, plane)
    second = jnp.where(core == 0, plane, row)
    quarter_tok = tok // 4

    local_index = jnp.arange(tok, dtype=jnp.int32)
    here = block * tok + local_index
    freq = rope_base ** (-2.0 * jnp.arange(head_dim // 2, dtype=f32) / head_dim)
    theta = here.astype(f32)[:, None] * freq[None, :]
    cosine = jnp.cos(theta)
    sine = jnp.sin(theta)
    scale = head_dim ** (-0.5)

    x_full = layer_input.astype(f32)
    scale_in = inv_scale(x_full)
    normed = (x_full * scale_in * attn_norm_gain).astype(bf16)
    k_raw = jnp.dot(normed, key_weight, preferred_element_type=f32)
    values = jnp.dot(normed, value_weight, preferred_element_type=f32).astype(bf16)
    k_scale = inv_scale(k_raw)
    keys = rotate(k_raw * k_scale * key_gain, cosine, sine).astype(bf16)
    marks = jnp.broadcast_to(segment_ids.astype(bf16)[None, :], (16, tok))
    own_pair = jnp.concatenate([keys, values, marks])
    left_one = shifted(own_pair, 1)
    left_two = shifted(own_pair, 2)
    q_raw = jnp.dot(normed, query_weight, preferred_element_type=f32)
    q_scale = inv_scale(q_raw)
    queries = (rotate(q_raw * q_scale * query_gain, cosine, sine) * scale).astype(bf16)

    weight_half = tok // 2
    own_weight = pick(output_weight.reshape(2, weight_half, width), core)
    got_weight = [send(own_weight, round_x(by)) for by in (1, 2, 3)]

    pairs = (left_two, left_one, own_pair)
    block_ref = block.astype(jnp.int32).reshape(1)
    segment = segment_ids.astype(f32)[:, None]
    context, log_total = attend(block_ref, segment, queries, pairs)

    got_context = [send(context, round_x(by)) for by in (1, 2, 3)]
    got_context[0], *got_weight = tied(got_context[0], *got_weight)
    own_weights = jnp.concatenate([own_weight, *got_weight])
    other_weights = send(own_weights, swap_cores())

    def columns(which):
        return jnp.concatenate(
            [
                jnp.where(which == 0, c[:, :weight_half], c[:, weight_half:])
                for c in (context, *got_context)
            ],
            axis=1,
        )

    branch = dot(columns(core), own_weights, (1, 0))
    branch = branch + dot(columns(1 - core), other_weights, (1, 0))
    middle = x_full + branch * inv_scale(branch) * attn_post_gain
    normed_two = (middle * inv_scale(middle) * ffw_norm_gain).astype(bf16)

    gate = dot(gate_weight, normed_two, (0, 1))
    up_val = dot(up_weight, normed_two, (0, 1))
    active, gelu_back = jax.vjp(lambda val: jax.nn.gelu(val, approximate=True), gate)
    hidden = (active * up_val).astype(bf16)

    def halves(values):
        groups = values.reshape(8, units // 8, tok)
        groups = jnp.concatenate([groups[:, :56], groups[:, 48:]], axis=1)
        pieces = groups.reshape(4, 4, 2, 56, tok)
        return (
            lax.dynamic_index_in_dim(pieces, core, 2, keepdims=False),
            lax.dynamic_index_in_dim(pieces, 1 - core, 2, keepdims=False),
        )

    def arranged(values):
        values = jnp.where(core == 0, values.swapaxes(0, 1), values)
        return jnp.stack([pick(values, (first + by) % 4) for by in range(4)]).reshape(4, 224, tok)

    hidden_own, hidden_give = halves(hidden)
    hidden_got = send(hidden_give, swap_cores())
    normed_two_got = send(normed_two, swap_cores())

    down_part = dot(hidden, down_weight, (0, 0)).astype(bf16).reshape(4, quarter_tok, width)
    branch_two = scatter_sum(down_part, lane, round_x)
    cot = pick(out_cotangent.reshape(4, quarter_tok, width), lane).astype(f32)
    final_scale = inv_scale(branch_two)
    d_branch_two, final_part = norm_back(branch_two, final_scale, ffw_post_gain, cot)
    d_branch_two = gather(d_branch_two.astype(bf16), lane, round_x).reshape(tok, width)
    d_branch_two_got = send(d_branch_two, swap_cores())

    branch_own = pick(branch.reshape(4, quarter_tok, width), lane)
    middle_own = pick(middle.reshape(4, quarter_tok, width), lane)
    out_own = (middle_own + branch_two * final_scale * ffw_post_gain).astype(bf16)

    d_hidden = dot(down_weight, d_branch_two, (1, 1))
    d_gate = gelu_back(d_hidden * up_val)[0].astype(bf16)
    d_up = (d_hidden * active).astype(bf16)
    d_gate_own, d_gate_give = halves(d_gate)
    d_up_own, d_up_give = halves(d_up)
    d_pair_got = send(jnp.stack([d_gate_give, d_up_give]), swap_cores())

    d_normed_two = (dot(d_gate, gate_weight, (0, 1)) + dot(d_up, up_weight, (0, 1))).astype(bf16)
    kept, *given = weight_parts(
        *(
            arranged(v)
            for v in (hidden_own, hidden_got, d_gate_own, d_pair_got[0], d_up_own, d_pair_got[1])
        ),
        d_branch_two,
        d_branch_two_got,
        normed_two,
        normed_two_got,
    )
    got = [send(part, round_first(by)) for by, part in zip((1, 2, 3), given, strict=True)]

    d_normed_two = scatter_sum(d_normed_two.reshape(4, quarter_tok, width), lane, round_x)
    d_middle, ffw_gain_part = norm_back(
        middle_own, inv_scale(middle_own), ffw_norm_gain, d_normed_two
    )
    d_middle = cot + d_middle
    d_branch, post_part = norm_back(branch_own, inv_scale(branch_own), attn_post_gain, d_middle)
    d_branch = gather(d_branch.astype(bf16), lane, round_x).reshape(tok, width)

    def added(first, second):
        return (first.astype(f32) + second.astype(f32)).astype(bf16)

    d_queries, left_far, left_near, summed = attend_back(
        block_ref, segment, log_total, d_branch, output_weight, queries, pairs
    )
    got_near = shifted(left_near, -1)
    got_far = shifted(left_far, -2)
    got_near, got_far, *got = tied(got_near, got_far, *got)
    fours = kept.astype(f32) + got[0].astype(f32) + (got[1].astype(f32) + got[2].astype(f32))
    fours = fours.astype(bf16).reshape(3, 4, 56, width).swapaxes(0, 1).reshape(4, 168, width)
    mine = pick(fours, second).astype(f32)
    got = [send(pick(fours, (second + by) % 4), round_second(by)) for by in (1, 2, 3)]
    summed = summed + got_near.astype(f32) + got_far.astype(f32)
    d_q_raw, q_gain_part = norm_back(
        q_raw, q_scale, query_gain, rotate(d_queries * scale, cosine, -sine)
    )
    d_q_raw = d_q_raw.astype(bf16)
    out_part = dot(context, d_branch, (0, 0)).astype(bf16)
    query_part = dot(d_q_raw, normed, (0, 0)).astype(bf16)

    d_k_raw, k_gain_part = norm_back(
        k_raw, k_scale, key_gain, rotate(summed[:tok], cosine, -sine)
    )
    d_k_raw = d_k_raw.astype(bf16)
    d_values = summed[tok:].astype(bf16)
    d_normed = (
        dot(d_q_raw, query_weight, (1, 1))
        + dot(d_k_raw, key_weight, (1, 1))
        + dot(d_values, value_weight, (1, 1))
    ).astype(bf16)
    d_kv = jnp.concatenate([d_k_raw, d_values], axis=1).T.reshape(2, 4, head_dim // 4, tok)
    d_kv = d_kv.transpose(1, 2, 0, 3).reshape(4, head_dim // 4, 2 * tok)
    d_both = jnp.concatenate([d_normed.reshape(4, quarter_tok, width), d_kv], axis=2)
    both = pick(d_both, lane).astype(f32)
    got_both = [send(pick(d_both, (lane + by) % 4), round_x(by)) for by in (1, 2, 3)]
    *got_both, got[0], got[1], got[2] = tied(*got_both, *got)
    mine = (mine + got[0].astype(f32) + (got[1].astype(f32) + got[2].astype(f32))).astype(bf16)
    got = [send(mine, round_second(by)) for by in (1, 2, 3)]
    for part in got_both:
        both = both + part.astype(f32)
    d_both = both
    d_normed = d_both[:, :width]
    d_kv = d_both[:, width:].astype(bf16)
    x_own = pick(x_full.reshape(4, quarter_tok, width), lane)
    d_input, attn_gain_part = norm_back(x_own, inv_scale(x_own), attn_norm_gain, d_normed)
    ends = gather(jnp.stack([out_own, (d_middle + d_input).astype(bf16)]), lane, round_x)

    kv_part = jnp.concatenate(
        [dot(d_kv[:, :tok], normed, (1, 0)), dot(d_kv[:, tok:], normed, (1, 0))]
    ).astype(bf16)
    gains = jnp.stack(
        [
            attn_gain_part,
            post_part,
            ffw_gain_part,
            final_part,
            jnp.pad(jnp.concatenate([q_gain_part, k_gain_part]), (0, width - 2 * head_dim)),
        ]
    ).astype(bf16)
    rest_part = jnp.concatenate(
        [kv_part.reshape(32, 4, width), jnp.pad(gains[:, None], ((0, 27), (0, 3), (0, 0)))], axis=1
    )
    pack = jnp.stack([out_part, query_part, rest_part.reshape(256, width)])
    pack = pack.reshape(3, 4, 4, 2, 8, width)
    pack_got = send(lax.dynamic_index_in_dim(pack, 1 - core, 3, keepdims=False), swap_cores())
    pack_got, *got = tied(pack_got, *got)
    quarter = jnp.zeros((4, *mine.shape), bf16)
    quarter = lax.dynamic_update_index_in_dim(quarter, mine, second, 0)
    for by, part in zip((1, 2, 3), got, strict=True):
        quarter = lax.dynamic_update_index_in_dim(quarter, part, (second + 4 - by) % 4, 0)
    turned = [send(quarter, round_first(by)) for by in (1, 2, 3)]
    other = send(quarter, swap_cores())
    pack = added(lax.dynamic_index_in_dim(pack, core, 3, keepdims=False), pack_got)
    pack = jnp.where(core == 0, pack.transpose(2, 0, 1, 3, 4), pack.transpose(1, 0, 2, 3, 4))
    pack = scatter_sum(pack, first, round_first).astype(bf16)
    pack, turned[0] = tied(pack, turned[0])
    pack = all_sum(pack, round_second).astype(bf16)
    where = jnp.stack([core, first, second]).astype(jnp.int32)
    grads = placed(where, [(quarter, False, 0), (other, True, 0)], [], units)
    pack, *grads = tied(pack, *grads)
    rest = gather(pack[2], lane, round_x)
    rest, pack, *turned = tied(rest, pack, *turned)
    others = [send(part, swap_cores()) for part in turned]
    pack = jnp.concatenate([pack[:2], rest]).reshape(6, 4, 8, width)
    pack = gather(pack, first, round_first)
    grads = placed(
        where, [(part, False, by) for by, part in zip((1, 2, 3), turned, strict=True)], grads, units
    )
    down_grad, gate_grad, up_grad = placed(
        where, [(part, True, by) for by, part in zip((1, 2, 3), others, strict=True)], grads, units
    )
    pack_got = send(pack, swap_cores())
    even = jnp.where(core == 0, pack, pack_got).transpose(1, 2, 0, 3, 4)
    odd = jnp.where(core == 0, pack_got, pack).transpose(1, 0, 2, 3, 4)
    pack = jnp.stack([even, odd], axis=3)
    out_grad = pack[0].reshape(256, width).astype(f32)
    query_grad = pack[1].reshape(256, width).T.astype(f32)
    rest = pack[2:].reshape(4, 32, 8, width)
    key_value = rest[:, :, :4].reshape(4, 2, head_dim // 4, width)
    key_grad = key_value[:, 0].reshape(head_dim, width).T.astype(f32)
    value_grad = key_value[:, 1].reshape(head_dim, width).T.astype(f32)
    gains = jnp.sum(rest[:, :5, 4].astype(f32), axis=0)
    layer_output = ends[:, 0].reshape(tok, width)
    input_grad = ends[:, 1].reshape(tok, width)
    return (
        layer_output,
        input_grad,
        gains[0],
        query_grad,
        key_grad,
        value_grad,
        gains[4, :head_dim],
        gains[4, head_dim : 2 * head_dim],
        out_grad,
        gains[1],
        gains[2],
        gate_grad.T,
        up_grad.T,
        down_grad,
        gains[3],
    )


def solution(mesh):
    rows = P("seq", None)
    return jax.shard_map(
        local,
        mesh=mesh,
        in_specs=(
            rows,
            P("seq"),
            rows,
            P(),
            P(None, "tensor"),
            P(),
            P(),
            P(),
            P(),
            P("tensor", None),
            P(),
            P(),
            P(None, "tensor"),
            P(None, "tensor"),
            P("tensor", None),
            P(),
        ),
        out_specs=(
            rows,
            rows,
            P(),
            P(None, "tensor"),
            P(),
            P(),
            P(),
            P(),
            P("tensor", None),
            P(),
            P(),
            P(None, "tensor"),
            P(None, "tensor"),
            P("tensor", None),
            P(),
        ),
        check_vma=False,
    )
```

```python
import functools

import jax
import jax.numpy as jnp
from jax import lax
from jax.experimental import pallas as pl
from jax.experimental.pallas import tpu as pltpu
from jax.sharding import PartitionSpec as P

WINDOW = 512

eps = 1e-06
rope_base = 10000.0
f32 = jnp.float32
bf16 = jnp.bfloat16
BOTH = ("seq", "tensor")


def places():
    return [(z, y, c, x) for z in range(4) for y in range(4) for c in range(2) for x in range(4)]


def number(z, y, c, x):
    return ((z * 4 + y) * 2 + c) * 4 + x


def route(move):
    return [(number(*p), number(*move(*p))) for p in places()]


def round_x(by):
    return route(lambda z, y, c, x: (z, y, c, (x + by) % 4))


def swap_cores():
    return route(lambda z, y, c, x: (z, y, 1 - c, x))


def round_first(by):
    return route(
        lambda z, y, c, x: (z, (y + by) % 4, c, x) if c == 0 else ((z + by) % 4, y, c, x)
    )


def round_second(by):
    return route(
        lambda z, y, c, x: ((z + by) % 4, y, c, x) if c == 0 else (z, (y + by) % 4, c, x)
    )


def send(value, pairs):
    return lax.ppermute(value, BOTH, pairs)


def shifted(value, by):
    pairs = [
        (i * 4 + x, (i + by) * 4 + x) for i in range(32) if 0 <= i + by < 32 for x in range(4)
    ]
    return send(value, pairs)


def pick(parts, index):
    return lax.dynamic_index_in_dim(parts, index, 0, keepdims=False)


def dot(first, second, over):
    return lax.dot_general(
        first, second, (((over[0],), (over[1],)), ((), ())), preferred_element_type=f32
    )


def scatter_sum(parts, index, turn):
    total = pick(parts, index).astype(f32)
    for by in (1, 2, 3):
        total = total + send(pick(parts, (index + by) % 4), turn(by)).astype(f32)
    return total


def all_sum(part, turn):
    far = part.astype(f32) + send(part, turn(2)).astype(f32)
    return far + (send(part, turn(1)).astype(f32) + send(part, turn(3)).astype(f32))


def gather(part, index, turn):
    whole = jnp.zeros((4, *part.shape), part.dtype)
    whole = lax.dynamic_update_index_in_dim(whole, part, index, 0)
    for by in (1, 2, 3):
        whole = lax.dynamic_update_index_in_dim(
            whole, send(part, turn(by)), (index + 4 - by) % 4, 0
        )
    return whole


def inv_scale(values):
    return lax.rsqrt(jnp.mean(values * values, axis=-1, keepdims=True) + eps)


def norm_back(values, scale, gain, grad):
    unit = values * scale
    weighted = grad * gain
    d_values = scale * (weighted - unit * jnp.mean(weighted * unit, axis=-1, keepdims=True))
    return (d_values, jnp.sum(grad * unit, axis=0))


def rotate(values, cosine, sine):
    half = values.shape[-1] // 2
    first = values[..., :half]
    second = values[..., half:]
    return jnp.concatenate(
        [first * cosine - second * sine, second * cosine + first * sine], axis=-1
    )


def padded(values, rows):
    return jnp.pad(values, ((0, rows - values.shape[0]), (0, 0)))


def tied(*values):
    return lax.optimization_barrier(values)


def weight_kernel(
    hid_own, hid_got, gate_own, gate_got, up_own, up_got, dy_own, dy_got, xn_own, xn_got, *outs
):
    mats = (
        (hid_own, hid_got, dy_own, dy_got),
        (gate_own, gate_got, xn_own, xn_got),
        (up_own, up_got, xn_own, xn_got),
    )
    for group, out in enumerate(outs):
        for index, (left_own, left_got, right_own, right_got) in enumerate(mats):
            total = jnp.dot(left_own[group], right_own[...], preferred_element_type=f32)
            total += jnp.dot(left_got[group], right_got[...], preferred_element_type=f32)
            out[224 * index : 224 * index + 224] = total.astype(bf16)


def weight_parts(*arrays):
    width = arrays[-1].shape[1]
    return pl.pallas_call(
        weight_kernel,
        out_shape=[jax.ShapeDtypeStruct((672, width), bf16)] * 4,
        in_specs=[pl.BlockSpec(memory_space=pltpu.VMEM)] * len(arrays),
        out_specs=[pl.BlockSpec(memory_space=pltpu.VMEM)] * 4,
        compiler_params=pltpu.CompilerParams(vmem_limit_bytes=40 * 1024 * 1024),
        cost_estimate=pl.CostEstimate(
            flops=2 * 2688 * 512 * width, bytes_accessed=12_000_000, transcendentals=0
        ),
    )(*arrays)


def masks(block, segment, pairs):
    tok = segment.shape[0]
    query = lax.broadcasted_iota(jnp.int32, (tok, tok), 0)
    key = lax.broadcasted_iota(jnp.int32, (tok, tok), 1)
    same = [segment == pair[2 * tok : 2 * tok + 16].astype(f32)[:1] for pair in pairs]
    return (
        same[0] & (key > query) & (block >= 2),
        same[1] & (block >= 1),
        same[2] & (key <= query),
    )


def attend_kernel(block, segment, queries, far, near, own, context, log_total):
    pairs = (far, near, own)
    tok = queries.shape[0]
    allowed = masks(block[0], segment[...], pairs)
    scores = [
        jnp.where(ok, dot(queries[...], pair[:tok], (1, 1)), -1e30)
        for ok, pair in zip(allowed, pairs, strict=True)
    ]
    top = functools.reduce(jnp.maximum, [jnp.max(s, axis=1, keepdims=True) for s in scores])
    weights = [jnp.exp(s - top) for s in scores]
    total = sum(jnp.sum(w, axis=1, keepdims=True) for w in weights)
    context[...] = sum(
        dot((w / total).astype(bf16), pair[tok : 2 * tok], (1, 0))
        for w, pair in zip(weights, pairs, strict=True)
    ).astype(bf16)
    log_total[...] = jnp.broadcast_to(top + jnp.log(total), log_total.shape)


def attend(block, segment, queries, pairs):
    tok, head_dim = queries.shape
    vmem = pl.BlockSpec(memory_space=pltpu.VMEM)
    return pl.pallas_call(
        attend_kernel,
        out_shape=[
            jax.ShapeDtypeStruct((tok, head_dim), bf16),
            jax.ShapeDtypeStruct((tok, 128), f32),
        ],
        in_specs=[pl.BlockSpec(memory_space=pltpu.SMEM)] + [vmem] * 5,
        out_specs=[vmem] * 2,
        cost_estimate=pl.CostEstimate(
            flops=12 * tok * tok * head_dim, bytes_accessed=1_500_000, transcendentals=3 * tok * tok
        ),
    )(block, segment, queries, *pairs)


def attend_back_kernel(
    block, segment, log_total, d_branch, weight, queries, far, near, own, d_queries, d_far, d_near, d_own
):
    pairs = (far, near, own)
    tok = queries.shape[0]
    d_context = dot(d_branch[...], weight[...], (1, 1)).astype(bf16)
    allowed = masks(block[0], segment[...], pairs)
    lse = log_total[:, :1]
    probs, d_probs = [], []
    for ok, pair in zip(allowed, pairs, strict=True):
        scores = jnp.where(ok, dot(queries[...], pair[:tok], (1, 1)), -1e30)
        probs.append(jnp.exp(scores - lse))
        d_probs.append(dot(d_context, pair[tok : 2 * tok], (1, 1)))
    mean = sum(
        jnp.sum(p * d, axis=1, keepdims=True) for p, d in zip(probs, d_probs, strict=True)
    )
    total = None
    for p, d, pair, out in zip(probs, d_probs, pairs, (d_far, d_near, d_own), strict=True):
        d_scores = (p * (d - mean)).astype(bf16)
        part = dot(d_scores, pair[:tok], (1, 0))
        total = part if total is None else total + part
        out[:tok] = dot(d_scores, queries[...], (0, 0)).astype(out.dtype)
        out[tok:] = dot(p.astype(bf16), d_context, (0, 0)).astype(out.dtype)
    d_queries[...] = total


def attend_back(block, segment, log_total, d_branch, weight, queries, pairs):
    tok, head_dim = queries.shape
    vmem = pl.BlockSpec(memory_space=pltpu.VMEM)
    return pl.pallas_call(
        attend_back_kernel,
        out_shape=[
            jax.ShapeDtypeStruct((tok, head_dim), f32),
            jax.ShapeDtypeStruct((2 * tok, head_dim), bf16),
            jax.ShapeDtypeStruct((2 * tok, head_dim), bf16),
            jax.ShapeDtypeStruct((2 * tok, head_dim), f32),
        ],
        in_specs=[pl.BlockSpec(memory_space=pltpu.SMEM)] + [vmem] * 8,
        out_specs=[vmem] * 4,
        cost_estimate=pl.CostEstimate(
            flops=30 * tok * tok * head_dim, bytes_accessed=3_500_000, transcendentals=3 * tok * tok
        ),
    )(block, segment, log_total, d_branch, weight, queries, *pairs)


def place_kernel(chunks, *outs):
    for mat, out in enumerate(outs):
        out[:48] = chunks[0, mat, :48].astype(f32)
        for index in (1, 2, 3):
            out[56 * index - 8 : 56 * index + 48] = chunks[index, mat].astype(f32)


def placed(chunks, units):
    width = chunks.shape[-1]
    return pl.pallas_call(
        place_kernel,
        grid=(8,),
        out_shape=[jax.ShapeDtypeStruct((units, width), f32)] * 3,
        in_specs=[pl.BlockSpec((4, 3, 56, width), lambda i: (i, 0, 0, 0))],
        out_specs=[pl.BlockSpec((units // 8, width), lambda i: (i, 0))] * 3,
        compiler_params=pltpu.CompilerParams(vmem_limit_bytes=40 * 1024 * 1024),
        cost_estimate=pl.CostEstimate(
            flops=0, bytes_accessed=chunks.size * 6, transcendentals=0
        ),
    )(chunks)


def local(
    layer_input,
    segment_ids,
    out_cotangent,
    attn_norm_gain,
    query_weight,
    key_weight,
    value_weight,
    query_gain,
    key_gain,
    output_weight,
    attn_post_gain,
    ffw_norm_gain,
    gate_weight,
    up_weight,
    down_weight,
    ffw_post_gain,
):
    tok, width = layer_input.shape
    head_dim = key_weight.shape[1]
    units = down_weight.shape[0]
    block = lax.axis_index("seq")
    lane = lax.axis_index("tensor")
    core = block % 2
    row = (block // 2) % 4
    plane = block // 8
    first = jnp.where(core == 0, row, plane)
    second = jnp.where(core == 0, plane, row)
    quarter_tok = tok // 4

    local_index = jnp.arange(tok, dtype=jnp.int32)
    here = block * tok + local_index
    freq = rope_base ** (-2.0 * jnp.arange(head_dim // 2, dtype=f32) / head_dim)
    theta = here.astype(f32)[:, None] * freq[None, :]
    cosine = jnp.cos(theta)
    sine = jnp.sin(theta)
    scale = head_dim ** (-0.5)

    x_full = layer_input.astype(f32)
    scale_in = inv_scale(x_full)
    normed = (x_full * scale_in * attn_norm_gain).astype(bf16)
    k_raw = jnp.dot(normed, key_weight, preferred_element_type=f32)
    values = jnp.dot(normed, value_weight, preferred_element_type=f32).astype(bf16)
    k_scale = inv_scale(k_raw)
    keys = rotate(k_raw * k_scale * key_gain, cosine, sine).astype(bf16)
    marks = jnp.broadcast_to(segment_ids.astype(bf16)[None, :], (16, tok))
    own_pair = jnp.concatenate([keys, values, marks])
    left_one = shifted(own_pair, 1)
    left_two = shifted(own_pair, 2)
    q_raw = jnp.dot(normed, query_weight, preferred_element_type=f32)
    q_scale = inv_scale(q_raw)
    queries = (rotate(q_raw * q_scale * query_gain, cosine, sine) * scale).astype(bf16)

    weight_half = tok // 2
    own_weight = pick(output_weight.reshape(2, weight_half, width), core)
    got_weight = [send(own_weight, round_x(by)) for by in (1, 2, 3)]

    pairs = (left_two, left_one, own_pair)
    block_ref = block.astype(jnp.int32).reshape(1)
    segment = segment_ids.astype(f32)[:, None]
    context, log_total = attend(block_ref, segment, queries, pairs)

    got_context = [send(context, round_x(by)) for by in (1, 2, 3)]
    *got_context, got_weight[0], got_weight[1], got_weight[2] = tied(*got_context, *got_weight)
    own_weights = jnp.concatenate([own_weight, *got_weight])
    other_weights = send(own_weights, swap_cores())

    def columns(which):
        return jnp.concatenate(
            [
                jnp.where(which == 0, c[:, :weight_half], c[:, weight_half:])
                for c in (context, *got_context)
            ],
            axis=1,
        )

    branch = dot(columns(core), own_weights, (1, 0))
    branch = branch + dot(columns(1 - core), other_weights, (1, 0))
    middle = x_full + branch * inv_scale(branch) * attn_post_gain
    normed_two = (middle * inv_scale(middle) * ffw_norm_gain).astype(bf16)

    gate = dot(gate_weight, normed_two, (0, 1))
    up_val = dot(up_weight, normed_two, (0, 1))
    active, gelu_back = jax.vjp(lambda val: jax.nn.gelu(val, approximate=True), gate)
    hidden = (active * up_val).astype(bf16)

    def halves(values):
        groups = values.reshape(8, units // 8, tok)
        groups = jnp.concatenate([groups[:, :56], groups[:, 48:]], axis=1)
        pieces = groups.reshape(4, 4, 2, 56, tok)
        return (
            lax.dynamic_index_in_dim(pieces, core, 2, keepdims=False),
            lax.dynamic_index_in_dim(pieces, 1 - core, 2, keepdims=False),
        )

    def arranged(values):
        values = jnp.where(core == 0, values.swapaxes(0, 1), values)
        return jnp.stack([pick(values, (first + by) % 4) for by in range(4)]).reshape(4, 224, tok)

    hidden_own, hidden_give = halves(hidden)
    hidden_got = send(hidden_give, swap_cores())
    normed_two_got = send(normed_two, swap_cores())

    down_part = dot(hidden, down_weight, (0, 0)).astype(bf16).reshape(4, quarter_tok, width)
    branch_two = scatter_sum(down_part, lane, round_x)
    cot = pick(out_cotangent.reshape(4, quarter_tok, width), lane).astype(f32)
    final_scale = inv_scale(branch_two)
    d_branch_two, final_part = norm_back(branch_two, final_scale, ffw_post_gain, cot)
    d_branch_two = gather(d_branch_two.astype(bf16), lane, round_x).reshape(tok, width)
    d_branch_two_got = send(d_branch_two, swap_cores())

    branch_own = pick(branch.reshape(4, quarter_tok, width), lane)
    middle_own = pick(middle.reshape(4, quarter_tok, width), lane)
    out_own = (middle_own + branch_two * final_scale * ffw_post_gain).astype(bf16)

    d_hidden = dot(down_weight, d_branch_two, (1, 1))
    d_gate = gelu_back(d_hidden * up_val)[0].astype(bf16)
    d_up = (d_hidden * active).astype(bf16)
    d_gate_own, d_gate_give = halves(d_gate)
    d_up_own, d_up_give = halves(d_up)
    d_pair_got = send(jnp.stack([d_gate_give, d_up_give]), swap_cores())

    d_normed_two = (dot(d_gate, gate_weight, (0, 1)) + dot(d_up, up_weight, (0, 1))).astype(bf16)
    kept, *given = weight_parts(
        *(
            arranged(v)
            for v in (hidden_own, hidden_got, d_gate_own, d_pair_got[0], d_up_own, d_pair_got[1])
        ),
        d_branch_two,
        d_branch_two_got,
        normed_two,
        normed_two_got,
    )
    got = [send(part, round_first(by)) for by, part in zip((1, 2, 3), given, strict=True)]

    d_normed_two = d_normed_two.reshape(4, quarter_tok, width)
    got_normed = [
        send(pick(d_normed_two, (lane + by) % 4), round_x(by)) for by in (1, 2, 3)
    ]
    *got_normed, kept = tied(*got_normed, kept)
    d_normed_two = pick(d_normed_two, lane).astype(f32)
    for part in got_normed:
        d_normed_two = d_normed_two + part.astype(f32)
    d_middle, ffw_gain_part = norm_back(
        middle_own, inv_scale(middle_own), ffw_norm_gain, d_normed_two
    )
    d_middle = cot + d_middle
    d_branch, post_part = norm_back(branch_own, inv_scale(branch_own), attn_post_gain, d_middle)
    d_branch = gather(d_branch.astype(bf16), lane, round_x).reshape(tok, width)
    d_branch, got[0], got[2] = tied(d_branch, got[0], got[2])

    def added(first, second):
        return (first.astype(f32) + second.astype(f32)).astype(bf16)

    d_queries, left_far, left_near, summed = attend_back(
        block_ref, segment, log_total, d_branch, output_weight, queries, pairs
    )
    got_near = shifted(left_near, -1)
    got_far = shifted(left_far, -2)
    got_near, got_far, *got = tied(got_near, got_far, *got)
    fours = kept.astype(f32) + got[0].astype(f32) + (got[1].astype(f32) + got[2].astype(f32))
    fours = fours.astype(bf16).reshape(3, 4, 56, width).swapaxes(0, 1).reshape(4, 168, width)
    mine = pick(fours, second).astype(f32)
    got = [send(pick(fours, (second + by) % 4), round_second(by)) for by in (1, 2, 3)]
    summed = summed + got_near.astype(f32) + got_far.astype(f32)
    d_q_raw, q_gain_part = norm_back(
        q_raw, q_scale, query_gain, rotate(d_queries * scale, cosine, -sine)
    )
    d_q_raw = d_q_raw.astype(bf16)
    out_part = dot(context, d_branch, (0, 0)).astype(bf16)
    query_part = dot(d_q_raw, normed, (0, 0)).astype(bf16)

    d_k_raw, k_gain_part = norm_back(
        k_raw, k_scale, key_gain, rotate(summed[:tok], cosine, -sine)
    )
    d_k_raw = d_k_raw.astype(bf16)
    d_values = summed[tok:].astype(bf16)
    d_normed = (
        dot(d_q_raw, query_weight, (1, 1))
        + dot(d_k_raw, key_weight, (1, 1))
        + dot(d_values, value_weight, (1, 1))
    ).astype(bf16)
    d_kv = jnp.concatenate([d_k_raw, d_values], axis=1).T.reshape(2, 4, head_dim // 4, tok)
    d_kv = d_kv.transpose(1, 2, 0, 3).reshape(4, head_dim // 4, 2 * tok)
    d_both = jnp.concatenate([d_normed.reshape(4, quarter_tok, width), d_kv], axis=2)
    both = pick(d_both, lane).astype(f32)
    got_both = [send(pick(d_both, (lane + by) % 4), round_x(by)) for by in (1, 2, 3)]
    *got_both, got[0], got[1], got[2] = tied(*got_both, *got)
    mine = (mine + got[0].astype(f32) + (got[1].astype(f32) + got[2].astype(f32))).astype(bf16)
    everyone = lax.all_gather(mine, "seq")
    for part in got_both:
        both = both + part.astype(f32)
    d_both = both
    d_normed = d_both[:, :width]
    d_kv = d_both[:, width:].astype(bf16)
    x_own = pick(x_full.reshape(4, quarter_tok, width), lane)
    d_input, attn_gain_part = norm_back(x_own, inv_scale(x_own), attn_norm_gain, d_normed)
    ends = gather(jnp.stack([out_own, (d_middle + d_input).astype(bf16)]), lane, round_x)

    kv_part = jnp.concatenate(
        [dot(d_kv[:, :tok], normed, (1, 0)), dot(d_kv[:, tok:], normed, (1, 0))]
    ).astype(bf16)
    gains = jnp.stack(
        [
            attn_gain_part,
            post_part,
            ffw_gain_part,
            final_part,
            jnp.pad(jnp.concatenate([q_gain_part, k_gain_part]), (0, width - 2 * head_dim)),
        ]
    ).astype(bf16)
    rest_part = jnp.concatenate([kv_part, padded(gains, 128)])
    pack = jnp.stack([out_part, query_part, rest_part])
    pack = pack.reshape(3, 4, 4, 2, 8, width)
    pack_got = send(lax.dynamic_index_in_dim(pack, 1 - core, 3, keepdims=False), swap_cores())
    pack = added(lax.dynamic_index_in_dim(pack, core, 3, keepdims=False), pack_got)
    pack = jnp.where(core == 0, pack.transpose(2, 0, 1, 3, 4), pack.transpose(1, 0, 2, 3, 4))
    pack = scatter_sum(pack, first, round_first).astype(bf16)
    pack = lax.optimization_barrier(pack)
    pack = all_sum(pack, round_second).astype(bf16)
    rest = gather(pack[2], lane, round_x)
    pack = jnp.concatenate([pack[:2], rest]).reshape(6, 4, 8, width)
    pack = gather(pack, first, round_first)
    pack_got = send(pack, swap_cores())
    down_grad, gate_grad, up_grad = placed(everyone.reshape(32, 3, 56, width), units)
    even = jnp.where(core == 0, pack, pack_got).transpose(1, 2, 0, 3, 4)
    odd = jnp.where(core == 0, pack_got, pack).transpose(1, 0, 2, 3, 4)
    pack = jnp.stack([even, odd], axis=3)
    out_grad = pack[0].reshape(256, width).astype(f32)
    query_grad = pack[1].reshape(256, width).T.astype(f32)
    rest = pack[2:].reshape(4, 256, width)
    key_grad = rest[:, :64].reshape(head_dim, width).T.astype(f32)
    value_grad = rest[:, 64:128].reshape(head_dim, width).T.astype(f32)
    gains = jnp.sum(rest[:, 128:136].astype(f32), axis=0)
    layer_output = ends[:, 0].reshape(tok, width)
    input_grad = ends[:, 1].reshape(tok, width)
    return (
        layer_output,
        input_grad,
        gains[0],
        query_grad,
        key_grad,
        value_grad,
        gains[4, :head_dim],
        gains[4, head_dim : 2 * head_dim],
        out_grad,
        gains[1],
        gains[2],
        gate_grad.T,
        up_grad.T,
        down_grad,
        gains[3],
    )


def solution(mesh):
    rows = P("seq", None)
    return jax.shard_map(
        local,
        mesh=mesh,
        in_specs=(
            rows,
            P("seq"),
            rows,
            P(),
            P(None, "tensor"),
            P(),
            P(),
            P(),
            P(),
            P("tensor", None),
            P(),
            P(),
            P(None, "tensor"),
            P(None, "tensor"),
            P("tensor", None),
            P(),
        ),
        out_specs=(
            rows,
            rows,
            P(),
            P(None, "tensor"),
            P(),
            P(),
            P(),
            P(),
            P("tensor", None),
            P(),
            P(),
            P(None, "tensor"),
            P(None, "tensor"),
            P("tensor", None),
            P(),
        ),
        check_vma=False,
    )
```

```python
import functools

import jax
import jax.numpy as jnp
import numpy as np
from jax import lax
from jax.experimental import pallas as pl
from jax.experimental.pallas import tpu as pltpu
from jax.sharding import PartitionSpec as P

WINDOW = 512

eps = 1e-06
rope_base = 10000.0
f32 = jnp.float32
bf16 = jnp.bfloat16
BOTH = ("seq", "tensor")


def places():
    return [(z, y, c, x) for z in range(4) for y in range(4) for c in range(2) for x in range(4)]


def number(z, y, c, x):
    return ((z * 4 + y) * 2 + c) * 4 + x


def route(move):
    return [(number(*p), number(*move(*p))) for p in places()]


def round_x(by):
    return route(lambda z, y, c, x: (z, y, c, (x + by) % 4))


def swap_cores():
    return route(lambda z, y, c, x: (z, y, 1 - c, x))


def along_first(flip):
    return route(lambda z, y, c, x: (z, y ^ flip, c, x) if c == 0 else (z ^ flip, y, c, x))


def round_first(by):
    return route(
        lambda z, y, c, x: (z, (y + by) % 4, c, x) if c == 0 else ((z + by) % 4, y, c, x)
    )


def round_second(by):
    return route(
        lambda z, y, c, x: ((z + by) % 4, y, c, x) if c == 0 else (z, (y + by) % 4, c, x)
    )


def send(value, pairs):
    return lax.ppermute(value, BOTH, pairs)


def shifted(value, by):
    pairs = [
        (i * 4 + x, (i + by) * 4 + x) for i in range(32) if 0 <= i + by < 32 for x in range(4)
    ]
    return send(value, pairs)


def pick(parts, index):
    return lax.dynamic_index_in_dim(parts, index, 0, keepdims=False)


def dot(first, second, over):
    return lax.dot_general(
        first, second, (((over[0],), (over[1],)), ((), ())), preferred_element_type=f32
    )


def scatter_sum(parts, index, turn):
    total = pick(parts, index).astype(f32)
    for by in (1, 2, 3):
        total = total + send(pick(parts, (index + by) % 4), turn(by)).astype(f32)
    return total


def all_sum(part, turn):
    far = part.astype(f32) + send(part, turn(2)).astype(f32)
    return far + (send(part, turn(1)).astype(f32) + send(part, turn(3)).astype(f32))


def gather(part, index, turn):
    whole = jnp.zeros((4, *part.shape), part.dtype)
    whole = lax.dynamic_update_index_in_dim(whole, part, index, 0)
    for by in (1, 2, 3):
        whole = lax.dynamic_update_index_in_dim(
            whole, send(part, turn(by)), (index + 4 - by) % 4, 0
        )
    return whole


def inv_scale(values):
    return lax.rsqrt(jnp.mean(values * values, axis=-1, keepdims=True) + eps)


def norm_back(values, scale, gain, grad):
    unit = values * scale
    weighted = grad * gain
    d_values = scale * (weighted - unit * jnp.mean(weighted * unit, axis=-1, keepdims=True))
    return (d_values, jnp.sum(grad * unit, axis=0))


def rotate(values, cosine, sine):
    half = values.shape[-1] // 2
    first = values[..., :half]
    second = values[..., half:]
    return jnp.concatenate(
        [first * cosine - second * sine, second * cosine + first * sine], axis=-1
    )


def padded(values, rows):
    return jnp.pad(values, ((0, rows - values.shape[0]), (0, 0)))


def added(first, second):
    return (first.astype(f32) + second.astype(f32)).astype(bf16)


def tied(*values):
    return lax.optimization_barrier(values)


def weight_kernel(
    hid_own, hid_got, gate_own, gate_got, up_own, up_got, dy_own, dy_got, xn_own, xn_got, *outs
):
    mats = (
        (hid_own, hid_got, dy_own, dy_got),
        (gate_own, gate_got, xn_own, xn_got),
        (up_own, up_got, xn_own, xn_got),
    )
    for group, out in enumerate(outs):
        for index, (left_own, left_got, right_own, right_got) in enumerate(mats):
            total = jnp.dot(left_own[group], right_own[...], preferred_element_type=f32)
            total += jnp.dot(left_got[group], right_got[...], preferred_element_type=f32)
            total = total.astype(bf16)
            out[112 * index : 112 * index + 112] = total[:112]
            out[336 + 112 * index : 448 + 112 * index] = total[112:]


def weight_parts(*arrays):
    width = arrays[-1].shape[1]
    return pl.pallas_call(
        weight_kernel,
        out_shape=[jax.ShapeDtypeStruct((672, width), bf16)] * 4,
        in_specs=[pl.BlockSpec(memory_space=pltpu.VMEM)] * len(arrays),
        out_specs=[pl.BlockSpec(memory_space=pltpu.VMEM)] * 4,
        compiler_params=pltpu.CompilerParams(vmem_limit_bytes=40 * 1024 * 1024),
        cost_estimate=pl.CostEstimate(
            flops=2 * 2688 * 512 * width, bytes_accessed=12_000_000, transcendentals=0
        ),
    )(*arrays)


def masks(block, segment, pairs):
    tok = segment.shape[0]
    query = lax.broadcasted_iota(jnp.int32, (tok, tok), 0)
    key = lax.broadcasted_iota(jnp.int32, (tok, tok), 1)
    same = [segment == pair[2 * tok : 2 * tok + 16].astype(f32)[:1] for pair in pairs]
    return (
        same[0] & (key > query) & (block >= 2),
        same[1] & (block >= 1),
        same[2] & (key <= query),
    )


def prepare_kernel(
    x, gain, key_weight, value_weight, query_weight, key_gain, query_gain, cosine, sine, marks, xn, pair, k_raw, q_raw, queries
):
    tok, head_dim = k_raw.shape
    full = x[...].astype(f32)
    low = (full * inv_scale(full) * gain[...]).astype(bf16)
    xn[...] = low
    cos, sin = cosine[...], sine[...]
    raw = dot(low, key_weight[...], (1, 0))
    k_raw[...] = raw
    pair[:tok] = rotate(raw * inv_scale(raw) * key_gain[...], cos, sin).astype(bf16)
    pair[tok : 2 * tok] = dot(low, value_weight[...], (1, 0)).astype(bf16)
    pair[2 * tok :] = jnp.broadcast_to(marks[...], (16, tok)).astype(bf16)
    raw = dot(low, query_weight[...], (1, 0))
    q_raw[...] = raw
    turned = rotate(raw * inv_scale(raw) * query_gain[...], cos, sin)
    queries[...] = (turned * head_dim**-0.5).astype(bf16)


def prepare(x, gain, weights, gains, cosine, sine, marks):
    tok, width = x.shape
    head_dim = weights[0].shape[1]
    vmem = pl.BlockSpec(memory_space=pltpu.VMEM)
    return pl.pallas_call(
        prepare_kernel,
        out_shape=[
            jax.ShapeDtypeStruct((tok, width), bf16),
            jax.ShapeDtypeStruct((2 * tok + 16, head_dim), bf16),
            jax.ShapeDtypeStruct((tok, head_dim), f32),
            jax.ShapeDtypeStruct((tok, head_dim), f32),
            jax.ShapeDtypeStruct((tok, head_dim), bf16),
        ],
        in_specs=[vmem] * 10,
        out_specs=[vmem] * 5,
        cost_estimate=pl.CostEstimate(
            flops=6 * tok * width * head_dim, bytes_accessed=4_000_000, transcendentals=4 * tok
        ),
    )(x, gain[None], *weights, *(g[None] for g in gains), cosine, sine, marks)


def attend_kernel(block, segment, queries, far, near, own, context, log_total):
    pairs = (far, near, own)
    tok = queries.shape[0]
    allowed = masks(block[0], segment[...], pairs)
    scores = [
        jnp.where(ok, dot(queries[...], pair[:tok], (1, 1)), -1e30)
        for ok, pair in zip(allowed, pairs, strict=True)
    ]
    top = functools.reduce(jnp.maximum, [jnp.max(s, axis=1, keepdims=True) for s in scores])
    weights = [jnp.exp(s - top) for s in scores]
    total = sum(jnp.sum(w, axis=1, keepdims=True) for w in weights)
    context[...] = sum(
        dot((w / total).astype(bf16), pair[tok : 2 * tok], (1, 0))
        for w, pair in zip(weights, pairs, strict=True)
    ).astype(bf16)
    log_total[...] = jnp.broadcast_to(top + jnp.log(total), log_total.shape)


def attend(block, segment, queries, pairs):
    tok, head_dim = queries.shape
    vmem = pl.BlockSpec(memory_space=pltpu.VMEM)
    return pl.pallas_call(
        attend_kernel,
        out_shape=[
            jax.ShapeDtypeStruct((tok, head_dim), bf16),
            jax.ShapeDtypeStruct((tok, 128), f32),
        ],
        in_specs=[pl.BlockSpec(memory_space=pltpu.SMEM)] + [vmem] * 5,
        out_specs=[vmem] * 2,
        cost_estimate=pl.CostEstimate(
            flops=12 * tok * tok * head_dim, bytes_accessed=1_500_000, transcendentals=3 * tok * tok
        ),
    )(block, segment, queries, *pairs)


def attend_back_kernel(
    block, segment, log_total, d_branch, weight, queries, far, near, own, d_queries, d_far, d_near, d_own
):
    pairs = (far, near, own)
    tok = queries.shape[0]
    d_context = dot(d_branch[...], weight[...], (1, 1)).astype(bf16)
    allowed = masks(block[0], segment[...], pairs)
    lse = log_total[:, :1]
    probs, d_probs = [], []
    for ok, pair in zip(allowed, pairs, strict=True):
        scores = jnp.where(ok, dot(queries[...], pair[:tok], (1, 1)), -1e30)
        probs.append(jnp.exp(scores - lse))
        d_probs.append(dot(d_context, pair[tok : 2 * tok], (1, 1)))
    mean = sum(
        jnp.sum(p * d, axis=1, keepdims=True) for p, d in zip(probs, d_probs, strict=True)
    )
    total = None
    for p, d, pair, out in zip(probs, d_probs, pairs, (d_far, d_near, d_own), strict=True):
        d_scores = (p * (d - mean)).astype(bf16)
        part = dot(d_scores, pair[:tok], (1, 0))
        total = part if total is None else total + part
        out[:tok] = dot(d_scores, queries[...], (0, 0)).astype(out.dtype)
        out[tok:] = dot(p.astype(bf16), d_context, (0, 0)).astype(out.dtype)
    d_queries[...] = total


def attend_back(block, segment, log_total, d_branch, weight, queries, pairs):
    tok, head_dim = queries.shape
    vmem = pl.BlockSpec(memory_space=pltpu.VMEM)
    return pl.pallas_call(
        attend_back_kernel,
        out_shape=[
            jax.ShapeDtypeStruct((tok, head_dim), f32),
            jax.ShapeDtypeStruct((2 * tok, head_dim), bf16),
            jax.ShapeDtypeStruct((2 * tok, head_dim), bf16),
            jax.ShapeDtypeStruct((2 * tok, head_dim), f32),
        ],
        in_specs=[pl.BlockSpec(memory_space=pltpu.SMEM)] + [vmem] * 8,
        out_specs=[vmem] * 4,
        cost_estimate=pl.CostEstimate(
            flops=30 * tok * tok * head_dim, bytes_accessed=3_500_000, transcendentals=3 * tok * tok
        ),
    )(block, segment, log_total, d_branch, weight, queries, *pairs)


def place_kernel(chunks, *outs):
    for mat, out in enumerate(outs):
        out[:48] = chunks[0, mat, :48].astype(f32)
        for index in (1, 2, 3):
            out[56 * index - 8 : 56 * index + 48] = chunks[index, mat].astype(f32)


def placed(chunks, units):
    width = chunks.shape[-1]
    return pl.pallas_call(
        place_kernel,
        grid=(8,),
        out_shape=[jax.ShapeDtypeStruct((units, width), f32)] * 3,
        in_specs=[pl.BlockSpec((4, 3, 56, width), lambda i: (i, 0, 0, 0))],
        out_specs=[pl.BlockSpec((units // 8, width), lambda i: (i, 0))] * 3,
        compiler_params=pltpu.CompilerParams(vmem_limit_bytes=60 * 1024 * 1024),
        cost_estimate=pl.CostEstimate(
            flops=0, bytes_accessed=chunks.size * 6, transcendentals=0
        ),
    )(chunks)


def finish_kernel(core_ref, own, got, out_grad, query_grad, key_grad, value_grad, gains, rows):
    core = core_ref[0]
    for pieces, other in ((own, 0), (got, 1)):
        even = core == other
        for along in range(4):
            for across in range(4):
                row = jnp.where(even, 8 * across + 2 * along, 8 * along + 2 * across + 1) * 8
                row = pl.ds(pl.multiple_of(row, 8), 8)
                for kind in range(6):
                    rows[kind, row] = pieces[along, kind, across].astype(f32)
    out_grad[...] = rows[0]
    query_grad[...] = rows[1].T
    for lane in range(4):
        key_grad[:, 64 * lane : 64 * lane + 64] = rows[2 + lane, :64].T
        value_grad[:, 64 * lane : 64 * lane + 64] = rows[2 + lane, 64:128].T
    gains[...] = sum(rows[2 + lane, 128:136] for lane in range(4))


def finished(core, own, got):
    width = own.shape[-1]
    vmem = pl.BlockSpec(memory_space=pltpu.VMEM)
    return pl.pallas_call(
        finish_kernel,
        out_shape=[
            jax.ShapeDtypeStruct((256, width), f32),
            jax.ShapeDtypeStruct((width, 256), f32),
            jax.ShapeDtypeStruct((width, 256), f32),
            jax.ShapeDtypeStruct((width, 256), f32),
            jax.ShapeDtypeStruct((8, width), f32),
        ],
        in_specs=[pl.BlockSpec(memory_space=pltpu.SMEM), vmem, vmem],
        out_specs=[vmem] * 5,
        scratch_shapes=[pltpu.VMEM((6, 256, width), f32)],
        compiler_params=pltpu.CompilerParams(vmem_limit_bytes=40 * 1024 * 1024),
        cost_estimate=pl.CostEstimate(flops=0, bytes_accessed=10_000_000, transcendentals=0),
    )(core, own, got)


def local(
    layer_input,
    segment_ids,
    out_cotangent,
    attn_norm_gain,
    query_weight,
    key_weight,
    value_weight,
    query_gain,
    key_gain,
    output_weight,
    attn_post_gain,
    ffw_norm_gain,
    gate_weight,
    up_weight,
    down_weight,
    ffw_post_gain,
):
    tok, width = layer_input.shape
    head_dim = key_weight.shape[1]
    units = down_weight.shape[0]
    block = lax.axis_index("seq")
    lane = lax.axis_index("tensor")
    core = block % 2
    row = (block // 2) % 4
    plane = block // 8
    first = jnp.where(core == 0, row, plane)
    second = jnp.where(core == 0, plane, row)
    quarter_tok = tok // 4

    freq = rope_base ** (-2.0 * np.arange(head_dim // 2) / head_dim)
    start = (np.arange(lax.axis_size("seq")) * tok)[:, None] * freq[None, :]
    inner = np.arange(tok)[:, None] * freq[None, :]
    start_cos = pick(jnp.asarray(np.cos(start), f32), block)[None]
    start_sin = pick(jnp.asarray(np.sin(start), f32), block)[None]
    inner_cos, inner_sin = jnp.asarray(np.cos(inner), f32), jnp.asarray(np.sin(inner), f32)
    cosine = start_cos * inner_cos - start_sin * inner_sin
    sine = start_sin * inner_cos + start_cos * inner_sin
    scale = head_dim ** (-0.5)

    x_full = layer_input.astype(f32)
    normed, own_pair, k_raw, q_raw, queries = prepare(
        layer_input,
        attn_norm_gain,
        (key_weight, value_weight, query_weight),
        (key_gain, query_gain),
        cosine,
        sine,
        segment_ids.astype(f32)[None, :],
    )
    left_one = shifted(own_pair, 1)
    left_two = shifted(own_pair, 2)
    q_scale, k_scale = inv_scale(q_raw), inv_scale(k_raw)

    weight_half = tok // 2
    own_weight = pick(output_weight.reshape(2, weight_half, width), core)
    got_weight = [send(own_weight, round_x(by)) for by in (1, 2, 3)]

    pairs = (left_two, left_one, own_pair)
    block_ref = block.astype(jnp.int32).reshape(1)
    segment = segment_ids.astype(f32)[:, None]
    context, log_total = attend(block_ref, segment, queries, pairs)

    got_context = [send(context, round_x(by)) for by in (1, 2, 3)]
    *got_context, got_weight[0], got_weight[1], got_weight[2] = tied(*got_context, *got_weight)
    own_weights = jnp.concatenate([own_weight, *got_weight])
    other_weights = send(own_weights, swap_cores())

    def columns(which):
        return jnp.concatenate(
            [
                jnp.where(which == 0, c[:, :weight_half], c[:, weight_half:])
                for c in (context, *got_context)
            ],
            axis=1,
        )

    branch = dot(columns(core), own_weights, (1, 0))
    branch = branch + dot(columns(1 - core), other_weights, (1, 0))
    middle = x_full + branch * inv_scale(branch) * attn_post_gain
    normed_two = (middle * inv_scale(middle) * ffw_norm_gain).astype(bf16)

    gate = dot(gate_weight, normed_two, (0, 1))
    up_val = dot(up_weight, normed_two, (0, 1))
    active, gelu_back = jax.vjp(lambda val: jax.nn.gelu(val, approximate=True), gate)
    hidden = (active * up_val).astype(bf16)

    def halves(values):
        groups = values.reshape(8, units // 8, tok)
        groups = jnp.concatenate([groups[:, :56], groups[:, 48:]], axis=1)
        pieces = groups.reshape(4, 4, 2, 56, tok)
        return (
            lax.dynamic_index_in_dim(pieces, core, 2, keepdims=False),
            lax.dynamic_index_in_dim(pieces, 1 - core, 2, keepdims=False),
        )

    def arranged(values):
        values = jnp.where(core == 0, values.swapaxes(0, 1), values)
        by_first = [pick(values, first ^ flip) for flip in range(4)]
        groups = [
            jnp.stack([by_first[i][2 * stream : 2 * stream + 2] for i in order])
            for stream, order in ((0, (0, 3)), (0, (1, 2)), (1, (0, 1)), (1, (3, 2)))
        ]
        return jnp.stack(groups).reshape(4, 224, tok)

    hidden_own, hidden_give = halves(hidden)
    hidden_got = send(hidden_give, swap_cores())
    normed_two_got = send(normed_two, swap_cores())

    down_part = dot(hidden, down_weight, (0, 0)).astype(bf16).reshape(4, quarter_tok, width)
    branch_two = scatter_sum(down_part, lane, round_x)
    cot = pick(out_cotangent.reshape(4, quarter_tok, width), lane).astype(f32)
    final_scale = inv_scale(branch_two)
    d_branch_two, final_part = norm_back(branch_two, final_scale, ffw_post_gain, cot)
    d_branch_two = gather(d_branch_two.astype(bf16), lane, round_x).reshape(tok, width)
    d_branch_two_got = send(d_branch_two, swap_cores())

    branch_own = pick(branch.reshape(4, quarter_tok, width), lane)
    middle_own = pick(middle.reshape(4, quarter_tok, width), lane)
    out_own = (middle_own + branch_two * final_scale * ffw_post_gain).astype(bf16)

    d_hidden = dot(down_weight, d_branch_two, (1, 1))
    d_gate = gelu_back(d_hidden * up_val)[0].astype(bf16)
    d_up = (d_hidden * active).astype(bf16)
    d_gate_own, d_gate_give = halves(d_gate)
    d_up_own, d_up_give = halves(d_up)
    d_pair_got = send(jnp.stack([d_gate_give, d_up_give]), swap_cores())

    d_normed_two = (dot(d_gate, gate_weight, (0, 1)) + dot(d_up, up_weight, (0, 1))).astype(bf16)
    keep_a, give_a, keep_b, give_b = weight_parts(
        *(
            arranged(v)
            for v in (hidden_own, hidden_got, d_gate_own, d_pair_got[0], d_up_own, d_pair_got[1])
        ),
        d_branch_two,
        d_branch_two_got,
        normed_two,
        normed_two_got,
    )
    got_a = send(give_a, along_first(1))
    got_b = send(give_b, along_first(3))

    d_normed_two = d_normed_two.reshape(4, quarter_tok, width)
    got_normed = [
        send(pick(d_normed_two, (lane + by) % 4), round_x(by)) for by in (1, 2, 3)
    ]
    *got_normed, keep_a = tied(*got_normed, keep_a)
    d_normed_two = pick(d_normed_two, lane).astype(f32)
    for part in got_normed:
        d_normed_two = d_normed_two + part.astype(f32)
    d_middle, ffw_gain_part = norm_back(
        middle_own, inv_scale(middle_own), ffw_norm_gain, d_normed_two
    )
    d_middle = cot + d_middle
    d_branch, post_part = norm_back(branch_own, inv_scale(branch_own), attn_post_gain, d_middle)
    d_branch = gather(d_branch.astype(bf16), lane, round_x).reshape(tok, width)
    keep_a, give_a = added(keep_a[:336], got_a[:336]), added(keep_a[336:], got_a[336:])
    keep_b, give_b = added(keep_b[:336], got_b[:336]), added(keep_b[336:], got_b[336:])
    d_branch, give_a, give_b = tied(d_branch, give_a, give_b)
    got_a = send(give_a, along_first(3))
    got_b = send(give_b, along_first(1))

    d_queries, left_far, left_near, summed = attend_back(
        block_ref, segment, log_total, d_branch, output_weight, queries, pairs
    )
    got_near = shifted(left_near, -1)
    got_far = shifted(left_far, -2)
    got_near, got_far, got_a, got_b = tied(got_near, got_far, got_a, got_b)
    fours = jnp.stack([added(keep_a, got_a), added(keep_b, got_b)])
    fours = fours.reshape(2, 3, 2, 56, width).swapaxes(1, 2).reshape(4, 168, width)
    mine = pick(fours, second).astype(f32)
    got = [send(pick(fours, (second + by) % 4), round_second(by)) for by in (1, 2, 3)]
    summed = summed + got_near.astype(f32) + got_far.astype(f32)
    d_q_raw, q_gain_part = norm_back(
        q_raw, q_scale, query_gain, rotate(d_queries * scale, cosine, -sine)
    )
    d_q_raw = d_q_raw.astype(bf16)
    out_part = dot(context, d_branch, (0, 0)).astype(bf16)
    query_part = dot(d_q_raw, normed, (0, 0)).astype(bf16)

    d_k_raw, k_gain_part = norm_back(
        k_raw, k_scale, key_gain, rotate(summed[:tok], cosine, -sine)
    )
    d_k_raw = d_k_raw.astype(bf16)
    d_values = summed[tok:].astype(bf16)
    d_normed = (
        dot(d_q_raw, query_weight, (1, 1))
        + dot(d_k_raw, key_weight, (1, 1))
        + dot(d_values, value_weight, (1, 1))
    ).astype(bf16)
    d_kv = jnp.concatenate([d_k_raw, d_values], axis=1).T.reshape(2, 4, head_dim // 4, tok)
    d_kv = d_kv.transpose(1, 2, 0, 3).reshape(4, head_dim // 4, 2 * tok)
    d_both = jnp.concatenate([d_normed.reshape(4, quarter_tok, width), d_kv], axis=2)
    d_both, *got = tied(d_both, *got)
    mine = (mine + got[0].astype(f32) + (got[1].astype(f32) + got[2].astype(f32))).astype(bf16)
    everyone = lax.all_gather(mine, "seq")
    both = pick(d_both, lane).astype(f32)
    got_both = [send(pick(d_both, (lane + by) % 4), round_x(by)) for by in (1, 2, 3)]
    for part in got_both:
        both = both + part.astype(f32)
    d_both = both
    d_normed = d_both[:, :width]
    d_kv = d_both[:, width:].astype(bf16)
    x_own = pick(x_full.reshape(4, quarter_tok, width), lane)
    d_input, attn_gain_part = norm_back(x_own, inv_scale(x_own), attn_norm_gain, d_normed)
    ends = gather(jnp.stack([out_own, (d_middle + d_input).astype(bf16)]), lane, round_x)

    kv_part = jnp.concatenate(
        [dot(d_kv[:, :tok], normed, (1, 0)), dot(d_kv[:, tok:], normed, (1, 0))]
    ).astype(bf16)
    gains = jnp.stack(
        [
            attn_gain_part,
            post_part,
            ffw_gain_part,
            final_part,
            jnp.pad(jnp.concatenate([q_gain_part, k_gain_part]), (0, width - 2 * head_dim)),
        ]
    ).astype(bf16)
    rest_part = jnp.concatenate([kv_part, padded(gains, 128)])
    pack = jnp.stack([out_part, query_part, rest_part])
    pack = pack.reshape(3, 4, 4, 2, 8, width)
    pack_got = send(lax.dynamic_index_in_dim(pack, 1 - core, 3, keepdims=False), swap_cores())
    pack = added(lax.dynamic_index_in_dim(pack, core, 3, keepdims=False), pack_got)
    pack = jnp.where(core == 0, pack.transpose(2, 0, 1, 3, 4), pack.transpose(1, 0, 2, 3, 4))
    pack = scatter_sum(pack, first, round_first).astype(bf16)
    pack = lax.optimization_barrier(pack)
    pack = all_sum(pack, round_second).astype(bf16)
    rest = gather(pack[2], lane, round_x)
    pack = jnp.concatenate([pack[:2], rest]).reshape(6, 4, 8, width)
    pack = gather(pack, first, round_first)
    pack_got = send(pack, swap_cores())
    down_grad, gate_grad, up_grad = placed(everyone.reshape(32, 3, 56, width), units)
    out_grad, query_grad, key_grad, value_grad, gains = finished(
        core.astype(jnp.int32).reshape(1), pack, pack_got
    )
    layer_output = ends[:, 0].reshape(tok, width)
    input_grad = ends[:, 1].reshape(tok, width)
    return (
        layer_output,
        input_grad,
        gains[0],
        query_grad,
        key_grad,
        value_grad,
        gains[4, :head_dim],
        gains[4, head_dim : 2 * head_dim],
        out_grad,
        gains[1],
        gains[2],
        gate_grad.T,
        up_grad.T,
        down_grad,
        gains[3],
    )


def solution(mesh):
    rows = P("seq", None)
    return jax.shard_map(
        local,
        mesh=mesh,
        in_specs=(
            rows,
            P("seq"),
            rows,
            P(),
            P(None, "tensor"),
            P(),
            P(),
            P(),
            P(),
            P("tensor", None),
            P(),
            P(),
            P(None, "tensor"),
            P(None, "tensor"),
            P("tensor", None),
            P(),
        ),
        out_specs=(
            rows,
            rows,
            P(),
            P(None, "tensor"),
            P(),
            P(),
            P(),
            P(),
            P("tensor", None),
            P(),
            P(),
            P(None, "tensor"),
            P(None, "tensor"),
            P("tensor", None),
            P(),
        ),
        check_vma=False,
    )
```

```python
import functools

import jax
import jax.numpy as jnp
import numpy as np
from jax import lax
from jax.experimental import pallas as pl
from jax.experimental.pallas import tpu as pltpu
from jax.sharding import PartitionSpec as P

WINDOW = 512

eps = 1e-06
rope_base = 10000.0
f32 = jnp.float32
bf16 = jnp.bfloat16
BOTH = ("seq", "tensor")


def places():
    return [(z, y, c, x) for z in range(4) for y in range(4) for c in range(2) for x in range(4)]


def number(z, y, c, x):
    return ((z * 4 + y) * 2 + c) * 4 + x


def route(move):
    return [(number(*p), number(*move(*p))) for p in places()]


def round_x(by):
    return route(lambda z, y, c, x: (z, y, c, (x + by) % 4))


def swap_cores():
    return route(lambda z, y, c, x: (z, y, 1 - c, x))


def along_first(flip):
    return route(lambda z, y, c, x: (z, y ^ flip, c, x) if c == 0 else (z ^ flip, y, c, x))


def round_first(by):
    return route(
        lambda z, y, c, x: (z, (y + by) % 4, c, x) if c == 0 else ((z + by) % 4, y, c, x)
    )


def round_second(by):
    return route(
        lambda z, y, c, x: ((z + by) % 4, y, c, x) if c == 0 else (z, (y + by) % 4, c, x)
    )


def send(value, pairs):
    return lax.ppermute(value, BOTH, pairs)


def shifted(value, by):
    pairs = [
        (i * 4 + x, (i + by) * 4 + x) for i in range(32) if 0 <= i + by < 32 for x in range(4)
    ]
    return send(value, pairs)


def pick(parts, index):
    return lax.dynamic_index_in_dim(parts, index, 0, keepdims=False)


def dot(first, second, over):
    return lax.dot_general(
        first, second, (((over[0],), (over[1],)), ((), ())), preferred_element_type=f32
    )


def scatter_sum(parts, index, turn):
    total = pick(parts, index).astype(f32)
    for by in (1, 2, 3):
        total = total + send(pick(parts, (index + by) % 4), turn(by)).astype(f32)
    return total


def all_sum(part, turn):
    far = part.astype(f32) + send(part, turn(2)).astype(f32)
    return far + (send(part, turn(1)).astype(f32) + send(part, turn(3)).astype(f32))


def gather(part, index, turn):
    whole = jnp.zeros((4, *part.shape), part.dtype)
    whole = lax.dynamic_update_index_in_dim(whole, part, index, 0)
    for by in (1, 2, 3):
        whole = lax.dynamic_update_index_in_dim(
            whole, send(part, turn(by)), (index + 4 - by) % 4, 0
        )
    return whole


def inv_scale(values):
    return lax.rsqrt(jnp.mean(values * values, axis=-1, keepdims=True) + eps)


def norm_back(values, scale, gain, grad):
    unit = values * scale
    weighted = grad * gain
    d_values = scale * (weighted - unit * jnp.mean(weighted * unit, axis=-1, keepdims=True))
    return (d_values, jnp.sum(grad * unit, axis=0))


def rotate(values, cosine, sine):
    half = values.shape[-1] // 2
    first = values[..., :half]
    second = values[..., half:]
    return jnp.concatenate(
        [first * cosine - second * sine, second * cosine + first * sine], axis=-1
    )


def padded(values, rows):
    return jnp.pad(values, ((0, rows - values.shape[0]), (0, 0)))


def added(first, second):
    return (first.astype(f32) + second.astype(f32)).astype(bf16)


def tied(*values):
    return lax.optimization_barrier(values)


def call(kernel, outs, *arrays, scalars=0, flops=0):
    vmem = pl.BlockSpec(memory_space=pltpu.VMEM)
    outs = [jax.ShapeDtypeStruct(*o) for o in outs]
    moved = sum(v.size * v.dtype.itemsize for v in (*arrays, *outs))
    return pl.pallas_call(
        kernel,
        out_shape=outs,
        in_specs=[pl.BlockSpec(memory_space=pltpu.SMEM)] * scalars
        + [vmem] * (len(arrays) - scalars),
        out_specs=[vmem] * len(outs),
        compiler_params=pltpu.CompilerParams(vmem_limit_bytes=40 * 1024 * 1024),
        cost_estimate=pl.CostEstimate(flops=flops, bytes_accessed=moved, transcendentals=0),
    )(*arrays)


def own_rows(ref, lane, rows):
    return ref[pl.ds(pl.multiple_of(lane * rows, rows), rows)].astype(f32)


def project_kernel(
    place, x, post_gain, ffw_gain, ctx0, ctx1, ctx2, ctx3, weight, own1, own2, own3, other1, other2, other3,
    branch, middle, normed
):
    even = place[1] == 0
    half = own1.shape[0]
    total = dot(ctx0[...], weight[...], (1, 0))
    for ctx, mine, theirs in ((ctx1, own1, other1), (ctx2, own2, other2), (ctx3, own3, other3)):
        low = jnp.where(even, mine[...], theirs[...])
        high = jnp.where(even, theirs[...], mine[...])
        total += dot(ctx[:, :half], low, (1, 0)) + dot(ctx[:, half:], high, (1, 0))
    branch[...] = total
    after = x[...].astype(f32) + total * inv_scale(total) * post_gain[...]
    middle[...] = after
    normed[...] = (after * inv_scale(after) * ffw_gain[...]).astype(bf16)


def forward_kernel(normed, gate_weight, up_weight, down_weight, gate, up, hidden, out, total):
    step = pl.program_id(0)
    gated = dot(gate_weight[...], normed[...], (1, 1))
    raised = dot(up_weight[...], normed[...], (1, 1))
    gate[...] = gated
    up[...] = raised
    hid = (jax.nn.gelu(gated, approximate=True) * raised).astype(bf16)
    hidden[...] = hid
    part = dot(hid, down_weight[...], (0, 0))

    @pl.when(step == 0)
    def _():
        total[...] = part

    @pl.when(step > 0)
    def _():
        total[...] += part

    @pl.when(step == pl.num_programs(0) - 1)
    def _():
        out[...] = total[...].astype(bf16)


def feed_forward(normed, gate_weight, up_weight, down_weight):
    tok, width = normed.shape
    units = down_weight.shape[0]
    steps = 4
    rows = pl.BlockSpec((units // steps, width), lambda i: (i, 0))
    tall = pl.BlockSpec((units // steps, tok), lambda i: (i, 0))
    whole = pl.BlockSpec((tok, width), lambda i: (0, 0))
    return pl.pallas_call(
        forward_kernel,
        grid=(steps,),
        out_shape=[
            jax.ShapeDtypeStruct((units, tok), f32),
            jax.ShapeDtypeStruct((units, tok), f32),
            jax.ShapeDtypeStruct((units, tok), bf16),
            jax.ShapeDtypeStruct((tok, width), bf16),
        ],
        in_specs=[whole, rows, rows, rows],
        out_specs=[tall, tall, tall, whole],
        scratch_shapes=[pltpu.VMEM((tok, width), f32)],
        compiler_params=pltpu.CompilerParams(vmem_limit_bytes=40 * 1024 * 1024),
        cost_estimate=pl.CostEstimate(
            flops=6 * tok * width * units,
            bytes_accessed=6 * units * width,
            transcendentals=tok * units,
        ),
    )(normed, gate_weight, up_weight, down_weight)


def final_kernel(place, p0, p1, p2, p3, middle, cotangent, gain, out, d_branch, part):
    lane = place[0]
    branch = p0[...].astype(f32) + p1[...].astype(f32) + p2[...].astype(f32) + p3[...].astype(f32)
    rows = branch.shape[0]
    scale = inv_scale(branch)
    cot = own_rows(cotangent, lane, rows)
    out[...] = (own_rows(middle, lane, rows) + branch * scale * gain[...]).astype(bf16)
    d_values, d_gain = norm_back(branch, scale, gain[...], cot)
    d_branch[...] = d_values.astype(bf16)
    part[...] = d_gain[None]


def between_kernel(
    place, p0, p1, p2, p3, middle, branch, cotangent, ffw_gain, post_gain,
    d_middle, d_branch, ffw_part, post_part
):
    lane = place[0]
    grad = p0[...].astype(f32) + p1[...].astype(f32) + p2[...].astype(f32) + p3[...].astype(f32)
    rows = grad.shape[0]
    after = own_rows(middle, lane, rows)
    before = own_rows(branch, lane, rows)
    d_values, d_gain = norm_back(after, inv_scale(after), ffw_gain[...], grad)
    ffw_part[...] = d_gain[None]
    d_values = own_rows(cotangent, lane, rows) + d_values
    d_middle[...] = d_values
    d_values, d_gain = norm_back(before, inv_scale(before), post_gain[...], d_values)
    d_branch[...] = d_values.astype(bf16)
    post_part[...] = d_gain[None]


def key_kernel(
    q_raw, k_raw, d_queries, d_own, d_near, d_far, cosine, sine, query_gain, key_gain, query_weight, key_weight,
    value_weight, d_query, payload, query_part, key_part
):
    tok, head_dim = q_raw.shape
    width = query_weight.shape[0]
    cos, sin = cosine[...], -sine[...]
    raw = q_raw[...]
    d_raw, d_gain = norm_back(
        raw, inv_scale(raw), query_gain[...], rotate(d_queries[...] * head_dim**-0.5, cos, sin)
    )
    query_part[...] = d_gain[None]
    d_low = d_raw.astype(bf16)
    d_query[...] = d_low
    total = dot(d_low, query_weight[...], (1, 1))
    summed = d_own[...] + d_near[...].astype(f32) + d_far[...].astype(f32)
    raw = k_raw[...]
    d_raw, d_gain = norm_back(raw, inv_scale(raw), key_gain[...], rotate(summed[:tok], cos, sin))
    key_part[...] = d_gain[None]
    total += dot(d_raw.astype(bf16), key_weight[...], (1, 1))
    total += dot(summed[tok:].astype(bf16), value_weight[...], (1, 1))
    payload[:, :width] = total.astype(bf16)
    payload[:, width : width + tok] = d_raw.T.astype(bf16)
    payload[:, width + tok :] = summed[tok:].T.astype(bf16)


def products_kernel(context, d_branch, d_query, normed, out):
    half = context.shape[1]
    out[:half] = dot(context[...], d_branch[...], (0, 0)).astype(bf16)
    out[half:] = dot(d_query[...], normed[...], (0, 0)).astype(bf16)


def entry_kernel(
    place, p0, p1, p2, p3, x, d_middle, gain, normed, post_part, ffw_part, final_part, query_part, key_part,
    input_grad, rest
):
    lane = place[0]
    both = p0[...].astype(f32) + p1[...].astype(f32) + p2[...].astype(f32) + p3[...].astype(f32)
    rows = both.shape[0]
    width = normed.shape[1]
    tok = normed.shape[0]
    full = own_rows(x, lane, rows)
    d_values, d_gain = norm_back(full, inv_scale(full), gain[...], both[:, :width])
    input_grad[...] = (d_middle[...] + d_values).astype(bf16)
    d_keys = both[:, width : width + tok].astype(bf16)
    d_values = both[:, width + tok :].astype(bf16)
    rest[:rows] = dot(d_keys, normed[...], (1, 0)).astype(bf16)
    rest[rows : 2 * rows] = dot(d_values, normed[...], (1, 0)).astype(bf16)
    heads = jnp.concatenate(
        [query_part[...], key_part[...], jnp.zeros((1, width - 2 * query_part.shape[1]), f32)], axis=1
    )
    index = lax.broadcasted_iota(jnp.int32, (16, width), 0)
    gains = jnp.zeros((16, width), f32)
    for at, part in enumerate((d_gain[None], post_part[...], ffw_part[...], final_part[...], heads)):
        gains = jnp.where(index == at, part, gains)
    rest[2 * rows : 2 * rows + 16] = gains.astype(bf16)
    rest[2 * rows + 16 :] = jnp.zeros((rest.shape[0] - 2 * rows - 16, width), bf16)


def weight_kernel(
    hid_own, hid_got, gate_own, gate_got, up_own, up_got, dy_own, dy_got, xn_own, xn_got, *outs
):
    mats = (
        (hid_own, hid_got, dy_own, dy_got),
        (gate_own, gate_got, xn_own, xn_got),
        (up_own, up_got, xn_own, xn_got),
    )
    for group, out in enumerate(outs):
        for index, (left_own, left_got, right_own, right_got) in enumerate(mats):
            total = jnp.dot(left_own[group], right_own[...], preferred_element_type=f32)
            total += jnp.dot(left_got[group], right_got[...], preferred_element_type=f32)
            total = total.astype(bf16)
            out[112 * index : 112 * index + 112] = total[:112]
            out[336 + 112 * index : 448 + 112 * index] = total[112:]


def weight_parts(*arrays):
    width = arrays[-1].shape[1]
    return pl.pallas_call(
        weight_kernel,
        out_shape=[jax.ShapeDtypeStruct((672, width), bf16)] * 4,
        in_specs=[pl.BlockSpec(memory_space=pltpu.VMEM)] * len(arrays),
        out_specs=[pl.BlockSpec(memory_space=pltpu.VMEM)] * 4,
        compiler_params=pltpu.CompilerParams(vmem_limit_bytes=40 * 1024 * 1024),
        cost_estimate=pl.CostEstimate(
            flops=2 * 2688 * 512 * width, bytes_accessed=12_000_000, transcendentals=0
        ),
    )(*arrays)


def masks(block, segment, pairs):
    tok = segment.shape[0]
    query = lax.broadcasted_iota(jnp.int32, (tok, tok), 0)
    key = lax.broadcasted_iota(jnp.int32, (tok, tok), 1)
    same = [segment == pair[2 * tok : 2 * tok + 16].astype(f32)[:1] for pair in pairs]
    return (
        same[0] & (key > query) & (block >= 2),
        same[1] & (block >= 1),
        same[2] & (key <= query),
    )


def prepare_kernel(
    place, x, gain, key_weight, value_weight, query_weight, key_gain, query_gain, start_cos, start_sin, inner_cos,
    inner_sin, marks, xn, pair, k_raw, q_raw, queries, cosine, sine
):
    tok, head_dim = k_raw.shape
    full = x[...].astype(f32)
    low = (full * inv_scale(full) * gain[...]).astype(bf16)
    xn[...] = low
    at = pl.ds(place[2], 1)
    cos = start_cos[at] * inner_cos[...] - start_sin[at] * inner_sin[...]
    sin = start_sin[at] * inner_cos[...] + start_cos[at] * inner_sin[...]
    cosine[...] = cos
    sine[...] = sin
    raw = dot(low, key_weight[...], (1, 0))
    k_raw[...] = raw
    pair[:tok] = rotate(raw * inv_scale(raw) * key_gain[...], cos, sin).astype(bf16)
    pair[tok : 2 * tok] = dot(low, value_weight[...], (1, 0)).astype(bf16)
    pair[2 * tok :] = jnp.broadcast_to(marks[...].astype(f32)[None], (16, tok)).astype(bf16)
    raw = dot(low, query_weight[...], (1, 0))
    q_raw[...] = raw
    turned = rotate(raw * inv_scale(raw) * query_gain[...], cos, sin)
    queries[...] = (turned * head_dim**-0.5).astype(bf16)


def attend_kernel(block, segment, queries, far, near, own, context, log_total):
    pairs = (far, near, own)
    tok = queries.shape[0]
    allowed = masks(block[0], segment[...], pairs)
    scores = [
        jnp.where(ok, dot(queries[...], pair[:tok], (1, 1)), -1e30)
        for ok, pair in zip(allowed, pairs, strict=True)
    ]
    top = functools.reduce(jnp.maximum, [jnp.max(s, axis=1, keepdims=True) for s in scores])
    weights = [jnp.exp(s - top) for s in scores]
    total = sum(jnp.sum(w, axis=1, keepdims=True) for w in weights)
    context[...] = sum(
        dot((w / total).astype(bf16), pair[tok : 2 * tok], (1, 0))
        for w, pair in zip(weights, pairs, strict=True)
    ).astype(bf16)
    log_total[...] = jnp.broadcast_to(top + jnp.log(total), log_total.shape)


def attend(block, segment, queries, pairs):
    tok, head_dim = queries.shape
    vmem = pl.BlockSpec(memory_space=pltpu.VMEM)
    return pl.pallas_call(
        attend_kernel,
        out_shape=[
            jax.ShapeDtypeStruct((tok, head_dim), bf16),
            jax.ShapeDtypeStruct((tok, 128), f32),
        ],
        in_specs=[pl.BlockSpec(memory_space=pltpu.SMEM)] + [vmem] * 5,
        out_specs=[vmem] * 2,
        cost_estimate=pl.CostEstimate(
            flops=12 * tok * tok * head_dim, bytes_accessed=1_500_000, transcendentals=3 * tok * tok
        ),
    )(block, segment, queries, *pairs)


def attend_back_kernel(
    block, segment, log_total, d_branch, weight, queries, far, near, own, d_queries, d_far, d_near, d_own
):
    pairs = (far, near, own)
    tok = queries.shape[0]
    d_context = dot(d_branch[...], weight[...], (1, 1)).astype(bf16)
    allowed = masks(block[0], segment[...], pairs)
    lse = log_total[:, :1]
    probs, d_probs = [], []
    for ok, pair in zip(allowed, pairs, strict=True):
        scores = jnp.where(ok, dot(queries[...], pair[:tok], (1, 1)), -1e30)
        probs.append(jnp.exp(scores - lse))
        d_probs.append(dot(d_context, pair[tok : 2 * tok], (1, 1)))
    mean = sum(
        jnp.sum(p * d, axis=1, keepdims=True) for p, d in zip(probs, d_probs, strict=True)
    )
    total = None
    for p, d, pair, out in zip(probs, d_probs, pairs, (d_far, d_near, d_own), strict=True):
        d_scores = (p * (d - mean)).astype(bf16)
        part = dot(d_scores, pair[:tok], (1, 0))
        total = part if total is None else total + part
        out[:tok] = dot(d_scores, queries[...], (0, 0)).astype(out.dtype)
        out[tok:] = dot(p.astype(bf16), d_context, (0, 0)).astype(out.dtype)
    d_queries[...] = total


def attend_back(block, segment, log_total, d_branch, weight, queries, pairs):
    tok, head_dim = queries.shape
    vmem = pl.BlockSpec(memory_space=pltpu.VMEM)
    return pl.pallas_call(
        attend_back_kernel,
        out_shape=[
            jax.ShapeDtypeStruct((tok, head_dim), f32),
            jax.ShapeDtypeStruct((2 * tok, head_dim), bf16),
            jax.ShapeDtypeStruct((2 * tok, head_dim), bf16),
            jax.ShapeDtypeStruct((2 * tok, head_dim), f32),
        ],
        in_specs=[pl.BlockSpec(memory_space=pltpu.SMEM)] + [vmem] * 8,
        out_specs=[vmem] * 4,
        cost_estimate=pl.CostEstimate(
            flops=30 * tok * tok * head_dim, bytes_accessed=3_500_000, transcendentals=3 * tok * tok
        ),
    )(block, segment, log_total, d_branch, weight, queries, *pairs)


def place_kernel(where_ref, *refs, turns, held):
    n = len(turns)
    parts, outs = refs[:n], refs[n + held : n + held + 3]
    stage, sems, tail_sems = refs[-3:]
    slots = stage.shape[0]
    core, first, second = where_ref[0], where_ref[1], where_ref[2]
    chunks = [
        (ref, i, base + i, other, flip)
        for ref, (other, flip, base) in zip(parts, turns, strict=True)
        for i in range(ref.shape[0])
    ]

    def place(index):
        _, _, across, other, flip = chunks[index]
        which = 1 - core if other else core
        along = (second if other else first) ^ flip
        y = jnp.where(which == 0, along, across)
        z = jnp.where(which == 0, across, along)
        odd = lax.rem(y, 2)
        row = 216 * (2 * z + y // 2) + 104 * odd + 48 * which + 8 * which * odd
        return pl.multiple_of(row, 8), (which == 1) | (odd == 1)

    def copies(index):
        slot = index % slots
        row, whole = place(index)
        for mat, out in enumerate(outs):
            yield (
                pltpu.make_async_copy(
                    stage.at[slot, mat, pl.ds(0, 48)],
                    out.at[pl.ds(row, 48)],
                    sems.at[slot, mat],
                ),
                pltpu.make_async_copy(
                    stage.at[slot, mat, pl.ds(48, 8)],
                    out.at[pl.ds(pl.multiple_of(row + 48, 8), 8)],
                    tail_sems.at[slot, mat],
                ),
                whole,
            )

    def finish(index):
        for most, tail, whole in copies(index):
            most.wait()
            pl.when(whole)(tail.wait)

    for index, (ref, i, *_) in enumerate(chunks):
        if index >= slots:
            finish(index - slots)
        stage[index % slots] = ref[i].astype(f32)
        for most, tail, whole in copies(index):
            most.start()
            pl.when(whole)(tail.start)
    for index in range(max(0, len(chunks) - slots), len(chunks)):
        finish(index)


def placed(where, parts, outs, units):
    arrays = [p[0].reshape(-1, 3, 56, p[0].shape[-1]) for p in parts]
    width = arrays[0].shape[-1]
    slots = 4
    return pl.pallas_call(
        functools.partial(
            place_kernel, turns=tuple(p[1:] for p in parts), held=len(outs)
        ),
        out_shape=[jax.ShapeDtypeStruct((units, width), f32)] * 3,
        in_specs=[pl.BlockSpec(memory_space=pltpu.SMEM)]
        + [pl.BlockSpec(memory_space=pltpu.VMEM)] * len(arrays)
        + [pl.BlockSpec(memory_space=pl.ANY)] * len(outs),
        out_specs=[pl.BlockSpec(memory_space=pl.ANY)] * 3,
        scratch_shapes=[
            pltpu.VMEM((slots, 3, 56, width), f32),
            pltpu.SemaphoreType.DMA((slots, 3)),
            pltpu.SemaphoreType.DMA((slots, 3)),
        ],
        input_output_aliases={1 + len(arrays) + i: i for i in range(len(outs))},
        compiler_params=pltpu.CompilerParams(vmem_limit_bytes=40 * 1024 * 1024),
        cost_estimate=pl.CostEstimate(
            flops=0, bytes_accessed=sum(p.size for p in arrays) * 6, transcendentals=0
        ),
    )(where, *arrays, *outs)


def finish_kernel(core_ref, own, got, out_grad, query_grad, key_grad, value_grad, gains, rows):
    core = core_ref[0]
    for pieces, other in ((own, 0), (got, 1)):
        even = core == other
        for along in range(4):
            for across in range(4):
                row = jnp.where(even, 8 * across + 2 * along, 8 * along + 2 * across + 1) * 8
                row = pl.ds(pl.multiple_of(row, 8), 8)
                for kind in range(6):
                    rows[kind, row] = pieces[along, kind, across].astype(f32)
    out_grad[...] = rows[0]
    query_grad[...] = rows[1].T
    for lane in range(4):
        key_grad[:, 64 * lane : 64 * lane + 64] = rows[2 + lane, :64].T
        value_grad[:, 64 * lane : 64 * lane + 64] = rows[2 + lane, 64:128].T
    gains[...] = sum(rows[2 + lane, 128:136] for lane in range(4))


def finished(core, own, got):
    width = own.shape[-1]
    vmem = pl.BlockSpec(memory_space=pltpu.VMEM)
    return pl.pallas_call(
        finish_kernel,
        out_shape=[
            jax.ShapeDtypeStruct((256, width), f32),
            jax.ShapeDtypeStruct((width, 256), f32),
            jax.ShapeDtypeStruct((width, 256), f32),
            jax.ShapeDtypeStruct((width, 256), f32),
            jax.ShapeDtypeStruct((8, width), f32),
        ],
        in_specs=[pl.BlockSpec(memory_space=pltpu.SMEM), vmem, vmem],
        out_specs=[vmem] * 5,
        scratch_shapes=[pltpu.VMEM((6, 256, width), f32)],
        compiler_params=pltpu.CompilerParams(vmem_limit_bytes=40 * 1024 * 1024),
        cost_estimate=pl.CostEstimate(flops=0, bytes_accessed=10_000_000, transcendentals=0),
    )(core, own, got)


def local(
    layer_input,
    segment_ids,
    out_cotangent,
    attn_norm_gain,
    query_weight,
    key_weight,
    value_weight,
    query_gain,
    key_gain,
    output_weight,
    attn_post_gain,
    ffw_norm_gain,
    gate_weight,
    up_weight,
    down_weight,
    ffw_post_gain,
):
    tok, width = layer_input.shape
    head_dim = key_weight.shape[1]
    units = down_weight.shape[0]
    block = lax.axis_index("seq")
    lane = lax.axis_index("tensor")
    core = block % 2
    row = (block // 2) % 4
    plane = block // 8
    first = jnp.where(core == 0, row, plane)
    second = jnp.where(core == 0, plane, row)
    quarter_tok = tok // 4

    place = jnp.stack([lane, core, block]).astype(jnp.int32)
    where = jnp.stack([core, first, second]).astype(jnp.int32)
    freq = rope_base ** (-2.0 * np.arange(head_dim // 2) / head_dim)
    start = (np.arange(lax.axis_size("seq")) * tok)[:, None] * freq[None, :]
    inner = np.arange(tok)[:, None] * freq[None, :]
    tables = [jnp.asarray(f(angle), f32) for angle in (start, inner) for f in (np.cos, np.sin)]

    square = (tok, head_dim)
    normed, own_pair, k_raw, q_raw, queries, cosine, sine = call(
        prepare_kernel,
        [
            ((tok, width), bf16),
            ((2 * tok + 16, head_dim), bf16),
            (square, f32),
            (square, f32),
            (square, bf16),
            ((tok, head_dim // 2), f32),
            ((tok, head_dim // 2), f32),
        ],
        place,
        layer_input,
        attn_norm_gain,
        key_weight,
        value_weight,
        query_weight,
        key_gain,
        query_gain,
        *tables,
        segment_ids,
        scalars=1,
        flops=6 * tok * width * head_dim,
    )
    left_one = shifted(own_pair, 1)
    left_two = shifted(own_pair, 2)

    weight_half = tok // 2
    own_weight, _ = tied(pick(output_weight.reshape(2, weight_half, width), core), own_pair)
    got_weight = [send(own_weight, round_x(by)) for by in (1, 2, 3)]

    pairs = (left_two, left_one, own_pair)
    block_ref = block.astype(jnp.int32).reshape(1)
    segment = segment_ids.astype(f32)[:, None]
    context, log_total = attend(block_ref, segment, queries, pairs)

    got_context = [send(context, round_x(by)) for by in (1, 2, 3)]
    *got_context, got_weight[0], got_weight[1], got_weight[2] = tied(*got_context, *got_weight)
    other_weight = [send(part, swap_cores()) for part in got_weight]
    branch, middle, normed_two = call(
        project_kernel,
        [((tok, width), f32), ((tok, width), f32), ((tok, width), bf16)],
        place,
        layer_input,
        attn_post_gain,
        ffw_norm_gain,
        context,
        *got_context,
        output_weight,
        *got_weight,
        *other_weight,
        scalars=1,
        flops=8 * tok * tok * width,
    )
    gate, up_val, hidden, down_part = feed_forward(
        normed_two, gate_weight.T, up_weight.T, down_weight
    )
    active, gelu_back = jax.vjp(lambda val: jax.nn.gelu(val, approximate=True), gate)

    def halves(values):
        groups = values.reshape(8, units // 8, tok)
        groups = jnp.concatenate([groups[:, :56], groups[:, 48:]], axis=1)
        pieces = groups.reshape(4, 4, 2, 56, tok)
        return (
            lax.dynamic_index_in_dim(pieces, core, 2, keepdims=False),
            lax.dynamic_index_in_dim(pieces, 1 - core, 2, keepdims=False),
        )

    def arranged(values):
        values = jnp.where(core == 0, values.swapaxes(0, 1), values)
        by_first = [pick(values, first ^ flip) for flip in range(4)]
        groups = [
            jnp.stack([by_first[i][2 * stream : 2 * stream + 2] for i in order])
            for stream, order in ((0, (0, 3)), (0, (1, 2)), (1, (0, 1)), (1, (3, 2)))
        ]
        return jnp.stack(groups).reshape(4, 224, tok)

    hidden_own, hidden_give = halves(hidden)
    hidden_got = send(hidden_give, swap_cores())
    normed_two_got = send(normed_two, swap_cores())

    def quarters(parts):
        parts = parts.reshape(4, quarter_tok, parts.shape[-1])
        given = [pick(parts, (lane + by) % 4) for by in (1, 2, 3)]
        return [pick(parts, lane)] + [
            send(part, round_x(by)) for by, part in zip((1, 2, 3), given, strict=True)
        ]

    piece = (quarter_tok, width)
    out_own, d_branch_two, final_part = call(
        final_kernel,
        [(piece, bf16), (piece, bf16), ((1, width), f32)],
        place,
        *quarters(down_part),
        middle,
        out_cotangent,
        ffw_post_gain,
        scalars=1,
    )
    d_branch_two = gather(d_branch_two, lane, round_x).reshape(tok, width)
    d_branch_two_got = send(d_branch_two, swap_cores())

    d_hidden = dot(down_weight, d_branch_two, (1, 1))
    d_gate = gelu_back(d_hidden * up_val)[0].astype(bf16)
    d_up = (d_hidden * active).astype(bf16)
    d_gate_own, d_gate_give = halves(d_gate)
    d_up_own, d_up_give = halves(d_up)
    d_pair_got = send(jnp.stack([d_gate_give, d_up_give]), swap_cores())

    d_normed_two = (dot(d_gate, gate_weight, (0, 1)) + dot(d_up, up_weight, (0, 1))).astype(bf16)
    keep_a, give_a, keep_b, give_b = weight_parts(
        *(
            arranged(v)
            for v in (hidden_own, hidden_got, d_gate_own, d_pair_got[0], d_up_own, d_pair_got[1])
        ),
        d_branch_two,
        d_branch_two_got,
        normed_two,
        normed_two_got,
    )
    got_a = send(give_a, along_first(1))
    got_b = send(give_b, along_first(3))

    *got_normed, keep_a, keep_b = tied(*quarters(d_normed_two), keep_a, keep_b)
    d_middle, d_branch, ffw_part, post_part = call(
        between_kernel,
        [(piece, f32), (piece, bf16), ((1, width), f32), ((1, width), f32)],
        place,
        *got_normed,
        middle,
        branch,
        out_cotangent,
        ffw_norm_gain,
        attn_post_gain,
        scalars=1,
    )
    d_branch = gather(d_branch, lane, round_x).reshape(tok, width)
    keep_a, give_a = added(keep_a[:336], got_a[:336]), added(keep_a[336:], got_a[336:])
    keep_b, give_b = added(keep_b[:336], got_b[:336]), added(keep_b[336:], got_b[336:])
    d_branch, give_a, give_b = tied(d_branch, give_a, give_b)
    got_a = send(give_a, along_first(3))
    got_b = send(give_b, along_first(1))

    d_queries, left_far, left_near, summed = attend_back(
        block_ref, segment, log_total, d_branch, output_weight, queries, pairs
    )
    got_near = shifted(left_near, -1)
    got_far = shifted(left_far, -2)
    got_near, got_far, got_a, got_b = tied(got_near, got_far, got_a, got_b)
    fours = jnp.stack([added(keep_a, got_a), added(keep_b, got_b)])
    fours = fours.reshape(2, 3, 2, 56, width).swapaxes(1, 2).reshape(4, 168, width)
    mine = pick(fours, second).astype(f32)
    got = [send(pick(fours, (second + by) % 4), round_second(by)) for by in (1, 2, 3)]
    d_query, payload, query_part, key_part = call(
        key_kernel,
        [
            (square, bf16),
            ((tok, width + 2 * tok), bf16),
            ((1, head_dim), f32),
            ((1, head_dim), f32),
        ],
        q_raw,
        k_raw,
        d_queries,
        summed,
        got_near,
        got_far,
        cosine,
        sine,
        query_gain,
        key_gain,
        query_weight,
        key_weight,
        value_weight,
        flops=6 * tok * width * head_dim,
    )
    payload, *got = tied(payload, *got)
    mine = (mine + got[0].astype(f32) + (got[1].astype(f32) + got[2].astype(f32))).astype(bf16)
    got = [send(mine, round_second(by)) for by in (1, 2, 3)]
    got_both = quarters(payload)
    (products,) = call(
        products_kernel,
        [((2 * head_dim, width), bf16)],
        context,
        d_branch,
        d_query,
        normed,
        flops=4 * tok * width * head_dim,
    )
    *got_both, got[0], got[1], got[2] = tied(*got_both, *got)
    quarter = jnp.zeros((4, *mine.shape), bf16)
    quarter = lax.dynamic_update_index_in_dim(quarter, mine, second, 0)
    for by, part in zip((1, 2, 3), got, strict=True):
        quarter = lax.dynamic_update_index_in_dim(quarter, part, (second + 4 - by) % 4, 0)
    near_a = send(quarter, along_first(1))
    near_b = send(quarter, along_first(3))
    other_own = send(quarter, swap_cores())
    input_own, rest_part = call(
        entry_kernel,
        [(piece, bf16), ((tok, width), bf16)],
        place,
        *got_both,
        layer_input,
        d_middle,
        attn_norm_gain,
        normed,
        post_part,
        ffw_part,
        final_part,
        query_part,
        key_part,
        scalars=1,
        flops=2 * 128 * tok * width,
    )
    pack = jnp.concatenate([products.reshape(2, 256, width), rest_part[None]])
    pack = pack.reshape(3, 4, 4, 2, 8, width)
    pack_got = send(lax.dynamic_index_in_dim(pack, 1 - core, 3, keepdims=False), swap_cores())
    pack = added(lax.dynamic_index_in_dim(pack, core, 3, keepdims=False), pack_got)
    pack = jnp.where(core == 0, pack.transpose(2, 0, 1, 3, 4), pack.transpose(1, 0, 2, 3, 4))
    given = [pick(pack, (first + by) % 4) for by in (1, 2, 3)]
    given = [send(part, round_first(by)) for by, part in zip((1, 2, 3), given, strict=True)]
    *given, near_a, near_b = tied(*given, near_a, near_b)
    far_a = send(near_b[:2], along_first(1))
    far_b = send(near_a[2:], along_first(3))
    other_a = send(near_a, swap_cores())
    other_b = send(near_b, swap_cores())
    pack = pick(pack, first).astype(f32)
    for part in given:
        pack = pack + part.astype(f32)
    pack = lax.optimization_barrier(pack.astype(bf16))
    pack = all_sum(pack, round_second).astype(bf16)
    pack, far_a, far_b = tied(pack, far_a, far_b)
    other_far_a = send(far_a, swap_cores())
    other_far_b = send(far_b, swap_cores())
    grads = placed(
        where,
        [
            (quarter, False, 0, 0),
            (near_a, False, 1, 0),
            (near_b, False, 3, 0),
            (other_own, True, 0, 0),
            (other_a, True, 1, 0),
            (other_b, True, 3, 0),
        ],
        [],
        units,
    )
    given = [send(pack[2], round_x(by)) for by in (1, 2, 3)]
    grads = list(grads)
    *given, grads[0] = tied(*given, grads[0])
    rest = jnp.zeros((4, *pack.shape[1:]), bf16)
    rest = lax.dynamic_update_index_in_dim(rest, pack[2], lane, 0)
    for by, part in zip((1, 2, 3), given, strict=True):
        rest = lax.dynamic_update_index_in_dim(rest, part, (lane + 4 - by) % 4, 0)
    pack = jnp.concatenate([pack[:2], rest])
    pack, out_own, input_own = tied(pack, out_own, input_own)
    ends = gather(jnp.stack([out_own, input_own]), lane, round_x)
    given = [send(pack, round_first(by)) for by in (1, 2, 3)]
    grads = placed(
        where,
        [
            (far_a, False, 2, 0),
            (far_b, False, 2, 2),
            (other_far_a, True, 2, 0),
            (other_far_b, True, 2, 2),
        ],
        grads,
        units,
    )
    *given, down_grad, gate_grad, up_grad = tied(*given, *grads)
    whole = jnp.zeros((4, *pack.shape), bf16)
    whole = lax.dynamic_update_index_in_dim(whole, pack, first, 0)
    for by, part in zip((1, 2, 3), given, strict=True):
        whole = lax.dynamic_update_index_in_dim(whole, part, (first + 4 - by) % 4, 0)
    pack_got = send(whole, swap_cores())
    out_grad, query_grad, key_grad, value_grad, gains = finished(
        core.astype(jnp.int32).reshape(1), whole, pack_got
    )
    layer_output = ends[:, 0].reshape(tok, width)
    input_grad = ends[:, 1].reshape(tok, width)
    return (
        layer_output,
        input_grad,
        gains[0],
        query_grad,
        key_grad,
        value_grad,
        gains[4, :head_dim],
        gains[4, head_dim : 2 * head_dim],
        out_grad,
        gains[1],
        gains[2],
        gate_grad.T,
        up_grad.T,
        down_grad,
        gains[3],
    )


def solution(mesh):
    rows = P("seq", None)
    return jax.shard_map(
        local,
        mesh=mesh,
        in_specs=(
            rows,
            P("seq"),
            rows,
            P(),
            P(None, "tensor"),
            P(),
            P(),
            P(),
            P(),
            P("tensor", None),
            P(),
            P(),
            P(None, "tensor"),
            P(None, "tensor"),
            P("tensor", None),
            P(),
        ),
        out_specs=(
            rows,
            rows,
            P(),
            P(None, "tensor"),
            P(),
            P(),
            P(),
            P(),
            P("tensor", None),
            P(),
            P(),
            P(None, "tensor"),
            P(None, "tensor"),
            P("tensor", None),
            P(),
        ),
        check_vma=False,
    )
```

```python
import functools

import jax
import jax.numpy as jnp
import numpy as np
from jax import lax
from jax.experimental import pallas as pl
from jax.experimental.pallas import tpu as pltpu
from jax.sharding import PartitionSpec as P

WINDOW = 512
VMEM = 60 * 1024 * 1024

eps = 1e-06
rope_base = 10000.0
f32 = jnp.float32
bf16 = jnp.bfloat16
BOTH = ("seq", "tensor")


def places():
    return [(z, y, c, x) for z in range(4) for y in range(4) for c in range(2) for x in range(4)]


def number(z, y, c, x):
    return ((z * 4 + y) * 2 + c) * 4 + x


def route(move):
    return [(number(*p), number(*move(*p))) for p in places()]


def round_x(by):
    return route(lambda z, y, c, x: (z, y, c, (x + by) % 4))


def swap_cores():
    return route(lambda z, y, c, x: (z, y, 1 - c, x))


def along_first(flip):
    return route(lambda z, y, c, x: (z, y ^ flip, c, x) if c == 0 else (z ^ flip, y, c, x))


def round_first(by):
    return route(
        lambda z, y, c, x: (z, (y + by) % 4, c, x) if c == 0 else ((z + by) % 4, y, c, x)
    )


def round_second(by):
    return route(
        lambda z, y, c, x: ((z + by) % 4, y, c, x) if c == 0 else (z, (y + by) % 4, c, x)
    )


def send(value, pairs):
    return lax.ppermute(value, BOTH, pairs)


def shifted(value, by):
    pairs = [
        (i * 4 + x, (i + by) * 4 + x) for i in range(32) if 0 <= i + by < 32 for x in range(4)
    ]
    return send(value, pairs)


def pick(parts, index):
    return lax.dynamic_index_in_dim(parts, index, 0, keepdims=False)


def dot(first, second, over):
    return lax.dot_general(
        first, second, (((over[0],), (over[1],)), ((), ())), preferred_element_type=f32
    )


def scatter_sum(parts, index, turn):
    total = pick(parts, index).astype(f32)
    for by in (1, 2, 3):
        total = total + send(pick(parts, (index + by) % 4), turn(by)).astype(f32)
    return total


def gather(part, index, turn):
    whole = jnp.zeros((4, *part.shape), part.dtype)
    whole = lax.dynamic_update_index_in_dim(whole, part, index, 0)
    for by in (1, 2, 3):
        whole = lax.dynamic_update_index_in_dim(
            whole, send(part, turn(by)), (index + 4 - by) % 4, 0
        )
    return whole


def inv_scale(values):
    return lax.rsqrt(jnp.mean(values * values, axis=-1, keepdims=True) + eps)


def norm_back(values, scale, gain, grad):
    unit = values * scale
    weighted = grad * gain
    d_values = scale * (weighted - unit * jnp.mean(weighted * unit, axis=-1, keepdims=True))
    return (d_values, jnp.sum(grad * unit, axis=0))


def rotate(values, cosine, sine):
    half = values.shape[-1] // 2
    first = values[..., :half]
    second = values[..., half:]
    return jnp.concatenate(
        [first * cosine - second * sine, second * cosine + first * sine], axis=-1
    )


def padded(values, rows):
    return jnp.pad(values, ((0, rows - values.shape[0]), (0, 0)))


def added(first, second):
    return (first.astype(f32) + second.astype(f32)).astype(bf16)


def tied(*values):
    return lax.optimization_barrier(values)


def call(kernel, outs, *arrays, scalars=0, flops=0):
    vmem = pl.BlockSpec(memory_space=pltpu.VMEM)
    outs = [jax.ShapeDtypeStruct(*o) for o in outs]
    moved = sum(v.size * v.dtype.itemsize for v in (*arrays, *outs))
    return pl.pallas_call(
        kernel,
        out_shape=outs,
        in_specs=[pl.BlockSpec(memory_space=pltpu.SMEM)] * scalars
        + [vmem] * (len(arrays) - scalars),
        out_specs=[vmem] * len(outs),
        compiler_params=pltpu.CompilerParams(vmem_limit_bytes=VMEM),
        cost_estimate=pl.CostEstimate(flops=flops, bytes_accessed=moved, transcendentals=0),
    )(*arrays)


def own_rows(ref, lane, rows):
    return ref[pl.ds(pl.multiple_of(lane * rows, rows), rows)].astype(f32)


def project_kernel(
    place, x, post_gain, ffw_gain, ctx0, ctx1, ctx2, ctx3, weight, own1, own2, own3, other1, other2, other3,
    branch, middle, normed
):
    even = place[1] == 0
    half = own1.shape[0]
    total = dot(ctx0[...], weight[...], (1, 0))
    for ctx, mine, theirs in ((ctx1, own1, other1), (ctx2, own2, other2), (ctx3, own3, other3)):
        low = jnp.where(even, mine[...], theirs[...])
        high = jnp.where(even, theirs[...], mine[...])
        total += dot(ctx[:, :half], low, (1, 0)) + dot(ctx[:, half:], high, (1, 0))
    branch[...] = total
    after = x[...].astype(f32) + total * inv_scale(total) * post_gain[...]
    middle[...] = after
    normed[...] = (after * inv_scale(after) * ffw_gain[...]).astype(bf16)


def forward_kernel(normed, gate_weight, up_weight, down_weight, gate, up, hidden, out, total):
    step = pl.program_id(0)
    gated = dot(gate_weight[...], normed[...], (1, 1))
    raised = dot(up_weight[...], normed[...], (1, 1))
    gate[...] = gated
    up[...] = raised
    hid = (jax.nn.gelu(gated, approximate=True) * raised).astype(bf16)
    hidden[...] = hid
    part = dot(hid, down_weight[...], (0, 0))

    @pl.when(step == 0)
    def _():
        total[...] = part

    @pl.when(step > 0)
    def _():
        total[...] += part

    @pl.when(step == pl.num_programs(0) - 1)
    def _():
        out[...] = total[...].astype(bf16)


def feed_forward(normed, gate_weight, up_weight, down_weight):
    tok, width = normed.shape
    units = down_weight.shape[0]
    steps = 4
    rows = pl.BlockSpec((units // steps, width), lambda i: (i, 0))
    tall = pl.BlockSpec((units // steps, tok), lambda i: (i, 0))
    whole = pl.BlockSpec((tok, width), lambda i: (0, 0))
    return pl.pallas_call(
        forward_kernel,
        grid=(steps,),
        out_shape=[
            jax.ShapeDtypeStruct((units, tok), f32),
            jax.ShapeDtypeStruct((units, tok), f32),
            jax.ShapeDtypeStruct((units, tok), bf16),
            jax.ShapeDtypeStruct((tok, width), bf16),
        ],
        in_specs=[whole, rows, rows, rows],
        out_specs=[tall, tall, tall, whole],
        scratch_shapes=[pltpu.VMEM((tok, width), f32)],
        compiler_params=pltpu.CompilerParams(vmem_limit_bytes=VMEM),
        cost_estimate=pl.CostEstimate(
            flops=6 * tok * width * units,
            bytes_accessed=6 * units * width,
            transcendentals=tok * units,
        ),
    )(normed, gate_weight, up_weight, down_weight)


def backward_kernel(
    d_branch, gate_weight, up_weight, down_weight, gate, up, d_gate, d_up, out, total
):
    step = pl.program_id(0)
    d_hidden = dot(down_weight[...], d_branch[...], (1, 1))
    value = gate[...]
    ratio = (2.0 / np.pi) ** 0.5
    bent = jnp.tanh(ratio * (value + 0.044715 * value * value * value))
    slope = 0.5 * (1.0 + bent)
    active = value * slope
    slope = slope + 0.5 * value * (1.0 - bent * bent) * ratio * (
        1.0 + 3.0 * 0.044715 * value * value
    )
    d_gated = (d_hidden * up[...] * slope).astype(bf16)
    d_raised = (d_hidden * active).astype(bf16)
    d_gate[...] = d_gated
    d_up[...] = d_raised
    part = dot(d_gated, gate_weight[...], (0, 0)) + dot(d_raised, up_weight[...], (0, 0))

    @pl.when(step == 0)
    def _():
        total[...] = part

    @pl.when(step > 0)
    def _():
        total[...] += part

    @pl.when(step == pl.num_programs(0) - 1)
    def _():
        out[...] = total[...].astype(bf16)


def feed_back(d_branch, gate_weight, up_weight, down_weight, gate, up):
    tok, width = d_branch.shape
    units = down_weight.shape[0]
    steps = 4
    rows = pl.BlockSpec((units // steps, width), lambda i: (i, 0))
    tall = pl.BlockSpec((units // steps, tok), lambda i: (i, 0))
    whole = pl.BlockSpec((tok, width), lambda i: (0, 0))
    return pl.pallas_call(
        backward_kernel,
        grid=(steps,),
        out_shape=[
            jax.ShapeDtypeStruct((units, tok), bf16),
            jax.ShapeDtypeStruct((units, tok), bf16),
            jax.ShapeDtypeStruct((tok, width), bf16),
        ],
        in_specs=[whole, rows, rows, rows, tall, tall],
        out_specs=[tall, tall, whole],
        scratch_shapes=[pltpu.VMEM((tok, width), f32)],
        compiler_params=pltpu.CompilerParams(vmem_limit_bytes=VMEM),
        cost_estimate=pl.CostEstimate(
            flops=6 * tok * width * units,
            bytes_accessed=6 * units * width,
            transcendentals=tok * units,
        ),
    )(d_branch, gate_weight, up_weight, down_weight, gate, up)


def final_kernel(place, p0, p1, p2, p3, middle, cotangent, gain, out, d_branch, part):
    lane = place[0]
    branch = p0[...].astype(f32) + p1[...].astype(f32) + p2[...].astype(f32) + p3[...].astype(f32)
    rows = branch.shape[0]
    scale = inv_scale(branch)
    cot = own_rows(cotangent, lane, rows)
    out[...] = (own_rows(middle, lane, rows) + branch * scale * gain[...]).astype(bf16)
    d_values, d_gain = norm_back(branch, scale, gain[...], cot)
    d_branch[...] = d_values.astype(bf16)
    part[...] = d_gain[None]


def between_kernel(
    place, p0, p1, p2, p3, middle, branch, cotangent, ffw_gain, post_gain,
    d_middle, d_branch, ffw_part, post_part
):
    lane = place[0]
    grad = p0[...].astype(f32) + p1[...].astype(f32) + p2[...].astype(f32) + p3[...].astype(f32)
    rows = grad.shape[0]
    after = own_rows(middle, lane, rows)
    before = own_rows(branch, lane, rows)
    d_values, d_gain = norm_back(after, inv_scale(after), ffw_gain[...], grad)
    ffw_part[...] = d_gain[None]
    d_values = own_rows(cotangent, lane, rows) + d_values
    d_middle[...] = d_values
    d_values, d_gain = norm_back(before, inv_scale(before), post_gain[...], d_values)
    d_branch[...] = d_values.astype(bf16)
    post_part[...] = d_gain[None]


def key_kernel(
    q_raw, k_raw, d_queries, d_own, d_near, d_far, cosine, sine, query_gain, key_gain, query_weight, key_weight,
    value_weight, d_query, payload, query_part, key_part
):
    tok, head_dim = q_raw.shape
    width = query_weight.shape[0]
    cos, sin = cosine[...], -sine[...]
    raw = q_raw[...]
    d_raw, d_gain = norm_back(
        raw, inv_scale(raw), query_gain[...], rotate(d_queries[...] * head_dim**-0.5, cos, sin)
    )
    query_part[...] = d_gain[None]
    d_low = d_raw.astype(bf16)
    d_query[...] = d_low
    total = dot(d_low, query_weight[...], (1, 1))
    summed = d_own[...] + d_near[...].astype(f32) + d_far[...].astype(f32)
    raw = k_raw[...]
    d_raw, d_gain = norm_back(raw, inv_scale(raw), key_gain[...], rotate(summed[:tok], cos, sin))
    key_part[...] = d_gain[None]
    total += dot(d_raw.astype(bf16), key_weight[...], (1, 1))
    total += dot(summed[tok:].astype(bf16), value_weight[...], (1, 1))
    payload[:, :width] = total.astype(bf16)
    payload[:, width : width + tok] = d_raw.T.astype(bf16)
    payload[:, width + tok :] = summed[tok:].T.astype(bf16)


def products_kernel(context, d_branch, d_query, normed, out):
    half = context.shape[1]
    out[:half] = dot(context[...], d_branch[...], (0, 0))
    out[half:] = dot(d_query[...], normed[...], (0, 0))


def entry_kernel(
    place, p0, p1, p2, p3, x, d_middle, gain, normed, post_part, ffw_part, final_part, query_part, key_part,
    products, input_grad, keep, give, rest
):
    lane, core = place[0], place[1]
    both = p0[...].astype(f32) + p1[...].astype(f32) + p2[...].astype(f32) + p3[...].astype(f32)
    rows = both.shape[0]
    width = normed.shape[1]
    tok = normed.shape[0]
    full = own_rows(x, lane, rows)
    d_values, d_gain = norm_back(full, inv_scale(full), gain[...], both[:, :width])
    input_grad[...] = (d_middle[...] + d_values).astype(bf16)
    d_keys = both[:, width : width + tok].astype(bf16)
    d_values = both[:, width + tok :].astype(bf16)
    rest[:rows] = dot(d_keys, normed[...], (1, 0))
    rest[rows : 2 * rows] = dot(d_values, normed[...], (1, 0))
    heads = jnp.concatenate(
        [query_part[...], key_part[...], jnp.zeros((1, width - 2 * query_part.shape[1]), f32)], axis=1
    )
    index = lax.broadcasted_iota(jnp.int32, (8, width), 0)
    gains = jnp.zeros((8, width), f32)
    for at, part in enumerate((d_gain[None], post_part[...], ffw_part[...], final_part[...], heads)):
        gains = jnp.where(index == at, part, gains)
    rest[2 * rows : 2 * rows + 8] = gains
    rest[2 * rows + 8 :] = jnp.zeros((rest.shape[0] - 2 * rows - 8, width), f32)
    for kind in range(3):
        source = rest if kind == 2 else products
        base = 256 if kind == 1 else 0
        for chip in range(16):
            at = base + 16 * chip
            keep[kind, chip] = source[pl.ds(pl.multiple_of(at + 8 * core, 8), 8)]
            give[kind, chip] = source[pl.ds(pl.multiple_of(at + 8 - 8 * core, 8), 8)].astype(bf16)


def merge_kernel(where, keep, got, *outs):
    core, first = where[0], where[1]
    for by, out in enumerate(outs):
        along = lax.rem(first + by, 4)
        for across in range(4):
            chip = jnp.where(core == 0, 4 * across + along, 4 * along + across)
            for kind in range(3):
                total = keep[kind, chip] + got[kind, chip].astype(f32)
                out[kind, across] = total.astype(out.dtype)


def weight_kernel(
    hid_own, hid_got, gate_own, gate_got, up_own, up_got, dy_own, dy_got, xn_own, xn_got, *outs
):
    mats = (
        (hid_own, hid_got, dy_own, dy_got),
        (gate_own, gate_got, xn_own, xn_got),
        (up_own, up_got, xn_own, xn_got),
    )
    for group, out in enumerate(outs):
        for index, (left_own, left_got, right_own, right_got) in enumerate(mats):
            total = jnp.dot(left_own[group], right_own[...], preferred_element_type=f32)
            total += jnp.dot(left_got[group], right_got[...], preferred_element_type=f32)
            total = total.astype(bf16)
            out[112 * index : 112 * index + 112] = total[:112]
            out[336 + 112 * index : 448 + 112 * index] = total[112:]


def weight_parts(*arrays):
    width = arrays[-1].shape[1]
    return pl.pallas_call(
        weight_kernel,
        out_shape=[jax.ShapeDtypeStruct((672, width), bf16)] * 4,
        in_specs=[pl.BlockSpec(memory_space=pltpu.VMEM)] * len(arrays),
        out_specs=[pl.BlockSpec(memory_space=pltpu.VMEM)] * 4,
        compiler_params=pltpu.CompilerParams(vmem_limit_bytes=VMEM),
        cost_estimate=pl.CostEstimate(
            flops=2 * 2688 * 512 * width, bytes_accessed=12_000_000, transcendentals=0
        ),
    )(*arrays)


def masks(block, segment, pairs):
    tok = segment.shape[0]
    query = lax.broadcasted_iota(jnp.int32, (tok, tok), 0)
    key = lax.broadcasted_iota(jnp.int32, (tok, tok), 1)
    same = [segment == pair[2 * tok : 2 * tok + 16].astype(f32)[:1] for pair in pairs]
    return (
        same[0] & (key > query) & (block >= 2),
        same[1] & (block >= 1),
        same[2] & (key <= query),
    )


def prepare_kernel(
    place, x, gain, key_weight, value_weight, query_weight, key_gain, query_gain, start_cos, start_sin, inner_cos,
    inner_sin, marks, xn, pair, k_raw, q_raw, queries, cosine, sine
):
    tok, head_dim = k_raw.shape
    full = x[...].astype(f32)
    low = (full * inv_scale(full) * gain[...]).astype(bf16)
    xn[...] = low
    at = pl.ds(place[2], 1)
    cos = start_cos[at] * inner_cos[...] - start_sin[at] * inner_sin[...]
    sin = start_sin[at] * inner_cos[...] + start_cos[at] * inner_sin[...]
    cosine[...] = cos
    sine[...] = sin
    raw = dot(low, key_weight[...], (1, 0))
    k_raw[...] = raw
    pair[:tok] = rotate(raw * inv_scale(raw) * key_gain[...], cos, sin).astype(bf16)
    pair[tok : 2 * tok] = dot(low, value_weight[...], (1, 0)).astype(bf16)
    pair[2 * tok :] = jnp.broadcast_to(marks[...].astype(f32)[None], (16, tok)).astype(bf16)
    raw = dot(low, query_weight[...], (1, 0))
    q_raw[...] = raw
    turned = rotate(raw * inv_scale(raw) * query_gain[...], cos, sin)
    queries[...] = (turned * head_dim**-0.5).astype(bf16)


def attend_kernel(block, segment, queries, far, near, own, context, log_total):
    pairs = (far, near, own)
    tok = queries.shape[0]
    allowed = masks(block[0], segment[...], pairs)
    scores = [
        jnp.where(ok, dot(queries[...], pair[:tok], (1, 1)), -1e30)
        for ok, pair in zip(allowed, pairs, strict=True)
    ]
    top = functools.reduce(jnp.maximum, [jnp.max(s, axis=1, keepdims=True) for s in scores])
    weights = [jnp.exp(s - top) for s in scores]
    total = sum(jnp.sum(w, axis=1, keepdims=True) for w in weights)
    context[...] = sum(
        dot((w / total).astype(bf16), pair[tok : 2 * tok], (1, 0))
        for w, pair in zip(weights, pairs, strict=True)
    ).astype(bf16)
    log_total[...] = jnp.broadcast_to(top + jnp.log(total), log_total.shape)


def attend(block, segment, queries, pairs):
    tok, head_dim = queries.shape
    vmem = pl.BlockSpec(memory_space=pltpu.VMEM)
    return pl.pallas_call(
        attend_kernel,
        out_shape=[
            jax.ShapeDtypeStruct((tok, head_dim), bf16),
            jax.ShapeDtypeStruct((tok, 128), f32),
        ],
        in_specs=[pl.BlockSpec(memory_space=pltpu.SMEM)] + [vmem] * 5,
        out_specs=[vmem] * 2,
        compiler_params=pltpu.CompilerParams(vmem_limit_bytes=VMEM),
        cost_estimate=pl.CostEstimate(
            flops=12 * tok * tok * head_dim, bytes_accessed=1_500_000, transcendentals=3 * tok * tok
        ),
    )(block, segment, queries, *pairs)


def attend_back_kernel(
    block, segment, log_total, d_branch, weight, queries, far, near, own, d_queries, d_far, d_near, d_own
):
    pairs = (far, near, own)
    tok = queries.shape[0]
    d_context = dot(d_branch[...], weight[...], (1, 1)).astype(bf16)
    allowed = masks(block[0], segment[...], pairs)
    lse = log_total[:, :1]
    probs, d_probs = [], []
    for ok, pair in zip(allowed, pairs, strict=True):
        scores = jnp.where(ok, dot(queries[...], pair[:tok], (1, 1)), -1e30)
        probs.append(jnp.exp(scores - lse))
        d_probs.append(dot(d_context, pair[tok : 2 * tok], (1, 1)))
    mean = sum(
        jnp.sum(p * d, axis=1, keepdims=True) for p, d in zip(probs, d_probs, strict=True)
    )
    total = None
    for p, d, pair, out in zip(probs, d_probs, pairs, (d_far, d_near, d_own), strict=True):
        d_scores = (p * (d - mean)).astype(bf16)
        part = dot(d_scores, pair[:tok], (1, 0))
        total = part if total is None else total + part
        out[:tok] = dot(d_scores, queries[...], (0, 0)).astype(out.dtype)
        out[tok:] = dot(p.astype(bf16), d_context, (0, 0)).astype(out.dtype)
    d_queries[...] = total


def attend_back(block, segment, log_total, d_branch, weight, queries, pairs):
    tok, head_dim = queries.shape
    vmem = pl.BlockSpec(memory_space=pltpu.VMEM)
    return pl.pallas_call(
        attend_back_kernel,
        out_shape=[
            jax.ShapeDtypeStruct((tok, head_dim), f32),
            jax.ShapeDtypeStruct((2 * tok, head_dim), bf16),
            jax.ShapeDtypeStruct((2 * tok, head_dim), bf16),
            jax.ShapeDtypeStruct((2 * tok, head_dim), f32),
        ],
        in_specs=[pl.BlockSpec(memory_space=pltpu.SMEM)] + [vmem] * 8,
        out_specs=[vmem] * 4,
        compiler_params=pltpu.CompilerParams(vmem_limit_bytes=VMEM),
        cost_estimate=pl.CostEstimate(
            flops=30 * tok * tok * head_dim, bytes_accessed=3_500_000, transcendentals=3 * tok * tok
        ),
    )(block, segment, log_total, d_branch, weight, queries, *pairs)


def place_kernel(where_ref, *refs, turns, held):
    n = len(turns)
    parts, outs = refs[:n], refs[n + held : n + held + 3]
    stage, sems, tail_sems = refs[-3:]
    slots = stage.shape[0]
    core, first, second = where_ref[0], where_ref[1], where_ref[2]
    chunks = [
        (ref, i, base + i, other, flip)
        for ref, (other, flip, base) in zip(parts, turns, strict=True)
        for i in range(ref.shape[0])
    ]

    def place(index):
        _, _, across, other, flip = chunks[index]
        which = 1 - core if other else core
        along = (second if other else first) ^ flip
        y = jnp.where(which == 0, along, across)
        z = jnp.where(which == 0, across, along)
        odd = lax.rem(y, 2)
        row = 216 * (2 * z + y // 2) + 104 * odd + 48 * which + 8 * which * odd
        return pl.multiple_of(row, 8), (which == 1) | (odd == 1)

    def copies(index):
        slot = index % slots
        row, whole = place(index)
        for mat, out in enumerate(outs):
            yield (
                pltpu.make_async_copy(
                    stage.at[slot, mat, pl.ds(0, 48)],
                    out.at[pl.ds(row, 48)],
                    sems.at[slot, mat],
                ),
                pltpu.make_async_copy(
                    stage.at[slot, mat, pl.ds(48, 8)],
                    out.at[pl.ds(pl.multiple_of(row + 48, 8), 8)],
                    tail_sems.at[slot, mat],
                ),
                whole,
            )

    def finish(index):
        for most, tail, whole in copies(index):
            most.wait()
            pl.when(whole)(tail.wait)

    for index, (ref, i, *_) in enumerate(chunks):
        if index >= slots:
            finish(index - slots)
        stage[index % slots] = ref[i].astype(f32)
        for most, tail, whole in copies(index):
            most.start()
            pl.when(whole)(tail.start)
    for index in range(max(0, len(chunks) - slots), len(chunks)):
        finish(index)


def placed(where, parts, outs, units):
    arrays = [p[0].reshape(-1, 3, 56, p[0].shape[-1]) for p in parts]
    width = arrays[0].shape[-1]
    slots = 4
    return pl.pallas_call(
        functools.partial(
            place_kernel, turns=tuple(p[1:] for p in parts), held=len(outs)
        ),
        out_shape=[jax.ShapeDtypeStruct((units, width), f32)] * 3,
        in_specs=[pl.BlockSpec(memory_space=pltpu.SMEM)]
        + [pl.BlockSpec(memory_space=pltpu.VMEM)] * len(arrays)
        + [pl.BlockSpec(memory_space=pl.ANY)] * len(outs),
        out_specs=[pl.BlockSpec(memory_space=pl.ANY)] * 3,
        scratch_shapes=[
            pltpu.VMEM((slots, 3, 56, width), f32),
            pltpu.SemaphoreType.DMA((slots, 3)),
            pltpu.SemaphoreType.DMA((slots, 3)),
        ],
        input_output_aliases={1 + len(arrays) + i: i for i in range(len(outs))},
        compiler_params=pltpu.CompilerParams(vmem_limit_bytes=VMEM),
        cost_estimate=pl.CostEstimate(
            flops=0, bytes_accessed=sum(p.size for p in arrays) * 6, transcendentals=0
        ),
    )(where, *arrays, *outs)


def finish_kernel(
    core_ref, own, got, out_grad, query_grad, key_grad, value_grad, attn, post, ffw, final, query, key, rows
):
    core = core_ref[0]
    for pieces, other in ((own, 0), (got, 1)):
        even = core == other
        for along in range(4):
            for across in range(4):
                row = jnp.where(even, 8 * across + 2 * along, 8 * along + 2 * across + 1) * 8
                row = pl.ds(pl.multiple_of(row, 8), 8)
                for kind in range(6):
                    rows[kind, row] = pieces[along, kind, across].astype(f32)
    out_grad[...] = rows[0]
    query_grad[...] = rows[1].T
    for lane in range(4):
        key_grad[:, 64 * lane : 64 * lane + 64] = rows[2 + lane, :64].T
        value_grad[:, 64 * lane : 64 * lane + 64] = rows[2 + lane, 64:128].T
    gains = sum(rows[2 + lane, 128:136] for lane in range(4))
    for at, out in enumerate((attn, post, ffw, final)):
        out[...] = gains[at]
    size = query.shape[0]
    query[...] = gains[4, :size]
    key[...] = gains[4, size : 2 * size]


def finished(core, own, got):
    width = own.shape[-1]
    vmem = pl.BlockSpec(memory_space=pltpu.VMEM)
    return pl.pallas_call(
        finish_kernel,
        out_shape=[
            jax.ShapeDtypeStruct((256, width), f32),
            jax.ShapeDtypeStruct((width, 256), f32),
            jax.ShapeDtypeStruct((width, 256), f32),
            jax.ShapeDtypeStruct((width, 256), f32),
            *[jax.ShapeDtypeStruct((width,), f32)] * 4,
            *[jax.ShapeDtypeStruct((256,), f32)] * 2,
        ],
        in_specs=[pl.BlockSpec(memory_space=pltpu.SMEM), vmem, vmem],
        out_specs=[vmem] * 10,
        scratch_shapes=[pltpu.VMEM((6, 256, width), f32)],
        compiler_params=pltpu.CompilerParams(vmem_limit_bytes=VMEM),
        cost_estimate=pl.CostEstimate(flops=0, bytes_accessed=10_000_000, transcendentals=0),
    )(core, own, got)


def local(
    layer_input,
    segment_ids,
    out_cotangent,
    attn_norm_gain,
    query_weight,
    key_weight,
    value_weight,
    query_gain,
    key_gain,
    output_weight,
    attn_post_gain,
    ffw_norm_gain,
    gate_weight,
    up_weight,
    down_weight,
    ffw_post_gain,
):
    tok, width = layer_input.shape
    head_dim = key_weight.shape[1]
    units = down_weight.shape[0]
    block = lax.axis_index("seq")
    lane = lax.axis_index("tensor")
    core = block % 2
    row = (block // 2) % 4
    plane = block // 8
    first = jnp.where(core == 0, row, plane)
    second = jnp.where(core == 0, plane, row)
    quarter_tok = tok // 4

    place = jnp.stack([lane, core, block]).astype(jnp.int32)
    where = jnp.stack([core, first, second]).astype(jnp.int32)
    freq = rope_base ** (-2.0 * np.arange(head_dim // 2) / head_dim)
    start = (np.arange(lax.axis_size("seq")) * tok)[:, None] * freq[None, :]
    inner = np.arange(tok)[:, None] * freq[None, :]
    tables = [jnp.asarray(f(angle), f32) for angle in (start, inner) for f in (np.cos, np.sin)]

    square = (tok, head_dim)
    normed, own_pair, k_raw, q_raw, queries, cosine, sine = call(
        prepare_kernel,
        [
            ((tok, width), bf16),
            ((2 * tok + 16, head_dim), bf16),
            (square, f32),
            (square, f32),
            (square, bf16),
            ((tok, head_dim // 2), f32),
            ((tok, head_dim // 2), f32),
        ],
        place,
        layer_input,
        attn_norm_gain,
        key_weight,
        value_weight,
        query_weight,
        key_gain,
        query_gain,
        *tables,
        segment_ids,
        scalars=1,
        flops=6 * tok * width * head_dim,
    )
    left_one = shifted(own_pair, 1)
    left_two = shifted(own_pair, 2)

    weight_half = tok // 2
    halved, _ = tied(output_weight, own_pair)
    own_weight = pick(halved.reshape(2, weight_half, width), core)
    got_weight = [send(own_weight, round_x(by)) for by in (1, 2, 3)]

    pairs = (left_two, left_one, own_pair)
    block_ref = block.astype(jnp.int32).reshape(1)
    segment = segment_ids.astype(f32)[:, None]
    context, log_total = attend(block_ref, segment, queries, pairs)

    got_context = [send(context, round_x(by)) for by in (1, 2, 3)]
    *got_context, got_weight[0], got_weight[1], got_weight[2] = tied(*got_context, *got_weight)
    other_weight = [send(part, swap_cores()) for part in got_weight]
    branch, middle, normed_two = call(
        project_kernel,
        [((tok, width), f32), ((tok, width), f32), ((tok, width), bf16)],
        place,
        layer_input,
        attn_post_gain,
        ffw_norm_gain,
        context,
        *got_context,
        output_weight,
        *got_weight,
        *other_weight,
        scalars=1,
        flops=8 * tok * tok * width,
    )
    gate, up_val, hidden, down_part = feed_forward(
        normed_two, gate_weight.T, up_weight.T, down_weight
    )

    def halves(values):
        groups = values.reshape(8, units // 8, tok)
        groups = jnp.concatenate([groups[:, :56], groups[:, 48:]], axis=1)
        pieces = groups.reshape(4, 4, 2, 56, tok)
        return (
            lax.dynamic_index_in_dim(pieces, core, 2, keepdims=False),
            lax.dynamic_index_in_dim(pieces, 1 - core, 2, keepdims=False),
        )

    def arranged(values):
        values = jnp.where(core == 0, values.swapaxes(0, 1), values)
        by_first = [pick(values, first ^ flip) for flip in range(4)]
        groups = [
            jnp.stack([by_first[i][2 * stream : 2 * stream + 2] for i in order])
            for stream, order in ((0, (0, 3)), (0, (1, 2)), (1, (0, 1)), (1, (3, 2)))
        ]
        return jnp.stack(groups).reshape(4, 224, tok)

    hidden_own, hidden_give = halves(hidden)
    hidden_got = send(hidden_give, swap_cores())
    normed_two_got = send(normed_two, swap_cores())

    def quarters(parts):
        parts = parts.reshape(4, quarter_tok, parts.shape[-1])
        given = [pick(parts, (lane + by) % 4) for by in (1, 2, 3)]
        return [pick(parts, lane)] + [
            send(part, round_x(by)) for by, part in zip((1, 2, 3), given, strict=True)
        ]

    piece = (quarter_tok, width)
    out_own, d_branch_two, final_part = call(
        final_kernel,
        [(piece, bf16), (piece, bf16), ((1, width), f32)],
        place,
        *quarters(down_part),
        middle,
        out_cotangent,
        ffw_post_gain,
        scalars=1,
    )
    d_branch_two = gather(d_branch_two, lane, round_x).reshape(tok, width)
    d_branch_two_got = send(d_branch_two, swap_cores())

    d_gate, d_up, d_normed_two = feed_back(
        d_branch_two, gate_weight.T, up_weight.T, down_weight, gate, up_val
    )
    d_gate_own, d_gate_give = halves(d_gate)
    d_up_own, d_up_give = halves(d_up)
    d_pair_got = send(jnp.stack([d_gate_give, d_up_give]), swap_cores())

    keep_a, give_a, keep_b, give_b = weight_parts(
        *(
            arranged(v)
            for v in (hidden_own, hidden_got, d_gate_own, d_pair_got[0], d_up_own, d_pair_got[1])
        ),
        d_branch_two,
        d_branch_two_got,
        normed_two,
        normed_two_got,
    )
    got_a = send(give_a, along_first(1))
    got_b = send(give_b, along_first(3))

    *got_normed, keep_a, keep_b = tied(*quarters(d_normed_two), keep_a, keep_b)
    d_middle, d_branch, ffw_part, post_part = call(
        between_kernel,
        [(piece, f32), (piece, bf16), ((1, width), f32), ((1, width), f32)],
        place,
        *got_normed,
        middle,
        branch,
        out_cotangent,
        ffw_norm_gain,
        attn_post_gain,
        scalars=1,
    )
    d_branch = gather(d_branch, lane, round_x).reshape(tok, width)
    d_queries, left_far, left_near, summed = attend_back(
        block_ref, segment, log_total, d_branch, output_weight, queries, pairs
    )
    got_near = shifted(left_near, -1)
    got_far = shifted(left_far, -2)
    got_near, got_far, got_a, got_b = tied(got_near, got_far, got_a, got_b)
    keep_a, give_a = added(keep_a[:336], got_a[:336]), added(keep_a[336:], got_a[336:])
    keep_b, give_b = added(keep_b[:336], got_b[:336]), added(keep_b[336:], got_b[336:])
    got_a = send(give_a, along_first(3))
    got_b = send(give_b, along_first(1))
    d_query, payload, query_part, key_part = call(
        key_kernel,
        [
            (square, bf16),
            ((tok, width + 2 * tok), bf16),
            ((1, head_dim), f32),
            ((1, head_dim), f32),
        ],
        q_raw,
        k_raw,
        d_queries,
        summed,
        got_near,
        got_far,
        cosine,
        sine,
        query_gain,
        key_gain,
        query_weight,
        key_weight,
        value_weight,
        flops=6 * tok * width * head_dim,
    )
    got_both = quarters(payload)
    (products,) = call(
        products_kernel,
        [((2 * head_dim, width), f32)],
        context,
        d_branch,
        d_query,
        normed,
        flops=4 * tok * width * head_dim,
    )
    *got_both, got_a, got_b = tied(*got_both, got_a, got_b)
    fours = jnp.stack([added(keep_a, got_a), added(keep_b, got_b)])
    fours = fours.reshape(2, 3, 2, 56, width).swapaxes(1, 2).reshape(4, 168, width)
    mine = pick(fours, second).astype(f32)
    got = [send(pick(fours, (second + by) % 4), round_second(by)) for by in (1, 2, 3)]
    input_own, keep, give = pl.pallas_call(
        entry_kernel,
        out_shape=[
            jax.ShapeDtypeStruct(piece, bf16),
            jax.ShapeDtypeStruct((3, 16, 8, width), f32),
            jax.ShapeDtypeStruct((3, 16, 8, width), bf16),
        ],
        in_specs=[pl.BlockSpec(memory_space=pltpu.SMEM)]
        + [pl.BlockSpec(memory_space=pltpu.VMEM)] * 14,
        out_specs=[pl.BlockSpec(memory_space=pltpu.VMEM)] * 3,
        scratch_shapes=[pltpu.VMEM((tok, width), f32)],
        compiler_params=pltpu.CompilerParams(vmem_limit_bytes=VMEM),
        cost_estimate=pl.CostEstimate(
            flops=256 * tok * width, bytes_accessed=12_000_000, transcendentals=0
        ),
    )(
        place,
        *got_both,
        layer_input,
        d_middle,
        attn_norm_gain,
        normed,
        post_part,
        ffw_part,
        final_part,
        query_part,
        key_part,
        products,
    )
    pack_got = send(give, swap_cores())
    pack_got, *got = tied(pack_got, *got)
    mine = (mine + got[0].astype(f32) + (got[1].astype(f32) + got[2].astype(f32))).astype(bf16)
    got = [send(mine, round_second(by)) for by in (1, 2, 3)]
    part = (3, 4, 8, width)
    pack, *given = call(
        merge_kernel, [(part, f32)] + [(part, bf16)] * 3, where, keep, pack_got, scalars=1
    )
    given = [send(part, round_first(by)) for by, part in zip((1, 2, 3), given, strict=True)]
    *given, got[0], got[1], got[2] = tied(*given, *got)
    quarter = jnp.zeros((4, *mine.shape), bf16)
    quarter = lax.dynamic_update_index_in_dim(quarter, mine, second, 0)
    for by, part in zip((1, 2, 3), got, strict=True):
        quarter = lax.dynamic_update_index_in_dim(quarter, part, (second + 4 - by) % 4, 0)
    for part in given:
        pack = pack + part.astype(f32)
    pack = lax.optimization_barrier(pack.astype(bf16))
    given = [send(pack, round_second(by)) for by in (1, 2, 3)]
    *given, quarter = tied(*given, quarter)
    pack = pack.astype(f32) + given[1].astype(f32) + (given[0].astype(f32) + given[2].astype(f32))
    pack = pack.astype(bf16)
    near_a = send(quarter, along_first(1))
    near_b = send(quarter, along_first(3))
    other_own = send(quarter, swap_cores())
    given = [send(pack[2], round_x(by)) for by in (1, 2, 3)]
    *given, near_a, near_b = tied(*given, near_a, near_b)
    far_a = send(near_b[:2], along_first(1))
    far_b = send(near_a[2:], along_first(3))
    other_a = send(near_a, swap_cores())
    other_b = send(near_b, swap_cores())
    grads = placed(
        where,
        [
            (quarter, False, 0, 0),
            (near_a, False, 1, 0),
            (near_b, False, 3, 0),
            (other_own, True, 0, 0),
            (other_a, True, 1, 0),
            (other_b, True, 3, 0),
        ],
        [],
        units,
    )
    rest = jnp.zeros((4, *pack.shape[1:]), bf16)
    rest = lax.dynamic_update_index_in_dim(rest, pack[2], lane, 0)
    for by, part in zip((1, 2, 3), given, strict=True):
        rest = lax.dynamic_update_index_in_dim(rest, part, (lane + 4 - by) % 4, 0)
    pack = jnp.concatenate([pack[:2], rest])
    pack, out_own, input_own = tied(pack, out_own, input_own)
    ends = gather(jnp.stack([out_own, input_own]), lane, round_x)
    given = [send(pack, round_first(by)) for by in (1, 2, 3)]
    grads = list(grads)
    *given, grads[0] = tied(*given, grads[0])
    whole = jnp.zeros((4, *pack.shape), bf16)
    whole = lax.dynamic_update_index_in_dim(whole, pack, first, 0)
    for by, part in zip((1, 2, 3), given, strict=True):
        whole = lax.dynamic_update_index_in_dim(whole, part, (first + 4 - by) % 4, 0)
    pack_got = send(whole, swap_cores())
    out_grad, query_grad, key_grad, value_grad, *gains = finished(
        core.astype(jnp.int32).reshape(1), whole, pack_got
    )
    other_far_a = send(far_a, swap_cores())
    other_far_b = send(far_b, swap_cores())
    down_grad, gate_grad, up_grad = placed(
        where,
        [
            (far_a, False, 2, 0),
            (far_b, False, 2, 2),
            (other_far_a, True, 2, 0),
            (other_far_b, True, 2, 2),
        ],
        grads,
        units,
    )
    layer_output = ends[:, 0].reshape(tok, width)
    input_grad = ends[:, 1].reshape(tok, width)
    return (
        layer_output,
        input_grad,
        gains[0],
        query_grad,
        key_grad,
        value_grad,
        gains[4],
        gains[5],
        out_grad,
        gains[1],
        gains[2],
        gate_grad.T,
        up_grad.T,
        down_grad,
        gains[3],
    )


def solution(mesh):
    rows = P("seq", None)
    return jax.shard_map(
        local,
        mesh=mesh,
        in_specs=(
            rows,
            P("seq"),
            rows,
            P(),
            P(None, "tensor"),
            P(),
            P(),
            P(),
            P(),
            P("tensor", None),
            P(),
            P(),
            P(None, "tensor"),
            P(None, "tensor"),
            P("tensor", None),
            P(),
        ),
        out_specs=(
            rows,
            rows,
            P(),
            P(None, "tensor"),
            P(),
            P(),
            P(),
            P(),
            P("tensor", None),
            P(),
            P(),
            P(None, "tensor"),
            P(None, "tensor"),
            P("tensor", None),
            P(),
        ),
        check_vma=False,
    )
```

```python
import functools

import jax
import jax.numpy as jnp
import numpy as np
from jax import lax
from jax.experimental import pallas as pl
from jax.experimental.pallas import tpu as pltpu
from jax.sharding import PartitionSpec as P

WINDOW = 512
SOME = 24 * 1024 * 1024
MOST = 60 * 1024 * 1024

eps = 1e-06
rope_base = 10000.0
f32 = jnp.float32
bf16 = jnp.bfloat16
BOTH = ("seq", "tensor")


def places():
    return [(z, y, c, x) for z in range(4) for y in range(4) for c in range(2) for x in range(4)]


def number(z, y, c, x):
    return ((z * 4 + y) * 2 + c) * 4 + x


def route(move):
    return [(number(*p), number(*move(*p))) for p in places()]


def round_x(by):
    return route(lambda z, y, c, x: (z, y, c, (x + by) % 4))


def swap_cores():
    return route(lambda z, y, c, x: (z, y, 1 - c, x))


def along_first(flip):
    return route(lambda z, y, c, x: (z, y ^ flip, c, x) if c == 0 else (z ^ flip, y, c, x))


def round_first(by):
    return route(
        lambda z, y, c, x: (z, (y + by) % 4, c, x) if c == 0 else ((z + by) % 4, y, c, x)
    )


def round_second(by):
    return route(
        lambda z, y, c, x: ((z + by) % 4, y, c, x) if c == 0 else (z, (y + by) % 4, c, x)
    )


def send(value, pairs):
    return lax.ppermute(value, BOTH, pairs)


def shifted(value, by):
    pairs = [
        (i * 4 + x, (i + by) * 4 + x) for i in range(32) if 0 <= i + by < 32 for x in range(4)
    ]
    return send(value, pairs)


def pick(parts, index):
    return lax.dynamic_index_in_dim(parts, index, 0, keepdims=False)


def dot(first, second, over):
    return lax.dot_general(
        first, second, (((over[0],), (over[1],)), ((), ())), preferred_element_type=f32
    )


def scatter_sum(parts, index, turn):
    total = pick(parts, index).astype(f32)
    for by in (1, 2, 3):
        total = total + send(pick(parts, (index + by) % 4), turn(by)).astype(f32)
    return total


def gather(part, index, turn):
    whole = jnp.zeros((4, *part.shape), part.dtype)
    whole = lax.dynamic_update_index_in_dim(whole, part, index, 0)
    for by in (1, 2, 3):
        whole = lax.dynamic_update_index_in_dim(
            whole, send(part, turn(by)), (index + 4 - by) % 4, 0
        )
    return whole


def inv_scale(values):
    return lax.rsqrt(jnp.mean(values * values, axis=-1, keepdims=True) + eps)


def norm_back(values, scale, gain, grad):
    unit = values * scale
    weighted = grad * gain
    d_values = scale * (weighted - unit * jnp.mean(weighted * unit, axis=-1, keepdims=True))
    return (d_values, jnp.sum(grad * unit, axis=0))


def rotate(values, cosine, sine):
    half = values.shape[-1] // 2
    first = values[..., :half]
    second = values[..., half:]
    return jnp.concatenate(
        [first * cosine - second * sine, second * cosine + first * sine], axis=-1
    )


def padded(values, rows):
    return jnp.pad(values, ((0, rows - values.shape[0]), (0, 0)))


def added(first, second):
    return (first.astype(f32) + second.astype(f32)).astype(bf16)


def tied(*values):
    return lax.optimization_barrier(values)


def call(kernel, outs, *arrays, scalars=0, flops=0, room=SOME):
    vmem = pl.BlockSpec(memory_space=pltpu.VMEM)
    outs = [jax.ShapeDtypeStruct(*o) for o in outs]
    moved = sum(v.size * v.dtype.itemsize for v in (*arrays, *outs))
    return pl.pallas_call(
        kernel,
        out_shape=outs,
        in_specs=[pl.BlockSpec(memory_space=pltpu.SMEM)] * scalars
        + [vmem] * (len(arrays) - scalars),
        out_specs=[vmem] * len(outs),
        compiler_params=pltpu.CompilerParams(vmem_limit_bytes=room),
        cost_estimate=pl.CostEstimate(flops=flops, bytes_accessed=moved, transcendentals=0),
    )(*arrays)


def own_rows(ref, lane, rows):
    return ref[pl.ds(pl.multiple_of(lane * rows, rows), rows)].astype(f32)


def project_kernel(
    place, x, post_gain, ffw_gain, ctx0, ctx1, ctx2, ctx3, weight, own1, own2, own3, other1, other2, other3,
    branch, middle, normed
):
    even = place[1] == 0
    half = own1.shape[0]
    total = dot(ctx0[...], weight[...], (1, 0))
    for ctx, mine, theirs in ((ctx1, own1, other1), (ctx2, own2, other2), (ctx3, own3, other3)):
        low = jnp.where(even, mine[...], theirs[...])
        high = jnp.where(even, theirs[...], mine[...])
        total += dot(ctx[:, :half], low, (1, 0)) + dot(ctx[:, half:], high, (1, 0))
    branch[...] = total
    after = x[...].astype(f32) + total * inv_scale(total) * post_gain[...]
    middle[...] = after
    normed[...] = (after * inv_scale(after) * ffw_gain[...]).astype(bf16)


def final_kernel(place, p0, p1, p2, p3, middle, cotangent, gain, out, d_branch, part):
    lane = place[0]
    branch = p0[...].astype(f32) + p1[...].astype(f32) + p2[...].astype(f32) + p3[...].astype(f32)
    rows = branch.shape[0]
    scale = inv_scale(branch)
    cot = own_rows(cotangent, lane, rows)
    out[...] = (own_rows(middle, lane, rows) + branch * scale * gain[...]).astype(bf16)
    d_values, d_gain = norm_back(branch, scale, gain[...], cot)
    d_branch[...] = d_values.astype(bf16)
    part[...] = d_gain[None]


def between_kernel(
    place, p0, p1, p2, p3, middle, branch, cotangent, ffw_gain, post_gain,
    d_middle, d_branch, ffw_part, post_part
):
    lane = place[0]
    grad = p0[...].astype(f32) + p1[...].astype(f32) + p2[...].astype(f32) + p3[...].astype(f32)
    rows = grad.shape[0]
    after = own_rows(middle, lane, rows)
    before = own_rows(branch, lane, rows)
    d_values, d_gain = norm_back(after, inv_scale(after), ffw_gain[...], grad)
    ffw_part[...] = d_gain[None]
    d_values = own_rows(cotangent, lane, rows) + d_values
    d_middle[...] = d_values
    d_values, d_gain = norm_back(before, inv_scale(before), post_gain[...], d_values)
    d_branch[...] = d_values.astype(bf16)
    post_part[...] = d_gain[None]


def key_kernel(
    q_raw, k_raw, d_queries, d_own, d_near, d_far, cosine, sine, query_gain, key_gain, query_weight, key_weight,
    value_weight, d_query, payload, query_part, key_part
):
    tok, head_dim = q_raw.shape
    width = query_weight.shape[0]
    cos, sin = cosine[...], -sine[...]
    raw = q_raw[...]
    d_raw, d_gain = norm_back(
        raw, inv_scale(raw), query_gain[...], rotate(d_queries[...] * head_dim**-0.5, cos, sin)
    )
    query_part[...] = d_gain[None]
    d_low = d_raw.astype(bf16)
    d_query[...] = d_low
    total = dot(d_low, query_weight[...], (1, 1))
    summed = d_own[...] + d_near[...].astype(f32) + d_far[...].astype(f32)
    raw = k_raw[...]
    d_raw, d_gain = norm_back(raw, inv_scale(raw), key_gain[...], rotate(summed[:tok], cos, sin))
    key_part[...] = d_gain[None]
    total += dot(d_raw.astype(bf16), key_weight[...], (1, 1))
    total += dot(summed[tok:].astype(bf16), value_weight[...], (1, 1))
    payload[:, :width] = total.astype(bf16)
    payload[:, width : width + tok] = d_raw.T.astype(bf16)
    payload[:, width + tok :] = summed[tok:].T.astype(bf16)


def products_kernel(context, d_branch, d_query, normed, out):
    half = context.shape[1]
    out[:half] = dot(context[...], d_branch[...], (0, 0))
    out[half:] = dot(d_query[...], normed[...], (0, 0))


def entry_kernel(
    place, p0, p1, p2, p3, x, d_middle, gain, normed, post_part, ffw_part, final_part, query_part, key_part,
    products, input_grad, keep, give, rest
):
    lane, core = place[0], place[1]
    both = p0[...].astype(f32) + p1[...].astype(f32) + p2[...].astype(f32) + p3[...].astype(f32)
    rows = both.shape[0]
    width = normed.shape[1]
    tok = normed.shape[0]
    full = own_rows(x, lane, rows)
    d_values, d_gain = norm_back(full, inv_scale(full), gain[...], both[:, :width])
    input_grad[...] = (d_middle[...] + d_values).astype(bf16)
    d_keys = both[:, width : width + tok].astype(bf16)
    d_values = both[:, width + tok :].astype(bf16)
    rest[:rows] = dot(d_keys, normed[...], (1, 0))
    rest[rows : 2 * rows] = dot(d_values, normed[...], (1, 0))
    heads = jnp.concatenate(
        [query_part[...], key_part[...], jnp.zeros((1, width - 2 * query_part.shape[1]), f32)], axis=1
    )
    index = lax.broadcasted_iota(jnp.int32, (8, width), 0)
    gains = jnp.zeros((8, width), f32)
    for at, part in enumerate((d_gain[None], post_part[...], ffw_part[...], final_part[...], heads)):
        gains = jnp.where(index == at, part, gains)
    rest[2 * rows : 2 * rows + 8] = gains
    rest[2 * rows + 8 :] = jnp.zeros((rest.shape[0] - 2 * rows - 8, width), f32)
    for kind in range(3):
        source = rest if kind == 2 else products
        base = 256 if kind == 1 else 0
        for chip in range(16):
            at = base + 16 * chip
            keep[kind, chip] = source[pl.ds(pl.multiple_of(at + 8 * core, 8), 8)]
            give[kind, chip] = source[pl.ds(pl.multiple_of(at + 8 - 8 * core, 8), 8)].astype(bf16)


def merge_kernel(where, keep, got, *outs):
    core, first = where[0], where[1]
    for by, out in enumerate(outs):
        along = lax.rem(first + by, 4)
        for across in range(4):
            chip = jnp.where(core == 0, 4 * across + along, 4 * along + across)
            for kind in range(3):
                total = keep[kind, chip] + got[kind, chip].astype(f32)
                out[kind, across] = total.astype(out.dtype)


def weight_kernel(
    hid_own, hid_got, gate_own, gate_got, up_own, up_got, dy_own, dy_got, xn_own, xn_got, *outs
):
    mats = (
        (hid_own, hid_got, dy_own, dy_got),
        (gate_own, gate_got, xn_own, xn_got),
        (up_own, up_got, xn_own, xn_got),
    )
    for group, out in enumerate(outs):
        for index, (left_own, left_got, right_own, right_got) in enumerate(mats):
            total = jnp.dot(left_own[group], right_own[...], preferred_element_type=f32)
            total += jnp.dot(left_got[group], right_got[...], preferred_element_type=f32)
            total = total.astype(bf16)
            out[112 * index : 112 * index + 112] = total[:112]
            out[336 + 112 * index : 448 + 112 * index] = total[112:]


def weight_parts(*arrays):
    width = arrays[-1].shape[1]
    return pl.pallas_call(
        weight_kernel,
        out_shape=[jax.ShapeDtypeStruct((672, width), bf16)] * 4,
        in_specs=[pl.BlockSpec(memory_space=pltpu.VMEM)] * len(arrays),
        out_specs=[pl.BlockSpec(memory_space=pltpu.VMEM)] * 4,
        compiler_params=pltpu.CompilerParams(vmem_limit_bytes=SOME),
        cost_estimate=pl.CostEstimate(
            flops=2 * 2688 * 512 * width, bytes_accessed=12_000_000, transcendentals=0
        ),
    )(*arrays)


def masks(block, segment, pairs):
    tok = segment.shape[0]
    query = lax.broadcasted_iota(jnp.int32, (tok, tok), 0)
    key = lax.broadcasted_iota(jnp.int32, (tok, tok), 1)
    same = [segment == pair[2 * tok : 2 * tok + 16].astype(f32)[:1] for pair in pairs]
    return (
        same[0] & (key > query) & (block >= 2),
        same[1] & (block >= 1),
        same[2] & (key <= query),
    )


def prepare_kernel(
    place, x, gain, key_weight, value_weight, query_weight, key_gain, query_gain, start_cos, start_sin, inner_cos,
    inner_sin, marks, xn, pair, k_raw, q_raw, queries, cosine, sine
):
    tok, head_dim = k_raw.shape
    full = x[...].astype(f32)
    low = (full * inv_scale(full) * gain[...]).astype(bf16)
    xn[...] = low
    at = pl.ds(place[2], 1)
    cos = start_cos[at] * inner_cos[...] - start_sin[at] * inner_sin[...]
    sin = start_sin[at] * inner_cos[...] + start_cos[at] * inner_sin[...]
    cosine[...] = cos
    sine[...] = sin
    raw = dot(low, key_weight[...], (1, 0))
    k_raw[...] = raw
    pair[:tok] = rotate(raw * inv_scale(raw) * key_gain[...], cos, sin).astype(bf16)
    pair[tok : 2 * tok] = dot(low, value_weight[...], (1, 0)).astype(bf16)
    pair[2 * tok :] = jnp.broadcast_to(marks[...].astype(f32)[None], (16, tok)).astype(bf16)
    raw = dot(low, query_weight[...], (1, 0))
    q_raw[...] = raw
    turned = rotate(raw * inv_scale(raw) * query_gain[...], cos, sin)
    queries[...] = (turned * head_dim**-0.5).astype(bf16)


def attend_kernel(block, segment, queries, far, near, own, context, log_total):
    pairs = (far, near, own)
    tok = queries.shape[0]
    allowed = masks(block[0], segment[...], pairs)
    scores = [
        jnp.where(ok, dot(queries[...], pair[:tok], (1, 1)), -1e30)
        for ok, pair in zip(allowed, pairs, strict=True)
    ]
    top = functools.reduce(jnp.maximum, [jnp.max(s, axis=1, keepdims=True) for s in scores])
    weights = [jnp.exp(s - top) for s in scores]
    total = sum(jnp.sum(w, axis=1, keepdims=True) for w in weights)
    context[...] = sum(
        dot((w / total).astype(bf16), pair[tok : 2 * tok], (1, 0))
        for w, pair in zip(weights, pairs, strict=True)
    ).astype(bf16)
    log_total[...] = jnp.broadcast_to(top + jnp.log(total), log_total.shape)


def attend(block, segment, queries, pairs):
    tok, head_dim = queries.shape
    vmem = pl.BlockSpec(memory_space=pltpu.VMEM)
    return pl.pallas_call(
        attend_kernel,
        out_shape=[
            jax.ShapeDtypeStruct((tok, head_dim), bf16),
            jax.ShapeDtypeStruct((tok, 128), f32),
        ],
        in_specs=[pl.BlockSpec(memory_space=pltpu.SMEM)] + [vmem] * 5,
        out_specs=[vmem] * 2,
        compiler_params=pltpu.CompilerParams(vmem_limit_bytes=SOME),
        cost_estimate=pl.CostEstimate(
            flops=12 * tok * tok * head_dim, bytes_accessed=1_500_000, transcendentals=3 * tok * tok
        ),
    )(block, segment, queries, *pairs)


def attend_back_kernel(
    block, segment, log_total, d_branch, weight, queries, far, near, own, d_queries, d_far, d_near, d_own
):
    pairs = (far, near, own)
    tok = queries.shape[0]
    d_context = dot(d_branch[...], weight[...], (1, 1)).astype(bf16)
    allowed = masks(block[0], segment[...], pairs)
    lse = log_total[:, :1]
    probs, d_probs = [], []
    for ok, pair in zip(allowed, pairs, strict=True):
        scores = jnp.where(ok, dot(queries[...], pair[:tok], (1, 1)), -1e30)
        probs.append(jnp.exp(scores - lse))
        d_probs.append(dot(d_context, pair[tok : 2 * tok], (1, 1)))
    mean = sum(
        jnp.sum(p * d, axis=1, keepdims=True) for p, d in zip(probs, d_probs, strict=True)
    )
    total = None
    for p, d, pair, out in zip(probs, d_probs, pairs, (d_far, d_near, d_own), strict=True):
        d_scores = (p * (d - mean)).astype(bf16)
        part = dot(d_scores, pair[:tok], (1, 0))
        total = part if total is None else total + part
        out[:tok] = dot(d_scores, queries[...], (0, 0)).astype(out.dtype)
        out[tok:] = dot(p.astype(bf16), d_context, (0, 0)).astype(out.dtype)
    d_queries[...] = total


def attend_back(block, segment, log_total, d_branch, weight, queries, pairs):
    tok, head_dim = queries.shape
    vmem = pl.BlockSpec(memory_space=pltpu.VMEM)
    return pl.pallas_call(
        attend_back_kernel,
        out_shape=[
            jax.ShapeDtypeStruct((tok, head_dim), f32),
            jax.ShapeDtypeStruct((2 * tok, head_dim), bf16),
            jax.ShapeDtypeStruct((2 * tok, head_dim), bf16),
            jax.ShapeDtypeStruct((2 * tok, head_dim), f32),
        ],
        in_specs=[pl.BlockSpec(memory_space=pltpu.SMEM)] + [vmem] * 8,
        out_specs=[vmem] * 4,
        compiler_params=pltpu.CompilerParams(vmem_limit_bytes=SOME),
        cost_estimate=pl.CostEstimate(
            flops=30 * tok * tok * head_dim, bytes_accessed=3_500_000, transcendentals=3 * tok * tok
        ),
    )(block, segment, log_total, d_branch, weight, queries, *pairs)


def place_kernel(where_ref, *refs, turns, held):
    n = len(turns)
    parts, outs = refs[:n], refs[n + held : n + held + 3]
    stage, sems, tail_sems = refs[-3:]
    slots = stage.shape[0]
    core, first, second = where_ref[0], where_ref[1], where_ref[2]
    chunks = [
        (ref, i, base + i, other, flip)
        for ref, (other, flip, base) in zip(parts, turns, strict=True)
        for i in range(ref.shape[0])
    ]

    def place(index):
        _, _, across, other, flip = chunks[index]
        which = 1 - core if other else core
        along = (second if other else first) ^ flip
        y = jnp.where(which == 0, along, across)
        z = jnp.where(which == 0, across, along)
        odd = lax.rem(y, 2)
        row = 216 * (2 * z + y // 2) + 104 * odd + 48 * which + 8 * which * odd
        return pl.multiple_of(row, 8), (which == 1) | (odd == 1)

    def copies(index):
        slot = index % slots
        row, whole = place(index)
        for mat, out in enumerate(outs):
            yield (
                pltpu.make_async_copy(
                    stage.at[slot, mat, pl.ds(0, 48)],
                    out.at[pl.ds(row, 48)],
                    sems.at[slot, mat],
                ),
                pltpu.make_async_copy(
                    stage.at[slot, mat, pl.ds(48, 8)],
                    out.at[pl.ds(pl.multiple_of(row + 48, 8), 8)],
                    tail_sems.at[slot, mat],
                ),
                whole,
            )

    def finish(index):
        for most, tail, whole in copies(index):
            most.wait()
            pl.when(whole)(tail.wait)

    for index, (ref, i, *_) in enumerate(chunks):
        if index >= slots:
            finish(index - slots)
        stage[index % slots] = ref[i].astype(f32)
        for most, tail, whole in copies(index):
            most.start()
            pl.when(whole)(tail.start)
    for index in range(max(0, len(chunks) - slots), len(chunks)):
        finish(index)


def placed(where, parts, outs, units):
    arrays = [p[0].reshape(-1, 3, 56, p[0].shape[-1]) for p in parts]
    width = arrays[0].shape[-1]
    slots = 4
    return pl.pallas_call(
        functools.partial(
            place_kernel, turns=tuple(p[1:] for p in parts), held=len(outs)
        ),
        out_shape=[jax.ShapeDtypeStruct((units, width), f32)] * 3,
        in_specs=[pl.BlockSpec(memory_space=pltpu.SMEM)]
        + [pl.BlockSpec(memory_space=pltpu.VMEM)] * len(arrays)
        + [pl.BlockSpec(memory_space=pl.ANY)] * len(outs),
        out_specs=[pl.BlockSpec(memory_space=pl.ANY)] * 3,
        scratch_shapes=[
            pltpu.VMEM((slots, 3, 56, width), f32),
            pltpu.SemaphoreType.DMA((slots, 3)),
            pltpu.SemaphoreType.DMA((slots, 3)),
        ],
        input_output_aliases={1 + len(arrays) + i: i for i in range(len(outs))},
        compiler_params=pltpu.CompilerParams(vmem_limit_bytes=SOME),
        cost_estimate=pl.CostEstimate(
            flops=0, bytes_accessed=sum(p.size for p in arrays) * 6, transcendentals=0
        ),
    )(where, *arrays, *outs)


def finish_kernel(
    core_ref, own, got, out_grad, query_grad, key_grad, value_grad, attn, post, ffw, final, query, key, rows
):
    core = core_ref[0]
    for pieces, other in ((own, 0), (got, 1)):
        even = core == other
        for along in range(4):
            for across in range(4):
                row = jnp.where(even, 8 * across + 2 * along, 8 * along + 2 * across + 1) * 8
                row = pl.ds(pl.multiple_of(row, 8), 8)
                for kind in range(6):
                    rows[kind, row] = pieces[along, kind, across].astype(f32)
    out_grad[...] = rows[0]
    query_grad[...] = rows[1].T
    for lane in range(4):
        key_grad[:, 64 * lane : 64 * lane + 64] = rows[2 + lane, :64].T
        value_grad[:, 64 * lane : 64 * lane + 64] = rows[2 + lane, 64:128].T
    gains = sum(rows[2 + lane, 128:136] for lane in range(4))
    for at, out in enumerate((attn, post, ffw, final)):
        out[...] = gains[at]
    size = query.shape[0]
    query[...] = gains[4, :size]
    key[...] = gains[4, size : 2 * size]


def finished(core, own, got):
    width = own.shape[-1]
    vmem = pl.BlockSpec(memory_space=pltpu.VMEM)
    return pl.pallas_call(
        finish_kernel,
        out_shape=[
            jax.ShapeDtypeStruct((256, width), f32),
            jax.ShapeDtypeStruct((width, 256), f32),
            jax.ShapeDtypeStruct((width, 256), f32),
            jax.ShapeDtypeStruct((width, 256), f32),
            *[jax.ShapeDtypeStruct((width,), f32)] * 4,
            *[jax.ShapeDtypeStruct((256,), f32)] * 2,
        ],
        in_specs=[pl.BlockSpec(memory_space=pltpu.SMEM), vmem, vmem],
        out_specs=[vmem] * 10,
        scratch_shapes=[pltpu.VMEM((6, 256, width), f32)],
        compiler_params=pltpu.CompilerParams(vmem_limit_bytes=SOME),
        cost_estimate=pl.CostEstimate(flops=0, bytes_accessed=10_000_000, transcendentals=0),
    )(core, own, got)


def local(
    layer_input,
    segment_ids,
    out_cotangent,
    attn_norm_gain,
    query_weight,
    key_weight,
    value_weight,
    query_gain,
    key_gain,
    output_weight,
    attn_post_gain,
    ffw_norm_gain,
    gate_weight,
    up_weight,
    down_weight,
    ffw_post_gain,
):
    tok, width = layer_input.shape
    head_dim = key_weight.shape[1]
    units = down_weight.shape[0]
    block = lax.axis_index("seq")
    lane = lax.axis_index("tensor")
    core = block % 2
    row = (block // 2) % 4
    plane = block // 8
    first = jnp.where(core == 0, row, plane)
    second = jnp.where(core == 0, plane, row)
    quarter_tok = tok // 4

    place = jnp.stack([lane, core, block]).astype(jnp.int32)
    where = jnp.stack([core, first, second]).astype(jnp.int32)
    freq = rope_base ** (-2.0 * np.arange(head_dim // 2) / head_dim)
    start = (np.arange(lax.axis_size("seq")) * tok)[:, None] * freq[None, :]
    inner = np.arange(tok)[:, None] * freq[None, :]
    tables = [jnp.asarray(f(angle), f32) for angle in (start, inner) for f in (np.cos, np.sin)]

    square = (tok, head_dim)
    normed, own_pair, k_raw, q_raw, queries, cosine, sine = call(
        prepare_kernel,
        [
            ((tok, width), bf16),
            ((2 * tok + 16, head_dim), bf16),
            (square, f32),
            (square, f32),
            (square, bf16),
            ((tok, head_dim // 2), f32),
            ((tok, head_dim // 2), f32),
        ],
        place,
        layer_input,
        attn_norm_gain,
        key_weight,
        value_weight,
        query_weight,
        key_gain,
        query_gain,
        *tables,
        segment_ids,
        scalars=1,
        flops=6 * tok * width * head_dim,
        room=MOST,
    )
    left_one = shifted(own_pair, 1)
    left_two = shifted(own_pair, 2)

    weight_half = tok // 2
    halved, _ = tied(output_weight, own_pair)
    own_weight = pick(halved.reshape(2, weight_half, width), core)
    got_weight = [send(own_weight, round_x(by)) for by in (1, 2, 3)]

    pairs = (left_two, left_one, own_pair)
    block_ref = block.astype(jnp.int32).reshape(1)
    segment = segment_ids.astype(f32)[:, None]
    context, log_total = attend(block_ref, segment, queries, pairs)

    got_context = [send(context, round_x(by)) for by in (1, 2, 3)]
    *got_context, got_weight[0], got_weight[1], got_weight[2] = tied(*got_context, *got_weight)
    other_weight = [send(part, swap_cores()) for part in got_weight]
    branch, middle, normed_two = call(
        project_kernel,
        [((tok, width), f32), ((tok, width), f32), ((tok, width), bf16)],
        place,
        layer_input,
        attn_post_gain,
        ffw_norm_gain,
        context,
        *got_context,
        output_weight,
        *got_weight,
        *other_weight,
        scalars=1,
        flops=8 * tok * tok * width,
    )
    gate = dot(gate_weight, normed_two, (0, 1))
    up_val = dot(up_weight, normed_two, (0, 1))
    active, gelu_back = jax.vjp(lambda val: jax.nn.gelu(val, approximate=True), gate)
    hidden = (active * up_val).astype(bf16)
    down_part = dot(hidden, down_weight, (0, 0)).astype(bf16)

    def halves(values):
        groups = values.reshape(8, units // 8, tok)
        groups = jnp.concatenate([groups[:, :56], groups[:, 48:]], axis=1)
        pieces = groups.reshape(4, 4, 2, 56, tok)
        return (
            lax.dynamic_index_in_dim(pieces, core, 2, keepdims=False),
            lax.dynamic_index_in_dim(pieces, 1 - core, 2, keepdims=False),
        )

    def arranged(values):
        values = jnp.where(core == 0, values.swapaxes(0, 1), values)
        by_first = [pick(values, first ^ flip) for flip in range(4)]
        groups = [
            jnp.stack([by_first[i][2 * stream : 2 * stream + 2] for i in order])
            for stream, order in ((0, (0, 3)), (0, (1, 2)), (1, (0, 1)), (1, (3, 2)))
        ]
        return jnp.stack(groups).reshape(4, 224, tok)

    hidden_own, hidden_give = halves(hidden)
    hidden_got = send(hidden_give, swap_cores())
    normed_two_got = send(normed_two, swap_cores())

    def quarters(parts):
        parts = parts.reshape(4, quarter_tok, parts.shape[-1])
        given = [pick(parts, (lane + by) % 4) for by in (1, 2, 3)]
        return [pick(parts, lane)] + [
            send(part, round_x(by)) for by, part in zip((1, 2, 3), given, strict=True)
        ]

    piece = (quarter_tok, width)
    out_own, d_branch_two, final_part = call(
        final_kernel,
        [(piece, bf16), (piece, bf16), ((1, width), f32)],
        place,
        *quarters(down_part),
        middle,
        out_cotangent,
        ffw_post_gain,
        scalars=1,
    )
    d_branch_two = gather(d_branch_two, lane, round_x).reshape(tok, width)
    d_branch_two_got = send(d_branch_two, swap_cores())

    d_hidden = dot(down_weight, d_branch_two, (1, 1))
    d_gate = gelu_back(d_hidden * up_val)[0].astype(bf16)
    d_up = (d_hidden * active).astype(bf16)
    d_normed_two = (dot(d_gate, gate_weight, (0, 1)) + dot(d_up, up_weight, (0, 1))).astype(bf16)
    d_gate_own, d_gate_give = halves(d_gate)
    d_up_own, d_up_give = halves(d_up)
    d_pair_got = send(jnp.stack([d_gate_give, d_up_give]), swap_cores())

    keep_a, give_a, keep_b, give_b = weight_parts(
        *(
            arranged(v)
            for v in (hidden_own, hidden_got, d_gate_own, d_pair_got[0], d_up_own, d_pair_got[1])
        ),
        d_branch_two,
        d_branch_two_got,
        normed_two,
        normed_two_got,
    )
    got_a = send(give_a, along_first(1))
    got_b = send(give_b, along_first(3))

    *got_normed, keep_a, keep_b = tied(*quarters(d_normed_two), keep_a, keep_b)
    d_middle, d_branch, ffw_part, post_part = call(
        between_kernel,
        [(piece, f32), (piece, bf16), ((1, width), f32), ((1, width), f32)],
        place,
        *got_normed,
        middle,
        branch,
        out_cotangent,
        ffw_norm_gain,
        attn_post_gain,
        scalars=1,
    )
    d_branch = gather(d_branch, lane, round_x).reshape(tok, width)
    d_queries, left_far, left_near, summed = attend_back(
        block_ref, segment, log_total, d_branch, output_weight, queries, pairs
    )
    got_near = shifted(left_near, -1)
    got_far = shifted(left_far, -2)
    got_near, got_far, got_a, got_b = tied(got_near, got_far, got_a, got_b)
    keep_a, give_a = added(keep_a[:336], got_a[:336]), added(keep_a[336:], got_a[336:])
    keep_b, give_b = added(keep_b[:336], got_b[:336]), added(keep_b[336:], got_b[336:])
    got_a = send(give_a, along_first(3))
    got_b = send(give_b, along_first(1))
    d_query, payload, query_part, key_part = call(
        key_kernel,
        [
            (square, bf16),
            ((tok, width + 2 * tok), bf16),
            ((1, head_dim), f32),
            ((1, head_dim), f32),
        ],
        q_raw,
        k_raw,
        d_queries,
        summed,
        got_near,
        got_far,
        cosine,
        sine,
        query_gain,
        key_gain,
        query_weight,
        key_weight,
        value_weight,
        flops=6 * tok * width * head_dim,
    )
    got_both = quarters(payload)
    (products,) = call(
        products_kernel,
        [((2 * head_dim, width), f32)],
        context,
        d_branch,
        d_query,
        normed,
        flops=4 * tok * width * head_dim,
    )
    *got_both, got_a, got_b = tied(*got_both, got_a, got_b)
    fours = jnp.stack([added(keep_a, got_a), added(keep_b, got_b)])
    fours = fours.reshape(2, 3, 2, 56, width).swapaxes(1, 2).reshape(4, 168, width)
    mine = pick(fours, second).astype(f32)
    got = [send(pick(fours, (second + by) % 4), round_second(by)) for by in (1, 2, 3)]
    input_own, keep, give = pl.pallas_call(
        entry_kernel,
        out_shape=[
            jax.ShapeDtypeStruct(piece, bf16),
            jax.ShapeDtypeStruct((3, 16, 8, width), f32),
            jax.ShapeDtypeStruct((3, 16, 8, width), bf16),
        ],
        in_specs=[pl.BlockSpec(memory_space=pltpu.SMEM)]
        + [pl.BlockSpec(memory_space=pltpu.VMEM)] * 14,
        out_specs=[pl.BlockSpec(memory_space=pltpu.VMEM)] * 3,
        scratch_shapes=[pltpu.VMEM((tok, width), f32)],
        compiler_params=pltpu.CompilerParams(vmem_limit_bytes=SOME),
        cost_estimate=pl.CostEstimate(
            flops=256 * tok * width, bytes_accessed=12_000_000, transcendentals=0
        ),
    )(
        place,
        *got_both,
        layer_input,
        d_middle,
        attn_norm_gain,
        normed,
        post_part,
        ffw_part,
        final_part,
        query_part,
        key_part,
        products,
    )
    pack_got = send(give, swap_cores())
    pack_got, *got = tied(pack_got, *got)
    mine = (mine + got[0].astype(f32) + (got[1].astype(f32) + got[2].astype(f32))).astype(bf16)
    part = (3, 4, 8, width)
    pack, *given = call(
        merge_kernel, [(part, f32)] + [(part, bf16)] * 3, where, keep, pack_got, scalars=1
    )
    given = [send(part, round_first(by)) for by, part in zip((1, 2, 3), given, strict=True)]
    for part in given:
        pack = pack + part.astype(f32)
    pack = pack.astype(bf16).reshape(96, width)
    both = lax.optimization_barrier(jnp.concatenate([mine, pack]))
    given = [send(both, round_second(by)) for by in (1, 2, 3)]
    quarter = jnp.zeros((4, *mine.shape), bf16)
    quarter = lax.dynamic_update_index_in_dim(quarter, both[:168], second, 0)
    for by, part in zip((1, 2, 3), given, strict=True):
        quarter = lax.dynamic_update_index_in_dim(quarter, part[:168], (second + 4 - by) % 4, 0)
    pack, *given = (part[168:].astype(f32) for part in (both, *given))
    pack = (pack + given[1] + (given[0] + given[2])).astype(bf16).reshape(3, 4, 8, width)
    near_a = send(quarter, along_first(1))
    near_b = send(quarter, along_first(3))
    other_own = send(quarter, swap_cores())
    given = [send(pack[2], round_x(by)) for by in (1, 2, 3)]
    *given, near_a, near_b = tied(*given, near_a, near_b)
    far_a = send(near_b[:2], along_first(1))
    far_b = send(near_a[2:], along_first(3))
    other_a = send(near_a, swap_cores())
    other_b = send(near_b, swap_cores())
    grads = placed(
        where,
        [
            (quarter, False, 0, 0),
            (near_a, False, 1, 0),
            (near_b, False, 3, 0),
            (other_own, True, 0, 0),
            (other_a, True, 1, 0),
            (other_b, True, 3, 0),
        ],
        [],
        units,
    )
    rest = jnp.zeros((4, *pack.shape[1:]), bf16)
    rest = lax.dynamic_update_index_in_dim(rest, pack[2], lane, 0)
    for by, part in zip((1, 2, 3), given, strict=True):
        rest = lax.dynamic_update_index_in_dim(rest, part, (lane + 4 - by) % 4, 0)
    pack = jnp.concatenate([pack[:2], rest])
    pack, out_own, input_own = tied(pack, out_own, input_own)
    ends = gather(jnp.stack([out_own, input_own]), lane, round_x)
    given = [send(pack, round_first(by)) for by in (1, 2, 3)]
    grads = list(grads)
    *given, grads[0] = tied(*given, grads[0])
    whole = jnp.zeros((4, *pack.shape), bf16)
    whole = lax.dynamic_update_index_in_dim(whole, pack, first, 0)
    for by, part in zip((1, 2, 3), given, strict=True):
        whole = lax.dynamic_update_index_in_dim(whole, part, (first + 4 - by) % 4, 0)
    pack_got = send(whole, swap_cores())
    out_grad, query_grad, key_grad, value_grad, *gains = finished(
        core.astype(jnp.int32).reshape(1), whole, pack_got
    )
    other_far_a = send(far_a, swap_cores())
    other_far_b = send(far_b, swap_cores())
    down_grad, gate_grad, up_grad = placed(
        where,
        [
            (far_a, False, 2, 0),
            (far_b, False, 2, 2),
            (other_far_a, True, 2, 0),
            (other_far_b, True, 2, 2),
        ],
        grads,
        units,
    )
    layer_output = ends[:, 0].reshape(tok, width)
    input_grad = ends[:, 1].reshape(tok, width)
    return (
        layer_output,
        input_grad,
        gains[0],
        query_grad,
        key_grad,
        value_grad,
        gains[4],
        gains[5],
        out_grad,
        gains[1],
        gains[2],
        gate_grad.T,
        up_grad.T,
        down_grad,
        gains[3],
    )


def solution(mesh):
    rows = P("seq", None)
    return jax.shard_map(
        local,
        mesh=mesh,
        in_specs=(
            rows,
            P("seq"),
            rows,
            P(),
            P(None, "tensor"),
            P(),
            P(),
            P(),
            P(),
            P("tensor", None),
            P(),
            P(),
            P(None, "tensor"),
            P(None, "tensor"),
            P("tensor", None),
            P(),
        ),
        out_specs=(
            rows,
            rows,
            P(),
            P(None, "tensor"),
            P(),
            P(),
            P(),
            P(),
            P("tensor", None),
            P(),
            P(),
            P(None, "tensor"),
            P(None, "tensor"),
            P("tensor", None),
            P(),
        ),
        check_vma=False,
    )
```

```python
import functools

import jax
import jax.numpy as jnp
import numpy as np
from jax import lax
from jax.experimental import pallas as pl
from jax.experimental.pallas import tpu as pltpu
from jax.sharding import PartitionSpec as P

WINDOW = 512
SOME = 24 * 1024 * 1024
MOST = 60 * 1024 * 1024

eps = 1e-06
rope_base = 10000.0
f32 = jnp.float32
bf16 = jnp.bfloat16
BOTH = ("seq", "tensor")


def places():
    return [(z, y, c, x) for z in range(4) for y in range(4) for c in range(2) for x in range(4)]


def number(z, y, c, x):
    return ((z * 4 + y) * 2 + c) * 4 + x


def route(move):
    return [(number(*p), number(*move(*p))) for p in places()]


def round_x(by):
    return route(lambda z, y, c, x: (z, y, c, (x + by) % 4))


def swap_cores():
    return route(lambda z, y, c, x: (z, y, 1 - c, x))


def along_first(flip):
    return route(lambda z, y, c, x: (z, y ^ flip, c, x) if c == 0 else (z ^ flip, y, c, x))


def round_first(by):
    return route(
        lambda z, y, c, x: (z, (y + by) % 4, c, x) if c == 0 else ((z + by) % 4, y, c, x)
    )


def round_second(by):
    return route(
        lambda z, y, c, x: ((z + by) % 4, y, c, x) if c == 0 else (z, (y + by) % 4, c, x)
    )


def send(value, pairs):
    return lax.ppermute(value, BOTH, pairs)


def shifted(value, by):
    pairs = [
        (i * 4 + x, (i + by) * 4 + x) for i in range(32) if 0 <= i + by < 32 for x in range(4)
    ]
    return send(value, pairs)


def pick(parts, index):
    return lax.dynamic_index_in_dim(parts, index, 0, keepdims=False)


def dot(first, second, over):
    return lax.dot_general(
        first, second, (((over[0],), (over[1],)), ((), ())), preferred_element_type=f32
    )


def scatter_sum(parts, index, turn):
    total = pick(parts, index).astype(f32)
    for by in (1, 2, 3):
        total = total + send(pick(parts, (index + by) % 4), turn(by)).astype(f32)
    return total


def gather(part, index, turn):
    whole = jnp.zeros((4, *part.shape), part.dtype)
    whole = lax.dynamic_update_index_in_dim(whole, part, index, 0)
    for by in (1, 2, 3):
        whole = lax.dynamic_update_index_in_dim(
            whole, send(part, turn(by)), (index + 4 - by) % 4, 0
        )
    return whole


def inv_scale(values):
    return lax.rsqrt(jnp.mean(values * values, axis=-1, keepdims=True) + eps)


def norm_back(values, scale, gain, grad):
    unit = values * scale
    weighted = grad * gain
    d_values = scale * (weighted - unit * jnp.mean(weighted * unit, axis=-1, keepdims=True))
    return (d_values, jnp.sum(grad * unit, axis=0))


def rotate(values, cosine, sine):
    half = values.shape[-1] // 2
    first = values[..., :half]
    second = values[..., half:]
    return jnp.concatenate(
        [first * cosine - second * sine, second * cosine + first * sine], axis=-1
    )


def padded(values, rows):
    return jnp.pad(values, ((0, rows - values.shape[0]), (0, 0)))


def added(first, second):
    return (first.astype(f32) + second.astype(f32)).astype(bf16)


def tied(*values):
    return lax.optimization_barrier(values)


def call(kernel, outs, *arrays, scalars=0, flops=0, room=SOME):
    vmem = pl.BlockSpec(memory_space=pltpu.VMEM)
    outs = [jax.ShapeDtypeStruct(*o) for o in outs]
    moved = sum(v.size * v.dtype.itemsize for v in (*arrays, *outs))
    return pl.pallas_call(
        kernel,
        out_shape=outs,
        in_specs=[pl.BlockSpec(memory_space=pltpu.SMEM)] * scalars
        + [vmem] * (len(arrays) - scalars),
        out_specs=[vmem] * len(outs),
        compiler_params=pltpu.CompilerParams(vmem_limit_bytes=room),
        cost_estimate=pl.CostEstimate(flops=flops, bytes_accessed=moved, transcendentals=0),
    )(*arrays)


def own_rows(ref, lane, rows):
    return ref[pl.ds(pl.multiple_of(lane * rows, rows), rows)].astype(f32)


def project_kernel(
    place, x, post_gain, ffw_gain, ctx0, ctx1, ctx2, ctx3, weight, own1, own2, own3, other1, other2, other3,
    branch, middle, normed
):
    even = place[1] == 0
    half = own1.shape[0]
    total = dot(ctx0[...], weight[...], (1, 0))
    for ctx, mine, theirs in ((ctx1, own1, other1), (ctx2, own2, other2), (ctx3, own3, other3)):
        low = jnp.where(even, mine[...], theirs[...])
        high = jnp.where(even, theirs[...], mine[...])
        total += dot(ctx[:, :half], low, (1, 0)) + dot(ctx[:, half:], high, (1, 0))
    branch[...] = total
    after = x[...].astype(f32) + total * inv_scale(total) * post_gain[...]
    middle[...] = after
    normed[...] = (after * inv_scale(after) * ffw_gain[...]).astype(bf16)


def final_kernel(place, p0, p1, p2, p3, middle, cotangent, gain, out, d_branch, part):
    lane = place[0]
    branch = p0[...].astype(f32) + p1[...].astype(f32) + p2[...].astype(f32) + p3[...].astype(f32)
    rows = branch.shape[0]
    scale = inv_scale(branch)
    cot = own_rows(cotangent, lane, rows)
    out[...] = (own_rows(middle, lane, rows) + branch * scale * gain[...]).astype(bf16)
    d_values, d_gain = norm_back(branch, scale, gain[...], cot)
    d_branch[...] = d_values.astype(bf16)
    part[...] = d_gain[None]


def between_kernel(
    place, p0, p1, p2, p3, middle, branch, cotangent, ffw_gain, post_gain,
    d_middle, d_branch, ffw_part, post_part
):
    lane = place[0]
    grad = p0[...].astype(f32) + p1[...].astype(f32) + p2[...].astype(f32) + p3[...].astype(f32)
    rows = grad.shape[0]
    after = own_rows(middle, lane, rows)
    before = own_rows(branch, lane, rows)
    d_values, d_gain = norm_back(after, inv_scale(after), ffw_gain[...], grad)
    ffw_part[...] = d_gain[None]
    d_values = own_rows(cotangent, lane, rows) + d_values
    d_middle[...] = d_values
    d_values, d_gain = norm_back(before, inv_scale(before), post_gain[...], d_values)
    d_branch[...] = d_values.astype(bf16)
    post_part[...] = d_gain[None]


def key_kernel(
    q_raw, k_raw, d_queries, d_own, d_near, d_far, cosine, sine, query_gain, key_gain, query_weight, key_weight,
    value_weight, d_query, payload, query_part, key_part
):
    tok, head_dim = q_raw.shape
    width = query_weight.shape[0]
    cos, sin = cosine[...], -sine[...]
    raw = q_raw[...]
    d_raw, d_gain = norm_back(
        raw, inv_scale(raw), query_gain[...], rotate(d_queries[...] * head_dim**-0.5, cos, sin)
    )
    query_part[...] = d_gain[None]
    d_low = d_raw.astype(bf16)
    d_query[...] = d_low
    total = dot(d_low, query_weight[...], (1, 1))
    summed = d_own[...] + d_near[...].astype(f32) + d_far[...].astype(f32)
    raw = k_raw[...]
    d_raw, d_gain = norm_back(raw, inv_scale(raw), key_gain[...], rotate(summed[:tok], cos, sin))
    key_part[...] = d_gain[None]
    total += dot(d_raw.astype(bf16), key_weight[...], (1, 1))
    total += dot(summed[tok:].astype(bf16), value_weight[...], (1, 1))
    payload[:, :width] = total.astype(bf16)
    payload[:, width : width + tok] = d_raw.T.astype(bf16)
    payload[:, width + tok :] = summed[tok:].T.astype(bf16)


def products_kernel(context, d_branch, d_query, normed, out):
    half = context.shape[1]
    out[:half] = dot(context[...], d_branch[...], (0, 0))
    out[half:] = dot(d_query[...], normed[...], (0, 0))


def entry_kernel(
    place, p0, p1, p2, p3, x, d_middle, gain, normed, post_part, ffw_part, final_part, query_part, key_part,
    products, input_grad, keep, give, rest
):
    lane, core = place[0], place[1]
    both = p0[...].astype(f32) + p1[...].astype(f32) + p2[...].astype(f32) + p3[...].astype(f32)
    rows = both.shape[0]
    width = normed.shape[1]
    tok = normed.shape[0]
    full = own_rows(x, lane, rows)
    d_values, d_gain = norm_back(full, inv_scale(full), gain[...], both[:, :width])
    input_grad[...] = (d_middle[...] + d_values).astype(bf16)
    d_keys = both[:, width : width + tok].astype(bf16)
    d_values = both[:, width + tok :].astype(bf16)
    rest[:rows] = dot(d_keys, normed[...], (1, 0))
    rest[rows : 2 * rows] = dot(d_values, normed[...], (1, 0))
    heads = jnp.concatenate(
        [query_part[...], key_part[...], jnp.zeros((1, width - 2 * query_part.shape[1]), f32)], axis=1
    )
    index = lax.broadcasted_iota(jnp.int32, (8, width), 0)
    gains = jnp.zeros((8, width), f32)
    for at, part in enumerate((d_gain[None], post_part[...], ffw_part[...], final_part[...], heads)):
        gains = jnp.where(index == at, part, gains)
    rest[2 * rows : 2 * rows + 8] = gains
    rest[2 * rows + 8 :] = jnp.zeros((rest.shape[0] - 2 * rows - 8, width), f32)
    for kind in range(3):
        source = rest if kind == 2 else products
        base = 256 if kind == 1 else 0
        for chip in range(16):
            at = base + 16 * chip
            keep[kind, chip] = source[pl.ds(pl.multiple_of(at + 8 * core, 8), 8)]
            give[kind, chip] = source[pl.ds(pl.multiple_of(at + 8 - 8 * core, 8), 8)].astype(bf16)


def merge_kernel(where, keep, got, *outs):
    core, first = where[0], where[1]
    for by, out in enumerate(outs):
        along = lax.rem(first + by, 4)
        for across in range(4):
            chip = jnp.where(core == 0, 4 * across + along, 4 * along + across)
            for kind in range(3):
                total = keep[kind, chip] + got[kind, chip].astype(f32)
                out[kind, across] = total.astype(out.dtype)


def weight_kernel(
    hid_own, hid_got, gate_own, gate_got, up_own, up_got, dy_own, dy_got, xn_own, xn_got, *outs
):
    mats = (
        (hid_own, hid_got, dy_own, dy_got),
        (gate_own, gate_got, xn_own, xn_got),
        (up_own, up_got, xn_own, xn_got),
    )
    for group, out in enumerate(outs):
        for index, (left_own, left_got, right_own, right_got) in enumerate(mats):
            total = jnp.dot(left_own[group], right_own[...], preferred_element_type=f32)
            total += jnp.dot(left_got[group], right_got[...], preferred_element_type=f32)
            total = total.astype(bf16)
            out[112 * index : 112 * index + 112] = total[:112]
            out[336 + 112 * index : 448 + 112 * index] = total[112:]


def weight_parts(*arrays):
    width = arrays[-1].shape[1]
    return pl.pallas_call(
        weight_kernel,
        out_shape=[jax.ShapeDtypeStruct((672, width), bf16)] * 4,
        in_specs=[pl.BlockSpec(memory_space=pltpu.VMEM)] * len(arrays),
        out_specs=[pl.BlockSpec(memory_space=pltpu.VMEM)] * 4,
        compiler_params=pltpu.CompilerParams(vmem_limit_bytes=SOME),
        cost_estimate=pl.CostEstimate(
            flops=2 * 2688 * 512 * width, bytes_accessed=12_000_000, transcendentals=0
        ),
    )(*arrays)


def masks(block, segment, pairs):
    tok = segment.shape[0]
    query = lax.broadcasted_iota(jnp.int32, (tok, tok), 0)
    key = lax.broadcasted_iota(jnp.int32, (tok, tok), 1)
    same = [segment == pair[2 * tok : 2 * tok + 16].astype(f32)[:1] for pair in pairs]
    return (
        same[0] & (key > query) & (block >= 2),
        same[1] & (block >= 1),
        same[2] & (key <= query),
    )


def prepare_kernel(
    place, x, gain, key_weight, value_weight, query_weight, key_gain, query_gain, start_cos, start_sin, inner_cos,
    inner_sin, marks, xn, pair, k_raw, q_raw, queries, cosine, sine
):
    tok, head_dim = k_raw.shape
    full = x[...].astype(f32)
    low = (full * inv_scale(full) * gain[...]).astype(bf16)
    xn[...] = low
    at = pl.ds(place[2], 1)
    cos = start_cos[at] * inner_cos[...] - start_sin[at] * inner_sin[...]
    sin = start_sin[at] * inner_cos[...] + start_cos[at] * inner_sin[...]
    cosine[...] = cos
    sine[...] = sin
    raw = dot(low, key_weight[...], (1, 0))
    k_raw[...] = raw
    pair[:tok] = rotate(raw * inv_scale(raw) * key_gain[...], cos, sin).astype(bf16)
    pair[tok : 2 * tok] = dot(low, value_weight[...], (1, 0)).astype(bf16)
    pair[2 * tok :] = jnp.broadcast_to(marks[...].astype(f32)[None], (16, tok)).astype(bf16)
    raw = dot(low, query_weight[...], (1, 0))
    q_raw[...] = raw
    turned = rotate(raw * inv_scale(raw) * query_gain[...], cos, sin)
    queries[...] = (turned * head_dim**-0.5).astype(bf16)


def attend_kernel(block, segment, queries, far, near, own, context, log_total):
    pairs = (far, near, own)
    tok = queries.shape[0]
    allowed = masks(block[0], segment[...], pairs)
    scores = [
        jnp.where(ok, dot(queries[...], pair[:tok], (1, 1)), -1e30)
        for ok, pair in zip(allowed, pairs, strict=True)
    ]
    top = functools.reduce(jnp.maximum, [jnp.max(s, axis=1, keepdims=True) for s in scores])
    weights = [jnp.exp(s - top) for s in scores]
    total = sum(jnp.sum(w, axis=1, keepdims=True) for w in weights)
    context[...] = sum(
        dot((w / total).astype(bf16), pair[tok : 2 * tok], (1, 0))
        for w, pair in zip(weights, pairs, strict=True)
    ).astype(bf16)
    log_total[...] = jnp.broadcast_to(top + jnp.log(total), log_total.shape)


def attend(block, segment, queries, pairs):
    tok, head_dim = queries.shape
    vmem = pl.BlockSpec(memory_space=pltpu.VMEM)
    return pl.pallas_call(
        attend_kernel,
        out_shape=[
            jax.ShapeDtypeStruct((tok, head_dim), bf16),
            jax.ShapeDtypeStruct((tok, 128), f32),
        ],
        in_specs=[pl.BlockSpec(memory_space=pltpu.SMEM)] + [vmem] * 5,
        out_specs=[vmem] * 2,
        compiler_params=pltpu.CompilerParams(vmem_limit_bytes=SOME),
        cost_estimate=pl.CostEstimate(
            flops=12 * tok * tok * head_dim, bytes_accessed=1_500_000, transcendentals=3 * tok * tok
        ),
    )(block, segment, queries, *pairs)


def attend_back_kernel(
    block, segment, log_total, d_branch, weight, queries, far, near, own, d_queries, d_far, d_near, d_own
):
    pairs = (far, near, own)
    tok = queries.shape[0]
    d_context = dot(d_branch[...], weight[...], (1, 1)).astype(bf16)
    allowed = masks(block[0], segment[...], pairs)
    lse = log_total[:, :1]
    probs, d_probs = [], []
    for ok, pair in zip(allowed, pairs, strict=True):
        scores = jnp.where(ok, dot(queries[...], pair[:tok], (1, 1)), -1e30)
        probs.append(jnp.exp(scores - lse))
        d_probs.append(dot(d_context, pair[tok : 2 * tok], (1, 1)))
    mean = sum(
        jnp.sum(p * d, axis=1, keepdims=True) for p, d in zip(probs, d_probs, strict=True)
    )
    total = None
    for p, d, pair, out in zip(probs, d_probs, pairs, (d_far, d_near, d_own), strict=True):
        d_scores = (p * (d - mean)).astype(bf16)
        part = dot(d_scores, pair[:tok], (1, 0))
        total = part if total is None else total + part
        out[:tok] = dot(d_scores, queries[...], (0, 0)).astype(out.dtype)
        out[tok:] = dot(p.astype(bf16), d_context, (0, 0)).astype(out.dtype)
    d_queries[...] = total


def attend_back(block, segment, log_total, d_branch, weight, queries, pairs):
    tok, head_dim = queries.shape
    vmem = pl.BlockSpec(memory_space=pltpu.VMEM)
    return pl.pallas_call(
        attend_back_kernel,
        out_shape=[
            jax.ShapeDtypeStruct((tok, head_dim), f32),
            jax.ShapeDtypeStruct((2 * tok, head_dim), bf16),
            jax.ShapeDtypeStruct((2 * tok, head_dim), bf16),
            jax.ShapeDtypeStruct((2 * tok, head_dim), f32),
        ],
        in_specs=[pl.BlockSpec(memory_space=pltpu.SMEM)] + [vmem] * 8,
        out_specs=[vmem] * 4,
        compiler_params=pltpu.CompilerParams(vmem_limit_bytes=SOME),
        cost_estimate=pl.CostEstimate(
            flops=30 * tok * tok * head_dim, bytes_accessed=3_500_000, transcendentals=3 * tok * tok
        ),
    )(block, segment, log_total, d_branch, weight, queries, *pairs)


def place_kernel(where_ref, *refs, turns, held):
    n = len(turns)
    parts, outs = refs[:n], refs[n + held : n + held + 3]
    stage, sems, tail_sems = refs[-3:]
    slots = stage.shape[0]
    core, first, second = where_ref[0], where_ref[1], where_ref[2]
    chunks = [
        (ref, i, base + i, other, flip)
        for ref, (other, flip, base) in zip(parts, turns, strict=True)
        for i in range(ref.shape[0])
    ]

    def place(index):
        _, _, across, other, flip = chunks[index]
        which = 1 - core if other else core
        along = (second if other else first) ^ flip
        y = jnp.where(which == 0, along, across)
        z = jnp.where(which == 0, across, along)
        odd = lax.rem(y, 2)
        row = 216 * (2 * z + y // 2) + 104 * odd + 48 * which + 8 * which * odd
        return pl.multiple_of(row, 8), (which == 1) | (odd == 1)

    def copies(index):
        slot = index % slots
        row, whole = place(index)
        for mat, out in enumerate(outs):
            yield (
                pltpu.make_async_copy(
                    stage.at[slot, mat, pl.ds(0, 48)],
                    out.at[pl.ds(row, 48)],
                    sems.at[slot, mat],
                ),
                pltpu.make_async_copy(
                    stage.at[slot, mat, pl.ds(48, 8)],
                    out.at[pl.ds(pl.multiple_of(row + 48, 8), 8)],
                    tail_sems.at[slot, mat],
                ),
                whole,
            )

    def finish(index):
        for most, tail, whole in copies(index):
            most.wait()
            pl.when(whole)(tail.wait)

    for index, (ref, i, *_) in enumerate(chunks):
        if index >= slots:
            finish(index - slots)
        stage[index % slots] = ref[i].astype(f32)
        for most, tail, whole in copies(index):
            most.start()
            pl.when(whole)(tail.start)
    for index in range(max(0, len(chunks) - slots), len(chunks)):
        finish(index)


def placed(where, parts, outs, units):
    arrays = [p[0].reshape(-1, 3, 56, p[0].shape[-1]) for p in parts]
    width = arrays[0].shape[-1]
    slots = 4
    return pl.pallas_call(
        functools.partial(
            place_kernel, turns=tuple(p[1:] for p in parts), held=len(outs)
        ),
        out_shape=[jax.ShapeDtypeStruct((units, width), f32)] * 3,
        in_specs=[pl.BlockSpec(memory_space=pltpu.SMEM)]
        + [pl.BlockSpec(memory_space=pltpu.VMEM)] * len(arrays)
        + [pl.BlockSpec(memory_space=pl.ANY)] * len(outs),
        out_specs=[pl.BlockSpec(memory_space=pl.ANY)] * 3,
        scratch_shapes=[
            pltpu.VMEM((slots, 3, 56, width), f32),
            pltpu.SemaphoreType.DMA((slots, 3)),
            pltpu.SemaphoreType.DMA((slots, 3)),
        ],
        input_output_aliases={1 + len(arrays) + i: i for i in range(len(outs))},
        compiler_params=pltpu.CompilerParams(vmem_limit_bytes=SOME),
        cost_estimate=pl.CostEstimate(
            flops=0, bytes_accessed=sum(p.size for p in arrays) * 6, transcendentals=0
        ),
    )(where, *arrays, *outs)


def finish_kernel(
    core_ref, own, got, out_grad, query_grad, key_grad, value_grad, attn, post, ffw, final, query, key, rows
):
    core = core_ref[0]
    for pieces, other in ((own, 0), (got, 1)):
        even = core == other
        for along in range(4):
            for across in range(4):
                row = jnp.where(even, 8 * across + 2 * along, 8 * along + 2 * across + 1) * 8
                row = pl.ds(pl.multiple_of(row, 8), 8)
                for kind in range(6):
                    rows[kind, row] = pieces[along, kind, across].astype(f32)
    out_grad[...] = rows[0]
    query_grad[...] = rows[1].T
    for lane in range(4):
        key_grad[:, 64 * lane : 64 * lane + 64] = rows[2 + lane, :64].T
        value_grad[:, 64 * lane : 64 * lane + 64] = rows[2 + lane, 64:128].T
    gains = sum(rows[2 + lane, 128:136] for lane in range(4))
    for at, out in enumerate((attn, post, ffw, final)):
        out[...] = gains[at]
    size = query.shape[0]
    query[...] = gains[4, :size]
    key[...] = gains[4, size : 2 * size]


def finished(core, own, got):
    width = own.shape[-1]
    vmem = pl.BlockSpec(memory_space=pltpu.VMEM)
    return pl.pallas_call(
        finish_kernel,
        out_shape=[
            jax.ShapeDtypeStruct((256, width), f32),
            jax.ShapeDtypeStruct((width, 256), f32),
            jax.ShapeDtypeStruct((width, 256), f32),
            jax.ShapeDtypeStruct((width, 256), f32),
            *[jax.ShapeDtypeStruct((width,), f32)] * 4,
            *[jax.ShapeDtypeStruct((256,), f32)] * 2,
        ],
        in_specs=[pl.BlockSpec(memory_space=pltpu.SMEM), vmem, vmem],
        out_specs=[vmem] * 10,
        scratch_shapes=[pltpu.VMEM((6, 256, width), f32)],
        compiler_params=pltpu.CompilerParams(vmem_limit_bytes=SOME),
        cost_estimate=pl.CostEstimate(flops=0, bytes_accessed=10_000_000, transcendentals=0),
    )(core, own, got)


def local(
    layer_input,
    segment_ids,
    out_cotangent,
    attn_norm_gain,
    query_weight,
    key_weight,
    value_weight,
    query_gain,
    key_gain,
    output_weight,
    attn_post_gain,
    ffw_norm_gain,
    gate_weight,
    up_weight,
    down_weight,
    ffw_post_gain,
):
    tok, width = layer_input.shape
    head_dim = key_weight.shape[1]
    units = down_weight.shape[0]
    block = lax.axis_index("seq")
    lane = lax.axis_index("tensor")
    core = block % 2
    row = (block // 2) % 4
    plane = block // 8
    first = jnp.where(core == 0, row, plane)
    second = jnp.where(core == 0, plane, row)
    quarter_tok = tok // 4

    place = jnp.stack([lane, core, block]).astype(jnp.int32)
    where = jnp.stack([core, first, second]).astype(jnp.int32)
    freq = rope_base ** (-2.0 * np.arange(head_dim // 2) / head_dim)
    start = (np.arange(lax.axis_size("seq")) * tok)[:, None] * freq[None, :]
    inner = np.arange(tok)[:, None] * freq[None, :]
    tables = [jnp.asarray(f(angle), f32) for angle in (start, inner) for f in (np.cos, np.sin)]

    square = (tok, head_dim)
    normed, own_pair, k_raw, q_raw, queries, cosine, sine = call(
        prepare_kernel,
        [
            ((tok, width), bf16),
            ((2 * tok + 16, head_dim), bf16),
            (square, f32),
            (square, f32),
            (square, bf16),
            ((tok, head_dim // 2), f32),
            ((tok, head_dim // 2), f32),
        ],
        place,
        layer_input,
        attn_norm_gain,
        key_weight,
        value_weight,
        query_weight,
        key_gain,
        query_gain,
        *tables,
        segment_ids,
        scalars=1,
        flops=6 * tok * width * head_dim,
        room=MOST,
    )
    left_one = shifted(own_pair, 1)
    left_two = shifted(own_pair, 2)

    weight_half = tok // 2
    halved, _ = tied(output_weight, own_pair)
    own_weight = pick(halved.reshape(2, weight_half, width), core)
    got_weight = [send(own_weight, round_x(by)) for by in (1, 2, 3)]

    pairs = (left_two, left_one, own_pair)
    block_ref = block.astype(jnp.int32).reshape(1)
    segment = segment_ids.astype(f32)[:, None]
    context, log_total = attend(block_ref, segment, queries, pairs)

    got_context = [send(context, round_x(by)) for by in (1, 2, 3)]
    *got_context, got_weight[0], got_weight[1], got_weight[2] = tied(*got_context, *got_weight)
    other_weight = [send(part, swap_cores()) for part in got_weight]
    branch, middle, normed_two = call(
        project_kernel,
        [((tok, width), f32), ((tok, width), f32), ((tok, width), bf16)],
        place,
        layer_input,
        attn_post_gain,
        ffw_norm_gain,
        context,
        *got_context,
        output_weight,
        *got_weight,
        *other_weight,
        scalars=1,
        flops=8 * tok * tok * width,
    )
    gate = dot(gate_weight, normed_two, (0, 1))
    up_val = dot(up_weight, normed_two, (0, 1))
    active, gelu_back = jax.vjp(lambda val: jax.nn.gelu(val, approximate=True), gate)
    hidden = (active * up_val).astype(bf16)
    down_part = dot(hidden, down_weight, (0, 0)).astype(bf16)

    def halves(values):
        groups = values.reshape(8, units // 8, tok)
        groups = jnp.concatenate([groups[:, :56], groups[:, 48:]], axis=1)
        pieces = groups.reshape(4, 4, 2, 56, tok)
        return (
            lax.dynamic_index_in_dim(pieces, core, 2, keepdims=False),
            lax.dynamic_index_in_dim(pieces, 1 - core, 2, keepdims=False),
        )

    def arranged(values):
        values = jnp.where(core == 0, values.swapaxes(0, 1), values)
        by_first = [pick(values, first ^ flip) for flip in range(4)]
        groups = [
            jnp.stack([by_first[i][2 * stream : 2 * stream + 2] for i in order])
            for stream, order in ((0, (0, 3)), (0, (1, 2)), (1, (0, 1)), (1, (3, 2)))
        ]
        return jnp.stack(groups).reshape(4, 224, tok)

    hidden_own, hidden_give = halves(hidden)
    hidden_got = send(hidden_give, swap_cores())
    normed_two_got = send(normed_two, swap_cores())

    def quarters(parts):
        parts = parts.reshape(4, quarter_tok, parts.shape[-1])
        given = [pick(parts, (lane + by) % 4) for by in (1, 2, 3)]
        return [pick(parts, lane)] + [
            send(part, round_x(by)) for by, part in zip((1, 2, 3), given, strict=True)
        ]

    piece = (quarter_tok, width)
    out_own, d_branch_two, final_part = call(
        final_kernel,
        [(piece, bf16), (piece, bf16), ((1, width), f32)],
        place,
        *quarters(down_part),
        middle,
        out_cotangent,
        ffw_post_gain,
        scalars=1,
    )
    d_branch_two = gather(d_branch_two, lane, round_x).reshape(tok, width)
    d_branch_two_got = send(d_branch_two, swap_cores())

    d_hidden = dot(down_weight, d_branch_two, (1, 1))
    d_gate = gelu_back(d_hidden * up_val)[0].astype(bf16)
    d_up = (d_hidden * active).astype(bf16)
    d_normed_two = (dot(d_gate, gate_weight, (0, 1)) + dot(d_up, up_weight, (0, 1))).astype(bf16)
    d_gate_own, d_gate_give = halves(d_gate)
    d_up_own, d_up_give = halves(d_up)
    d_pair_got = send(jnp.stack([d_gate_give, d_up_give]), swap_cores())

    keep_a, give_a, keep_b, give_b = weight_parts(
        *(
            arranged(v)
            for v in (hidden_own, hidden_got, d_gate_own, d_pair_got[0], d_up_own, d_pair_got[1])
        ),
        d_branch_two,
        d_branch_two_got,
        normed_two,
        normed_two_got,
    )
    got_a = send(give_a, along_first(1))
    got_b = send(give_b, along_first(3))

    *got_normed, keep_a, keep_b = tied(*quarters(d_normed_two), keep_a, keep_b)
    d_middle, d_branch, ffw_part, post_part = call(
        between_kernel,
        [(piece, f32), (piece, bf16), ((1, width), f32), ((1, width), f32)],
        place,
        *got_normed,
        middle,
        branch,
        out_cotangent,
        ffw_norm_gain,
        attn_post_gain,
        scalars=1,
    )
    d_branch = gather(d_branch, lane, round_x).reshape(tok, width)
    d_queries, left_far, left_near, summed = attend_back(
        block_ref, segment, log_total, d_branch, output_weight, queries, pairs
    )
    got_near = shifted(left_near, -1)
    got_far = shifted(left_far, -2)
    got_near, got_far, got_a, got_b = tied(got_near, got_far, got_a, got_b)
    keep_a, give_a = added(keep_a[:336], got_a[:336]), added(keep_a[336:], got_a[336:])
    keep_b, give_b = added(keep_b[:336], got_b[:336]), added(keep_b[336:], got_b[336:])
    got_a = send(give_a, along_first(3))
    got_b = send(give_b, along_first(1))
    d_query, payload, query_part, key_part = call(
        key_kernel,
        [
            (square, bf16),
            ((tok, width + 2 * tok), bf16),
            ((1, head_dim), f32),
            ((1, head_dim), f32),
        ],
        q_raw,
        k_raw,
        d_queries,
        summed,
        got_near,
        got_far,
        cosine,
        sine,
        query_gain,
        key_gain,
        query_weight,
        key_weight,
        value_weight,
        flops=6 * tok * width * head_dim,
    )
    got_both = quarters(payload)
    (products,) = call(
        products_kernel,
        [((2 * head_dim, width), f32)],
        context,
        d_branch,
        d_query,
        normed,
        flops=4 * tok * width * head_dim,
    )
    *got_both, got_a, got_b = tied(*got_both, got_a, got_b)
    fours = jnp.stack([added(keep_a, got_a), added(keep_b, got_b)])
    fours = fours.reshape(2, 3, 2, 56, width).swapaxes(1, 2).reshape(4, 168, width)
    mine = pick(fours, second).astype(f32)
    got = [send(pick(fours, (second + by) % 4), round_second(by)) for by in (1, 2, 3)]
    input_own, keep, give = pl.pallas_call(
        entry_kernel,
        out_shape=[
            jax.ShapeDtypeStruct(piece, bf16),
            jax.ShapeDtypeStruct((3, 16, 8, width), f32),
            jax.ShapeDtypeStruct((3, 16, 8, width), bf16),
        ],
        in_specs=[pl.BlockSpec(memory_space=pltpu.SMEM)]
        + [pl.BlockSpec(memory_space=pltpu.VMEM)] * 14,
        out_specs=[pl.BlockSpec(memory_space=pltpu.VMEM)] * 3,
        scratch_shapes=[pltpu.VMEM((tok, width), f32)],
        compiler_params=pltpu.CompilerParams(vmem_limit_bytes=SOME),
        cost_estimate=pl.CostEstimate(
            flops=256 * tok * width, bytes_accessed=12_000_000, transcendentals=0
        ),
    )(
        place,
        *got_both,
        layer_input,
        d_middle,
        attn_norm_gain,
        normed,
        post_part,
        ffw_part,
        final_part,
        query_part,
        key_part,
        products,
    )
    pack_got = send(give, swap_cores())
    pack_got, *got = tied(pack_got, *got)
    mine = (mine + got[0].astype(f32) + (got[1].astype(f32) + got[2].astype(f32))).astype(bf16)
    part = (3, 4, 8, width)
    pack, *given = call(
        merge_kernel, [(part, f32)] + [(part, bf16)] * 3, where, keep, pack_got, scalars=1
    )
    given = [send(part, round_first(by)) for by, part in zip((1, 2, 3), given, strict=True)]
    for part in given:
        pack = pack + part.astype(f32)
    pack = pack.astype(bf16).reshape(96, width)
    both = lax.optimization_barrier(jnp.concatenate([mine, pack]))
    given = [send(both, round_second(by)) for by in (1, 2, 3)]
    quarter = jnp.zeros((4, *mine.shape), bf16)
    quarter = lax.dynamic_update_index_in_dim(quarter, both[:168], second, 0)
    for by, part in zip((1, 2, 3), given, strict=True):
        quarter = lax.dynamic_update_index_in_dim(quarter, part[:168], (second + 4 - by) % 4, 0)
    pack, *given = (part[168:].astype(f32) for part in (both, *given))
    pack = (pack + given[1] + (given[0] + given[2])).astype(bf16).reshape(3, 4, 8, width)
    near_a = send(quarter, along_first(1))
    near_b = send(quarter, along_first(3))
    other_own = send(quarter, swap_cores())
    given = [send(pack[2], round_x(by)) for by in (1, 2, 3)]
    *given, near_a, near_b = tied(*given, near_a, near_b)
    far_a = send(near_b[:2], along_first(1))
    far_b = send(near_a[2:], along_first(3))
    other_a = send(near_a, swap_cores())
    other_b = send(near_b, swap_cores())
    grads = placed(
        where,
        [
            (quarter, False, 0, 0),
            (near_a, False, 1, 0),
            (near_b, False, 3, 0),
            (other_own, True, 0, 0),
            (other_a, True, 1, 0),
            (other_b, True, 3, 0),
        ],
        [],
        units,
    )
    rest = jnp.zeros((4, *pack.shape[1:]), bf16)
    rest = lax.dynamic_update_index_in_dim(rest, pack[2], lane, 0)
    for by, part in zip((1, 2, 3), given, strict=True):
        rest = lax.dynamic_update_index_in_dim(rest, part, (lane + 4 - by) % 4, 0)
    pack = jnp.concatenate([pack[:2], rest])
    pack, out_own, input_own = tied(pack, out_own, input_own)
    own_ends = jnp.stack([out_own, input_own])
    got_ends = [send(own_ends, round_x(by)) for by in (1, 2, 3)]
    given = [send(pack, round_first(by)) for by in (1, 2, 3)]
    grads = list(grads)
    *got_ends, given[0], given[1], given[2], far_a, far_b, grads[0] = tied(
        *got_ends, *given, far_a, far_b, grads[0]
    )
    ends = jnp.zeros((4, *own_ends.shape), bf16)
    ends = lax.dynamic_update_index_in_dim(ends, own_ends, lane, 0)
    for by, part in zip((1, 2, 3), got_ends, strict=True):
        ends = lax.dynamic_update_index_in_dim(ends, part, (lane + 4 - by) % 4, 0)
    whole = jnp.zeros((4, *pack.shape), bf16)
    whole = lax.dynamic_update_index_in_dim(whole, pack, first, 0)
    for by, part in zip((1, 2, 3), given, strict=True):
        whole = lax.dynamic_update_index_in_dim(whole, part, (first + 4 - by) % 4, 0)
    pack_got = send(whole, swap_cores())
    out_grad, query_grad, key_grad, value_grad, *gains = finished(
        core.astype(jnp.int32).reshape(1), whole, pack_got
    )
    other_far_a = send(far_a, swap_cores())
    other_far_b = send(far_b, swap_cores())
    other_far_a, other_far_b, out_grad = tied(other_far_a, other_far_b, out_grad)
    down_grad, gate_grad, up_grad = placed(
        where,
        [
            (far_a, False, 2, 0),
            (far_b, False, 2, 2),
            (other_far_a, True, 2, 0),
            (other_far_b, True, 2, 2),
        ],
        grads,
        units,
    )
    layer_output = ends[:, 0].reshape(tok, width)
    input_grad = ends[:, 1].reshape(tok, width)
    return (
        layer_output,
        input_grad,
        gains[0],
        query_grad,
        key_grad,
        value_grad,
        gains[4],
        gains[5],
        out_grad,
        gains[1],
        gains[2],
        gate_grad.T,
        up_grad.T,
        down_grad,
        gains[3],
    )


def solution(mesh):
    rows = P("seq", None)
    return jax.shard_map(
        local,
        mesh=mesh,
        in_specs=(
            rows,
            P("seq"),
            rows,
            P(),
            P(None, "tensor"),
            P(),
            P(),
            P(),
            P(),
            P("tensor", None),
            P(),
            P(),
            P(None, "tensor"),
            P(None, "tensor"),
            P("tensor", None),
            P(),
        ),
        out_specs=(
            rows,
            rows,
            P(),
            P(None, "tensor"),
            P(),
            P(),
            P(),
            P(),
            P("tensor", None),
            P(),
            P(),
            P(None, "tensor"),
            P(None, "tensor"),
            P("tensor", None),
            P(),
        ),
        check_vma=False,
    )
```

```python
import functools

import jax
import jax.numpy as jnp
import numpy as np
from jax import lax
from jax.experimental import pallas as pl
from jax.experimental.pallas import tpu as pltpu
from jax.sharding import PartitionSpec as P

WINDOW = 512
SOME = 24 * 1024 * 1024
MOST = 60 * 1024 * 1024

eps = 1e-06
rope_base = 10000.0
f32 = jnp.float32
bf16 = jnp.bfloat16
BOTH = ("seq", "tensor")


def places():
    return [(z, y, c, x) for z in range(4) for y in range(4) for c in range(2) for x in range(4)]


def number(z, y, c, x):
    return ((z * 4 + y) * 2 + c) * 4 + x


def route(move):
    return [(number(*p), number(*move(*p))) for p in places()]


def round_x(by):
    return route(lambda z, y, c, x: (z, y, c, (x + by) % 4))


def swap_cores():
    return route(lambda z, y, c, x: (z, y, 1 - c, x))


def along_first(flip):
    return route(lambda z, y, c, x: (z, y ^ flip, c, x) if c == 0 else (z ^ flip, y, c, x))


def round_first(by):
    return route(
        lambda z, y, c, x: (z, (y + by) % 4, c, x) if c == 0 else ((z + by) % 4, y, c, x)
    )


def round_second(by):
    return route(
        lambda z, y, c, x: ((z + by) % 4, y, c, x) if c == 0 else (z, (y + by) % 4, c, x)
    )


def send(value, pairs):
    return lax.ppermute(value, BOTH, pairs)


def shifted(value, by):
    pairs = [
        (i * 4 + x, (i + by) * 4 + x) for i in range(32) if 0 <= i + by < 32 for x in range(4)
    ]
    return send(value, pairs)


def pick(parts, index):
    return lax.dynamic_index_in_dim(parts, index, 0, keepdims=False)


def dot(first, second, over):
    return lax.dot_general(
        first, second, (((over[0],), (over[1],)), ((), ())), preferred_element_type=f32
    )


def scatter_sum(parts, index, turn):
    total = pick(parts, index).astype(f32)
    for by in (1, 2, 3):
        total = total + send(pick(parts, (index + by) % 4), turn(by)).astype(f32)
    return total


def gather(part, index, turn):
    whole = jnp.zeros((4, *part.shape), part.dtype)
    whole = lax.dynamic_update_index_in_dim(whole, part, index, 0)
    for by in (1, 2, 3):
        whole = lax.dynamic_update_index_in_dim(
            whole, send(part, turn(by)), (index + 4 - by) % 4, 0
        )
    return whole


def inv_scale(values):
    return lax.rsqrt(jnp.mean(values * values, axis=-1, keepdims=True) + eps)


def norm_back(values, scale, gain, grad):
    unit = values * scale
    weighted = grad * gain
    d_values = scale * (weighted - unit * jnp.mean(weighted * unit, axis=-1, keepdims=True))
    return (d_values, jnp.sum(grad * unit, axis=0))


def rotate(values, cosine, sine):
    half = values.shape[-1] // 2
    first = values[..., :half]
    second = values[..., half:]
    return jnp.concatenate(
        [first * cosine - second * sine, second * cosine + first * sine], axis=-1
    )


def padded(values, rows):
    return jnp.pad(values, ((0, rows - values.shape[0]), (0, 0)))


def added(first, second):
    return (first.astype(f32) + second.astype(f32)).astype(bf16)


def tied(*values):
    return lax.optimization_barrier(values)


def call(kernel, outs, *arrays, scalars=0, flops=0, room=SOME):
    vmem = pl.BlockSpec(memory_space=pltpu.VMEM)
    outs = [jax.ShapeDtypeStruct(*o) for o in outs]
    moved = sum(v.size * v.dtype.itemsize for v in (*arrays, *outs))
    return pl.pallas_call(
        kernel,
        out_shape=outs,
        in_specs=[pl.BlockSpec(memory_space=pltpu.SMEM)] * scalars
        + [vmem] * (len(arrays) - scalars),
        out_specs=[vmem] * len(outs),
        compiler_params=pltpu.CompilerParams(vmem_limit_bytes=room),
        cost_estimate=pl.CostEstimate(flops=flops, bytes_accessed=moved, transcendentals=0),
    )(*arrays)


def own_rows(ref, lane, rows):
    return ref[pl.ds(pl.multiple_of(lane * rows, rows), rows)].astype(f32)


def project_kernel(
    place, x, post_gain, ffw_gain, ctx0, ctx1, ctx2, ctx3, weight, own1, own2, own3, other1, other2, other3,
    branch, middle, normed
):
    even = place[1] == 0
    half = own1.shape[0]
    total = dot(ctx0[...], weight[...], (1, 0))
    for ctx, mine, theirs in ((ctx1, own1, other1), (ctx2, own2, other2), (ctx3, own3, other3)):
        low = jnp.where(even, mine[...], theirs[...])
        high = jnp.where(even, theirs[...], mine[...])
        total += dot(ctx[:, :half], low, (1, 0)) + dot(ctx[:, half:], high, (1, 0))
    branch[...] = total
    after = x[...].astype(f32) + total * inv_scale(total) * post_gain[...]
    middle[...] = after
    normed[...] = (after * inv_scale(after) * ffw_gain[...]).astype(bf16)


def final_kernel(place, p0, p1, p2, p3, middle, cotangent, gain, out, d_branch, part):
    lane = place[0]
    branch = p0[...].astype(f32) + p1[...].astype(f32) + p2[...].astype(f32) + p3[...].astype(f32)
    rows = branch.shape[0]
    scale = inv_scale(branch)
    cot = own_rows(cotangent, lane, rows)
    out[...] = (own_rows(middle, lane, rows) + branch * scale * gain[...]).astype(bf16)
    d_values, d_gain = norm_back(branch, scale, gain[...], cot)
    d_branch[...] = d_values.astype(bf16)
    part[...] = d_gain[None]


def between_kernel(
    place, p0, p1, p2, p3, middle, branch, cotangent, ffw_gain, post_gain,
    d_middle, d_branch, ffw_part, post_part
):
    lane = place[0]
    grad = p0[...].astype(f32) + p1[...].astype(f32) + p2[...].astype(f32) + p3[...].astype(f32)
    rows = grad.shape[0]
    after = own_rows(middle, lane, rows)
    before = own_rows(branch, lane, rows)
    d_values, d_gain = norm_back(after, inv_scale(after), ffw_gain[...], grad)
    ffw_part[...] = d_gain[None]
    d_values = own_rows(cotangent, lane, rows) + d_values
    d_middle[...] = d_values
    d_values, d_gain = norm_back(before, inv_scale(before), post_gain[...], d_values)
    d_branch[...] = d_values.astype(bf16)
    post_part[...] = d_gain[None]


def key_kernel(
    q_raw, k_raw, d_queries, d_own, d_near, d_far, cosine, sine, query_gain, key_gain, query_weight, key_weight,
    value_weight, d_query, payload, query_part, key_part
):
    tok, head_dim = q_raw.shape
    width = query_weight.shape[0]
    cos, sin = cosine[...], -sine[...]
    raw = q_raw[...]
    d_raw, d_gain = norm_back(
        raw, inv_scale(raw), query_gain[...], rotate(d_queries[...] * head_dim**-0.5, cos, sin)
    )
    query_part[...] = d_gain[None]
    d_low = d_raw.astype(bf16)
    d_query[...] = d_low
    total = dot(d_low, query_weight[...], (1, 1))
    summed = d_own[...] + d_near[...].astype(f32) + d_far[...].astype(f32)
    raw = k_raw[...]
    d_raw, d_gain = norm_back(raw, inv_scale(raw), key_gain[...], rotate(summed[:tok], cos, sin))
    key_part[...] = d_gain[None]
    total += dot(d_raw.astype(bf16), key_weight[...], (1, 1))
    total += dot(summed[tok:].astype(bf16), value_weight[...], (1, 1))
    payload[:, :width] = total.astype(bf16)
    payload[:, width : width + tok] = d_raw.T.astype(bf16)
    payload[:, width + tok :] = summed[tok:].T.astype(bf16)


def products_kernel(context, d_branch, d_query, normed, out):
    half = context.shape[1]
    out[:half] = dot(context[...], d_branch[...], (0, 0))
    out[half:] = dot(d_query[...], normed[...], (0, 0))


def entry_kernel(
    place, p0, p1, p2, p3, x, d_middle, gain, normed, post_part, ffw_part, final_part, query_part, key_part,
    products, input_grad, keep, give, rest
):
    lane, core = place[0], place[1]
    both = p0[...].astype(f32) + p1[...].astype(f32) + p2[...].astype(f32) + p3[...].astype(f32)
    rows = both.shape[0]
    width = normed.shape[1]
    tok = normed.shape[0]
    full = own_rows(x, lane, rows)
    d_values, d_gain = norm_back(full, inv_scale(full), gain[...], both[:, :width])
    input_grad[...] = (d_middle[...] + d_values).astype(bf16)
    d_keys = both[:, width : width + tok].astype(bf16)
    d_values = both[:, width + tok :].astype(bf16)
    rest[:rows] = dot(d_keys, normed[...], (1, 0))
    rest[rows : 2 * rows] = dot(d_values, normed[...], (1, 0))
    heads = jnp.concatenate(
        [query_part[...], key_part[...], jnp.zeros((1, width - 2 * query_part.shape[1]), f32)], axis=1
    )
    index = lax.broadcasted_iota(jnp.int32, (8, width), 0)
    gains = jnp.zeros((8, width), f32)
    for at, part in enumerate((d_gain[None], post_part[...], ffw_part[...], final_part[...], heads)):
        gains = jnp.where(index == at, part, gains)
    rest[2 * rows : 2 * rows + 8] = gains
    rest[2 * rows + 8 :] = jnp.zeros((rest.shape[0] - 2 * rows - 8, width), f32)
    for kind in range(3):
        source = rest if kind == 2 else products
        base = 256 if kind == 1 else 0
        for chip in range(16):
            at = base + 16 * chip
            keep[kind, chip] = source[pl.ds(pl.multiple_of(at + 8 * core, 8), 8)]
            give[kind, chip] = source[pl.ds(pl.multiple_of(at + 8 - 8 * core, 8), 8)].astype(bf16)


def merge_kernel(where, keep, got, *outs):
    core, first = where[0], where[1]
    for by, out in enumerate(outs):
        along = lax.rem(first + by, 4)
        for across in range(4):
            chip = jnp.where(core == 0, 4 * across + along, 4 * along + across)
            for kind in range(3):
                total = keep[kind, chip] + got[kind, chip].astype(f32)
                out[kind, across] = total.astype(out.dtype)


def weight_kernel(
    hid_own, hid_got, gate_own, gate_got, up_own, up_got, dy_own, dy_got, xn_own, xn_got, *outs
):
    mats = (
        (hid_own, hid_got, dy_own, dy_got),
        (gate_own, gate_got, xn_own, xn_got),
        (up_own, up_got, xn_own, xn_got),
    )
    for group, out in enumerate(outs):
        for index, (left_own, left_got, right_own, right_got) in enumerate(mats):
            total = jnp.dot(left_own[group], right_own[...], preferred_element_type=f32)
            total += jnp.dot(left_got[group], right_got[...], preferred_element_type=f32)
            total = total.astype(bf16)
            out[112 * index : 112 * index + 112] = total[:112]
            out[336 + 112 * index : 448 + 112 * index] = total[112:]


def weight_parts(*arrays):
    width = arrays[-1].shape[1]
    return pl.pallas_call(
        weight_kernel,
        out_shape=[jax.ShapeDtypeStruct((672, width), bf16)] * 4,
        in_specs=[pl.BlockSpec(memory_space=pltpu.VMEM)] * len(arrays),
        out_specs=[pl.BlockSpec(memory_space=pltpu.VMEM)] * 4,
        compiler_params=pltpu.CompilerParams(vmem_limit_bytes=SOME),
        cost_estimate=pl.CostEstimate(
            flops=2 * 2688 * 512 * width, bytes_accessed=12_000_000, transcendentals=0
        ),
    )(*arrays)


def masks(block, segment, pairs):
    tok = segment.shape[0]
    query = lax.broadcasted_iota(jnp.int32, (tok, tok), 0)
    key = lax.broadcasted_iota(jnp.int32, (tok, tok), 1)
    same = [segment == pair[2 * tok : 2 * tok + 16].astype(f32)[:1] for pair in pairs]
    return (
        same[0] & (key > query) & (block >= 2),
        same[1] & (block >= 1),
        same[2] & (key <= query),
    )


def prepare_kernel(
    place, x, gain, key_weight, value_weight, query_weight, key_gain, query_gain, start_cos, start_sin, inner_cos,
    inner_sin, marks, xn, pair, k_raw, q_raw, queries, cosine, sine
):
    tok, head_dim = k_raw.shape
    full = x[...].astype(f32)
    low = (full * inv_scale(full) * gain[...]).astype(bf16)
    xn[...] = low
    at = pl.ds(place[2], 1)
    cos = start_cos[at] * inner_cos[...] - start_sin[at] * inner_sin[...]
    sin = start_sin[at] * inner_cos[...] + start_cos[at] * inner_sin[...]
    cosine[...] = cos
    sine[...] = sin
    raw = dot(low, key_weight[...], (1, 0))
    k_raw[...] = raw
    pair[:tok] = rotate(raw * inv_scale(raw) * key_gain[...], cos, sin).astype(bf16)
    pair[tok : 2 * tok] = dot(low, value_weight[...], (1, 0)).astype(bf16)
    pair[2 * tok :] = jnp.broadcast_to(marks[...].astype(f32)[None], (16, tok)).astype(bf16)
    raw = dot(low, query_weight[...], (1, 0))
    q_raw[...] = raw
    turned = rotate(raw * inv_scale(raw) * query_gain[...], cos, sin)
    queries[...] = (turned * head_dim**-0.5).astype(bf16)


def attend_kernel(block, segment, queries, far, near, own, context, log_total):
    pairs = (far, near, own)
    tok = queries.shape[0]
    allowed = masks(block[0], segment[...], pairs)
    scores = [
        jnp.where(ok, dot(queries[...], pair[:tok], (1, 1)), -1e30)
        for ok, pair in zip(allowed, pairs, strict=True)
    ]
    top = functools.reduce(jnp.maximum, [jnp.max(s, axis=1, keepdims=True) for s in scores])
    weights = [jnp.exp(s - top) for s in scores]
    total = sum(jnp.sum(w, axis=1, keepdims=True) for w in weights)
    context[...] = sum(
        dot((w / total).astype(bf16), pair[tok : 2 * tok], (1, 0))
        for w, pair in zip(weights, pairs, strict=True)
    ).astype(bf16)
    log_total[...] = jnp.broadcast_to(top + jnp.log(total), log_total.shape)


def attend(block, segment, queries, pairs):
    tok, head_dim = queries.shape
    vmem = pl.BlockSpec(memory_space=pltpu.VMEM)
    return pl.pallas_call(
        attend_kernel,
        out_shape=[
            jax.ShapeDtypeStruct((tok, head_dim), bf16),
            jax.ShapeDtypeStruct((tok, 128), f32),
        ],
        in_specs=[pl.BlockSpec(memory_space=pltpu.SMEM)] + [vmem] * 5,
        out_specs=[vmem] * 2,
        compiler_params=pltpu.CompilerParams(vmem_limit_bytes=SOME),
        cost_estimate=pl.CostEstimate(
            flops=12 * tok * tok * head_dim, bytes_accessed=1_500_000, transcendentals=3 * tok * tok
        ),
    )(block, segment, queries, *pairs)


def attend_back_kernel(
    block, segment, log_total, d_branch, weight, queries, far, near, own, d_queries, d_far, d_near, d_own
):
    pairs = (far, near, own)
    tok = queries.shape[0]
    d_context = dot(d_branch[...], weight[...], (1, 1)).astype(bf16)
    allowed = masks(block[0], segment[...], pairs)
    lse = log_total[:, :1]
    probs, d_probs = [], []
    for ok, pair in zip(allowed, pairs, strict=True):
        scores = jnp.where(ok, dot(queries[...], pair[:tok], (1, 1)), -1e30)
        probs.append(jnp.exp(scores - lse))
        d_probs.append(dot(d_context, pair[tok : 2 * tok], (1, 1)))
    mean = sum(
        jnp.sum(p * d, axis=1, keepdims=True) for p, d in zip(probs, d_probs, strict=True)
    )
    total = None
    for p, d, pair, out in zip(probs, d_probs, pairs, (d_far, d_near, d_own), strict=True):
        d_scores = (p * (d - mean)).astype(bf16)
        part = dot(d_scores, pair[:tok], (1, 0))
        total = part if total is None else total + part
        out[:tok] = dot(d_scores, queries[...], (0, 0)).astype(out.dtype)
        out[tok:] = dot(p.astype(bf16), d_context, (0, 0)).astype(out.dtype)
    d_queries[...] = total


def attend_back(block, segment, log_total, d_branch, weight, queries, pairs):
    tok, head_dim = queries.shape
    vmem = pl.BlockSpec(memory_space=pltpu.VMEM)
    return pl.pallas_call(
        attend_back_kernel,
        out_shape=[
            jax.ShapeDtypeStruct((tok, head_dim), f32),
            jax.ShapeDtypeStruct((2 * tok, head_dim), bf16),
            jax.ShapeDtypeStruct((2 * tok, head_dim), bf16),
            jax.ShapeDtypeStruct((2 * tok, head_dim), f32),
        ],
        in_specs=[pl.BlockSpec(memory_space=pltpu.SMEM)] + [vmem] * 8,
        out_specs=[vmem] * 4,
        compiler_params=pltpu.CompilerParams(vmem_limit_bytes=SOME),
        cost_estimate=pl.CostEstimate(
            flops=30 * tok * tok * head_dim, bytes_accessed=3_500_000, transcendentals=3 * tok * tok
        ),
    )(block, segment, log_total, d_branch, weight, queries, *pairs)


def place_kernel(where_ref, *refs, turns, held):
    n = len(turns)
    parts, outs = refs[:n], refs[n + held : n + held + 3]
    stage, sems, tail_sems = refs[-3:]
    slots = stage.shape[0]
    core, first, second = where_ref[0], where_ref[1], where_ref[2]
    chunks = [
        (ref, i, base + i, other, flip)
        for ref, (other, flip, base) in zip(parts, turns, strict=True)
        for i in range(ref.shape[0])
    ]

    def place(index):
        _, _, across, other, flip = chunks[index]
        which = 1 - core if other else core
        along = (second if other else first) ^ flip
        y = jnp.where(which == 0, along, across)
        z = jnp.where(which == 0, across, along)
        odd = lax.rem(y, 2)
        row = 216 * (2 * z + y // 2) + 104 * odd + 48 * which + 8 * which * odd
        return pl.multiple_of(row, 8), (which == 1) | (odd == 1)

    def copies(index):
        slot = index % slots
        row, whole = place(index)
        for mat, out in enumerate(outs):
            yield (
                pltpu.make_async_copy(
                    stage.at[slot, mat, pl.ds(0, 48)],
                    out.at[pl.ds(row, 48)],
                    sems.at[slot, mat],
                ),
                pltpu.make_async_copy(
                    stage.at[slot, mat, pl.ds(48, 8)],
                    out.at[pl.ds(pl.multiple_of(row + 48, 8), 8)],
                    tail_sems.at[slot, mat],
                ),
                whole,
            )

    def finish(index):
        for most, tail, whole in copies(index):
            most.wait()
            pl.when(whole)(tail.wait)

    for index, (ref, i, *_) in enumerate(chunks):
        if index >= slots:
            finish(index - slots)
        stage[index % slots] = ref[i].astype(f32)
        for most, tail, whole in copies(index):
            most.start()
            pl.when(whole)(tail.start)
    for index in range(max(0, len(chunks) - slots), len(chunks)):
        finish(index)


def placed(where, parts, outs, units):
    arrays = [p[0].reshape(-1, 3, 56, p[0].shape[-1]) for p in parts]
    width = arrays[0].shape[-1]
    slots = 4
    return pl.pallas_call(
        functools.partial(
            place_kernel, turns=tuple(p[1:] for p in parts), held=len(outs)
        ),
        out_shape=[jax.ShapeDtypeStruct((units, width), f32)] * 3,
        in_specs=[pl.BlockSpec(memory_space=pltpu.SMEM)]
        + [pl.BlockSpec(memory_space=pltpu.VMEM)] * len(arrays)
        + [pl.BlockSpec(memory_space=pl.ANY)] * len(outs),
        out_specs=[pl.BlockSpec(memory_space=pl.ANY)] * 3,
        scratch_shapes=[
            pltpu.VMEM((slots, 3, 56, width), f32),
            pltpu.SemaphoreType.DMA((slots, 3)),
            pltpu.SemaphoreType.DMA((slots, 3)),
        ],
        input_output_aliases={1 + len(arrays) + i: i for i in range(len(outs))},
        compiler_params=pltpu.CompilerParams(vmem_limit_bytes=SOME),
        cost_estimate=pl.CostEstimate(
            flops=0, bytes_accessed=sum(p.size for p in arrays) * 6, transcendentals=0
        ),
    )(where, *arrays, *outs)


def finish_kernel(
    core_ref, own, got, out_grad, query_grad, key_grad, value_grad, attn, post, ffw, final, query, key, rows
):
    core = core_ref[0]
    for pieces, other in ((own, 0), (got, 1)):
        even = core == other
        for along in range(4):
            for across in range(4):
                row = jnp.where(even, 8 * across + 2 * along, 8 * along + 2 * across + 1) * 8
                row = pl.ds(pl.multiple_of(row, 8), 8)
                for kind in range(6):
                    rows[kind, row] = pieces[along, kind, across].astype(f32)
    out_grad[...] = rows[0]
    query_grad[...] = rows[1].T
    for lane in range(4):
        key_grad[:, 64 * lane : 64 * lane + 64] = rows[2 + lane, :64].T
        value_grad[:, 64 * lane : 64 * lane + 64] = rows[2 + lane, 64:128].T
    gains = sum(rows[2 + lane, 128:136] for lane in range(4))
    for at, out in enumerate((attn, post, ffw, final)):
        out[...] = gains[at]
    size = query.shape[0]
    query[...] = gains[4, :size]
    key[...] = gains[4, size : 2 * size]


def finished(core, own, got):
    width = own.shape[-1]
    vmem = pl.BlockSpec(memory_space=pltpu.VMEM)
    return pl.pallas_call(
        finish_kernel,
        out_shape=[
            jax.ShapeDtypeStruct((256, width), f32),
            jax.ShapeDtypeStruct((width, 256), f32),
            jax.ShapeDtypeStruct((width, 256), f32),
            jax.ShapeDtypeStruct((width, 256), f32),
            *[jax.ShapeDtypeStruct((width,), f32)] * 4,
            *[jax.ShapeDtypeStruct((256,), f32)] * 2,
        ],
        in_specs=[pl.BlockSpec(memory_space=pltpu.SMEM), vmem, vmem],
        out_specs=[vmem] * 10,
        scratch_shapes=[pltpu.VMEM((6, 256, width), f32)],
        compiler_params=pltpu.CompilerParams(vmem_limit_bytes=SOME),
        cost_estimate=pl.CostEstimate(flops=0, bytes_accessed=10_000_000, transcendentals=0),
    )(core, own, got)


def local(
    layer_input,
    segment_ids,
    out_cotangent,
    attn_norm_gain,
    query_weight,
    key_weight,
    value_weight,
    query_gain,
    key_gain,
    output_weight,
    attn_post_gain,
    ffw_norm_gain,
    gate_weight,
    up_weight,
    down_weight,
    ffw_post_gain,
):
    tok, width = layer_input.shape
    head_dim = key_weight.shape[1]
    units = down_weight.shape[0]
    block = lax.axis_index("seq")
    lane = lax.axis_index("tensor")
    core = block % 2
    row = (block // 2) % 4
    plane = block // 8
    first = jnp.where(core == 0, row, plane)
    second = jnp.where(core == 0, plane, row)
    quarter_tok = tok // 4

    place = jnp.stack([lane, core, block]).astype(jnp.int32)
    where = jnp.stack([core, first, second]).astype(jnp.int32)
    freq = rope_base ** (-2.0 * np.arange(head_dim // 2) / head_dim)
    start = (np.arange(lax.axis_size("seq")) * tok)[:, None] * freq[None, :]
    inner = np.arange(tok)[:, None] * freq[None, :]
    tables = [jnp.asarray(f(angle), f32) for angle in (start, inner) for f in (np.cos, np.sin)]

    square = (tok, head_dim)
    normed, own_pair, k_raw, q_raw, queries, cosine, sine = call(
        prepare_kernel,
        [
            ((tok, width), bf16),
            ((2 * tok + 16, head_dim), bf16),
            (square, f32),
            (square, f32),
            (square, bf16),
            ((tok, head_dim // 2), f32),
            ((tok, head_dim // 2), f32),
        ],
        place,
        layer_input,
        attn_norm_gain,
        key_weight,
        value_weight,
        query_weight,
        key_gain,
        query_gain,
        *tables,
        segment_ids,
        scalars=1,
        flops=6 * tok * width * head_dim,
        room=MOST,
    )
    left_one = shifted(own_pair, 1)
    left_two = shifted(own_pair, 2)

    weight_half = tok // 2
    halved, _ = tied(output_weight, own_pair)
    own_weight = pick(halved.reshape(2, weight_half, width), core)
    got_weight = [send(own_weight, round_x(by)) for by in (1, 2, 3)]

    pairs = (left_two, left_one, own_pair)
    block_ref = block.astype(jnp.int32).reshape(1)
    segment = segment_ids.astype(f32)[:, None]
    context, log_total = attend(block_ref, segment, queries, pairs)

    got_context = [send(context, round_x(by)) for by in (1, 2, 3)]
    *got_context, got_weight[0], got_weight[1], got_weight[2] = tied(*got_context, *got_weight)
    other_weight = [send(part, swap_cores()) for part in got_weight]
    branch, middle, normed_two = call(
        project_kernel,
        [((tok, width), f32), ((tok, width), f32), ((tok, width), bf16)],
        place,
        layer_input,
        attn_post_gain,
        ffw_norm_gain,
        context,
        *got_context,
        output_weight,
        *got_weight,
        *other_weight,
        scalars=1,
        flops=8 * tok * tok * width,
    )
    gate = dot(gate_weight, normed_two, (0, 1))
    up_val = dot(up_weight, normed_two, (0, 1))
    active, gelu_back = jax.vjp(lambda val: jax.nn.gelu(val, approximate=True), gate)
    hidden = (active * up_val).astype(bf16)
    down_part = dot(hidden, down_weight, (0, 0)).astype(bf16)

    def halves(values):
        groups = values.reshape(8, units // 8, tok)
        groups = jnp.concatenate([groups[:, :56], groups[:, 48:]], axis=1)
        pieces = groups.reshape(4, 4, 2, 56, tok)
        return (
            lax.dynamic_index_in_dim(pieces, core, 2, keepdims=False),
            lax.dynamic_index_in_dim(pieces, 1 - core, 2, keepdims=False),
        )

    def arranged(values):
        values = jnp.where(core == 0, values.swapaxes(0, 1), values)
        by_first = [pick(values, first ^ flip) for flip in range(4)]
        groups = [
            jnp.stack([by_first[i][2 * stream : 2 * stream + 2] for i in order])
            for stream, order in ((0, (0, 3)), (0, (1, 2)), (1, (0, 1)), (1, (3, 2)))
        ]
        return jnp.stack(groups).reshape(4, 224, tok)

    hidden_own, hidden_give = halves(hidden)
    hidden_got = send(hidden_give, swap_cores())
    normed_two_got = send(normed_two, swap_cores())

    def quarters(parts):
        parts = parts.reshape(4, quarter_tok, parts.shape[-1])
        given = [pick(parts, (lane + by) % 4) for by in (1, 2, 3)]
        return [pick(parts, lane)] + [
            send(part, round_x(by)) for by, part in zip((1, 2, 3), given, strict=True)
        ]

    piece = (quarter_tok, width)
    out_own, d_branch_two, final_part = call(
        final_kernel,
        [(piece, bf16), (piece, bf16), ((1, width), f32)],
        place,
        *quarters(down_part),
        middle,
        out_cotangent,
        ffw_post_gain,
        scalars=1,
    )
    d_branch_two = gather(d_branch_two, lane, round_x).reshape(tok, width)
    d_branch_two_got = send(d_branch_two, swap_cores())

    d_hidden = dot(down_weight, d_branch_two, (1, 1))
    d_gate = gelu_back(d_hidden * up_val)[0].astype(bf16)
    d_up = (d_hidden * active).astype(bf16)
    d_normed_two = (dot(d_gate, gate_weight, (0, 1)) + dot(d_up, up_weight, (0, 1))).astype(bf16)
    d_gate_own, d_gate_give = halves(d_gate)
    d_up_own, d_up_give = halves(d_up)
    d_pair_got = send(jnp.stack([d_gate_give, d_up_give]), swap_cores())

    keep_a, give_a, keep_b, give_b = weight_parts(
        *(
            arranged(v)
            for v in (hidden_own, hidden_got, d_gate_own, d_pair_got[0], d_up_own, d_pair_got[1])
        ),
        d_branch_two,
        d_branch_two_got,
        normed_two,
        normed_two_got,
    )
    got_a = send(give_a, along_first(1))
    got_b = send(give_b, along_first(3))

    *got_normed, keep_a, keep_b = tied(*quarters(d_normed_two), keep_a, keep_b)
    d_middle, d_branch, ffw_part, post_part = call(
        between_kernel,
        [(piece, f32), (piece, bf16), ((1, width), f32), ((1, width), f32)],
        place,
        *got_normed,
        middle,
        branch,
        out_cotangent,
        ffw_norm_gain,
        attn_post_gain,
        scalars=1,
    )
    d_branch = gather(d_branch, lane, round_x).reshape(tok, width)
    d_queries, left_far, left_near, summed = attend_back(
        block_ref, segment, log_total, d_branch, output_weight, queries, pairs
    )
    got_near = shifted(left_near, -1)
    got_far = shifted(left_far, -2)
    got_near, got_far, got_a, got_b = tied(got_near, got_far, got_a, got_b)
    keep_a, give_a = added(keep_a[:336], got_a[:336]), added(keep_a[336:], got_a[336:])
    keep_b, give_b = added(keep_b[:336], got_b[:336]), added(keep_b[336:], got_b[336:])
    got_a = send(give_a, along_first(3))
    got_b = send(give_b, along_first(1))
    d_query, payload, query_part, key_part = call(
        key_kernel,
        [
            (square, bf16),
            ((tok, width + 2 * tok), bf16),
            ((1, head_dim), f32),
            ((1, head_dim), f32),
        ],
        q_raw,
        k_raw,
        d_queries,
        summed,
        got_near,
        got_far,
        cosine,
        sine,
        query_gain,
        key_gain,
        query_weight,
        key_weight,
        value_weight,
        flops=6 * tok * width * head_dim,
    )
    got_both = quarters(payload)
    (products,) = call(
        products_kernel,
        [((2 * head_dim, width), f32)],
        context,
        d_branch,
        d_query,
        normed,
        flops=4 * tok * width * head_dim,
    )
    *got_both, got_a, got_b = tied(*got_both, got_a, got_b)
    fours = jnp.stack([added(keep_a, got_a), added(keep_b, got_b)])
    fours = fours.reshape(2, 3, 2, 56, width).swapaxes(1, 2).reshape(4, 168, width)
    mine = pick(fours, second).astype(f32)
    got = [send(pick(fours, (second + by) % 4), round_second(by)) for by in (1, 2, 3)]
    input_own, keep, give = pl.pallas_call(
        entry_kernel,
        out_shape=[
            jax.ShapeDtypeStruct(piece, bf16),
            jax.ShapeDtypeStruct((3, 16, 8, width), f32),
            jax.ShapeDtypeStruct((3, 16, 8, width), bf16),
        ],
        in_specs=[pl.BlockSpec(memory_space=pltpu.SMEM)]
        + [pl.BlockSpec(memory_space=pltpu.VMEM)] * 14,
        out_specs=[pl.BlockSpec(memory_space=pltpu.VMEM)] * 3,
        scratch_shapes=[pltpu.VMEM((tok, width), f32)],
        compiler_params=pltpu.CompilerParams(vmem_limit_bytes=SOME),
        cost_estimate=pl.CostEstimate(
            flops=256 * tok * width, bytes_accessed=12_000_000, transcendentals=0
        ),
    )(
        place,
        *got_both,
        layer_input,
        d_middle,
        attn_norm_gain,
        normed,
        post_part,
        ffw_part,
        final_part,
        query_part,
        key_part,
        products,
    )
    pack_got = send(give, swap_cores())
    pack_got, *got = tied(pack_got, *got)
    mine = (mine + got[0].astype(f32) + (got[1].astype(f32) + got[2].astype(f32))).astype(bf16)
    part = (3, 4, 8, width)
    pack, *given = call(
        merge_kernel, [(part, f32)] + [(part, bf16)] * 3, where, keep, pack_got, scalars=1
    )
    given = [send(part, round_first(by)) for by, part in zip((1, 2, 3), given, strict=True)]
    for part in given:
        pack = pack + part.astype(f32)
    pack = pack.astype(bf16).reshape(96, width)
    both = lax.optimization_barrier(jnp.concatenate([mine, pack]))
    given = [send(both, round_second(by)) for by in (1, 2, 3)]
    quarter = jnp.zeros((4, *mine.shape), bf16)
    quarter = lax.dynamic_update_index_in_dim(quarter, both[:168], second, 0)
    for by, part in zip((1, 2, 3), given, strict=True):
        quarter = lax.dynamic_update_index_in_dim(quarter, part[:168], (second + 4 - by) % 4, 0)
    pack, *given = (part[168:].astype(f32) for part in (both, *given))
    pack = (pack + given[1] + (given[0] + given[2])).astype(bf16).reshape(3, 4, 8, width)
    near_a = send(quarter, along_first(1))
    near_b = send(quarter, along_first(3))
    other_own = send(quarter, swap_cores())
    given = [send(pack[2], round_x(by)) for by in (1, 2, 3)]
    *given, near_a, near_b = tied(*given, near_a, near_b)
    far_a = send(near_b[:2], along_first(1))
    far_b = send(near_a[2:], along_first(3))
    other_a = send(near_a, swap_cores())
    other_b = send(near_b, swap_cores())
    grads = placed(
        where,
        [
            (quarter, False, 0, 0),
            (near_a, False, 1, 0),
            (near_b, False, 3, 0),
            (other_own, True, 0, 0),
            (other_a, True, 1, 0),
            (other_b, True, 3, 0),
        ],
        [],
        units,
    )
    rest = jnp.zeros((4, *pack.shape[1:]), bf16)
    rest = lax.dynamic_update_index_in_dim(rest, pack[2], lane, 0)
    for by, part in zip((1, 2, 3), given, strict=True):
        rest = lax.dynamic_update_index_in_dim(rest, part, (lane + 4 - by) % 4, 0)
    pack = jnp.concatenate([pack[:2], rest])
    pack, out_own, input_own = tied(pack, out_own, input_own)
    ends = gather(jnp.stack([out_own, input_own]), lane, round_x)
    given = [send(pack, round_first(by)) for by in (1, 2, 3)]
    grads = list(grads)
    *given, far_a, far_b, grads[0] = tied(*given, far_a, far_b, grads[0])
    whole = jnp.zeros((4, *pack.shape), bf16)
    whole = lax.dynamic_update_index_in_dim(whole, pack, first, 0)
    for by, part in zip((1, 2, 3), given, strict=True):
        whole = lax.dynamic_update_index_in_dim(whole, part, (first + 4 - by) % 4, 0)
    pack_got = send(whole, swap_cores())
    out_grad, query_grad, key_grad, value_grad, *gains = finished(
        core.astype(jnp.int32).reshape(1), whole, pack_got
    )
    other_far_a = send(far_a, swap_cores())
    other_far_b = send(far_b, swap_cores())
    other_far_a, other_far_b, out_grad = tied(other_far_a, other_far_b, out_grad)
    down_grad, gate_grad, up_grad = placed(
        where,
        [
            (far_a, False, 2, 0),
            (far_b, False, 2, 2),
            (other_far_a, True, 2, 0),
            (other_far_b, True, 2, 2),
        ],
        grads,
        units,
    )
    layer_output = ends[:, 0].reshape(tok, width)
    input_grad = ends[:, 1].reshape(tok, width)
    return (
        layer_output,
        input_grad,
        gains[0],
        query_grad,
        key_grad,
        value_grad,
        gains[4],
        gains[5],
        out_grad,
        gains[1],
        gains[2],
        gate_grad.T,
        up_grad.T,
        down_grad,
        gains[3],
    )


def solution(mesh):
    rows = P("seq", None)
    return jax.shard_map(
        local,
        mesh=mesh,
        in_specs=(
            rows,
            P("seq"),
            rows,
            P(),
            P(None, "tensor"),
            P(),
            P(),
            P(),
            P(),
            P("tensor", None),
            P(),
            P(),
            P(None, "tensor"),
            P(None, "tensor"),
            P("tensor", None),
            P(),
        ),
        out_specs=(
            rows,
            rows,
            P(),
            P(None, "tensor"),
            P(),
            P(),
            P(),
            P(),
            P("tensor", None),
            P(),
            P(),
            P(None, "tensor"),
            P(None, "tensor"),
            P("tensor", None),
            P(),
        ),
        check_vma=False,
    )
```

```python
import functools

import jax
import jax.numpy as jnp
import numpy as np
from jax import lax
from jax.experimental import pallas as pl
from jax.experimental.pallas import tpu as pltpu
from jax.sharding import PartitionSpec as P

WINDOW = 512
SOME = 24 * 1024 * 1024
MOST = 60 * 1024 * 1024

eps = 1e-06
rope_base = 10000.0
f32 = jnp.float32
bf16 = jnp.bfloat16
BOTH = ("seq", "tensor")


def places():
    return [(z, y, c, x) for z in range(4) for y in range(4) for c in range(2) for x in range(4)]


def number(z, y, c, x):
    return ((z * 4 + y) * 2 + c) * 4 + x


def route(move):
    return [(number(*p), number(*move(*p))) for p in places()]


def round_x(by):
    return route(lambda z, y, c, x: (z, y, c, (x + by) % 4))


def swap_cores():
    return route(lambda z, y, c, x: (z, y, 1 - c, x))


def along_first(flip):
    return route(lambda z, y, c, x: (z, y ^ flip, c, x) if c == 0 else (z ^ flip, y, c, x))


def round_first(by):
    return route(
        lambda z, y, c, x: (z, (y + by) % 4, c, x) if c == 0 else ((z + by) % 4, y, c, x)
    )


def round_second(by):
    return route(
        lambda z, y, c, x: ((z + by) % 4, y, c, x) if c == 0 else (z, (y + by) % 4, c, x)
    )


def send(value, pairs):
    return lax.ppermute(value, BOTH, pairs)


def shifted(value, by):
    pairs = [
        (i * 4 + x, (i + by) * 4 + x) for i in range(32) if 0 <= i + by < 32 for x in range(4)
    ]
    return send(value, pairs)


def pick(parts, index):
    return lax.dynamic_index_in_dim(parts, index, 0, keepdims=False)


def dot(first, second, over):
    return lax.dot_general(
        first, second, (((over[0],), (over[1],)), ((), ())), preferred_element_type=f32
    )


def scatter_sum(parts, index, turn):
    total = pick(parts, index).astype(f32)
    for by in (1, 2, 3):
        total = total + send(pick(parts, (index + by) % 4), turn(by)).astype(f32)
    return total


def gather(part, index, turn):
    whole = jnp.zeros((4, *part.shape), part.dtype)
    whole = lax.dynamic_update_index_in_dim(whole, part, index, 0)
    for by in (1, 2, 3):
        whole = lax.dynamic_update_index_in_dim(
            whole, send(part, turn(by)), (index + 4 - by) % 4, 0
        )
    return whole


def inv_scale(values):
    return lax.rsqrt(jnp.mean(values * values, axis=-1, keepdims=True) + eps)


def norm_back(values, scale, gain, grad):
    unit = values * scale
    weighted = grad * gain
    d_values = scale * (weighted - unit * jnp.mean(weighted * unit, axis=-1, keepdims=True))
    return (d_values, jnp.sum(grad * unit, axis=0))


def rotate(values, cosine, sine):
    half = values.shape[-1] // 2
    first = values[..., :half]
    second = values[..., half:]
    return jnp.concatenate(
        [first * cosine - second * sine, second * cosine + first * sine], axis=-1
    )


def padded(values, rows):
    return jnp.pad(values, ((0, rows - values.shape[0]), (0, 0)))


def added(first, second):
    return (first.astype(f32) + second.astype(f32)).astype(bf16)


def tied(*values):
    return lax.optimization_barrier(values)


def call(kernel, outs, *arrays, scalars=0, flops=0, room=SOME, scratch=()):
    vmem = pl.BlockSpec(memory_space=pltpu.VMEM)
    outs = [jax.ShapeDtypeStruct(*o) for o in outs]
    moved = sum(v.size * v.dtype.itemsize for v in (*arrays, *outs))
    return pl.pallas_call(
        kernel,
        out_shape=outs,
        in_specs=[pl.BlockSpec(memory_space=pltpu.SMEM)] * scalars
        + [vmem] * (len(arrays) - scalars),
        out_specs=[vmem] * len(outs),
        scratch_shapes=scratch,
        compiler_params=pltpu.CompilerParams(vmem_limit_bytes=room),
        cost_estimate=pl.CostEstimate(flops=flops, bytes_accessed=moved, transcendentals=0),
    )(*arrays)


def own_rows(ref, lane, rows):
    return ref[pl.ds(pl.multiple_of(lane * rows, rows), rows)].astype(f32)


def project_kernel(
    place, x, post_gain, ffw_gain, ctx0, ctx1, ctx2, ctx3, weight, own1, own2, own3, other1, other2, other3,
    branch, middle, normed
):
    even = place[1] == 0
    half = own1.shape[0]
    total = dot(ctx0[...], weight[...], (1, 0))
    for ctx, mine, theirs in ((ctx1, own1, other1), (ctx2, own2, other2), (ctx3, own3, other3)):
        low = jnp.where(even, mine[...], theirs[...])
        high = jnp.where(even, theirs[...], mine[...])
        total += dot(ctx[:, :half], low, (1, 0)) + dot(ctx[:, half:], high, (1, 0))
    branch[...] = total
    after = x[...].astype(f32) + total * inv_scale(total) * post_gain[...]
    middle[...] = after
    normed[...] = (after * inv_scale(after) * ffw_gain[...]).astype(bf16)


def final_kernel(place, p0, p1, p2, p3, middle, cotangent, gain, out, d_branch, part):
    lane = place[0]
    branch = p0[...].astype(f32) + p1[...].astype(f32) + p2[...].astype(f32) + p3[...].astype(f32)
    rows = branch.shape[0]
    scale = inv_scale(branch)
    cot = own_rows(cotangent, lane, rows)
    out[...] = (own_rows(middle, lane, rows) + branch * scale * gain[...]).astype(bf16)
    d_values, d_gain = norm_back(branch, scale, gain[...], cot)
    d_branch[...] = d_values.astype(bf16)
    part[...] = d_gain[None]


def between_kernel(
    place, p0, p1, p2, p3, middle, branch, cotangent, ffw_gain, post_gain,
    d_middle, d_branch, ffw_part, post_part
):
    lane = place[0]
    grad = p0[...].astype(f32) + p1[...].astype(f32) + p2[...].astype(f32) + p3[...].astype(f32)
    rows = grad.shape[0]
    after = own_rows(middle, lane, rows)
    before = own_rows(branch, lane, rows)
    d_values, d_gain = norm_back(after, inv_scale(after), ffw_gain[...], grad)
    ffw_part[...] = d_gain[None]
    d_values = own_rows(cotangent, lane, rows) + d_values
    d_middle[...] = d_values
    d_values, d_gain = norm_back(before, inv_scale(before), post_gain[...], d_values)
    d_branch[...] = d_values.astype(bf16)
    post_part[...] = d_gain[None]


def key_kernel(
    q_raw, k_raw, d_queries, d_own, d_near, d_far, cosine, sine, query_gain, key_gain, query_weight, key_weight,
    value_weight, d_query, payload, query_part, key_part
):
    tok, head_dim = q_raw.shape
    width = query_weight.shape[0]
    cos, sin = cosine[...], -sine[...]
    raw = q_raw[...]
    d_raw, d_gain = norm_back(
        raw, inv_scale(raw), query_gain[...], rotate(d_queries[...] * head_dim**-0.5, cos, sin)
    )
    query_part[...] = d_gain[None]
    d_low = d_raw.astype(bf16)
    d_query[...] = d_low
    total = dot(d_low, query_weight[...], (1, 1))
    summed = d_own[...] + d_near[...].astype(f32) + d_far[...].astype(f32)
    raw = k_raw[...]
    d_raw, d_gain = norm_back(raw, inv_scale(raw), key_gain[...], rotate(summed[:tok], cos, sin))
    key_part[...] = d_gain[None]
    total += dot(d_raw.astype(bf16), key_weight[...], (1, 1))
    total += dot(summed[tok:].astype(bf16), value_weight[...], (1, 1))
    payload[:, :width] = total.astype(bf16)
    payload[:, width : width + tok] = d_raw.T.astype(bf16)
    payload[:, width + tok :] = summed[tok:].T.astype(bf16)


def products_kernel(context, d_branch, d_query, normed, out):
    half = context.shape[1]
    out[:half] = dot(context[...], d_branch[...], (0, 0))
    out[half:] = dot(d_query[...], normed[...], (0, 0))


def entry_kernel(
    place, p0, p1, p2, p3, x, d_middle, gain, normed, post_part, ffw_part, final_part, query_part, key_part,
    products, input_grad, keep, give, rest
):
    lane, core = place[0], place[1]
    both = p0[...].astype(f32) + p1[...].astype(f32) + p2[...].astype(f32) + p3[...].astype(f32)
    rows = both.shape[0]
    width = normed.shape[1]
    tok = normed.shape[0]
    full = own_rows(x, lane, rows)
    d_values, d_gain = norm_back(full, inv_scale(full), gain[...], both[:, :width])
    input_grad[...] = (d_middle[...] + d_values).astype(bf16)
    d_keys = both[:, width : width + tok].astype(bf16)
    d_values = both[:, width + tok :].astype(bf16)
    rest[:rows] = dot(d_keys, normed[...], (1, 0))
    rest[rows : 2 * rows] = dot(d_values, normed[...], (1, 0))
    heads = jnp.concatenate(
        [query_part[...], key_part[...], jnp.zeros((1, width - 2 * query_part.shape[1]), f32)], axis=1
    )
    index = lax.broadcasted_iota(jnp.int32, (8, width), 0)
    gains = jnp.zeros((8, width), f32)
    for at, part in enumerate((d_gain[None], post_part[...], ffw_part[...], final_part[...], heads)):
        gains = jnp.where(index == at, part, gains)
    rest[2 * rows : 2 * rows + 8] = gains
    rest[2 * rows + 8 :] = jnp.zeros((rest.shape[0] - 2 * rows - 8, width), f32)
    for kind in range(3):
        source = rest if kind == 2 else products
        base = 256 if kind == 1 else 0
        for chip in range(16):
            at = base + 16 * chip
            keep[kind, chip] = source[pl.ds(pl.multiple_of(at + 8 * core, 8), 8)]
            give[kind, chip] = source[pl.ds(pl.multiple_of(at + 8 - 8 * core, 8), 8)].astype(bf16)


def merge_kernel(where, keep, got, *outs):
    core, first = where[0], where[1]
    for by, out in enumerate(outs):
        along = lax.rem(first + by, 4)
        for across in range(4):
            chip = jnp.where(core == 0, 4 * across + along, 4 * along + across)
            for kind in range(3):
                total = keep[kind, chip] + got[kind, chip].astype(f32)
                out[kind, across] = total.astype(out.dtype)


def weight_kernel(
    hid_own, hid_got, gate_own, gate_got, up_own, up_got, dy_own, dy_got, xn_own, xn_got, *outs
):
    mats = (
        (hid_own, hid_got, dy_own, dy_got),
        (gate_own, gate_got, xn_own, xn_got),
        (up_own, up_got, xn_own, xn_got),
    )
    for group, out in enumerate(outs):
        for index, (left_own, left_got, right_own, right_got) in enumerate(mats):
            total = jnp.dot(left_own[group], right_own[...], preferred_element_type=f32)
            total += jnp.dot(left_got[group], right_got[...], preferred_element_type=f32)
            total = total.astype(bf16)
            out[112 * index : 112 * index + 112] = total[:112]
            out[336 + 112 * index : 448 + 112 * index] = total[112:]


def weight_parts(*arrays):
    width = arrays[-1].shape[1]
    return pl.pallas_call(
        weight_kernel,
        out_shape=[jax.ShapeDtypeStruct((672, width), bf16)] * 4,
        in_specs=[pl.BlockSpec(memory_space=pltpu.VMEM)] * len(arrays),
        out_specs=[pl.BlockSpec(memory_space=pltpu.VMEM)] * 4,
        compiler_params=pltpu.CompilerParams(vmem_limit_bytes=SOME),
        cost_estimate=pl.CostEstimate(
            flops=2 * 2688 * 512 * width, bytes_accessed=12_000_000, transcendentals=0
        ),
    )(*arrays)


def halve_kernel(keep_a, got_a, keep_b, got_b, *outs):
    for keep, got, half in ((keep_a, got_a, outs[:2]), (keep_b, got_b, outs[2:])):
        for index, out in enumerate(half):
            rows = pl.ds(336 * index, 336)
            out[...] = (keep[rows].astype(f32) + got[rows].astype(f32)).astype(bf16)


def deal_kernel(where, keep_a, got_a, keep_b, got_b, *refs):
    outs, total = refs[:-1], refs[-1]
    total[0] = keep_a[...].astype(f32) + got_a[...].astype(f32)
    total[1] = keep_b[...].astype(f32) + got_b[...].astype(f32)
    for by, out in enumerate(outs):
        across = lax.rem(where[2] + by, 4)
        for mat in range(3):
            row = pl.multiple_of(112 * mat + 56 * lax.rem(across, 2), 8)
            out[mat] = total[across // 2, pl.ds(row, 56)].astype(out.dtype)


def masks(block, segment, pairs):
    tok = segment.shape[0]
    query = lax.broadcasted_iota(jnp.int32, (tok, tok), 0)
    key = lax.broadcasted_iota(jnp.int32, (tok, tok), 1)
    same = [segment == pair[2 * tok : 2 * tok + 16].astype(f32)[:1] for pair in pairs]
    return (
        same[0] & (key > query) & (block >= 2),
        same[1] & (block >= 1),
        same[2] & (key <= query),
    )


def prepare_kernel(
    place, x, gain, key_weight, value_weight, query_weight, key_gain, query_gain, start_cos, start_sin, inner_cos,
    inner_sin, marks, xn, pair, k_raw, q_raw, queries, cosine, sine
):
    tok, head_dim = k_raw.shape
    full = x[...].astype(f32)
    low = (full * inv_scale(full) * gain[...]).astype(bf16)
    xn[...] = low
    at = pl.ds(place[2], 1)
    cos = start_cos[at] * inner_cos[...] - start_sin[at] * inner_sin[...]
    sin = start_sin[at] * inner_cos[...] + start_cos[at] * inner_sin[...]
    cosine[...] = cos
    sine[...] = sin
    raw = dot(low, key_weight[...], (1, 0))
    k_raw[...] = raw
    pair[:tok] = rotate(raw * inv_scale(raw) * key_gain[...], cos, sin).astype(bf16)
    pair[tok : 2 * tok] = dot(low, value_weight[...], (1, 0)).astype(bf16)
    pair[2 * tok :] = jnp.broadcast_to(marks[...].astype(f32)[None], (16, tok)).astype(bf16)
    raw = dot(low, query_weight[...], (1, 0))
    q_raw[...] = raw
    turned = rotate(raw * inv_scale(raw) * query_gain[...], cos, sin)
    queries[...] = (turned * head_dim**-0.5).astype(bf16)


def attend_kernel(block, segment, queries, far, near, own, context, log_total):
    pairs = (far, near, own)
    tok = queries.shape[0]
    allowed = masks(block[0], segment[...], pairs)
    scores = [
        jnp.where(ok, dot(queries[...], pair[:tok], (1, 1)), -1e30)
        for ok, pair in zip(allowed, pairs, strict=True)
    ]
    top = functools.reduce(jnp.maximum, [jnp.max(s, axis=1, keepdims=True) for s in scores])
    weights = [jnp.exp(s - top) for s in scores]
    total = sum(jnp.sum(w, axis=1, keepdims=True) for w in weights)
    context[...] = sum(
        dot((w / total).astype(bf16), pair[tok : 2 * tok], (1, 0))
        for w, pair in zip(weights, pairs, strict=True)
    ).astype(bf16)
    log_total[...] = jnp.broadcast_to(top + jnp.log(total), log_total.shape)


def attend(block, segment, queries, pairs):
    tok, head_dim = queries.shape
    vmem = pl.BlockSpec(memory_space=pltpu.VMEM)
    return pl.pallas_call(
        attend_kernel,
        out_shape=[
            jax.ShapeDtypeStruct((tok, head_dim), bf16),
            jax.ShapeDtypeStruct((tok, 128), f32),
        ],
        in_specs=[pl.BlockSpec(memory_space=pltpu.SMEM)] + [vmem] * 5,
        out_specs=[vmem] * 2,
        compiler_params=pltpu.CompilerParams(vmem_limit_bytes=SOME),
        cost_estimate=pl.CostEstimate(
            flops=12 * tok * tok * head_dim, bytes_accessed=1_500_000, transcendentals=3 * tok * tok
        ),
    )(block, segment, queries, *pairs)


def attend_back_kernel(
    block, segment, log_total, d_branch, weight, queries, far, near, own, d_queries, d_far, d_near, d_own
):
    pairs = (far, near, own)
    tok = queries.shape[0]
    d_context = dot(d_branch[...], weight[...], (1, 1)).astype(bf16)
    allowed = masks(block[0], segment[...], pairs)
    lse = log_total[:, :1]
    probs, d_probs = [], []
    for ok, pair in zip(allowed, pairs, strict=True):
        scores = jnp.where(ok, dot(queries[...], pair[:tok], (1, 1)), -1e30)
        probs.append(jnp.exp(scores - lse))
        d_probs.append(dot(d_context, pair[tok : 2 * tok], (1, 1)))
    mean = sum(
        jnp.sum(p * d, axis=1, keepdims=True) for p, d in zip(probs, d_probs, strict=True)
    )
    total = None
    for p, d, pair, out in zip(probs, d_probs, pairs, (d_far, d_near, d_own), strict=True):
        d_scores = (p * (d - mean)).astype(bf16)
        part = dot(d_scores, pair[:tok], (1, 0))
        total = part if total is None else total + part
        out[:tok] = dot(d_scores, queries[...], (0, 0)).astype(out.dtype)
        out[tok:] = dot(p.astype(bf16), d_context, (0, 0)).astype(out.dtype)
    d_queries[...] = total


def attend_back(block, segment, log_total, d_branch, weight, queries, pairs):
    tok, head_dim = queries.shape
    vmem = pl.BlockSpec(memory_space=pltpu.VMEM)
    return pl.pallas_call(
        attend_back_kernel,
        out_shape=[
            jax.ShapeDtypeStruct((tok, head_dim), f32),
            jax.ShapeDtypeStruct((2 * tok, head_dim), bf16),
            jax.ShapeDtypeStruct((2 * tok, head_dim), bf16),
            jax.ShapeDtypeStruct((2 * tok, head_dim), f32),
        ],
        in_specs=[pl.BlockSpec(memory_space=pltpu.SMEM)] + [vmem] * 8,
        out_specs=[vmem] * 4,
        compiler_params=pltpu.CompilerParams(vmem_limit_bytes=SOME),
        cost_estimate=pl.CostEstimate(
            flops=30 * tok * tok * head_dim, bytes_accessed=3_500_000, transcendentals=3 * tok * tok
        ),
    )(block, segment, log_total, d_branch, weight, queries, *pairs)


def place_kernel(where_ref, *refs, turns, held):
    n = len(turns)
    parts, outs = refs[:n], refs[n + held : n + held + 3]
    stage, sems, tail_sems = refs[-3:]
    slots = stage.shape[0]
    core, first, second = where_ref[0], where_ref[1], where_ref[2]
    chunks = [
        (ref, i, base + i, other, flip)
        for ref, (other, flip, base) in zip(parts, turns, strict=True)
        for i in range(ref.shape[0])
    ]

    def place(index):
        _, _, across, other, flip = chunks[index]
        which = 1 - core if other else core
        along = (second if other else first) ^ flip
        y = jnp.where(which == 0, along, across)
        z = jnp.where(which == 0, across, along)
        odd = lax.rem(y, 2)
        row = 216 * (2 * z + y // 2) + 104 * odd + 48 * which + 8 * which * odd
        return pl.multiple_of(row, 8), (which == 1) | (odd == 1)

    def copies(index):
        slot = index % slots
        row, whole = place(index)
        for mat, out in enumerate(outs):
            yield (
                pltpu.make_async_copy(
                    stage.at[slot, mat, pl.ds(0, 48)],
                    out.at[pl.ds(row, 48)],
                    sems.at[slot, mat],
                ),
                pltpu.make_async_copy(
                    stage.at[slot, mat, pl.ds(48, 8)],
                    out.at[pl.ds(pl.multiple_of(row + 48, 8), 8)],
                    tail_sems.at[slot, mat],
                ),
                whole,
            )

    def finish(index):
        for most, tail, whole in copies(index):
            most.wait()
            pl.when(whole)(tail.wait)

    for index, (ref, i, *_) in enumerate(chunks):
        if index >= slots:
            finish(index - slots)
        stage[index % slots] = ref[i].astype(f32)
        for most, tail, whole in copies(index):
            most.start()
            pl.when(whole)(tail.start)
    for index in range(max(0, len(chunks) - slots), len(chunks)):
        finish(index)


def placed(where, parts, outs, units):
    arrays = [p[0].reshape(-1, 3, 56, p[0].shape[-1]) for p in parts]
    width = arrays[0].shape[-1]
    slots = 4
    return pl.pallas_call(
        functools.partial(
            place_kernel, turns=tuple(p[1:] for p in parts), held=len(outs)
        ),
        out_shape=[jax.ShapeDtypeStruct((units, width), f32)] * 3,
        in_specs=[pl.BlockSpec(memory_space=pltpu.SMEM)]
        + [pl.BlockSpec(memory_space=pltpu.VMEM)] * len(arrays)
        + [pl.BlockSpec(memory_space=pl.ANY)] * len(outs),
        out_specs=[pl.BlockSpec(memory_space=pl.ANY)] * 3,
        scratch_shapes=[
            pltpu.VMEM((slots, 3, 56, width), f32),
            pltpu.SemaphoreType.DMA((slots, 3)),
            pltpu.SemaphoreType.DMA((slots, 3)),
        ],
        input_output_aliases={1 + len(arrays) + i: i for i in range(len(outs))},
        compiler_params=pltpu.CompilerParams(vmem_limit_bytes=SOME),
        cost_estimate=pl.CostEstimate(
            flops=0, bytes_accessed=sum(p.size for p in arrays) * 6, transcendentals=0
        ),
    )(where, *arrays, *outs)


def finish_kernel(
    core_ref, own, got, out_grad, query_grad, key_grad, value_grad, attn, post, ffw, final, query, key, rows
):
    core = core_ref[0]
    for pieces, other in ((own, 0), (got, 1)):
        even = core == other
        for along in range(4):
            for across in range(4):
                row = jnp.where(even, 8 * across + 2 * along, 8 * along + 2 * across + 1) * 8
                row = pl.ds(pl.multiple_of(row, 8), 8)
                for kind in range(6):
                    rows[kind, row] = pieces[along, kind, across].astype(f32)
    out_grad[...] = rows[0]
    query_grad[...] = rows[1].T
    for lane in range(4):
        key_grad[:, 64 * lane : 64 * lane + 64] = rows[2 + lane, :64].T
        value_grad[:, 64 * lane : 64 * lane + 64] = rows[2 + lane, 64:128].T
    gains = sum(rows[2 + lane, 128:136] for lane in range(4))
    for at, out in enumerate((attn, post, ffw, final)):
        out[...] = gains[at]
    size = query.shape[0]
    query[...] = gains[4, :size]
    key[...] = gains[4, size : 2 * size]


def finished(core, own, got):
    width = own.shape[-1]
    vmem = pl.BlockSpec(memory_space=pltpu.VMEM)
    return pl.pallas_call(
        finish_kernel,
        out_shape=[
            jax.ShapeDtypeStruct((256, width), f32),
            jax.ShapeDtypeStruct((width, 256), f32),
            jax.ShapeDtypeStruct((width, 256), f32),
            jax.ShapeDtypeStruct((width, 256), f32),
            *[jax.ShapeDtypeStruct((width,), f32)] * 4,
            *[jax.ShapeDtypeStruct((256,), f32)] * 2,
        ],
        in_specs=[pl.BlockSpec(memory_space=pltpu.SMEM), vmem, vmem],
        out_specs=[vmem] * 10,
        scratch_shapes=[pltpu.VMEM((6, 256, width), f32)],
        compiler_params=pltpu.CompilerParams(vmem_limit_bytes=SOME),
        cost_estimate=pl.CostEstimate(flops=0, bytes_accessed=10_000_000, transcendentals=0),
    )(core, own, got)


def local(
    layer_input,
    segment_ids,
    out_cotangent,
    attn_norm_gain,
    query_weight,
    key_weight,
    value_weight,
    query_gain,
    key_gain,
    output_weight,
    attn_post_gain,
    ffw_norm_gain,
    gate_weight,
    up_weight,
    down_weight,
    ffw_post_gain,
):
    tok, width = layer_input.shape
    head_dim = key_weight.shape[1]
    units = down_weight.shape[0]
    block = lax.axis_index("seq")
    lane = lax.axis_index("tensor")
    core = block % 2
    row = (block // 2) % 4
    plane = block // 8
    first = jnp.where(core == 0, row, plane)
    second = jnp.where(core == 0, plane, row)
    quarter_tok = tok // 4

    place = jnp.stack([lane, core, block]).astype(jnp.int32)
    where = jnp.stack([core, first, second]).astype(jnp.int32)
    freq = rope_base ** (-2.0 * np.arange(head_dim // 2) / head_dim)
    start = (np.arange(lax.axis_size("seq")) * tok)[:, None] * freq[None, :]
    inner = np.arange(tok)[:, None] * freq[None, :]
    tables = [jnp.asarray(f(angle), f32) for angle in (start, inner) for f in (np.cos, np.sin)]

    square = (tok, head_dim)
    normed, own_pair, k_raw, q_raw, queries, cosine, sine = call(
        prepare_kernel,
        [
            ((tok, width), bf16),
            ((2 * tok + 16, head_dim), bf16),
            (square, f32),
            (square, f32),
            (square, bf16),
            ((tok, head_dim // 2), f32),
            ((tok, head_dim // 2), f32),
        ],
        place,
        layer_input,
        attn_norm_gain,
        key_weight,
        value_weight,
        query_weight,
        key_gain,
        query_gain,
        *tables,
        segment_ids,
        scalars=1,
        flops=6 * tok * width * head_dim,
        room=MOST,
    )
    left_one = shifted(own_pair, 1)
    left_two = shifted(own_pair, 2)

    weight_half = tok // 2
    halved, _ = tied(output_weight, own_pair)
    own_weight = pick(halved.reshape(2, weight_half, width), core)
    got_weight = [send(own_weight, round_x(by)) for by in (1, 2, 3)]

    pairs = (left_two, left_one, own_pair)
    block_ref = block.astype(jnp.int32).reshape(1)
    segment = segment_ids.astype(f32)[:, None]
    context, log_total = attend(block_ref, segment, queries, pairs)

    got_context = [send(context, round_x(by)) for by in (1, 2, 3)]
    *got_context, got_weight[0], got_weight[1], got_weight[2] = tied(*got_context, *got_weight)
    other_weight = [send(part, swap_cores()) for part in got_weight]
    branch, middle, normed_two = call(
        project_kernel,
        [((tok, width), f32), ((tok, width), f32), ((tok, width), bf16)],
        place,
        layer_input,
        attn_post_gain,
        ffw_norm_gain,
        context,
        *got_context,
        output_weight,
        *got_weight,
        *other_weight,
        scalars=1,
        flops=8 * tok * tok * width,
    )
    gate = dot(gate_weight, normed_two, (0, 1))
    up_val = dot(up_weight, normed_two, (0, 1))
    active, gelu_back = jax.vjp(lambda val: jax.nn.gelu(val, approximate=True), gate)
    hidden = (active * up_val).astype(bf16)
    down_part = dot(hidden, down_weight, (0, 0)).astype(bf16)

    def halves(values):
        groups = values.reshape(8, units // 8, tok)
        groups = jnp.concatenate([groups[:, :56], groups[:, 48:]], axis=1)
        pieces = groups.reshape(4, 4, 2, 56, tok)
        return (
            lax.dynamic_index_in_dim(pieces, core, 2, keepdims=False),
            lax.dynamic_index_in_dim(pieces, 1 - core, 2, keepdims=False),
        )

    def arranged(values):
        values = jnp.where(core == 0, values.swapaxes(0, 1), values)
        by_first = [pick(values, first ^ flip) for flip in range(4)]
        groups = [
            jnp.stack([by_first[i][2 * stream : 2 * stream + 2] for i in order])
            for stream, order in ((0, (0, 3)), (0, (1, 2)), (1, (0, 1)), (1, (3, 2)))
        ]
        return jnp.stack(groups).reshape(4, 224, tok)

    hidden_own, hidden_give = halves(hidden)
    hidden_got = send(hidden_give, swap_cores())
    normed_two_got = send(normed_two, swap_cores())

    def quarters(parts):
        parts = parts.reshape(4, quarter_tok, parts.shape[-1])
        given = [pick(parts, (lane + by) % 4) for by in (1, 2, 3)]
        return [pick(parts, lane)] + [
            send(part, round_x(by)) for by, part in zip((1, 2, 3), given, strict=True)
        ]

    piece = (quarter_tok, width)
    out_own, d_branch_two, final_part = call(
        final_kernel,
        [(piece, bf16), (piece, bf16), ((1, width), f32)],
        place,
        *quarters(down_part),
        middle,
        out_cotangent,
        ffw_post_gain,
        scalars=1,
    )
    d_branch_two = gather(d_branch_two, lane, round_x).reshape(tok, width)
    d_branch_two_got = send(d_branch_two, swap_cores())

    d_hidden = dot(down_weight, d_branch_two, (1, 1))
    d_gate = gelu_back(d_hidden * up_val)[0].astype(bf16)
    d_up = (d_hidden * active).astype(bf16)
    d_normed_two = (dot(d_gate, gate_weight, (0, 1)) + dot(d_up, up_weight, (0, 1))).astype(bf16)
    d_gate_own, d_gate_give = halves(d_gate)
    d_up_own, d_up_give = halves(d_up)
    d_pair_got = send(jnp.stack([d_gate_give, d_up_give]), swap_cores())

    keep_a, give_a, keep_b, give_b = weight_parts(
        *(
            arranged(v)
            for v in (hidden_own, hidden_got, d_gate_own, d_pair_got[0], d_up_own, d_pair_got[1])
        ),
        d_branch_two,
        d_branch_two_got,
        normed_two,
        normed_two_got,
    )
    got_a = send(give_a, along_first(1))
    got_b = send(give_b, along_first(3))

    *got_normed, keep_a, keep_b = tied(*quarters(d_normed_two), keep_a, keep_b)
    d_middle, d_branch, ffw_part, post_part = call(
        between_kernel,
        [(piece, f32), (piece, bf16), ((1, width), f32), ((1, width), f32)],
        place,
        *got_normed,
        middle,
        branch,
        out_cotangent,
        ffw_norm_gain,
        attn_post_gain,
        scalars=1,
    )
    d_branch = gather(d_branch, lane, round_x).reshape(tok, width)
    d_queries, left_far, left_near, summed = attend_back(
        block_ref, segment, log_total, d_branch, output_weight, queries, pairs
    )
    got_near = shifted(left_near, -1)
    got_far = shifted(left_far, -2)
    got_near, got_far, got_a, got_b = tied(got_near, got_far, got_a, got_b)
    keep_a, give_a, keep_b, give_b = call(
        halve_kernel, [((336, width), bf16)] * 4, keep_a, got_a, keep_b, got_b
    )
    got_a = send(give_a, along_first(3))
    got_b = send(give_b, along_first(1))
    d_query, payload, query_part, key_part = call(
        key_kernel,
        [
            (square, bf16),
            ((tok, width + 2 * tok), bf16),
            ((1, head_dim), f32),
            ((1, head_dim), f32),
        ],
        q_raw,
        k_raw,
        d_queries,
        summed,
        got_near,
        got_far,
        cosine,
        sine,
        query_gain,
        key_gain,
        query_weight,
        key_weight,
        value_weight,
        flops=6 * tok * width * head_dim,
    )
    got_both = quarters(payload)
    (products,) = call(
        products_kernel,
        [((2 * head_dim, width), f32)],
        context,
        d_branch,
        d_query,
        normed,
        flops=4 * tok * width * head_dim,
    )
    *got_both, got_a, got_b = tied(*got_both, got_a, got_b)
    chunk = (3, 56, width)
    mine, *given = call(
        deal_kernel,
        [(chunk, f32)] + [(chunk, bf16)] * 3,
        where,
        keep_a,
        got_a,
        keep_b,
        got_b,
        scalars=1,
        scratch=[pltpu.VMEM((2, 336, width), f32)],
    )
    got = [send(part, round_second(by)) for by, part in zip((1, 2, 3), given, strict=True)]
    input_own, keep, give = pl.pallas_call(
        entry_kernel,
        out_shape=[
            jax.ShapeDtypeStruct(piece, bf16),
            jax.ShapeDtypeStruct((3, 16, 8, width), f32),
            jax.ShapeDtypeStruct((3, 16, 8, width), bf16),
        ],
        in_specs=[pl.BlockSpec(memory_space=pltpu.SMEM)]
        + [pl.BlockSpec(memory_space=pltpu.VMEM)] * 14,
        out_specs=[pl.BlockSpec(memory_space=pltpu.VMEM)] * 3,
        scratch_shapes=[pltpu.VMEM((tok, width), f32)],
        compiler_params=pltpu.CompilerParams(vmem_limit_bytes=SOME),
        cost_estimate=pl.CostEstimate(
            flops=256 * tok * width, bytes_accessed=12_000_000, transcendentals=0
        ),
    )(
        place,
        *got_both,
        layer_input,
        d_middle,
        attn_norm_gain,
        normed,
        post_part,
        ffw_part,
        final_part,
        query_part,
        key_part,
        products,
    )
    pack_got = send(give, swap_cores())
    part = (3, 4, 8, width)
    pack, *given = call(
        merge_kernel, [(part, f32)] + [(part, bf16)] * 3, where, keep, pack_got, scalars=1
    )
    given = [send(part, round_first(by)) for by, part in zip((1, 2, 3), given, strict=True)]
    *given, got[0], got[1], got[2] = tied(*given, *got)
    mine = mine + got[0].astype(f32) + (got[1].astype(f32) + got[2].astype(f32))
    mine = mine.astype(bf16).reshape(168, width)
    for part in given:
        pack = pack + part.astype(f32)
    pack = pack.astype(bf16).reshape(96, width)
    both = lax.optimization_barrier(jnp.concatenate([mine, pack]))
    given = [send(both, round_second(by)) for by in (1, 2, 3)]
    quarter = jnp.zeros((4, *mine.shape), bf16)
    quarter = lax.dynamic_update_index_in_dim(quarter, both[:168], second, 0)
    for by, part in zip((1, 2, 3), given, strict=True):
        quarter = lax.dynamic_update_index_in_dim(quarter, part[:168], (second + 4 - by) % 4, 0)
    pack, *given = (part[168:].astype(f32) for part in (both, *given))
    pack = (pack + given[1] + (given[0] + given[2])).astype(bf16).reshape(3, 4, 8, width)
    near_a = send(quarter, along_first(1))
    near_b = send(quarter, along_first(3))
    other_own = send(quarter, swap_cores())
    ends = jnp.concatenate([pack[2].reshape(32, width), out_own, input_own])
    given = [send(ends, round_x(by)) for by in (1, 2, 3)]
    *given, near_a, near_b = tied(*given, near_a, near_b)
    far_a = send(near_b[:2], along_first(1))
    far_b = send(near_a[2:], along_first(3))
    other_a = send(near_a, swap_cores())
    other_b = send(near_b, swap_cores())
    grads = placed(
        where,
        [
            (quarter, False, 0, 0),
            (near_a, False, 1, 0),
            (near_b, False, 3, 0),
            (other_own, True, 0, 0),
            (other_a, True, 1, 0),
            (other_b, True, 3, 0),
        ],
        [],
        units,
    )
    whole = jnp.zeros((4, *ends.shape), bf16)
    whole = lax.dynamic_update_index_in_dim(whole, ends, lane, 0)
    for by, part in zip((1, 2, 3), given, strict=True):
        whole = lax.dynamic_update_index_in_dim(whole, part, (lane + 4 - by) % 4, 0)
    layer_output = whole[:, 32:96].reshape(tok, width)
    input_grad = whole[:, 96:].reshape(tok, width)
    pack = jnp.concatenate([pack[:2], whole[:, :32].reshape(4, 4, 8, width)])
    given = [send(pack, round_first(by)) for by in (1, 2, 3)]
    grads = list(grads)
    *given, far_a, far_b, grads[0] = tied(*given, far_a, far_b, grads[0])
    whole = jnp.zeros((4, *pack.shape), bf16)
    whole = lax.dynamic_update_index_in_dim(whole, pack, first, 0)
    for by, part in zip((1, 2, 3), given, strict=True):
        whole = lax.dynamic_update_index_in_dim(whole, part, (first + 4 - by) % 4, 0)
    pack_got = send(whole, swap_cores())
    out_grad, query_grad, key_grad, value_grad, *gains = finished(
        core.astype(jnp.int32).reshape(1), whole, pack_got
    )
    other_far_a = send(far_a, swap_cores())
    other_far_b = send(far_b, swap_cores())
    other_far_a, other_far_b, out_grad = tied(other_far_a, other_far_b, out_grad)
    down_grad, gate_grad, up_grad = placed(
        where,
        [
            (far_a, False, 2, 0),
            (far_b, False, 2, 2),
            (other_far_a, True, 2, 0),
            (other_far_b, True, 2, 2),
        ],
        grads,
        units,
    )
    return (
        layer_output,
        input_grad,
        gains[0],
        query_grad,
        key_grad,
        value_grad,
        gains[4],
        gains[5],
        out_grad,
        gains[1],
        gains[2],
        gate_grad.T,
        up_grad.T,
        down_grad,
        gains[3],
    )


def solution(mesh):
    rows = P("seq", None)
    return jax.shard_map(
        local,
        mesh=mesh,
        in_specs=(
            rows,
            P("seq"),
            rows,
            P(),
            P(None, "tensor"),
            P(),
            P(),
            P(),
            P(),
            P("tensor", None),
            P(),
            P(),
            P(None, "tensor"),
            P(None, "tensor"),
            P("tensor", None),
            P(),
        ),
        out_specs=(
            rows,
            rows,
            P(),
            P(None, "tensor"),
            P(),
            P(),
            P(),
            P(),
            P("tensor", None),
            P(),
            P(),
            P(None, "tensor"),
            P(None, "tensor"),
            P("tensor", None),
            P(),
        ),
        check_vma=False,
    )
```

```python
import functools

import jax
import jax.numpy as jnp
import numpy as np
from jax import lax
from jax.experimental import pallas as pl
from jax.experimental.pallas import tpu as pltpu
from jax.sharding import PartitionSpec as P

WINDOW = 512
SOME = 24 * 1024 * 1024
MOST = 60 * 1024 * 1024

eps = 1e-06
rope_base = 10000.0
f32 = jnp.float32
bf16 = jnp.bfloat16
BOTH = ("seq", "tensor")


def places():
    return [(z, y, c, x) for z in range(4) for y in range(4) for c in range(2) for x in range(4)]


def number(z, y, c, x):
    return ((z * 4 + y) * 2 + c) * 4 + x


def route(move):
    return [(number(*p), number(*move(*p))) for p in places()]


def round_x(by):
    return route(lambda z, y, c, x: (z, y, c, (x + by) % 4))


def swap_cores():
    return route(lambda z, y, c, x: (z, y, 1 - c, x))


def along_first(flip):
    return route(lambda z, y, c, x: (z, y ^ flip, c, x) if c == 0 else (z ^ flip, y, c, x))


def round_first(by):
    return route(
        lambda z, y, c, x: (z, (y + by) % 4, c, x) if c == 0 else ((z + by) % 4, y, c, x)
    )


def round_second(by):
    return route(
        lambda z, y, c, x: ((z + by) % 4, y, c, x) if c == 0 else (z, (y + by) % 4, c, x)
    )


def send(value, pairs):
    return lax.ppermute(value, BOTH, pairs)


def shifted(value, by):
    pairs = [
        (i * 4 + x, (i + by) * 4 + x) for i in range(32) if 0 <= i + by < 32 for x in range(4)
    ]
    return send(value, pairs)


def pick(parts, index, axis=0):
    return lax.dynamic_index_in_dim(
        parts, index, axis, keepdims=False, allow_negative_indices=False
    )


def put(parts, part, index):
    return lax.dynamic_update_index_in_dim(parts, part, index, 0, allow_negative_indices=False)


def dot(first, second, over):
    return lax.dot_general(
        first, second, (((over[0],), (over[1],)), ((), ())), preferred_element_type=f32
    )


def joined(own, got, after):
    whole = put(jnp.zeros((4, *own.shape), own.dtype), own, after[0])
    for by, part in zip((1, 2, 3), got, strict=True):
        whole = put(whole, part, after[4 - by])
    return whole


def gather(part, after, turn):
    return joined(part, [send(part, turn(by)) for by in (1, 2, 3)], after)


def inv_scale(values):
    return lax.rsqrt(jnp.mean(values * values, axis=-1, keepdims=True) + eps)


def norm_back(values, scale, gain, grad):
    unit = values * scale
    weighted = grad * gain
    d_values = scale * (weighted - unit * jnp.mean(weighted * unit, axis=-1, keepdims=True))
    return (d_values, jnp.sum(grad * unit, axis=0))


def rotate(values, cosine, sine):
    half = values.shape[-1] // 2
    first = values[..., :half]
    second = values[..., half:]
    return jnp.concatenate(
        [first * cosine - second * sine, second * cosine + first * sine], axis=-1
    )


def padded(values, rows):
    return jnp.pad(values, ((0, rows - values.shape[0]), (0, 0)))


def added(first, second):
    return (first.astype(f32) + second.astype(f32)).astype(bf16)


def tied(*values):
    return lax.optimization_barrier(values)


def call(kernel, outs, *arrays, scalars=0, flops=0, room=SOME, scratch=()):
    vmem = pl.BlockSpec(memory_space=pltpu.VMEM)
    outs = [jax.ShapeDtypeStruct(*o) for o in outs]
    moved = sum(v.size * v.dtype.itemsize for v in (*arrays, *outs))
    return pl.pallas_call(
        kernel,
        out_shape=outs,
        in_specs=[pl.BlockSpec(memory_space=pltpu.SMEM)] * scalars
        + [vmem] * (len(arrays) - scalars),
        out_specs=[vmem] * len(outs),
        scratch_shapes=scratch,
        compiler_params=pltpu.CompilerParams(vmem_limit_bytes=room),
        cost_estimate=pl.CostEstimate(flops=flops, bytes_accessed=moved, transcendentals=0),
    )(*arrays)


def own_rows(ref, lane, rows):
    return ref[pl.ds(pl.multiple_of(lane * rows, rows), rows)].astype(f32)


def project_kernel(
    place, x, post_gain, ffw_gain, ctx0, ctx1, ctx2, ctx3, weight, own1, own2, own3, other1, other2, other3,
    branch, middle, normed
):
    even = place[1] == 0
    half = own1.shape[0]
    total = dot(ctx0[...], weight[...], (1, 0))
    for ctx, mine, theirs in ((ctx1, own1, other1), (ctx2, own2, other2), (ctx3, own3, other3)):
        low = jnp.where(even, mine[...], theirs[...])
        high = jnp.where(even, theirs[...], mine[...])
        total += dot(ctx[:, :half], low, (1, 0)) + dot(ctx[:, half:], high, (1, 0))
    branch[...] = total
    after = x[...].astype(f32) + total * inv_scale(total) * post_gain[...]
    middle[...] = after
    normed[...] = (after * inv_scale(after) * ffw_gain[...]).astype(bf16)


def final_kernel(place, p0, p1, p2, p3, middle, cotangent, gain, out, d_branch, part):
    lane = place[0]
    branch = p0[...].astype(f32) + p1[...].astype(f32) + p2[...].astype(f32) + p3[...].astype(f32)
    rows = branch.shape[0]
    scale = inv_scale(branch)
    cot = own_rows(cotangent, lane, rows)
    out[...] = (own_rows(middle, lane, rows) + branch * scale * gain[...]).astype(bf16)
    d_values, d_gain = norm_back(branch, scale, gain[...], cot)
    d_branch[...] = d_values.astype(bf16)
    part[...] = d_gain[None]


def between_kernel(
    place, p0, p1, p2, p3, middle, branch, cotangent, ffw_gain, post_gain,
    d_middle, d_branch, ffw_part, post_part
):
    lane = place[0]
    grad = p0[...].astype(f32) + p1[...].astype(f32) + p2[...].astype(f32) + p3[...].astype(f32)
    rows = grad.shape[0]
    after = own_rows(middle, lane, rows)
    before = own_rows(branch, lane, rows)
    d_values, d_gain = norm_back(after, inv_scale(after), ffw_gain[...], grad)
    ffw_part[...] = d_gain[None]
    d_values = own_rows(cotangent, lane, rows) + d_values
    d_middle[...] = d_values
    d_values, d_gain = norm_back(before, inv_scale(before), post_gain[...], d_values)
    d_branch[...] = d_values.astype(bf16)
    post_part[...] = d_gain[None]


def key_kernel(
    q_raw, k_raw, d_queries, d_own, d_near, d_far, cosine, sine, query_gain, key_gain, query_weight, key_weight,
    value_weight, d_query, payload, query_part, key_part
):
    tok, head_dim = q_raw.shape
    width = query_weight.shape[0]
    cos, sin = cosine[...], -sine[...]
    raw = q_raw[...]
    d_raw, d_gain = norm_back(
        raw, inv_scale(raw), query_gain[...], rotate(d_queries[...] * head_dim**-0.5, cos, sin)
    )
    query_part[...] = d_gain[None]
    d_low = d_raw.astype(bf16)
    d_query[...] = d_low
    total = dot(d_low, query_weight[...], (1, 1))
    summed = d_own[...] + d_near[...].astype(f32) + d_far[...].astype(f32)
    raw = k_raw[...]
    d_raw, d_gain = norm_back(raw, inv_scale(raw), key_gain[...], rotate(summed[:tok], cos, sin))
    key_part[...] = d_gain[None]
    total += dot(d_raw.astype(bf16), key_weight[...], (1, 1))
    total += dot(summed[tok:].astype(bf16), value_weight[...], (1, 1))
    payload[:, :width] = total.astype(bf16)
    payload[:, width : width + tok] = d_raw.T.astype(bf16)
    payload[:, width + tok :] = summed[tok:].T.astype(bf16)


def products_kernel(context, d_branch, d_query, normed, out):
    half = context.shape[1]
    out[:half] = dot(context[...], d_branch[...], (0, 0))
    out[half:] = dot(d_query[...], normed[...], (0, 0))


def entry_kernel(
    place, p0, p1, p2, p3, x, d_middle, gain, normed, post_part, ffw_part, final_part, query_part, key_part,
    products, input_grad, keep, give, rest
):
    lane, core = place[0], place[1]
    both = p0[...].astype(f32) + p1[...].astype(f32) + p2[...].astype(f32) + p3[...].astype(f32)
    rows = both.shape[0]
    width = normed.shape[1]
    tok = normed.shape[0]
    full = own_rows(x, lane, rows)
    d_values, d_gain = norm_back(full, inv_scale(full), gain[...], both[:, :width])
    input_grad[...] = (d_middle[...] + d_values).astype(bf16)
    d_keys = both[:, width : width + tok].astype(bf16)
    d_values = both[:, width + tok :].astype(bf16)
    rest[:rows] = dot(d_keys, normed[...], (1, 0))
    rest[rows : 2 * rows] = dot(d_values, normed[...], (1, 0))
    heads = jnp.concatenate(
        [query_part[...], key_part[...], jnp.zeros((1, width - 2 * query_part.shape[1]), f32)], axis=1
    )
    index = lax.broadcasted_iota(jnp.int32, (8, width), 0)
    gains = jnp.zeros((8, width), f32)
    for at, part in enumerate((d_gain[None], post_part[...], ffw_part[...], final_part[...], heads)):
        gains = jnp.where(index == at, part, gains)
    rest[2 * rows : 2 * rows + 8] = gains
    rest[2 * rows + 8 :] = jnp.zeros((rest.shape[0] - 2 * rows - 8, width), f32)
    for kind in range(3):
        source = rest if kind == 2 else products
        base = 256 if kind == 1 else 0
        for chip in range(16):
            at = base + 16 * chip
            keep[kind, chip] = source[pl.ds(pl.multiple_of(at + 8 * core, 8), 8)]
            give[kind, chip] = source[pl.ds(pl.multiple_of(at + 8 - 8 * core, 8), 8)].astype(bf16)


def merge_kernel(where, keep, got, *outs):
    core, first = where[0], where[1]
    for by, out in enumerate(outs):
        along = lax.rem(first + by, 4)
        for across in range(4):
            chip = jnp.where(core == 0, 4 * across + along, 4 * along + across)
            for kind in range(3):
                total = keep[kind, chip] + got[kind, chip].astype(f32)
                out[kind, across] = total.astype(out.dtype)


def weight_kernel(
    hid_own, hid_got, gate_own, gate_got, up_own, up_got, dy_own, dy_got, xn_own, xn_got, *outs
):
    mats = (
        (hid_own, hid_got, dy_own, dy_got),
        (gate_own, gate_got, xn_own, xn_got),
        (up_own, up_got, xn_own, xn_got),
    )
    for group, out in enumerate(outs):
        for index, (left_own, left_got, right_own, right_got) in enumerate(mats):
            total = jnp.dot(left_own[group], right_own[...], preferred_element_type=f32)
            total += jnp.dot(left_got[group], right_got[...], preferred_element_type=f32)
            total = total.astype(bf16)
            out[112 * index : 112 * index + 112] = total[:112]
            out[336 + 112 * index : 448 + 112 * index] = total[112:]


def weight_parts(*arrays):
    width = arrays[-1].shape[1]
    return pl.pallas_call(
        weight_kernel,
        out_shape=[jax.ShapeDtypeStruct((672, width), bf16)] * 4,
        in_specs=[pl.BlockSpec(memory_space=pltpu.VMEM)] * len(arrays),
        out_specs=[pl.BlockSpec(memory_space=pltpu.VMEM)] * 4,
        compiler_params=pltpu.CompilerParams(vmem_limit_bytes=SOME),
        cost_estimate=pl.CostEstimate(
            flops=2 * 2688 * 512 * width, bytes_accessed=12_000_000, transcendentals=0
        ),
    )(*arrays)


def halve_kernel(keep_a, got_a, keep_b, got_b, *outs):
    for keep, got, half in ((keep_a, got_a, outs[:2]), (keep_b, got_b, outs[2:])):
        for index, out in enumerate(half):
            rows = pl.ds(336 * index, 336)
            out[...] = (keep[rows].astype(f32) + got[rows].astype(f32)).astype(bf16)


def deal_kernel(where, keep_a, got_a, keep_b, got_b, *refs):
    outs, total = refs[:-1], refs[-1]
    total[0] = keep_a[...].astype(f32) + got_a[...].astype(f32)
    total[1] = keep_b[...].astype(f32) + got_b[...].astype(f32)
    for by, out in enumerate(outs):
        across = lax.rem(where[2] + by, 4)
        for mat in range(3):
            row = pl.multiple_of(112 * mat + 56 * lax.rem(across, 2), 8)
            out[mat] = total[across // 2, pl.ds(row, 56)].astype(out.dtype)


def masks(block, segment, pairs):
    tok = segment.shape[0]
    query = lax.broadcasted_iota(jnp.int32, (tok, tok), 0)
    key = lax.broadcasted_iota(jnp.int32, (tok, tok), 1)
    same = [segment == pair[2 * tok : 2 * tok + 16].astype(f32)[:1] for pair in pairs]
    return (
        same[0] & (key > query) & (block >= 2),
        same[1] & (block >= 1),
        same[2] & (key <= query),
    )


def prepare_kernel(
    place, x, gain, key_weight, value_weight, query_weight, key_gain, query_gain, start_cos, start_sin, inner_cos,
    inner_sin, marks, xn, pair, k_raw, q_raw, queries, cosine, sine
):
    tok, head_dim = k_raw.shape
    full = x[...].astype(f32)
    low = (full * inv_scale(full) * gain[...]).astype(bf16)
    xn[...] = low
    at = pl.ds(place[2], 1)
    cos = start_cos[at] * inner_cos[...] - start_sin[at] * inner_sin[...]
    sin = start_sin[at] * inner_cos[...] + start_cos[at] * inner_sin[...]
    cosine[...] = cos
    sine[...] = sin
    raw = dot(low, key_weight[...], (1, 0))
    k_raw[...] = raw
    pair[:tok] = rotate(raw * inv_scale(raw) * key_gain[...], cos, sin).astype(bf16)
    pair[tok : 2 * tok] = dot(low, value_weight[...], (1, 0)).astype(bf16)
    pair[2 * tok :] = jnp.broadcast_to(marks[...].astype(f32)[None], (16, tok)).astype(bf16)
    raw = dot(low, query_weight[...], (1, 0))
    q_raw[...] = raw
    turned = rotate(raw * inv_scale(raw) * query_gain[...], cos, sin)
    queries[...] = (turned * head_dim**-0.5).astype(bf16)


def attend_kernel(block, segment, queries, far, near, own, context, log_total):
    pairs = (far, near, own)
    tok = queries.shape[0]
    allowed = masks(block[0], segment[...], pairs)
    scores = [
        jnp.where(ok, dot(queries[...], pair[:tok], (1, 1)), -1e30)
        for ok, pair in zip(allowed, pairs, strict=True)
    ]
    top = functools.reduce(jnp.maximum, [jnp.max(s, axis=1, keepdims=True) for s in scores])
    weights = [jnp.exp(s - top) for s in scores]
    total = sum(jnp.sum(w, axis=1, keepdims=True) for w in weights)
    context[...] = sum(
        dot((w / total).astype(bf16), pair[tok : 2 * tok], (1, 0))
        for w, pair in zip(weights, pairs, strict=True)
    ).astype(bf16)
    log_total[...] = jnp.broadcast_to(top + jnp.log(total), log_total.shape)


def attend(block, segment, queries, pairs):
    tok, head_dim = queries.shape
    vmem = pl.BlockSpec(memory_space=pltpu.VMEM)
    return pl.pallas_call(
        attend_kernel,
        out_shape=[
            jax.ShapeDtypeStruct((tok, head_dim), bf16),
            jax.ShapeDtypeStruct((tok, 128), f32),
        ],
        in_specs=[pl.BlockSpec(memory_space=pltpu.SMEM)] + [vmem] * 5,
        out_specs=[vmem] * 2,
        compiler_params=pltpu.CompilerParams(vmem_limit_bytes=SOME),
        cost_estimate=pl.CostEstimate(
            flops=12 * tok * tok * head_dim, bytes_accessed=1_500_000, transcendentals=3 * tok * tok
        ),
    )(block, segment, queries, *pairs)


def attend_back_kernel(
    block, segment, log_total, d_branch, weight, queries, far, near, own, d_queries, d_far, d_near, d_own
):
    pairs = (far, near, own)
    tok = queries.shape[0]
    d_context = dot(d_branch[...], weight[...], (1, 1)).astype(bf16)
    allowed = masks(block[0], segment[...], pairs)
    lse = log_total[:, :1]
    probs, d_probs = [], []
    for ok, pair in zip(allowed, pairs, strict=True):
        scores = jnp.where(ok, dot(queries[...], pair[:tok], (1, 1)), -1e30)
        probs.append(jnp.exp(scores - lse))
        d_probs.append(dot(d_context, pair[tok : 2 * tok], (1, 1)))
    mean = sum(
        jnp.sum(p * d, axis=1, keepdims=True) for p, d in zip(probs, d_probs, strict=True)
    )
    total = None
    for p, d, pair, out in zip(probs, d_probs, pairs, (d_far, d_near, d_own), strict=True):
        d_scores = (p * (d - mean)).astype(bf16)
        part = dot(d_scores, pair[:tok], (1, 0))
        total = part if total is None else total + part
        out[:tok] = dot(d_scores, queries[...], (0, 0)).astype(out.dtype)
        out[tok:] = dot(p.astype(bf16), d_context, (0, 0)).astype(out.dtype)
    d_queries[...] = total


def attend_back(block, segment, log_total, d_branch, weight, queries, pairs):
    tok, head_dim = queries.shape
    vmem = pl.BlockSpec(memory_space=pltpu.VMEM)
    return pl.pallas_call(
        attend_back_kernel,
        out_shape=[
            jax.ShapeDtypeStruct((tok, head_dim), f32),
            jax.ShapeDtypeStruct((2 * tok, head_dim), bf16),
            jax.ShapeDtypeStruct((2 * tok, head_dim), bf16),
            jax.ShapeDtypeStruct((2 * tok, head_dim), f32),
        ],
        in_specs=[pl.BlockSpec(memory_space=pltpu.SMEM)] + [vmem] * 8,
        out_specs=[vmem] * 4,
        compiler_params=pltpu.CompilerParams(vmem_limit_bytes=SOME),
        cost_estimate=pl.CostEstimate(
            flops=30 * tok * tok * head_dim, bytes_accessed=3_500_000, transcendentals=3 * tok * tok
        ),
    )(block, segment, log_total, d_branch, weight, queries, *pairs)


def place_kernel(where_ref, *refs, turns, held):
    n = len(turns)
    parts, outs = refs[:n], refs[n + held : n + held + 3]
    stage, sems, tail_sems = refs[-3:]
    slots = stage.shape[0]
    core, first, second = where_ref[0], where_ref[1], where_ref[2]
    chunks = [
        (ref, i, base + i, other, flip)
        for ref, (other, flip, base) in zip(parts, turns, strict=True)
        for i in range(ref.shape[0])
    ]

    def place(index):
        _, _, across, other, flip = chunks[index]
        which = 1 - core if other else core
        along = (second if other else first) ^ flip
        y = jnp.where(which == 0, along, across)
        z = jnp.where(which == 0, across, along)
        odd = lax.rem(y, 2)
        row = 216 * (2 * z + y // 2) + 104 * odd + 48 * which + 8 * which * odd
        return pl.multiple_of(row, 8), (which == 1) | (odd == 1)

    def copies(index):
        slot = index % slots
        row, whole = place(index)
        for mat, out in enumerate(outs):
            yield (
                pltpu.make_async_copy(
                    stage.at[slot, mat, pl.ds(0, 48)],
                    out.at[pl.ds(row, 48)],
                    sems.at[slot, mat],
                ),
                pltpu.make_async_copy(
                    stage.at[slot, mat, pl.ds(48, 8)],
                    out.at[pl.ds(pl.multiple_of(row + 48, 8), 8)],
                    tail_sems.at[slot, mat],
                ),
                whole,
            )

    def finish(index):
        for most, tail, whole in copies(index):
            most.wait()
            pl.when(whole)(tail.wait)

    for index, (ref, i, *_) in enumerate(chunks):
        if index >= slots:
            finish(index - slots)
        stage[index % slots] = ref[i].astype(f32)
        for most, tail, whole in copies(index):
            most.start()
            pl.when(whole)(tail.start)
    for index in range(max(0, len(chunks) - slots), len(chunks)):
        finish(index)


def placed(where, parts, outs, units):
    arrays = [p[0].reshape(-1, 3, 56, p[0].shape[-1]) for p in parts]
    width = arrays[0].shape[-1]
    slots = 4
    return pl.pallas_call(
        functools.partial(
            place_kernel, turns=tuple(p[1:] for p in parts), held=len(outs)
        ),
        out_shape=[jax.ShapeDtypeStruct((units, width), f32)] * 3,
        in_specs=[pl.BlockSpec(memory_space=pltpu.SMEM)]
        + [pl.BlockSpec(memory_space=pltpu.VMEM)] * len(arrays)
        + [pl.BlockSpec(memory_space=pl.ANY)] * len(outs),
        out_specs=[pl.BlockSpec(memory_space=pl.ANY)] * 3,
        scratch_shapes=[
            pltpu.VMEM((slots, 3, 56, width), f32),
            pltpu.SemaphoreType.DMA((slots, 3)),
            pltpu.SemaphoreType.DMA((slots, 3)),
        ],
        input_output_aliases={1 + len(arrays) + i: i for i in range(len(outs))},
        compiler_params=pltpu.CompilerParams(vmem_limit_bytes=SOME),
        cost_estimate=pl.CostEstimate(
            flops=0, bytes_accessed=sum(p.size for p in arrays) * 6, transcendentals=0
        ),
    )(where, *arrays, *outs)


def finish_kernel(
    core_ref, own, got, out_grad, query_grad, key_grad, value_grad, attn, post, ffw, final, query, key, rows
):
    core = core_ref[0]
    for pieces, other in ((own, 0), (got, 1)):
        even = core == other
        for along in range(4):
            for across in range(4):
                row = jnp.where(even, 8 * across + 2 * along, 8 * along + 2 * across + 1) * 8
                row = pl.ds(pl.multiple_of(row, 8), 8)
                for kind in range(6):
                    rows[kind, row] = pieces[along, kind, across].astype(f32)
    out_grad[...] = rows[0]
    query_grad[...] = rows[1].T
    for lane in range(4):
        key_grad[:, 64 * lane : 64 * lane + 64] = rows[2 + lane, :64].T
        value_grad[:, 64 * lane : 64 * lane + 64] = rows[2 + lane, 64:128].T
    gains = sum(rows[2 + lane, 128:136] for lane in range(4))
    for at, out in enumerate((attn, post, ffw, final)):
        out[...] = gains[at]
    size = query.shape[0]
    query[...] = gains[4, :size]
    key[...] = gains[4, size : 2 * size]


def finished(core, own, got):
    width = own.shape[-1]
    vmem = pl.BlockSpec(memory_space=pltpu.VMEM)
    return pl.pallas_call(
        finish_kernel,
        out_shape=[
            jax.ShapeDtypeStruct((256, width), f32),
            jax.ShapeDtypeStruct((width, 256), f32),
            jax.ShapeDtypeStruct((width, 256), f32),
            jax.ShapeDtypeStruct((width, 256), f32),
            *[jax.ShapeDtypeStruct((width,), f32)] * 4,
            *[jax.ShapeDtypeStruct((256,), f32)] * 2,
        ],
        in_specs=[pl.BlockSpec(memory_space=pltpu.SMEM), vmem, vmem],
        out_specs=[vmem] * 10,
        scratch_shapes=[pltpu.VMEM((6, 256, width), f32)],
        compiler_params=pltpu.CompilerParams(vmem_limit_bytes=SOME),
        cost_estimate=pl.CostEstimate(flops=0, bytes_accessed=10_000_000, transcendentals=0),
    )(core, own, got)


def local(
    layer_input,
    segment_ids,
    out_cotangent,
    attn_norm_gain,
    query_weight,
    key_weight,
    value_weight,
    query_gain,
    key_gain,
    output_weight,
    attn_post_gain,
    ffw_norm_gain,
    gate_weight,
    up_weight,
    down_weight,
    ffw_post_gain,
):
    tok, width = layer_input.shape
    head_dim = key_weight.shape[1]
    units = down_weight.shape[0]
    block = lax.axis_index("seq")
    lane = lax.axis_index("tensor")
    core = lax.rem(block, 2)
    row = lax.rem(lax.div(block, 2), 4)
    plane = lax.div(block, 8)
    first = lax.select(core == 0, row, plane)
    second = lax.select(core == 0, plane, row)
    place = jnp.stack([lane, core, block])
    where = jnp.stack([core, first, second])
    afters = [lax.rem(at + by, 4) for at in (lane, first, second) for by in range(4)]
    flips = [first ^ flip for flip in range(1, 4)]
    place, where, core, other_core, *places_at = tied(
        place, where, core, 1 - core, *afters, *flips
    )
    lanes, firsts, seconds = places_at[:4], places_at[4:8], places_at[8:12]
    flips = [firsts[0], *places_at[12:]]
    even = core == 0
    quarter_tok = tok // 4

    freq = rope_base ** (-2.0 * np.arange(head_dim // 2) / head_dim)
    start = (np.arange(lax.axis_size("seq")) * tok)[:, None] * freq[None, :]
    inner = np.arange(tok)[:, None] * freq[None, :]
    tables = [jnp.asarray(f(angle), f32) for angle in (start, inner) for f in (np.cos, np.sin)]

    square = (tok, head_dim)
    normed, own_pair, k_raw, q_raw, queries, cosine, sine = call(
        prepare_kernel,
        [
            ((tok, width), bf16),
            ((2 * tok + 16, head_dim), bf16),
            (square, f32),
            (square, f32),
            (square, bf16),
            ((tok, head_dim // 2), f32),
            ((tok, head_dim // 2), f32),
        ],
        place,
        layer_input,
        attn_norm_gain,
        key_weight,
        value_weight,
        query_weight,
        key_gain,
        query_gain,
        *tables,
        segment_ids,
        scalars=1,
        flops=6 * tok * width * head_dim,
        room=MOST,
    )
    left_one = shifted(own_pair, 1)
    left_two = shifted(own_pair, 2)

    weight_half = tok // 2
    halved, _ = tied(output_weight, own_pair)
    own_weight = pick(halved.reshape(2, weight_half, width), core)
    got_weight = [send(own_weight, round_x(by)) for by in (1, 2, 3)]

    pairs = (left_two, left_one, own_pair)
    block_ref = place[2:]
    segment = segment_ids.astype(f32)[:, None]
    context, log_total = attend(block_ref, segment, queries, pairs)

    got_context = [send(context, round_x(by)) for by in (1, 2, 3)]
    *got_context, got_weight[0], got_weight[1], got_weight[2] = tied(*got_context, *got_weight)
    other_weight = [send(part, swap_cores()) for part in got_weight]
    branch, middle, normed_two = call(
        project_kernel,
        [((tok, width), f32), ((tok, width), f32), ((tok, width), bf16)],
        place,
        layer_input,
        attn_post_gain,
        ffw_norm_gain,
        context,
        *got_context,
        output_weight,
        *got_weight,
        *other_weight,
        scalars=1,
        flops=8 * tok * tok * width,
    )
    gate = dot(gate_weight, normed_two, (0, 1))
    up_val = dot(up_weight, normed_two, (0, 1))
    active, gelu_back = jax.vjp(lambda val: jax.nn.gelu(val, approximate=True), gate)
    hidden = (active * up_val).astype(bf16)
    down_part = dot(hidden, down_weight, (0, 0)).astype(bf16)

    def halves(values):
        groups = values.reshape(8, units // 8, tok)
        groups = jnp.concatenate([groups[:, :56], groups[:, 48:]], axis=1)
        pieces = groups.reshape(4, 4, 2, 56, tok)
        return pick(pieces, core, 2), pick(pieces, other_core, 2)

    def arranged(values):
        values = jnp.where(even, values.swapaxes(0, 1), values)
        by_first = [pick(values, flip) for flip in flips]
        groups = [
            jnp.stack([by_first[i][2 * stream : 2 * stream + 2] for i in order])
            for stream, order in ((0, (0, 3)), (0, (1, 2)), (1, (0, 1)), (1, (3, 2)))
        ]
        return jnp.stack(groups).reshape(4, 224, tok)

    hidden_own, hidden_give = halves(hidden)
    hidden_got = send(hidden_give, swap_cores())
    normed_two_got = send(normed_two, swap_cores())

    def quarters(parts):
        parts = parts.reshape(4, quarter_tok, parts.shape[-1])
        given = [pick(parts, at) for at in lanes[1:]]
        return [pick(parts, lanes[0])] + [
            send(part, round_x(by)) for by, part in zip((1, 2, 3), given, strict=True)
        ]

    piece = (quarter_tok, width)
    out_own, d_branch_two, final_part = call(
        final_kernel,
        [(piece, bf16), (piece, bf16), ((1, width), f32)],
        place,
        *quarters(down_part),
        middle,
        out_cotangent,
        ffw_post_gain,
        scalars=1,
    )
    d_branch_two = gather(d_branch_two, lanes, round_x).reshape(tok, width)
    d_branch_two_got = send(d_branch_two, swap_cores())

    d_hidden = dot(down_weight, d_branch_two, (1, 1))
    d_gate = gelu_back(d_hidden * up_val)[0].astype(bf16)
    d_up = (d_hidden * active).astype(bf16)
    d_normed_two = (dot(d_gate, gate_weight, (0, 1)) + dot(d_up, up_weight, (0, 1))).astype(bf16)
    d_gate_own, d_gate_give = halves(d_gate)
    d_up_own, d_up_give = halves(d_up)
    d_pair_got = send(jnp.stack([d_gate_give, d_up_give]), swap_cores())

    keep_a, give_a, keep_b, give_b = weight_parts(
        *(
            arranged(v)
            for v in (hidden_own, hidden_got, d_gate_own, d_pair_got[0], d_up_own, d_pair_got[1])
        ),
        d_branch_two,
        d_branch_two_got,
        normed_two,
        normed_two_got,
    )
    got_a = send(give_a, along_first(1))
    got_b = send(give_b, along_first(3))

    *got_normed, keep_a, keep_b = tied(*quarters(d_normed_two), keep_a, keep_b)
    d_middle, d_branch, ffw_part, post_part = call(
        between_kernel,
        [(piece, f32), (piece, bf16), ((1, width), f32), ((1, width), f32)],
        place,
        *got_normed,
        middle,
        branch,
        out_cotangent,
        ffw_norm_gain,
        attn_post_gain,
        scalars=1,
    )
    d_branch = gather(d_branch, lanes, round_x).reshape(tok, width)
    d_queries, left_far, left_near, summed = attend_back(
        block_ref, segment, log_total, d_branch, output_weight, queries, pairs
    )
    got_near = shifted(left_near, -1)
    got_far = shifted(left_far, -2)
    got_near, got_far, got_a, got_b = tied(got_near, got_far, got_a, got_b)
    keep_a, give_a, keep_b, give_b = call(
        halve_kernel, [((336, width), bf16)] * 4, keep_a, got_a, keep_b, got_b
    )
    got_a = send(give_a, along_first(3))
    got_b = send(give_b, along_first(1))
    d_query, payload, query_part, key_part = call(
        key_kernel,
        [
            (square, bf16),
            ((tok, width + 2 * tok), bf16),
            ((1, head_dim), f32),
            ((1, head_dim), f32),
        ],
        q_raw,
        k_raw,
        d_queries,
        summed,
        got_near,
        got_far,
        cosine,
        sine,
        query_gain,
        key_gain,
        query_weight,
        key_weight,
        value_weight,
        flops=6 * tok * width * head_dim,
    )
    got_both = quarters(payload)
    (products,) = call(
        products_kernel,
        [((2 * head_dim, width), f32)],
        context,
        d_branch,
        d_query,
        normed,
        flops=4 * tok * width * head_dim,
    )
    *got_both, got_a, got_b = tied(*got_both, got_a, got_b)
    chunk = (3, 56, width)
    mine, *given = call(
        deal_kernel,
        [(chunk, f32)] + [(chunk, bf16)] * 3,
        where,
        keep_a,
        got_a,
        keep_b,
        got_b,
        scalars=1,
        scratch=[pltpu.VMEM((2, 336, width), f32)],
    )
    got = [send(part, round_second(by)) for by, part in zip((1, 2, 3), given, strict=True)]
    input_own, keep, give = pl.pallas_call(
        entry_kernel,
        out_shape=[
            jax.ShapeDtypeStruct(piece, bf16),
            jax.ShapeDtypeStruct((3, 16, 8, width), f32),
            jax.ShapeDtypeStruct((3, 16, 8, width), bf16),
        ],
        in_specs=[pl.BlockSpec(memory_space=pltpu.SMEM)]
        + [pl.BlockSpec(memory_space=pltpu.VMEM)] * 14,
        out_specs=[pl.BlockSpec(memory_space=pltpu.VMEM)] * 3,
        scratch_shapes=[pltpu.VMEM((tok, width), f32)],
        compiler_params=pltpu.CompilerParams(vmem_limit_bytes=SOME),
        cost_estimate=pl.CostEstimate(
            flops=256 * tok * width, bytes_accessed=12_000_000, transcendentals=0
        ),
    )(
        place,
        *got_both,
        layer_input,
        d_middle,
        attn_norm_gain,
        normed,
        post_part,
        ffw_part,
        final_part,
        query_part,
        key_part,
        products,
    )
    pack_got = send(give, swap_cores())
    part = (3, 4, 8, width)
    pack, *given = call(
        merge_kernel, [(part, f32)] + [(part, bf16)] * 3, where, keep, pack_got, scalars=1
    )
    given = [send(part, round_first(by)) for by, part in zip((1, 2, 3), given, strict=True)]
    *given, got[0], got[1], got[2] = tied(*given, *got)
    mine = mine + got[0].astype(f32) + (got[1].astype(f32) + got[2].astype(f32))
    mine = mine.astype(bf16).reshape(168, width)
    for part in given:
        pack = pack + part.astype(f32)
    pack = pack.astype(bf16).reshape(96, width)
    both = lax.optimization_barrier(jnp.concatenate([mine, pack]))
    given = [send(both, round_second(by)) for by in (1, 2, 3)]
    quarter = joined(both[:168], [part[:168] for part in given], seconds)
    pack, *given = (part[168:].astype(f32) for part in (both, *given))
    pack = (pack + given[1] + (given[0] + given[2])).astype(bf16).reshape(3, 4, 8, width)
    near_a = send(quarter, along_first(1))
    near_b = send(quarter, along_first(3))
    other_own = send(quarter, swap_cores())
    ends = jnp.concatenate([pack[2].reshape(32, width), out_own, input_own])
    given = [send(ends, round_x(by)) for by in (1, 2, 3)]
    *given, near_a, near_b = tied(*given, near_a, near_b)
    far_a = send(near_b[:2], along_first(1))
    far_b = send(near_a[2:], along_first(3))
    other_a = send(near_a, swap_cores())
    other_b = send(near_b, swap_cores())
    grads = placed(
        where,
        [
            (quarter, False, 0, 0),
            (near_a, False, 1, 0),
            (near_b, False, 3, 0),
            (other_own, True, 0, 0),
            (other_a, True, 1, 0),
            (other_b, True, 3, 0),
        ],
        [],
        units,
    )
    whole = joined(ends, given, lanes)
    layer_output = whole[:, 32:96].reshape(tok, width)
    input_grad = whole[:, 96:].reshape(tok, width)
    pack = jnp.concatenate([pack[:2], whole[:, :32].reshape(4, 4, 8, width)])
    given = [send(pack, round_first(by)) for by in (1, 2, 3)]
    grads = list(grads)
    *given, far_a, far_b, grads[0] = tied(*given, far_a, far_b, grads[0])
    whole = joined(pack, given, firsts)
    pack_got = send(whole, swap_cores())
    out_grad, query_grad, key_grad, value_grad, *gains = finished(
        where[:1], whole, pack_got
    )
    other_far_a = send(far_a, swap_cores())
    other_far_b = send(far_b, swap_cores())
    other_far_a, other_far_b, out_grad = tied(other_far_a, other_far_b, out_grad)
    down_grad, gate_grad, up_grad = placed(
        where,
        [
            (far_a, False, 2, 0),
            (far_b, False, 2, 2),
            (other_far_a, True, 2, 0),
            (other_far_b, True, 2, 2),
        ],
        grads,
        units,
    )
    return (
        layer_output,
        input_grad,
        gains[0],
        query_grad,
        key_grad,
        value_grad,
        gains[4],
        gains[5],
        out_grad,
        gains[1],
        gains[2],
        gate_grad.T,
        up_grad.T,
        down_grad,
        gains[3],
    )


def solution(mesh):
    rows = P("seq", None)
    return jax.shard_map(
        local,
        mesh=mesh,
        in_specs=(
            rows,
            P("seq"),
            rows,
            P(),
            P(None, "tensor"),
            P(),
            P(),
            P(),
            P(),
            P("tensor", None),
            P(),
            P(),
            P(None, "tensor"),
            P(None, "tensor"),
            P("tensor", None),
            P(),
        ),
        out_specs=(
            rows,
            rows,
            P(),
            P(None, "tensor"),
            P(),
            P(),
            P(),
            P(),
            P("tensor", None),
            P(),
            P(),
            P(None, "tensor"),
            P(None, "tensor"),
            P("tensor", None),
            P(),
        ),
        check_vma=False,
    )
```

```python
import functools

import jax
import jax.numpy as jnp
import numpy as np
from jax import lax
from jax.experimental import pallas as pl
from jax.experimental.pallas import tpu as pltpu
from jax.sharding import PartitionSpec as P

WINDOW = 512
SOME = 24 * 1024 * 1024
MOST = 60 * 1024 * 1024

eps = 1e-06
rope_base = 10000.0
f32 = jnp.float32
bf16 = jnp.bfloat16
BOTH = ("seq", "tensor")


def places():
    return [(z, y, c, x) for z in range(4) for y in range(4) for c in range(2) for x in range(4)]


def number(z, y, c, x):
    return ((z * 4 + y) * 2 + c) * 4 + x


def route(move):
    return [(number(*p), number(*move(*p))) for p in places()]


def round_x(by):
    return route(lambda z, y, c, x: (z, y, c, (x + by) % 4))


def swap_cores():
    return route(lambda z, y, c, x: (z, y, 1 - c, x))


def along_first(flip):
    return route(lambda z, y, c, x: (z, y ^ flip, c, x) if c == 0 else (z ^ flip, y, c, x))


def round_first(by):
    return route(
        lambda z, y, c, x: (z, (y + by) % 4, c, x) if c == 0 else ((z + by) % 4, y, c, x)
    )


def round_second(by):
    return route(
        lambda z, y, c, x: ((z + by) % 4, y, c, x) if c == 0 else (z, (y + by) % 4, c, x)
    )


def send(value, pairs):
    return lax.ppermute(value, BOTH, pairs)


def shifted(value, by):
    pairs = [
        (i * 4 + x, (i + by) * 4 + x) for i in range(32) if 0 <= i + by < 32 for x in range(4)
    ]
    return send(value, pairs)


def pick(parts, index, axis=0):
    return lax.dynamic_index_in_dim(
        parts, index, axis, keepdims=False, allow_negative_indices=False
    )


def put(parts, part, index):
    return lax.dynamic_update_index_in_dim(parts, part, index, 0, allow_negative_indices=False)


def dot(first, second, over):
    return lax.dot_general(
        first, second, (((over[0],), (over[1],)), ((), ())), preferred_element_type=f32
    )


def joined(own, got, after):
    whole = put(jnp.zeros((4, *own.shape), own.dtype), own, after[0])
    for by, part in zip((1, 2, 3), got, strict=True):
        whole = put(whole, part, after[4 - by])
    return whole


def gather(part, after, turn):
    return joined(part, [send(part, turn(by)) for by in (1, 2, 3)], after)


def inv_scale(values):
    return lax.rsqrt(jnp.mean(values * values, axis=-1, keepdims=True) + eps)


def norm_back(values, scale, gain, grad):
    unit = values * scale
    weighted = grad * gain
    d_values = scale * (weighted - unit * jnp.mean(weighted * unit, axis=-1, keepdims=True))
    return (d_values, jnp.sum(grad * unit, axis=0))


def rotate(values, cosine, sine):
    half = values.shape[-1] // 2
    first = values[..., :half]
    second = values[..., half:]
    return jnp.concatenate(
        [first * cosine - second * sine, second * cosine + first * sine], axis=-1
    )


def padded(values, rows):
    return jnp.pad(values, ((0, rows - values.shape[0]), (0, 0)))


def added(first, second):
    return (first.astype(f32) + second.astype(f32)).astype(bf16)


def tied(*values):
    return lax.optimization_barrier(values)


def call(kernel, outs, *arrays, scalars=0, flops=0, room=SOME, scratch=()):
    vmem = pl.BlockSpec(memory_space=pltpu.VMEM)
    outs = [jax.ShapeDtypeStruct(*o) for o in outs]
    moved = sum(v.size * v.dtype.itemsize for v in (*arrays, *outs))
    return pl.pallas_call(
        kernel,
        out_shape=outs,
        in_specs=[pl.BlockSpec(memory_space=pltpu.SMEM)] * scalars
        + [vmem] * (len(arrays) - scalars),
        out_specs=[vmem] * len(outs),
        scratch_shapes=scratch,
        compiler_params=pltpu.CompilerParams(vmem_limit_bytes=room),
        cost_estimate=pl.CostEstimate(flops=flops, bytes_accessed=moved, transcendentals=0),
    )(*arrays)


def own_rows(ref, lane, rows):
    return ref[pl.ds(pl.multiple_of(lane * rows, rows), rows)].astype(f32)


def project_kernel(
    place, x, post_gain, ffw_gain, ctx0, ctx1, ctx2, ctx3, weight, own1, own2, own3, other1, other2, other3,
    branch, middle, normed
):
    even = place[1] == 0
    half = own1.shape[0]
    total = dot(ctx0[...], weight[...], (1, 0))
    for ctx, mine, theirs in ((ctx1, own1, other1), (ctx2, own2, other2), (ctx3, own3, other3)):
        low = jnp.where(even, mine[...], theirs[...])
        high = jnp.where(even, theirs[...], mine[...])
        total += dot(ctx[:, :half], low, (1, 0)) + dot(ctx[:, half:], high, (1, 0))
    branch[...] = total
    after = x[...].astype(f32) + total * inv_scale(total) * post_gain[...]
    middle[...] = after
    normed[...] = (after * inv_scale(after) * ffw_gain[...]).astype(bf16)


def final_kernel(place, p0, p1, p2, p3, middle, cotangent, gain, out, d_branch, part):
    lane = place[0]
    branch = p0[...].astype(f32) + p1[...].astype(f32) + p2[...].astype(f32) + p3[...].astype(f32)
    rows = branch.shape[0]
    scale = inv_scale(branch)
    cot = own_rows(cotangent, lane, rows)
    out[...] = (own_rows(middle, lane, rows) + branch * scale * gain[...]).astype(bf16)
    d_values, d_gain = norm_back(branch, scale, gain[...], cot)
    d_branch[...] = d_values.astype(bf16)
    part[...] = d_gain[None]


def between_kernel(
    place, p0, p1, p2, p3, middle, branch, cotangent, ffw_gain, post_gain,
    d_middle, d_branch, ffw_part, post_part
):
    lane = place[0]
    grad = p0[...].astype(f32) + p1[...].astype(f32) + p2[...].astype(f32) + p3[...].astype(f32)
    rows = grad.shape[0]
    after = own_rows(middle, lane, rows)
    before = own_rows(branch, lane, rows)
    d_values, d_gain = norm_back(after, inv_scale(after), ffw_gain[...], grad)
    ffw_part[...] = d_gain[None]
    d_values = own_rows(cotangent, lane, rows) + d_values
    d_middle[...] = d_values
    d_values, d_gain = norm_back(before, inv_scale(before), post_gain[...], d_values)
    d_branch[...] = d_values.astype(bf16)
    post_part[...] = d_gain[None]


def key_kernel(
    q_raw, k_raw, d_queries, d_own, d_near, d_far, cosine, sine, query_gain, key_gain, query_weight, key_weight,
    value_weight, d_query, payload, query_part, key_part
):
    tok, head_dim = q_raw.shape
    width = query_weight.shape[0]
    cos, sin = cosine[...], -sine[...]
    raw = q_raw[...]
    d_raw, d_gain = norm_back(
        raw, inv_scale(raw), query_gain[...], rotate(d_queries[...] * head_dim**-0.5, cos, sin)
    )
    query_part[...] = d_gain[None]
    d_low = d_raw.astype(bf16)
    d_query[...] = d_low
    total = dot(d_low, query_weight[...], (1, 1))
    summed = d_own[...] + d_near[...].astype(f32) + d_far[...].astype(f32)
    raw = k_raw[...]
    d_raw, d_gain = norm_back(raw, inv_scale(raw), key_gain[...], rotate(summed[:tok], cos, sin))
    key_part[...] = d_gain[None]
    total += dot(d_raw.astype(bf16), key_weight[...], (1, 1))
    total += dot(summed[tok:].astype(bf16), value_weight[...], (1, 1))
    payload[:, :width] = total.astype(bf16)
    payload[:, width : width + tok] = d_raw.T.astype(bf16)
    payload[:, width + tok :] = summed[tok:].T.astype(bf16)


def products_kernel(context, d_branch, d_query, normed, out):
    half = context.shape[1]
    out[:half] = dot(context[...], d_branch[...], (0, 0))
    out[half:] = dot(d_query[...], normed[...], (0, 0))


def entry_kernel(
    place, p0, p1, p2, p3, x, d_middle, gain, normed, post_part, ffw_part, final_part, query_part, key_part,
    products, input_grad, keep, give, rest
):
    lane, core = place[0], place[1]
    both = p0[...].astype(f32) + p1[...].astype(f32) + p2[...].astype(f32) + p3[...].astype(f32)
    rows = both.shape[0]
    width = normed.shape[1]
    tok = normed.shape[0]
    full = own_rows(x, lane, rows)
    d_values, d_gain = norm_back(full, inv_scale(full), gain[...], both[:, :width])
    input_grad[...] = (d_middle[...] + d_values).astype(bf16)
    d_keys = both[:, width : width + tok].astype(bf16)
    d_values = both[:, width + tok :].astype(bf16)
    rest[:rows] = dot(d_keys, normed[...], (1, 0))
    rest[rows : 2 * rows] = dot(d_values, normed[...], (1, 0))
    heads = jnp.concatenate(
        [query_part[...], key_part[...], jnp.zeros((1, width - 2 * query_part.shape[1]), f32)], axis=1
    )
    index = lax.broadcasted_iota(jnp.int32, (8, width), 0)
    gains = jnp.zeros((8, width), f32)
    for at, part in enumerate((d_gain[None], post_part[...], ffw_part[...], final_part[...], heads)):
        gains = jnp.where(index == at, part, gains)
    rest[2 * rows : 2 * rows + 8] = gains
    rest[2 * rows + 8 :] = jnp.zeros((rest.shape[0] - 2 * rows - 8, width), f32)
    for kind in range(3):
        source = rest if kind == 2 else products
        base = 256 if kind == 1 else 0
        for chip in range(16):
            at = base + 16 * chip
            keep[kind, chip] = source[pl.ds(pl.multiple_of(at + 8 * core, 8), 8)]
            give[kind, chip] = source[pl.ds(pl.multiple_of(at + 8 - 8 * core, 8), 8)].astype(bf16)


def merge_kernel(where, keep, got, *outs):
    core, first = where[0], where[1]
    for by, out in enumerate(outs):
        along = lax.rem(first + by, 4)
        for across in range(4):
            chip = jnp.where(core == 0, 4 * across + along, 4 * along + across)
            for kind in range(3):
                total = keep[kind, chip] + got[kind, chip].astype(f32)
                out[kind, across] = total.astype(out.dtype)


def weight_kernel(
    hid_own, hid_got, gate_own, gate_got, up_own, up_got, dy_own, dy_got, xn_own, xn_got, *outs
):
    mats = (
        (hid_own, hid_got, dy_own, dy_got),
        (gate_own, gate_got, xn_own, xn_got),
        (up_own, up_got, xn_own, xn_got),
    )
    for group, out in enumerate(outs):
        for index, (left_own, left_got, right_own, right_got) in enumerate(mats):
            total = jnp.dot(left_own[group], right_own[...], preferred_element_type=f32)
            total += jnp.dot(left_got[group], right_got[...], preferred_element_type=f32)
            total = total.astype(bf16)
            out[112 * index : 112 * index + 112] = total[:112]
            out[336 + 112 * index : 448 + 112 * index] = total[112:]


def weight_parts(*arrays):
    width = arrays[-1].shape[1]
    return pl.pallas_call(
        weight_kernel,
        out_shape=[jax.ShapeDtypeStruct((672, width), bf16)] * 4,
        in_specs=[pl.BlockSpec(memory_space=pltpu.VMEM)] * len(arrays),
        out_specs=[pl.BlockSpec(memory_space=pltpu.VMEM)] * 4,
        compiler_params=pltpu.CompilerParams(vmem_limit_bytes=SOME),
        cost_estimate=pl.CostEstimate(
            flops=2 * 2688 * 512 * width, bytes_accessed=12_000_000, transcendentals=0
        ),
    )(*arrays)


def halve_kernel(keep_a, got_a, keep_b, got_b, *outs):
    for keep, got, half in ((keep_a, got_a, outs[:2]), (keep_b, got_b, outs[2:])):
        for index, out in enumerate(half):
            rows = pl.ds(336 * index, 336)
            out[...] = (keep[rows].astype(f32) + got[rows].astype(f32)).astype(bf16)


def deal_kernel(where, keep_a, got_a, keep_b, got_b, *refs):
    outs, total = refs[:-1], refs[-1]
    total[0] = keep_a[...].astype(f32) + got_a[...].astype(f32)
    total[1] = keep_b[...].astype(f32) + got_b[...].astype(f32)
    for by, out in enumerate(outs):
        across = lax.rem(where[2] + by, 4)
        for mat in range(3):
            row = pl.multiple_of(112 * mat + 56 * lax.rem(across, 2), 8)
            out[mat] = total[across // 2, pl.ds(row, 56)].astype(out.dtype)


def masks(block, pairs):
    tok = pairs[0].shape[1]
    query = lax.broadcasted_iota(jnp.int32, (tok, tok), 0)
    key = lax.broadcasted_iota(jnp.int32, (tok, tok), 1)
    rows = [pair[2 * tok : 2 * tok + 16].astype(f32)[:1] for pair in pairs]
    segment = jnp.broadcast_to(rows[2], (tok, tok)).T
    same = [segment == row for row in rows]
    return (
        same[0] & (key > query) & (block >= 2),
        same[1] & (block >= 1),
        same[2] & (key <= query),
    )


def prepare_kernel(
    place, x, gain, key_weight, value_weight, query_weight, key_gain, query_gain, start_cos, start_sin, inner_cos,
    inner_sin, marks, xn, pair, k_raw, q_raw, queries, cosine, sine
):
    tok, head_dim = k_raw.shape
    full = x[...].astype(f32)
    low = (full * inv_scale(full) * gain[...]).astype(bf16)
    xn[...] = low
    at = pl.ds(place[2], 1)
    cos = start_cos[at] * inner_cos[...] - start_sin[at] * inner_sin[...]
    sin = start_sin[at] * inner_cos[...] + start_cos[at] * inner_sin[...]
    cosine[...] = cos
    sine[...] = sin
    raw = dot(low, key_weight[...], (1, 0))
    k_raw[...] = raw
    pair[:tok] = rotate(raw * inv_scale(raw) * key_gain[...], cos, sin).astype(bf16)
    pair[tok : 2 * tok] = dot(low, value_weight[...], (1, 0)).astype(bf16)
    pair[2 * tok :] = jnp.broadcast_to(marks[...].astype(f32)[None], (16, tok)).astype(bf16)
    raw = dot(low, query_weight[...], (1, 0))
    q_raw[...] = raw
    turned = rotate(raw * inv_scale(raw) * query_gain[...], cos, sin)
    queries[...] = (turned * head_dim**-0.5).astype(bf16)


def attend_kernel(place, queries, far, near, own, context, log_total):
    pairs = (far, near, own)
    tok = queries.shape[0]
    allowed = masks(place[2], pairs)
    scores = [
        jnp.where(ok, dot(queries[...], pair[:tok], (1, 1)), -1e30)
        for ok, pair in zip(allowed, pairs, strict=True)
    ]
    top = functools.reduce(jnp.maximum, [jnp.max(s, axis=1, keepdims=True) for s in scores])
    weights = [jnp.exp(s - top) for s in scores]
    total = sum(jnp.sum(w, axis=1, keepdims=True) for w in weights)
    context[...] = sum(
        dot((w / total).astype(bf16), pair[tok : 2 * tok], (1, 0))
        for w, pair in zip(weights, pairs, strict=True)
    ).astype(bf16)
    log_total[...] = jnp.broadcast_to(top + jnp.log(total), log_total.shape)


def attend(place, queries, pairs):
    tok, head_dim = queries.shape
    vmem = pl.BlockSpec(memory_space=pltpu.VMEM)
    return pl.pallas_call(
        attend_kernel,
        out_shape=[
            jax.ShapeDtypeStruct((tok, head_dim), bf16),
            jax.ShapeDtypeStruct((tok, 128), f32),
        ],
        in_specs=[pl.BlockSpec(memory_space=pltpu.SMEM)] + [vmem] * 4,
        out_specs=[vmem] * 2,
        compiler_params=pltpu.CompilerParams(vmem_limit_bytes=SOME),
        cost_estimate=pl.CostEstimate(
            flops=12 * tok * tok * head_dim, bytes_accessed=1_500_000, transcendentals=3 * tok * tok
        ),
    )(place, queries, *pairs)


def attend_back_kernel(
    place, log_total, d_branch, weight, queries, far, near, own, d_queries, d_far, d_near, d_own
):
    pairs = (far, near, own)
    tok = queries.shape[0]
    d_context = dot(d_branch[...], weight[...], (1, 1)).astype(bf16)
    allowed = masks(place[2], pairs)
    lse = log_total[:, :1]
    probs, d_probs = [], []
    for ok, pair in zip(allowed, pairs, strict=True):
        scores = jnp.where(ok, dot(queries[...], pair[:tok], (1, 1)), -1e30)
        probs.append(jnp.exp(scores - lse))
        d_probs.append(dot(d_context, pair[tok : 2 * tok], (1, 1)))
    mean = sum(
        jnp.sum(p * d, axis=1, keepdims=True) for p, d in zip(probs, d_probs, strict=True)
    )
    total = None
    for p, d, pair, out in zip(probs, d_probs, pairs, (d_far, d_near, d_own), strict=True):
        d_scores = (p * (d - mean)).astype(bf16)
        part = dot(d_scores, pair[:tok], (1, 0))
        total = part if total is None else total + part
        out[:tok] = dot(d_scores, queries[...], (0, 0)).astype(out.dtype)
        out[tok:] = dot(p.astype(bf16), d_context, (0, 0)).astype(out.dtype)
    d_queries[...] = total


def attend_back(place, log_total, d_branch, weight, queries, pairs):
    tok, head_dim = queries.shape
    vmem = pl.BlockSpec(memory_space=pltpu.VMEM)
    return pl.pallas_call(
        attend_back_kernel,
        out_shape=[
            jax.ShapeDtypeStruct((tok, head_dim), f32),
            jax.ShapeDtypeStruct((2 * tok, head_dim), bf16),
            jax.ShapeDtypeStruct((2 * tok, head_dim), bf16),
            jax.ShapeDtypeStruct((2 * tok, head_dim), f32),
        ],
        in_specs=[pl.BlockSpec(memory_space=pltpu.SMEM)] + [vmem] * 7,
        out_specs=[vmem] * 4,
        compiler_params=pltpu.CompilerParams(vmem_limit_bytes=SOME),
        cost_estimate=pl.CostEstimate(
            flops=30 * tok * tok * head_dim, bytes_accessed=3_500_000, transcendentals=3 * tok * tok
        ),
    )(place, log_total, d_branch, weight, queries, *pairs)


def place_kernel(where_ref, *refs, turns, held):
    n = len(turns)
    parts, outs = refs[:n], refs[n + held : n + held + 3]
    stage, sems, tail_sems = refs[-3:]
    slots = stage.shape[0]
    core, first, second = where_ref[0], where_ref[1], where_ref[2]
    chunks = [
        (ref, i, base + i, other, flip)
        for ref, (other, flip, base) in zip(parts, turns, strict=True)
        for i in range(ref.shape[0])
    ]

    def place(index):
        _, _, across, other, flip = chunks[index]
        which = 1 - core if other else core
        along = (second if other else first) ^ flip
        y = jnp.where(which == 0, along, across)
        z = jnp.where(which == 0, across, along)
        odd = lax.rem(y, 2)
        row = 216 * (2 * z + y // 2) + 104 * odd + 48 * which + 8 * which * odd
        return pl.multiple_of(row, 8), (which == 1) | (odd == 1)

    def copies(index):
        slot = index % slots
        row, whole = place(index)
        for mat, out in enumerate(outs):
            yield (
                pltpu.make_async_copy(
                    stage.at[slot, mat, pl.ds(0, 48)],
                    out.at[pl.ds(row, 48)],
                    sems.at[slot, mat],
                ),
                pltpu.make_async_copy(
                    stage.at[slot, mat, pl.ds(48, 8)],
                    out.at[pl.ds(pl.multiple_of(row + 48, 8), 8)],
                    tail_sems.at[slot, mat],
                ),
                whole,
            )

    def finish(index):
        for most, tail, whole in copies(index):
            most.wait()
            pl.when(whole)(tail.wait)

    for index, (ref, i, *_) in enumerate(chunks):
        if index >= slots:
            finish(index - slots)
        stage[index % slots] = ref[i].astype(f32)
        for most, tail, whole in copies(index):
            most.start()
            pl.when(whole)(tail.start)
    for index in range(max(0, len(chunks) - slots), len(chunks)):
        finish(index)


def placed(where, parts, outs, units):
    arrays = [p[0].reshape(-1, 3, 56, p[0].shape[-1]) for p in parts]
    width = arrays[0].shape[-1]
    slots = 4
    return pl.pallas_call(
        functools.partial(
            place_kernel, turns=tuple(p[1:] for p in parts), held=len(outs)
        ),
        out_shape=[jax.ShapeDtypeStruct((units, width), f32)] * 3,
        in_specs=[pl.BlockSpec(memory_space=pltpu.SMEM)]
        + [pl.BlockSpec(memory_space=pltpu.VMEM)] * len(arrays)
        + [pl.BlockSpec(memory_space=pl.ANY)] * len(outs),
        out_specs=[pl.BlockSpec(memory_space=pl.ANY)] * 3,
        scratch_shapes=[
            pltpu.VMEM((slots, 3, 56, width), f32),
            pltpu.SemaphoreType.DMA((slots, 3)),
            pltpu.SemaphoreType.DMA((slots, 3)),
        ],
        input_output_aliases={1 + len(arrays) + i: i for i in range(len(outs))},
        compiler_params=pltpu.CompilerParams(vmem_limit_bytes=SOME),
        cost_estimate=pl.CostEstimate(
            flops=0, bytes_accessed=sum(p.size for p in arrays) * 6, transcendentals=0
        ),
    )(where, *arrays, *outs)


def finish_kernel(
    core_ref, own, got, out_grad, query_grad, key_grad, value_grad, attn, post, ffw, final, query, key, rows
):
    core = core_ref[0]
    for pieces, other in ((own, 0), (got, 1)):
        even = core == other
        for along in range(4):
            for across in range(4):
                row = jnp.where(even, 8 * across + 2 * along, 8 * along + 2 * across + 1) * 8
                row = pl.ds(pl.multiple_of(row, 8), 8)
                for kind in range(6):
                    rows[kind, row] = pieces[along, kind, across].astype(f32)
    out_grad[...] = rows[0]
    query_grad[...] = rows[1].T
    for lane in range(4):
        key_grad[:, 64 * lane : 64 * lane + 64] = rows[2 + lane, :64].T
        value_grad[:, 64 * lane : 64 * lane + 64] = rows[2 + lane, 64:128].T
    gains = sum(rows[2 + lane, 128:136] for lane in range(4))
    for at, out in enumerate((attn, post, ffw, final)):
        out[...] = gains[at]
    size = query.shape[0]
    query[...] = gains[4, :size]
    key[...] = gains[4, size : 2 * size]


def finished(core, own, got):
    width = own.shape[-1]
    vmem = pl.BlockSpec(memory_space=pltpu.VMEM)
    return pl.pallas_call(
        finish_kernel,
        out_shape=[
            jax.ShapeDtypeStruct((256, width), f32),
            jax.ShapeDtypeStruct((width, 256), f32),
            jax.ShapeDtypeStruct((width, 256), f32),
            jax.ShapeDtypeStruct((width, 256), f32),
            *[jax.ShapeDtypeStruct((width,), f32)] * 4,
            *[jax.ShapeDtypeStruct((256,), f32)] * 2,
        ],
        in_specs=[pl.BlockSpec(memory_space=pltpu.SMEM), vmem, vmem],
        out_specs=[vmem] * 10,
        scratch_shapes=[pltpu.VMEM((6, 256, width), f32)],
        compiler_params=pltpu.CompilerParams(vmem_limit_bytes=SOME),
        cost_estimate=pl.CostEstimate(flops=0, bytes_accessed=10_000_000, transcendentals=0),
    )(core, own, got)


def local(
    layer_input,
    segment_ids,
    out_cotangent,
    attn_norm_gain,
    query_weight,
    key_weight,
    value_weight,
    query_gain,
    key_gain,
    output_weight,
    attn_post_gain,
    ffw_norm_gain,
    gate_weight,
    up_weight,
    down_weight,
    ffw_post_gain,
):
    tok, width = layer_input.shape
    head_dim = key_weight.shape[1]
    units = down_weight.shape[0]
    block = lax.axis_index("seq")
    lane = lax.axis_index("tensor")
    core = lax.rem(block, 2)
    row = lax.rem(lax.div(block, 2), 4)
    plane = lax.div(block, 8)
    first = lax.select(core == 0, row, plane)
    second = lax.select(core == 0, plane, row)
    place = jnp.stack([lane, core, block])
    where = jnp.stack([core, first, second])
    afters = [lax.rem(at + by, 4) for at in (lane, first, second) for by in range(4)]
    flips = [first ^ flip for flip in range(1, 4)]
    place, where, core, other_core, even, *places_at = tied(
        place, where, core, 1 - core, core == 0, *afters, *flips
    )
    lanes, firsts, seconds = places_at[:4], places_at[4:8], places_at[8:12]
    flips = [firsts[0], *places_at[12:]]
    quarter_tok = tok // 4

    freq = rope_base ** (-2.0 * np.arange(head_dim // 2) / head_dim)
    start = (np.arange(lax.axis_size("seq")) * tok)[:, None] * freq[None, :]
    inner = np.arange(tok)[:, None] * freq[None, :]
    tables = [jnp.asarray(f(angle), f32) for angle in (start, inner) for f in (np.cos, np.sin)]

    square = (tok, head_dim)
    normed, own_pair, k_raw, q_raw, queries, cosine, sine = call(
        prepare_kernel,
        [
            ((tok, width), bf16),
            ((2 * tok + 16, head_dim), bf16),
            (square, f32),
            (square, f32),
            (square, bf16),
            ((tok, head_dim // 2), f32),
            ((tok, head_dim // 2), f32),
        ],
        place,
        layer_input,
        attn_norm_gain,
        key_weight,
        value_weight,
        query_weight,
        key_gain,
        query_gain,
        *tables,
        segment_ids,
        scalars=1,
        flops=6 * tok * width * head_dim,
        room=MOST,
    )
    left_one = shifted(own_pair, 1)
    left_two = shifted(own_pair, 2)

    weight_half = tok // 2
    halved, _ = tied(output_weight, own_pair)
    own_weight = pick(halved.reshape(2, weight_half, width), core)
    got_weight = [send(own_weight, round_x(by)) for by in (1, 2, 3)]

    pairs = (left_two, left_one, own_pair)
    context, log_total = attend(place, queries, pairs)

    got_context = [send(context, round_x(by)) for by in (1, 2, 3)]
    *got_context, got_weight[0], got_weight[1], got_weight[2] = tied(*got_context, *got_weight)
    other_weight = [send(part, swap_cores()) for part in got_weight]
    branch, middle, normed_two = call(
        project_kernel,
        [((tok, width), f32), ((tok, width), f32), ((tok, width), bf16)],
        place,
        layer_input,
        attn_post_gain,
        ffw_norm_gain,
        context,
        *got_context,
        output_weight,
        *got_weight,
        *other_weight,
        scalars=1,
        flops=8 * tok * tok * width,
    )
    gate = dot(gate_weight, normed_two, (0, 1))
    up_val = dot(up_weight, normed_two, (0, 1))
    active, gelu_back = jax.vjp(lambda val: jax.nn.gelu(val, approximate=True), gate)
    hidden = (active * up_val).astype(bf16)
    down_part = dot(hidden, down_weight, (0, 0)).astype(bf16)

    def halves(values):
        groups = values.reshape(8, units // 8, tok)
        groups = jnp.concatenate([groups[:, :56], groups[:, 48:]], axis=1)
        pieces = groups.reshape(4, 4, 2, 56, tok)
        return pick(pieces, core, 2), pick(pieces, other_core, 2)

    def arranged(values):
        values = jnp.where(even, values.swapaxes(0, 1), values)
        by_first = [pick(values, flip) for flip in flips]
        groups = [
            jnp.stack([by_first[i][2 * stream : 2 * stream + 2] for i in order])
            for stream, order in ((0, (0, 3)), (0, (1, 2)), (1, (0, 1)), (1, (3, 2)))
        ]
        return jnp.stack(groups).reshape(4, 224, tok)

    hidden_own, hidden_give = halves(hidden)
    hidden_got = send(hidden_give, swap_cores())
    normed_two_got = send(normed_two, swap_cores())

    def quarters(parts):
        parts = parts.reshape(4, quarter_tok, parts.shape[-1])
        given = [pick(parts, at) for at in lanes[1:]]
        return [pick(parts, lanes[0])] + [
            send(part, round_x(by)) for by, part in zip((1, 2, 3), given, strict=True)
        ]

    piece = (quarter_tok, width)
    out_own, d_branch_two, final_part = call(
        final_kernel,
        [(piece, bf16), (piece, bf16), ((1, width), f32)],
        place,
        *quarters(down_part),
        middle,
        out_cotangent,
        ffw_post_gain,
        scalars=1,
    )
    d_branch_two = gather(d_branch_two, lanes, round_x).reshape(tok, width)
    d_branch_two_got = send(d_branch_two, swap_cores())

    d_hidden = dot(down_weight, d_branch_two, (1, 1))
    d_gate = gelu_back(d_hidden * up_val)[0].astype(bf16)
    d_up = (d_hidden * active).astype(bf16)
    d_normed_two = (dot(d_gate, gate_weight, (0, 1)) + dot(d_up, up_weight, (0, 1))).astype(bf16)
    d_gate_own, d_gate_give = halves(d_gate)
    d_up_own, d_up_give = halves(d_up)
    d_pair_got = send(jnp.stack([d_gate_give, d_up_give]), swap_cores())

    keep_a, give_a, keep_b, give_b = weight_parts(
        *(
            arranged(v)
            for v in (hidden_own, hidden_got, d_gate_own, d_pair_got[0], d_up_own, d_pair_got[1])
        ),
        d_branch_two,
        d_branch_two_got,
        normed_two,
        normed_two_got,
    )
    got_a = send(give_a, along_first(1))
    got_b = send(give_b, along_first(3))

    *got_normed, keep_a, keep_b = tied(*quarters(d_normed_two), keep_a, keep_b)
    d_middle, d_branch, ffw_part, post_part = call(
        between_kernel,
        [(piece, f32), (piece, bf16), ((1, width), f32), ((1, width), f32)],
        place,
        *got_normed,
        middle,
        branch,
        out_cotangent,
        ffw_norm_gain,
        attn_post_gain,
        scalars=1,
    )
    d_branch = gather(d_branch, lanes, round_x).reshape(tok, width)
    d_queries, left_far, left_near, summed = attend_back(
        place, log_total, d_branch, output_weight, queries, pairs
    )
    got_near = shifted(left_near, -1)
    got_far = shifted(left_far, -2)
    got_near, got_far, got_a, got_b = tied(got_near, got_far, got_a, got_b)
    keep_a, give_a, keep_b, give_b = call(
        halve_kernel, [((336, width), bf16)] * 4, keep_a, got_a, keep_b, got_b
    )
    got_a = send(give_a, along_first(3))
    got_b = send(give_b, along_first(1))
    d_query, payload, query_part, key_part = call(
        key_kernel,
        [
            (square, bf16),
            ((tok, width + 2 * tok), bf16),
            ((1, head_dim), f32),
            ((1, head_dim), f32),
        ],
        q_raw,
        k_raw,
        d_queries,
        summed,
        got_near,
        got_far,
        cosine,
        sine,
        query_gain,
        key_gain,
        query_weight,
        key_weight,
        value_weight,
        flops=6 * tok * width * head_dim,
    )
    got_both = quarters(payload)
    (products,) = call(
        products_kernel,
        [((2 * head_dim, width), f32)],
        context,
        d_branch,
        d_query,
        normed,
        flops=4 * tok * width * head_dim,
    )
    *got_both, got_a, got_b = tied(*got_both, got_a, got_b)
    chunk = (3, 56, width)
    mine, *given = call(
        deal_kernel,
        [(chunk, f32)] + [(chunk, bf16)] * 3,
        where,
        keep_a,
        got_a,
        keep_b,
        got_b,
        scalars=1,
        scratch=[pltpu.VMEM((2, 336, width), f32)],
    )
    got = [send(part, round_second(by)) for by, part in zip((1, 2, 3), given, strict=True)]
    input_own, keep, give = pl.pallas_call(
        entry_kernel,
        out_shape=[
            jax.ShapeDtypeStruct(piece, bf16),
            jax.ShapeDtypeStruct((3, 16, 8, width), f32),
            jax.ShapeDtypeStruct((3, 16, 8, width), bf16),
        ],
        in_specs=[pl.BlockSpec(memory_space=pltpu.SMEM)]
        + [pl.BlockSpec(memory_space=pltpu.VMEM)] * 14,
        out_specs=[pl.BlockSpec(memory_space=pltpu.VMEM)] * 3,
        scratch_shapes=[pltpu.VMEM((tok, width), f32)],
        compiler_params=pltpu.CompilerParams(vmem_limit_bytes=SOME),
        cost_estimate=pl.CostEstimate(
            flops=256 * tok * width, bytes_accessed=12_000_000, transcendentals=0
        ),
    )(
        place,
        *got_both,
        layer_input,
        d_middle,
        attn_norm_gain,
        normed,
        post_part,
        ffw_part,
        final_part,
        query_part,
        key_part,
        products,
    )
    pack_got = send(give, swap_cores())
    part = (3, 4, 8, width)
    pack, *given = call(
        merge_kernel, [(part, f32)] + [(part, bf16)] * 3, where, keep, pack_got, scalars=1
    )
    given = [send(part, round_first(by)) for by, part in zip((1, 2, 3), given, strict=True)]
    *given, got[0], got[1], got[2] = tied(*given, *got)
    mine = mine + got[0].astype(f32) + (got[1].astype(f32) + got[2].astype(f32))
    mine = mine.astype(bf16).reshape(168, width)
    for part in given:
        pack = pack + part.astype(f32)
    pack = pack.astype(bf16).reshape(96, width)
    both = lax.optimization_barrier(jnp.concatenate([mine, pack]))
    given = [send(both, round_second(by)) for by in (1, 2, 3)]
    ends = jnp.concatenate([out_own, input_own])
    got_ends = [send(ends, round_x(by)) for by in (1, 2, 3)]
    given[0], given[1], given[2], *got_ends = tied(*given, *got_ends)
    ends = joined(ends, got_ends, lanes)
    layer_output = ends[:, :64].reshape(tok, width)
    input_grad = ends[:, 64:].reshape(tok, width)
    quarter = joined(both[:168], [part[:168] for part in given], seconds)
    pack, *given = (part[168:].astype(f32) for part in (both, *given))
    pack = (pack + given[1] + (given[0] + given[2])).astype(bf16).reshape(3, 4, 8, width)
    near_a = send(quarter, along_first(1))
    near_b = send(quarter, along_first(3))
    other_own = send(quarter, swap_cores())
    given = [send(pack[2], round_x(by)) for by in (1, 2, 3)]
    *given, near_a, near_b = tied(*given, near_a, near_b)
    far_a = send(near_b[:2], along_first(1))
    far_b = send(near_a[2:], along_first(3))
    other_a = send(near_a, swap_cores())
    other_b = send(near_b, swap_cores())
    grads = placed(
        where,
        [
            (quarter, False, 0, 0),
            (near_a, False, 1, 0),
            (near_b, False, 3, 0),
            (other_own, True, 0, 0),
            (other_a, True, 1, 0),
            (other_b, True, 3, 0),
        ],
        [],
        units,
    )
    pack = jnp.concatenate([pack[:2], joined(pack[2], given, lanes)])
    given = [send(pack, round_first(by)) for by in (1, 2, 3)]
    grads = list(grads)
    *given, far_a, far_b, grads[0] = tied(*given, far_a, far_b, grads[0])
    whole = joined(pack, given, firsts)
    pack_got = send(whole, swap_cores())
    out_grad, query_grad, key_grad, value_grad, *gains = finished(
        where, whole, pack_got
    )
    other_far_a = send(far_a, swap_cores())
    other_far_b = send(far_b, swap_cores())
    other_far_a, other_far_b, out_grad = tied(other_far_a, other_far_b, out_grad)
    down_grad, gate_grad, up_grad = placed(
        where,
        [
            (far_a, False, 2, 0),
            (far_b, False, 2, 2),
            (other_far_a, True, 2, 0),
            (other_far_b, True, 2, 2),
        ],
        grads,
        units,
    )
    return (
        layer_output,
        input_grad,
        gains[0],
        query_grad,
        key_grad,
        value_grad,
        gains[4],
        gains[5],
        out_grad,
        gains[1],
        gains[2],
        gate_grad.T,
        up_grad.T,
        down_grad,
        gains[3],
    )


def solution(mesh):
    rows = P("seq", None)
    return jax.shard_map(
        local,
        mesh=mesh,
        in_specs=(
            rows,
            P("seq"),
            rows,
            P(),
            P(None, "tensor"),
            P(),
            P(),
            P(),
            P(),
            P("tensor", None),
            P(),
            P(),
            P(None, "tensor"),
            P(None, "tensor"),
            P("tensor", None),
            P(),
        ),
        out_specs=(
            rows,
            rows,
            P(),
            P(None, "tensor"),
            P(),
            P(),
            P(),
            P(),
            P("tensor", None),
            P(),
            P(),
            P(None, "tensor"),
            P(None, "tensor"),
            P("tensor", None),
            P(),
        ),
        check_vma=False,
    )
```

```python
import functools

import jax
import jax.numpy as jnp
import numpy as np
from jax import lax
from jax.experimental import pallas as pl
from jax.experimental.pallas import tpu as pltpu
from jax.sharding import PartitionSpec as P

WINDOW = 512
SOME = 24 * 1024 * 1024
MOST = 60 * 1024 * 1024

eps = 1e-06
rope_base = 10000.0
f32 = jnp.float32
bf16 = jnp.bfloat16
BOTH = ("seq", "tensor")


def places():
    return [(z, y, c, x) for z in range(4) for y in range(4) for c in range(2) for x in range(4)]


def number(z, y, c, x):
    return ((z * 4 + y) * 2 + c) * 4 + x


def route(move):
    return [(number(*p), number(*move(*p))) for p in places()]


def round_x(by):
    return route(lambda z, y, c, x: (z, y, c, (x + by) % 4))


def swap_cores():
    return route(lambda z, y, c, x: (z, y, 1 - c, x))


def along_first(flip):
    return route(lambda z, y, c, x: (z, y ^ flip, c, x) if c == 0 else (z ^ flip, y, c, x))


def round_first(by):
    return route(
        lambda z, y, c, x: (z, (y + by) % 4, c, x) if c == 0 else ((z + by) % 4, y, c, x)
    )


def round_second(by):
    return route(
        lambda z, y, c, x: ((z + by) % 4, y, c, x) if c == 0 else (z, (y + by) % 4, c, x)
    )


def send(value, pairs):
    return lax.ppermute(value, BOTH, pairs)


def shifted(value, by):
    pairs = [
        (i * 4 + x, (i + by) * 4 + x) for i in range(32) if 0 <= i + by < 32 for x in range(4)
    ]
    return send(value, pairs)


def pick(parts, index, axis=0):
    return lax.dynamic_index_in_dim(
        parts, index, axis, keepdims=False, allow_negative_indices=False
    )


def put(parts, part, index):
    return lax.dynamic_update_index_in_dim(parts, part, index, 0, allow_negative_indices=False)


def dot(first, second, over):
    return lax.dot_general(
        first, second, (((over[0],), (over[1],)), ((), ())), preferred_element_type=f32
    )


def joined(own, got, after):
    whole = put(jnp.zeros((4, *own.shape), own.dtype), own, after[0])
    for by, part in zip((1, 2, 3), got, strict=True):
        whole = put(whole, part, after[4 - by])
    return whole


def gather(part, after, turn):
    return joined(part, [send(part, turn(by)) for by in (1, 2, 3)], after)


def inv_scale(values):
    return lax.rsqrt(jnp.mean(values * values, axis=-1, keepdims=True) + eps)


def norm_back(values, scale, gain, grad):
    unit = values * scale
    weighted = grad * gain
    d_values = scale * (weighted - unit * jnp.mean(weighted * unit, axis=-1, keepdims=True))
    return (d_values, jnp.sum(grad * unit, axis=0))


def rotate(values, cosine, sine):
    half = values.shape[-1] // 2
    first = values[..., :half]
    second = values[..., half:]
    return jnp.concatenate(
        [first * cosine - second * sine, second * cosine + first * sine], axis=-1
    )


def padded(values, rows):
    return jnp.pad(values, ((0, rows - values.shape[0]), (0, 0)))


def added(first, second):
    return (first.astype(f32) + second.astype(f32)).astype(bf16)


def tied(*values):
    return lax.optimization_barrier(values)


def call(kernel, outs, *arrays, scalars=0, flops=0, room=SOME, scratch=()):
    vmem = pl.BlockSpec(memory_space=pltpu.VMEM)
    outs = [jax.ShapeDtypeStruct(*o) for o in outs]
    moved = sum(v.size * v.dtype.itemsize for v in (*arrays, *outs))
    return pl.pallas_call(
        kernel,
        out_shape=outs,
        in_specs=[pl.BlockSpec(memory_space=pltpu.SMEM)] * scalars
        + [vmem] * (len(arrays) - scalars),
        out_specs=[vmem] * len(outs),
        scratch_shapes=scratch,
        compiler_params=pltpu.CompilerParams(vmem_limit_bytes=room),
        cost_estimate=pl.CostEstimate(flops=flops, bytes_accessed=moved, transcendentals=0),
    )(*arrays)


def own_rows(ref, lane, rows):
    return ref[pl.ds(pl.multiple_of(lane * rows, rows), rows)].astype(f32)


def project_kernel(
    place, x, post_gain, ffw_gain, ctx0, ctx1, ctx2, ctx3, weight, own1, own2, own3, other1, other2, other3,
    branch, middle, normed
):
    even = place[1] == 0
    half = own1.shape[0]
    total = dot(ctx0[...], weight[...], (1, 0))
    for ctx, mine, theirs in ((ctx1, own1, other1), (ctx2, own2, other2), (ctx3, own3, other3)):
        low = jnp.where(even, mine[...], theirs[...])
        high = jnp.where(even, theirs[...], mine[...])
        total += dot(ctx[:, :half], low, (1, 0)) + dot(ctx[:, half:], high, (1, 0))
    branch[...] = total
    after = x[...].astype(f32) + total * inv_scale(total) * post_gain[...]
    middle[...] = after
    normed[...] = (after * inv_scale(after) * ffw_gain[...]).astype(bf16)


def final_kernel(place, p0, p1, p2, p3, middle, cotangent, gain, out, d_branch, part):
    lane = place[0]
    branch = p0[...].astype(f32) + p1[...].astype(f32) + p2[...].astype(f32) + p3[...].astype(f32)
    rows = branch.shape[0]
    scale = inv_scale(branch)
    cot = own_rows(cotangent, lane, rows)
    out[...] = (own_rows(middle, lane, rows) + branch * scale * gain[...]).astype(bf16)
    d_values, d_gain = norm_back(branch, scale, gain[...], cot)
    d_branch[...] = d_values.astype(bf16)
    part[...] = d_gain[None]


def between_kernel(
    place, p0, p1, p2, p3, middle, branch, cotangent, ffw_gain, post_gain,
    d_middle, d_branch, ffw_part, post_part
):
    lane = place[0]
    grad = p0[...].astype(f32) + p1[...].astype(f32) + p2[...].astype(f32) + p3[...].astype(f32)
    rows = grad.shape[0]
    after = own_rows(middle, lane, rows)
    before = own_rows(branch, lane, rows)
    d_values, d_gain = norm_back(after, inv_scale(after), ffw_gain[...], grad)
    ffw_part[...] = d_gain[None]
    d_values = own_rows(cotangent, lane, rows) + d_values
    d_middle[...] = d_values
    d_values, d_gain = norm_back(before, inv_scale(before), post_gain[...], d_values)
    d_branch[...] = d_values.astype(bf16)
    post_part[...] = d_gain[None]


def key_kernel(
    q_raw, k_raw, d_queries, d_own, d_near, d_far, cosine, sine, query_gain, key_gain, query_weight, key_weight,
    value_weight, d_query, payload, query_part, key_part
):
    tok, head_dim = q_raw.shape
    width = query_weight.shape[0]
    cos, sin = cosine[...], -sine[...]
    raw = q_raw[...]
    d_raw, d_gain = norm_back(
        raw, inv_scale(raw), query_gain[...], rotate(d_queries[...] * head_dim**-0.5, cos, sin)
    )
    query_part[...] = d_gain[None]
    d_low = d_raw.astype(bf16)
    d_query[...] = d_low
    total = dot(d_low, query_weight[...], (1, 1))
    summed = d_own[...] + d_near[...].astype(f32) + d_far[...].astype(f32)
    raw = k_raw[...]
    d_raw, d_gain = norm_back(raw, inv_scale(raw), key_gain[...], rotate(summed[:tok], cos, sin))
    key_part[...] = d_gain[None]
    total += dot(d_raw.astype(bf16), key_weight[...], (1, 1))
    total += dot(summed[tok:].astype(bf16), value_weight[...], (1, 1))
    payload[:, :width] = total.astype(bf16)
    payload[:, width : width + tok] = d_raw.T.astype(bf16)
    payload[:, width + tok :] = summed[tok:].T.astype(bf16)


def products_kernel(context, d_branch, d_query, normed, out):
    half = context.shape[1]
    out[:half] = dot(context[...], d_branch[...], (0, 0))
    out[half:] = dot(d_query[...], normed[...], (0, 0))


def entry_kernel(
    place, p0, p1, p2, p3, x, d_middle, gain, normed, post_part, ffw_part, final_part, query_part, key_part,
    products, input_grad, keep, give, rest
):
    lane, core = place[0], place[1]
    both = p0[...].astype(f32) + p1[...].astype(f32) + p2[...].astype(f32) + p3[...].astype(f32)
    rows = both.shape[0]
    width = normed.shape[1]
    tok = normed.shape[0]
    full = own_rows(x, lane, rows)
    d_values, d_gain = norm_back(full, inv_scale(full), gain[...], both[:, :width])
    input_grad[...] = (d_middle[...] + d_values).astype(bf16)
    d_keys = both[:, width : width + tok].astype(bf16)
    d_values = both[:, width + tok :].astype(bf16)
    rest[:rows] = dot(d_keys, normed[...], (1, 0))
    rest[rows : 2 * rows] = dot(d_values, normed[...], (1, 0))
    heads = jnp.concatenate(
        [query_part[...], key_part[...], jnp.zeros((1, width - 2 * query_part.shape[1]), f32)], axis=1
    )
    index = lax.broadcasted_iota(jnp.int32, (8, width), 0)
    gains = jnp.zeros((8, width), f32)
    for at, part in enumerate((d_gain[None], post_part[...], ffw_part[...], final_part[...], heads)):
        gains = jnp.where(index == at, part, gains)
    rest[2 * rows : 2 * rows + 8] = gains
    rest[2 * rows + 8 :] = jnp.zeros((rest.shape[0] - 2 * rows - 8, width), f32)
    for kind in range(3):
        source = rest if kind == 2 else products
        base = 256 if kind == 1 else 0
        for chip in range(16):
            at = base + 16 * chip
            keep[kind, chip] = source[pl.ds(pl.multiple_of(at + 8 * core, 8), 8)]
            give[kind, chip] = source[pl.ds(pl.multiple_of(at + 8 - 8 * core, 8), 8)].astype(bf16)


def merge_kernel(where, keep, got, *outs):
    core, first = where[0], where[1]
    for by, out in enumerate(outs):
        along = lax.rem(first + by, 4)
        for across in range(4):
            chip = jnp.where(core == 0, 4 * across + along, 4 * along + across)
            for kind in range(3):
                total = keep[kind, chip] + got[kind, chip].astype(f32)
                out[kind, across] = total.astype(out.dtype)


def weight_kernel(
    hid_own, hid_got, gate_own, gate_got, up_own, up_got, dy_own, dy_got, xn_own, xn_got, *outs
):
    mats = (
        (hid_own, hid_got, dy_own, dy_got),
        (gate_own, gate_got, xn_own, xn_got),
        (up_own, up_got, xn_own, xn_got),
    )
    for group, out in enumerate(outs):
        for index, (left_own, left_got, right_own, right_got) in enumerate(mats):
            total = jnp.dot(left_own[group], right_own[...], preferred_element_type=f32)
            total += jnp.dot(left_got[group], right_got[...], preferred_element_type=f32)
            total = total.astype(bf16)
            out[112 * index : 112 * index + 112] = total[:112]
            out[336 + 112 * index : 448 + 112 * index] = total[112:]


def weight_parts(*arrays):
    width = arrays[-1].shape[1]
    return pl.pallas_call(
        weight_kernel,
        out_shape=[jax.ShapeDtypeStruct((672, width), bf16)] * 4,
        in_specs=[pl.BlockSpec(memory_space=pltpu.VMEM)] * len(arrays),
        out_specs=[pl.BlockSpec(memory_space=pltpu.VMEM)] * 4,
        compiler_params=pltpu.CompilerParams(vmem_limit_bytes=SOME),
        cost_estimate=pl.CostEstimate(
            flops=2 * 2688 * 512 * width, bytes_accessed=12_000_000, transcendentals=0
        ),
    )(*arrays)


def halve_kernel(keep_a, got_a, keep_b, got_b, *outs):
    for keep, got, half in ((keep_a, got_a, outs[:2]), (keep_b, got_b, outs[2:])):
        for index, out in enumerate(half):
            rows = pl.ds(336 * index, 336)
            out[...] = (keep[rows].astype(f32) + got[rows].astype(f32)).astype(bf16)


def deal_kernel(where, keep_a, got_a, keep_b, got_b, *refs):
    outs, total = refs[:-1], refs[-1]
    total[0] = keep_a[...].astype(f32) + got_a[...].astype(f32)
    total[1] = keep_b[...].astype(f32) + got_b[...].astype(f32)
    for by, out in enumerate(outs):
        across = lax.rem(where[2] + by, 4)
        for mat in range(3):
            row = pl.multiple_of(112 * mat + 56 * lax.rem(across, 2), 8)
            out[mat] = total[across // 2, pl.ds(row, 56)].astype(out.dtype)


def masks(block, pairs):
    tok = pairs[0].shape[1]
    query = lax.broadcasted_iota(jnp.int32, (tok, tok), 0)
    key = lax.broadcasted_iota(jnp.int32, (tok, tok), 1)
    rows = [pair[2 * tok : 2 * tok + 16].astype(f32)[:1] for pair in pairs]
    segment = jnp.broadcast_to(rows[2], (tok, tok)).T
    same = [segment == row for row in rows]
    return (
        same[0] & (key > query) & (block >= 2),
        same[1] & (block >= 1),
        same[2] & (key <= query),
    )


def prepare_kernel(
    place, x, gain, key_weight, value_weight, query_weight, key_gain, query_gain, start_cos, start_sin, inner_cos,
    inner_sin, marks, xn, pair, k_raw, q_raw, queries, cosine, sine
):
    tok, head_dim = k_raw.shape
    full = x[...].astype(f32)
    low = (full * inv_scale(full) * gain[...]).astype(bf16)
    xn[...] = low
    at = pl.ds(place[2], 1)
    cos = start_cos[at] * inner_cos[...] - start_sin[at] * inner_sin[...]
    sin = start_sin[at] * inner_cos[...] + start_cos[at] * inner_sin[...]
    cosine[...] = cos
    sine[...] = sin
    raw = dot(low, key_weight[...], (1, 0))
    k_raw[...] = raw
    pair[:tok] = rotate(raw * inv_scale(raw) * key_gain[...], cos, sin).astype(bf16)
    pair[tok : 2 * tok] = dot(low, value_weight[...], (1, 0)).astype(bf16)
    pair[2 * tok :] = jnp.broadcast_to(marks[...].astype(f32)[None], (16, tok)).astype(bf16)
    raw = dot(low, query_weight[...], (1, 0))
    q_raw[...] = raw
    turned = rotate(raw * inv_scale(raw) * query_gain[...], cos, sin)
    queries[...] = (turned * head_dim**-0.5).astype(bf16)


def attend_kernel(place, queries, far, near, own, context, log_total):
    pairs = (far, near, own)
    tok = queries.shape[0]
    allowed = masks(place[2], pairs)
    scores = [
        jnp.where(ok, dot(queries[...], pair[:tok], (1, 1)), -1e30)
        for ok, pair in zip(allowed, pairs, strict=True)
    ]
    top = functools.reduce(jnp.maximum, [jnp.max(s, axis=1, keepdims=True) for s in scores])
    weights = [jnp.exp(s - top) for s in scores]
    total = sum(jnp.sum(w, axis=1, keepdims=True) for w in weights)
    context[...] = sum(
        dot((w / total).astype(bf16), pair[tok : 2 * tok], (1, 0))
        for w, pair in zip(weights, pairs, strict=True)
    ).astype(bf16)
    log_total[...] = jnp.broadcast_to(top + jnp.log(total), log_total.shape)


def attend(place, queries, pairs):
    tok, head_dim = queries.shape
    vmem = pl.BlockSpec(memory_space=pltpu.VMEM)
    return pl.pallas_call(
        attend_kernel,
        out_shape=[
            jax.ShapeDtypeStruct((tok, head_dim), bf16),
            jax.ShapeDtypeStruct((tok, 128), f32),
        ],
        in_specs=[pl.BlockSpec(memory_space=pltpu.SMEM)] + [vmem] * 4,
        out_specs=[vmem] * 2,
        compiler_params=pltpu.CompilerParams(vmem_limit_bytes=SOME),
        cost_estimate=pl.CostEstimate(
            flops=12 * tok * tok * head_dim, bytes_accessed=1_500_000, transcendentals=3 * tok * tok
        ),
    )(place, queries, *pairs)


def attend_back_kernel(
    place, log_total, d_branch, weight, queries, far, near, own, d_queries, d_far, d_near, d_own
):
    pairs = (far, near, own)
    tok = queries.shape[0]
    d_context = dot(d_branch[...], weight[...], (1, 1)).astype(bf16)
    allowed = masks(place[2], pairs)
    lse = log_total[:, :1]
    probs, d_probs = [], []
    for ok, pair in zip(allowed, pairs, strict=True):
        scores = jnp.where(ok, dot(queries[...], pair[:tok], (1, 1)), -1e30)
        probs.append(jnp.exp(scores - lse))
        d_probs.append(dot(d_context, pair[tok : 2 * tok], (1, 1)))
    mean = sum(
        jnp.sum(p * d, axis=1, keepdims=True) for p, d in zip(probs, d_probs, strict=True)
    )
    total = None
    for p, d, pair, out in zip(probs, d_probs, pairs, (d_far, d_near, d_own), strict=True):
        d_scores = (p * (d - mean)).astype(bf16)
        part = dot(d_scores, pair[:tok], (1, 0))
        total = part if total is None else total + part
        out[:tok] = dot(d_scores, queries[...], (0, 0)).astype(out.dtype)
        out[tok:] = dot(p.astype(bf16), d_context, (0, 0)).astype(out.dtype)
    d_queries[...] = total


def attend_back(place, log_total, d_branch, weight, queries, pairs):
    tok, head_dim = queries.shape
    vmem = pl.BlockSpec(memory_space=pltpu.VMEM)
    return pl.pallas_call(
        attend_back_kernel,
        out_shape=[
            jax.ShapeDtypeStruct((tok, head_dim), f32),
            jax.ShapeDtypeStruct((2 * tok, head_dim), bf16),
            jax.ShapeDtypeStruct((2 * tok, head_dim), bf16),
            jax.ShapeDtypeStruct((2 * tok, head_dim), f32),
        ],
        in_specs=[pl.BlockSpec(memory_space=pltpu.SMEM)] + [vmem] * 7,
        out_specs=[vmem] * 4,
        compiler_params=pltpu.CompilerParams(vmem_limit_bytes=SOME),
        cost_estimate=pl.CostEstimate(
            flops=30 * tok * tok * head_dim, bytes_accessed=3_500_000, transcendentals=3 * tok * tok
        ),
    )(place, log_total, d_branch, weight, queries, *pairs)


def place_kernel(where_ref, *refs, turns, held):
    n = len(turns)
    parts, outs = refs[:n], refs[n + held : n + held + 3]
    stage, sems, tail_sems = refs[-3:]
    slots = stage.shape[0]
    core, first, second = where_ref[0], where_ref[1], where_ref[2]
    chunks = [
        (ref, i, base + i, other, flip)
        for ref, (other, flip, base) in zip(parts, turns, strict=True)
        for i in range(ref.shape[0])
    ]

    def place(index):
        _, _, across, other, flip = chunks[index]
        which = 1 - core if other else core
        along = (second if other else first) ^ flip
        y = jnp.where(which == 0, along, across)
        z = jnp.where(which == 0, across, along)
        odd = lax.rem(y, 2)
        row = 216 * (2 * z + y // 2) + 104 * odd + 48 * which + 8 * which * odd
        return pl.multiple_of(row, 8), (which == 1) | (odd == 1)

    def copies(index):
        slot = index % slots
        row, whole = place(index)
        for mat, out in enumerate(outs):
            yield (
                pltpu.make_async_copy(
                    stage.at[slot, mat, pl.ds(0, 48)],
                    out.at[pl.ds(row, 48)],
                    sems.at[slot, mat],
                ),
                pltpu.make_async_copy(
                    stage.at[slot, mat, pl.ds(48, 8)],
                    out.at[pl.ds(pl.multiple_of(row + 48, 8), 8)],
                    tail_sems.at[slot, mat],
                ),
                whole,
            )

    def finish(index):
        for most, tail, whole in copies(index):
            most.wait()
            pl.when(whole)(tail.wait)

    for index, (ref, i, *_) in enumerate(chunks):
        if index >= slots:
            finish(index - slots)
        stage[index % slots] = ref[i].astype(f32)
        for most, tail, whole in copies(index):
            most.start()
            pl.when(whole)(tail.start)
    for index in range(max(0, len(chunks) - slots), len(chunks)):
        finish(index)


def placed(where, parts, outs, units):
    arrays = [p[0].reshape(-1, 3, 56, p[0].shape[-1]) for p in parts]
    width = arrays[0].shape[-1]
    slots = 4
    return pl.pallas_call(
        functools.partial(
            place_kernel, turns=tuple(p[1:] for p in parts), held=len(outs)
        ),
        out_shape=[jax.ShapeDtypeStruct((units, width), f32)] * 3,
        in_specs=[pl.BlockSpec(memory_space=pltpu.SMEM)]
        + [pl.BlockSpec(memory_space=pltpu.VMEM)] * len(arrays)
        + [pl.BlockSpec(memory_space=pl.ANY)] * len(outs),
        out_specs=[pl.BlockSpec(memory_space=pl.ANY)] * 3,
        scratch_shapes=[
            pltpu.VMEM((slots, 3, 56, width), f32),
            pltpu.SemaphoreType.DMA((slots, 3)),
            pltpu.SemaphoreType.DMA((slots, 3)),
        ],
        input_output_aliases={1 + len(arrays) + i: i for i in range(len(outs))},
        compiler_params=pltpu.CompilerParams(vmem_limit_bytes=SOME),
        cost_estimate=pl.CostEstimate(
            flops=0, bytes_accessed=sum(p.size for p in arrays) * 6, transcendentals=0
        ),
    )(where, *arrays, *outs)


def sorted_rows(core, own, got, rows, kinds):
    for pieces, other in ((own, 0), (got, 1)):
        even = core == other
        for along in range(4):
            for across in range(4):
                row = jnp.where(even, 8 * across + 2 * along, 8 * along + 2 * across + 1) * 8
                row = pl.ds(pl.multiple_of(row, 8), 8)
                for kind in range(kinds):
                    rows[kind, row] = pieces(kind, along, across).astype(f32)


def square_kernel(where, own, got, out_grad, query_grad, rows):
    sorted_rows(
        where[0],
        lambda kind, along, across: own[along, kind, across],
        lambda kind, along, across: got[along, kind, across],
        rows,
        2,
    )
    out_grad[...] = rows[0]
    query_grad[...] = rows[1].T


def finish_kernel(
    where, own, got, key_grad, value_grad, attn, post, ffw, final, query, key, rows
):
    sorted_rows(
        where[0],
        lambda lane, along, across: own[lane, along, across],
        lambda lane, along, across: got[lane, along, across],
        rows,
        4,
    )
    for lane in range(4):
        key_grad[:, 64 * lane : 64 * lane + 64] = rows[lane, :64].T
        value_grad[:, 64 * lane : 64 * lane + 64] = rows[lane, 64:128].T
    gains = sum(rows[lane, 128:136] for lane in range(4))
    for at, out in enumerate((attn, post, ffw, final)):
        out[...] = gains[at]
    size = query.shape[0]
    query[...] = gains[4, :size]
    key[...] = gains[4, size : 2 * size]


def local(
    layer_input,
    segment_ids,
    out_cotangent,
    attn_norm_gain,
    query_weight,
    key_weight,
    value_weight,
    query_gain,
    key_gain,
    output_weight,
    attn_post_gain,
    ffw_norm_gain,
    gate_weight,
    up_weight,
    down_weight,
    ffw_post_gain,
):
    tok, width = layer_input.shape
    head_dim = key_weight.shape[1]
    units = down_weight.shape[0]
    block = lax.axis_index("seq")
    lane = lax.axis_index("tensor")
    core = lax.rem(block, 2)
    row = lax.rem(lax.div(block, 2), 4)
    plane = lax.div(block, 8)
    first = lax.select(core == 0, row, plane)
    second = lax.select(core == 0, plane, row)
    place = jnp.stack([lane, core, block])
    where = jnp.stack([core, first, second])
    afters = [lax.rem(at + by, 4) for at in (lane, first, second) for by in range(4)]
    flips = [first ^ flip for flip in range(1, 4)]
    place, where, core, other_core, even, *places_at = tied(
        place, where, core, 1 - core, core == 0, *afters, *flips
    )
    lanes, firsts, seconds = places_at[:4], places_at[4:8], places_at[8:12]
    flips = [firsts[0], *places_at[12:]]
    quarter_tok = tok // 4

    freq = rope_base ** (-2.0 * np.arange(head_dim // 2) / head_dim)
    start = (np.arange(lax.axis_size("seq")) * tok)[:, None] * freq[None, :]
    inner = np.arange(tok)[:, None] * freq[None, :]
    tables = [jnp.asarray(f(angle), f32) for angle in (start, inner) for f in (np.cos, np.sin)]

    square = (tok, head_dim)
    normed, own_pair, k_raw, q_raw, queries, cosine, sine = call(
        prepare_kernel,
        [
            ((tok, width), bf16),
            ((2 * tok + 16, head_dim), bf16),
            (square, f32),
            (square, f32),
            (square, bf16),
            ((tok, head_dim // 2), f32),
            ((tok, head_dim // 2), f32),
        ],
        place,
        layer_input,
        attn_norm_gain,
        key_weight,
        value_weight,
        query_weight,
        key_gain,
        query_gain,
        *tables,
        segment_ids,
        scalars=1,
        flops=6 * tok * width * head_dim,
        room=MOST,
    )
    left_one = shifted(own_pair, 1)
    left_two = shifted(own_pair, 2)

    weight_half = tok // 2
    halved, _ = tied(output_weight, own_pair)
    own_weight = pick(halved.reshape(2, weight_half, width), core)
    got_weight = [send(own_weight, round_x(by)) for by in (1, 2, 3)]

    pairs = (left_two, left_one, own_pair)
    context, log_total = attend(place, queries, pairs)

    got_context = [send(context, round_x(by)) for by in (1, 2, 3)]
    *got_context, got_weight[0], got_weight[1], got_weight[2] = tied(*got_context, *got_weight)
    other_weight = [send(part, swap_cores()) for part in got_weight]
    branch, middle, normed_two = call(
        project_kernel,
        [((tok, width), f32), ((tok, width), f32), ((tok, width), bf16)],
        place,
        layer_input,
        attn_post_gain,
        ffw_norm_gain,
        context,
        *got_context,
        output_weight,
        *got_weight,
        *other_weight,
        scalars=1,
        flops=8 * tok * tok * width,
    )
    gate = dot(gate_weight, normed_two, (0, 1))
    up_val = dot(up_weight, normed_two, (0, 1))
    active, gelu_back = jax.vjp(lambda val: jax.nn.gelu(val, approximate=True), gate)
    hidden = (active * up_val).astype(bf16)
    down_part = dot(hidden, down_weight, (0, 0)).astype(bf16)

    def halves(values):
        groups = values.reshape(8, units // 8, tok)
        groups = jnp.concatenate([groups[:, :56], groups[:, 48:]], axis=1)
        pieces = groups.reshape(4, 4, 2, 56, tok)
        return pick(pieces, core, 2), pick(pieces, other_core, 2)

    def arranged(values):
        values = jnp.where(even, values.swapaxes(0, 1), values)
        by_first = [pick(values, flip) for flip in flips]
        groups = [
            jnp.stack([by_first[i][2 * stream : 2 * stream + 2] for i in order])
            for stream, order in ((0, (0, 3)), (0, (1, 2)), (1, (0, 1)), (1, (3, 2)))
        ]
        return jnp.stack(groups).reshape(4, 224, tok)

    hidden_own, hidden_give = halves(hidden)
    hidden_got = send(hidden_give, swap_cores())
    normed_two_got = send(normed_two, swap_cores())

    def quarters(parts):
        parts = parts.reshape(4, quarter_tok, parts.shape[-1])
        given = [pick(parts, at) for at in lanes[1:]]
        return [pick(parts, lanes[0])] + [
            send(part, round_x(by)) for by, part in zip((1, 2, 3), given, strict=True)
        ]

    piece = (quarter_tok, width)
    out_own, d_branch_two, final_part = call(
        final_kernel,
        [(piece, bf16), (piece, bf16), ((1, width), f32)],
        place,
        *quarters(down_part),
        middle,
        out_cotangent,
        ffw_post_gain,
        scalars=1,
    )
    d_branch_two = gather(d_branch_two, lanes, round_x).reshape(tok, width)
    d_branch_two_got = send(d_branch_two, swap_cores())

    d_hidden = dot(down_weight, d_branch_two, (1, 1))
    d_gate = gelu_back(d_hidden * up_val)[0].astype(bf16)
    d_up = (d_hidden * active).astype(bf16)
    d_normed_two = (dot(d_gate, gate_weight, (0, 1)) + dot(d_up, up_weight, (0, 1))).astype(bf16)
    d_gate_own, d_gate_give = halves(d_gate)
    d_up_own, d_up_give = halves(d_up)
    d_pair_got = send(jnp.stack([d_gate_give, d_up_give]), swap_cores())

    keep_a, give_a, keep_b, give_b = weight_parts(
        *(
            arranged(v)
            for v in (hidden_own, hidden_got, d_gate_own, d_pair_got[0], d_up_own, d_pair_got[1])
        ),
        d_branch_two,
        d_branch_two_got,
        normed_two,
        normed_two_got,
    )
    got_a = send(give_a, along_first(1))
    got_b = send(give_b, along_first(3))

    *got_normed, keep_a, keep_b = tied(*quarters(d_normed_two), keep_a, keep_b)
    d_middle, d_branch, ffw_part, post_part = call(
        between_kernel,
        [(piece, f32), (piece, bf16), ((1, width), f32), ((1, width), f32)],
        place,
        *got_normed,
        middle,
        branch,
        out_cotangent,
        ffw_norm_gain,
        attn_post_gain,
        scalars=1,
    )
    d_branch = gather(d_branch, lanes, round_x).reshape(tok, width)
    d_queries, left_far, left_near, summed = attend_back(
        place, log_total, d_branch, output_weight, queries, pairs
    )
    got_near = shifted(left_near, -1)
    got_far = shifted(left_far, -2)
    got_near, got_far, got_a, got_b = tied(got_near, got_far, got_a, got_b)
    keep_a, give_a, keep_b, give_b = call(
        halve_kernel, [((336, width), bf16)] * 4, keep_a, got_a, keep_b, got_b
    )
    got_a = send(give_a, along_first(3))
    got_b = send(give_b, along_first(1))
    d_query, payload, query_part, key_part = call(
        key_kernel,
        [
            (square, bf16),
            ((tok, width + 2 * tok), bf16),
            ((1, head_dim), f32),
            ((1, head_dim), f32),
        ],
        q_raw,
        k_raw,
        d_queries,
        summed,
        got_near,
        got_far,
        cosine,
        sine,
        query_gain,
        key_gain,
        query_weight,
        key_weight,
        value_weight,
        flops=6 * tok * width * head_dim,
    )
    got_both = quarters(payload)
    (products,) = call(
        products_kernel,
        [((2 * head_dim, width), f32)],
        context,
        d_branch,
        d_query,
        normed,
        flops=4 * tok * width * head_dim,
    )
    *got_both, got_a, got_b = tied(*got_both, got_a, got_b)
    chunk = (3, 56, width)
    mine, *given = call(
        deal_kernel,
        [(chunk, f32)] + [(chunk, bf16)] * 3,
        where,
        keep_a,
        got_a,
        keep_b,
        got_b,
        scalars=1,
        scratch=[pltpu.VMEM((2, 336, width), f32)],
    )
    got = [send(part, round_second(by)) for by, part in zip((1, 2, 3), given, strict=True)]
    input_own, keep, give = pl.pallas_call(
        entry_kernel,
        out_shape=[
            jax.ShapeDtypeStruct(piece, bf16),
            jax.ShapeDtypeStruct((3, 16, 8, width), f32),
            jax.ShapeDtypeStruct((3, 16, 8, width), bf16),
        ],
        in_specs=[pl.BlockSpec(memory_space=pltpu.SMEM)]
        + [pl.BlockSpec(memory_space=pltpu.VMEM)] * 14,
        out_specs=[pl.BlockSpec(memory_space=pltpu.VMEM)] * 3,
        scratch_shapes=[pltpu.VMEM((tok, width), f32)],
        compiler_params=pltpu.CompilerParams(vmem_limit_bytes=SOME),
        cost_estimate=pl.CostEstimate(
            flops=256 * tok * width, bytes_accessed=12_000_000, transcendentals=0
        ),
    )(
        place,
        *got_both,
        layer_input,
        d_middle,
        attn_norm_gain,
        normed,
        post_part,
        ffw_part,
        final_part,
        query_part,
        key_part,
        products,
    )
    pack_got = send(give, swap_cores())
    part = (3, 4, 8, width)
    pack, *given = call(
        merge_kernel, [(part, f32)] + [(part, bf16)] * 3, where, keep, pack_got, scalars=1
    )
    given = [send(part, round_first(by)) for by, part in zip((1, 2, 3), given, strict=True)]
    *given, got[0], got[1], got[2] = tied(*given, *got)
    mine = mine + got[0].astype(f32) + (got[1].astype(f32) + got[2].astype(f32))
    mine = mine.astype(bf16).reshape(168, width)
    for part in given:
        pack = pack + part.astype(f32)
    pack = pack.astype(bf16).reshape(96, width)
    both = lax.optimization_barrier(jnp.concatenate([mine, pack]))
    given = [send(both, round_second(by)) for by in (1, 2, 3)]
    ends = jnp.concatenate([out_own, input_own])
    got_ends = [send(ends, round_x(by)) for by in (1, 2, 3)]
    given[0], given[1], given[2], *got_ends = tied(*given, *got_ends)
    ends = joined(ends, got_ends, lanes)
    layer_output = ends[:, :64].reshape(tok, width)
    input_grad = ends[:, 64:].reshape(tok, width)
    quarter = joined(both[:168], [part[:168] for part in given], seconds)
    pack, *given = (part[168:].astype(f32) for part in (both, *given))
    pack = (pack + given[1] + (given[0] + given[2])).astype(bf16).reshape(3, 4, 8, width)
    given = [send(pack, round_first(by)) for by in (1, 2, 3)]
    given[0], quarter = tied(given[0], quarter)
    near_a = send(quarter, along_first(1))
    near_b = send(quarter, along_first(3))
    other_own = send(quarter, swap_cores())
    pack = joined(pack, given, firsts)
    pack_got = send(pack, swap_cores())
    rest = pack[:, 2]
    given = [send(rest, round_x(by)) for by in (1, 2, 3)]
    out_grad, query_grad = call(
        square_kernel,
        [((256, width), f32), ((width, 256), f32)],
        where,
        pack,
        pack_got,
        scalars=1,
        scratch=[pltpu.VMEM((2, 256, width), f32)],
    )
    *given, near_a, near_b = tied(*given, near_a, near_b)
    far_a = send(near_b[:2], along_first(1))
    far_b = send(near_a[2:], along_first(3))
    other_a = send(near_a, swap_cores())
    other_b = send(near_b, swap_cores())
    rest = joined(rest, given, lanes)
    rest_got = send(rest, swap_cores())
    grads = placed(
        where,
        [
            (quarter, False, 0, 0),
            (near_a, False, 1, 0),
            (near_b, False, 3, 0),
            (other_own, True, 0, 0),
            (other_a, True, 1, 0),
            (other_b, True, 3, 0),
        ],
        [],
        units,
    )
    key_grad, value_grad, *gains = call(
        finish_kernel,
        [((width, 256), f32)] * 2 + [((width,), f32)] * 4 + [((256,), f32)] * 2,
        where,
        rest,
        rest_got,
        scalars=1,
        scratch=[pltpu.VMEM((4, 256, width), f32)],
    )
    far_a, far_b, *grads = tied(far_a, far_b, *grads)
    other_far_a = send(far_a, swap_cores())
    other_far_b = send(far_b, swap_cores())
    down_grad, gate_grad, up_grad = placed(
        where,
        [
            (far_a, False, 2, 0),
            (far_b, False, 2, 2),
            (other_far_a, True, 2, 0),
            (other_far_b, True, 2, 2),
        ],
        grads,
        units,
    )
    return (
        layer_output,
        input_grad,
        gains[0],
        query_grad,
        key_grad,
        value_grad,
        gains[4],
        gains[5],
        out_grad,
        gains[1],
        gains[2],
        gate_grad.T,
        up_grad.T,
        down_grad,
        gains[3],
    )


def solution(mesh):
    rows = P("seq", None)
    return jax.shard_map(
        local,
        mesh=mesh,
        in_specs=(
            rows,
            P("seq"),
            rows,
            P(),
            P(None, "tensor"),
            P(),
            P(),
            P(),
            P(),
            P("tensor", None),
            P(),
            P(),
            P(None, "tensor"),
            P(None, "tensor"),
            P("tensor", None),
            P(),
        ),
        out_specs=(
            rows,
            rows,
            P(),
            P(None, "tensor"),
            P(),
            P(),
            P(),
            P(),
            P("tensor", None),
            P(),
            P(),
            P(None, "tensor"),
            P(None, "tensor"),
            P("tensor", None),
            P(),
        ),
        check_vma=False,
    )
```

```python
import functools

import jax
import jax.numpy as jnp
import numpy as np
from jax import lax
from jax.experimental import pallas as pl
from jax.experimental.pallas import tpu as pltpu
from jax.sharding import PartitionSpec as P

WINDOW = 512
SOME = 24 * 1024 * 1024
MOST = 60 * 1024 * 1024

eps = 1e-06
rope_base = 10000.0
f32 = jnp.float32
bf16 = jnp.bfloat16
BOTH = ("seq", "tensor")


def places():
    return [(z, y, c, x) for z in range(4) for y in range(4) for c in range(2) for x in range(4)]


def number(z, y, c, x):
    return ((z * 4 + y) * 2 + c) * 4 + x


def route(move):
    return [(number(*p), number(*move(*p))) for p in places()]


def round_x(by):
    return route(lambda z, y, c, x: (z, y, c, (x + by) % 4))


def swap_cores():
    return route(lambda z, y, c, x: (z, y, 1 - c, x))


def along_first(flip):
    return route(lambda z, y, c, x: (z, y ^ flip, c, x) if c == 0 else (z ^ flip, y, c, x))


def round_first(by):
    return route(
        lambda z, y, c, x: (z, (y + by) % 4, c, x) if c == 0 else ((z + by) % 4, y, c, x)
    )


def round_second(by):
    return route(
        lambda z, y, c, x: ((z + by) % 4, y, c, x) if c == 0 else (z, (y + by) % 4, c, x)
    )


def send(value, pairs):
    return lax.ppermute(value, BOTH, pairs)


def shifted(value, by):
    pairs = [
        (i * 4 + x, (i + by) * 4 + x) for i in range(32) if 0 <= i + by < 32 for x in range(4)
    ]
    return send(value, pairs)


def pick(parts, index, axis=0):
    return lax.dynamic_index_in_dim(
        parts, index, axis, keepdims=False, allow_negative_indices=False
    )


def put(parts, part, index):
    return lax.dynamic_update_index_in_dim(parts, part, index, 0, allow_negative_indices=False)


def dot(first, second, over):
    return lax.dot_general(
        first, second, (((over[0],), (over[1],)), ((), ())), preferred_element_type=f32
    )


def joined(own, got, after):
    whole = put(jnp.zeros((4, *own.shape), own.dtype), own, after[0])
    for by, part in zip((1, 2, 3), got, strict=True):
        whole = put(whole, part, after[4 - by])
    return whole


def gather(part, after, turn):
    return joined(part, [send(part, turn(by)) for by in (1, 2, 3)], after)


def inv_scale(values):
    return lax.rsqrt(jnp.mean(values * values, axis=-1, keepdims=True) + eps)


def norm_back(values, scale, gain, grad):
    unit = values * scale
    weighted = grad * gain
    d_values = scale * (weighted - unit * jnp.mean(weighted * unit, axis=-1, keepdims=True))
    return (d_values, jnp.sum(grad * unit, axis=0))


def rotate(values, cosine, sine):
    half = values.shape[-1] // 2
    first = values[..., :half]
    second = values[..., half:]
    return jnp.concatenate(
        [first * cosine - second * sine, second * cosine + first * sine], axis=-1
    )


def padded(values, rows):
    return jnp.pad(values, ((0, rows - values.shape[0]), (0, 0)))


def added(first, second):
    return (first.astype(f32) + second.astype(f32)).astype(bf16)


def tied(*values):
    return lax.optimization_barrier(values)


def call(kernel, outs, *arrays, scalars=0, flops=0, room=SOME, scratch=()):
    vmem = pl.BlockSpec(memory_space=pltpu.VMEM)
    outs = [jax.ShapeDtypeStruct(*o) for o in outs]
    moved = sum(v.size * v.dtype.itemsize for v in (*arrays, *outs))
    return pl.pallas_call(
        kernel,
        out_shape=outs,
        in_specs=[pl.BlockSpec(memory_space=pltpu.SMEM)] * scalars
        + [vmem] * (len(arrays) - scalars),
        out_specs=[vmem] * len(outs),
        scratch_shapes=scratch,
        compiler_params=pltpu.CompilerParams(vmem_limit_bytes=room),
        cost_estimate=pl.CostEstimate(flops=flops, bytes_accessed=moved, transcendentals=0),
    )(*arrays)


def own_rows(ref, lane, rows):
    return ref[pl.ds(pl.multiple_of(lane * rows, rows), rows)].astype(f32)


def project_kernel(
    place, x, post_gain, ffw_gain, ctx0, ctx1, ctx2, ctx3, weight, own1, own2, own3, other1, other2, other3,
    branch, middle, normed
):
    even = place[1] == 0
    half = own1.shape[0]
    total = dot(ctx0[...], weight[...], (1, 0))
    for ctx, mine, theirs in ((ctx1, own1, other1), (ctx2, own2, other2), (ctx3, own3, other3)):
        low = jnp.where(even, mine[...], theirs[...])
        high = jnp.where(even, theirs[...], mine[...])
        total += dot(ctx[:, :half], low, (1, 0)) + dot(ctx[:, half:], high, (1, 0))
    branch[...] = total
    after = x[...].astype(f32) + total * inv_scale(total) * post_gain[...]
    middle[...] = after
    normed[...] = (after * inv_scale(after) * ffw_gain[...]).astype(bf16)


def final_kernel(place, p0, p1, p2, p3, middle, cotangent, gain, out, d_branch, part):
    lane = place[0]
    branch = p0[...].astype(f32) + p1[...].astype(f32) + p2[...].astype(f32) + p3[...].astype(f32)
    rows = branch.shape[0]
    scale = inv_scale(branch)
    cot = own_rows(cotangent, lane, rows)
    out[...] = (own_rows(middle, lane, rows) + branch * scale * gain[...]).astype(bf16)
    d_values, d_gain = norm_back(branch, scale, gain[...], cot)
    d_branch[...] = d_values.astype(bf16)
    part[...] = d_gain[None]


def between_kernel(
    place, p0, p1, p2, p3, middle, branch, cotangent, ffw_gain, post_gain,
    d_middle, d_branch, ffw_part, post_part
):
    lane = place[0]
    grad = p0[...].astype(f32) + p1[...].astype(f32) + p2[...].astype(f32) + p3[...].astype(f32)
    rows = grad.shape[0]
    after = own_rows(middle, lane, rows)
    before = own_rows(branch, lane, rows)
    d_values, d_gain = norm_back(after, inv_scale(after), ffw_gain[...], grad)
    ffw_part[...] = d_gain[None]
    d_values = own_rows(cotangent, lane, rows) + d_values
    d_middle[...] = d_values
    d_values, d_gain = norm_back(before, inv_scale(before), post_gain[...], d_values)
    d_branch[...] = d_values.astype(bf16)
    post_part[...] = d_gain[None]


def key_kernel(
    q_raw, k_raw, d_queries, d_own, d_near, d_far, cosine, sine, query_gain, key_gain, query_weight, key_weight,
    value_weight, d_query, payload, query_part, key_part
):
    tok, head_dim = q_raw.shape
    width = query_weight.shape[0]
    cos, sin = cosine[...], -sine[...]
    raw = q_raw[...]
    d_raw, d_gain = norm_back(
        raw, inv_scale(raw), query_gain[...], rotate(d_queries[...] * head_dim**-0.5, cos, sin)
    )
    query_part[...] = d_gain[None]
    d_low = d_raw.astype(bf16)
    d_query[...] = d_low
    total = dot(d_low, query_weight[...], (1, 1))
    summed = d_own[...] + d_near[...].astype(f32) + d_far[...].astype(f32)
    raw = k_raw[...]
    d_raw, d_gain = norm_back(raw, inv_scale(raw), key_gain[...], rotate(summed[:tok], cos, sin))
    key_part[...] = d_gain[None]
    total += dot(d_raw.astype(bf16), key_weight[...], (1, 1))
    total += dot(summed[tok:].astype(bf16), value_weight[...], (1, 1))
    payload[:, :width] = total.astype(bf16)
    payload[:, width : width + tok] = d_raw.T.astype(bf16)
    payload[:, width + tok :] = summed[tok:].T.astype(bf16)


def products_kernel(context, d_branch, d_query, normed, out):
    half = context.shape[1]
    out[:half] = dot(context[...], d_branch[...], (0, 0))
    out[half:] = dot(d_query[...], normed[...], (0, 0))


def entry_kernel(
    place, p0, p1, p2, p3, x, d_middle, gain, normed, post_part, ffw_part, final_part, query_part, key_part,
    products, input_grad, keep, give, rest
):
    lane, core = place[0], place[1]
    both = p0[...].astype(f32) + p1[...].astype(f32) + p2[...].astype(f32) + p3[...].astype(f32)
    rows = both.shape[0]
    width = normed.shape[1]
    tok = normed.shape[0]
    full = own_rows(x, lane, rows)
    d_values, d_gain = norm_back(full, inv_scale(full), gain[...], both[:, :width])
    input_grad[...] = (d_middle[...] + d_values).astype(bf16)
    d_keys = both[:, width : width + tok].astype(bf16)
    d_values = both[:, width + tok :].astype(bf16)
    rest[:rows] = dot(d_keys, normed[...], (1, 0))
    rest[rows : 2 * rows] = dot(d_values, normed[...], (1, 0))
    heads = jnp.concatenate(
        [query_part[...], key_part[...], jnp.zeros((1, width - 2 * query_part.shape[1]), f32)], axis=1
    )
    index = lax.broadcasted_iota(jnp.int32, (8, width), 0)
    gains = jnp.zeros((8, width), f32)
    for at, part in enumerate((d_gain[None], post_part[...], ffw_part[...], final_part[...], heads)):
        gains = jnp.where(index == at, part, gains)
    rest[2 * rows : 2 * rows + 8] = gains
    rest[2 * rows + 8 :] = jnp.zeros((rest.shape[0] - 2 * rows - 8, width), f32)
    for kind in range(3):
        source = rest if kind == 2 else products
        base = 256 if kind == 1 else 0
        for chip in range(16):
            at = base + 16 * chip
            keep[kind, chip] = source[pl.ds(pl.multiple_of(at + 8 * core, 8), 8)]
            give[kind, chip] = source[pl.ds(pl.multiple_of(at + 8 - 8 * core, 8), 8)].astype(bf16)


def merge_kernel(where, keep, got, *outs):
    core, first = where[0], where[1]
    for by, out in enumerate(outs):
        along = lax.rem(first + by, 4)
        for across in range(4):
            chip = jnp.where(core == 0, 4 * across + along, 4 * along + across)
            for kind in range(3):
                total = keep[kind, chip] + got[kind, chip].astype(f32)
                out[kind, across] = total.astype(out.dtype)


def weight_kernel(
    hid_own, hid_got, gate_own, gate_got, up_own, up_got, dy_own, dy_got, xn_own, xn_got, *outs
):
    mats = (
        (hid_own, hid_got, dy_own, dy_got),
        (gate_own, gate_got, xn_own, xn_got),
        (up_own, up_got, xn_own, xn_got),
    )
    for group, out in enumerate(outs):
        for index, (left_own, left_got, right_own, right_got) in enumerate(mats):
            total = jnp.dot(left_own[group], right_own[...], preferred_element_type=f32)
            total += jnp.dot(left_got[group], right_got[...], preferred_element_type=f32)
            total = total.astype(bf16)
            out[112 * index : 112 * index + 112] = total[:112]
            out[336 + 112 * index : 448 + 112 * index] = total[112:]


def weight_parts(*arrays):
    width = arrays[-1].shape[1]
    return pl.pallas_call(
        weight_kernel,
        out_shape=[jax.ShapeDtypeStruct((672, width), bf16)] * 4,
        in_specs=[pl.BlockSpec(memory_space=pltpu.VMEM)] * len(arrays),
        out_specs=[pl.BlockSpec(memory_space=pltpu.VMEM)] * 4,
        compiler_params=pltpu.CompilerParams(vmem_limit_bytes=SOME),
        cost_estimate=pl.CostEstimate(
            flops=2 * 2688 * 512 * width, bytes_accessed=12_000_000, transcendentals=0
        ),
    )(*arrays)


def halve_kernel(keep_a, got_a, keep_b, got_b, *outs):
    for keep, got, half in ((keep_a, got_a, outs[:2]), (keep_b, got_b, outs[2:])):
        for index, out in enumerate(half):
            rows = pl.ds(336 * index, 336)
            out[...] = (keep[rows].astype(f32) + got[rows].astype(f32)).astype(bf16)


def deal_kernel(where, keep_a, got_a, keep_b, got_b, *refs):
    outs, total = refs[:-1], refs[-1]
    total[0] = keep_a[...].astype(f32) + got_a[...].astype(f32)
    total[1] = keep_b[...].astype(f32) + got_b[...].astype(f32)
    for by, out in enumerate(outs):
        across = lax.rem(where[2] + by, 4)
        for mat in range(3):
            row = pl.multiple_of(112 * mat + 56 * lax.rem(across, 2), 8)
            out[mat] = total[across // 2, pl.ds(row, 56)].astype(out.dtype)


def masks(block, pairs):
    tok = pairs[0].shape[1]
    query = lax.broadcasted_iota(jnp.int32, (tok, tok), 0)
    key = lax.broadcasted_iota(jnp.int32, (tok, tok), 1)
    rows = [pair[2 * tok : 2 * tok + 16].astype(f32)[:1] for pair in pairs]
    segment = jnp.broadcast_to(rows[2], (tok, tok)).T
    same = [segment == row for row in rows]
    return (
        same[0] & (key > query) & (block >= 2),
        same[1] & (block >= 1),
        same[2] & (key <= query),
    )


def prepare_kernel(
    place, x, gain, key_weight, value_weight, query_weight, key_gain, query_gain, start_cos, start_sin, inner_cos,
    inner_sin, marks, xn, pair, k_raw, q_raw, queries, cosine, sine
):
    tok, head_dim = k_raw.shape
    full = x[...].astype(f32)
    low = (full * inv_scale(full) * gain[...]).astype(bf16)
    xn[...] = low
    at = pl.ds(place[2], 1)
    cos = start_cos[at] * inner_cos[...] - start_sin[at] * inner_sin[...]
    sin = start_sin[at] * inner_cos[...] + start_cos[at] * inner_sin[...]
    cosine[...] = cos
    sine[...] = sin
    raw = dot(low, key_weight[...], (1, 0))
    k_raw[...] = raw
    pair[:tok] = rotate(raw * inv_scale(raw) * key_gain[...], cos, sin).astype(bf16)
    pair[tok : 2 * tok] = dot(low, value_weight[...], (1, 0)).astype(bf16)
    pair[2 * tok :] = jnp.broadcast_to(marks[...].astype(f32)[None], (16, tok)).astype(bf16)
    raw = dot(low, query_weight[...], (1, 0))
    q_raw[...] = raw
    turned = rotate(raw * inv_scale(raw) * query_gain[...], cos, sin)
    queries[...] = (turned * head_dim**-0.5).astype(bf16)


def attend_kernel(place, queries, far, near, own, context, log_total):
    pairs = (far, near, own)
    tok = queries.shape[0]
    allowed = masks(place[2], pairs)
    scores = [
        jnp.where(ok, dot(queries[...], pair[:tok], (1, 1)), -1e30)
        for ok, pair in zip(allowed, pairs, strict=True)
    ]
    top = functools.reduce(jnp.maximum, [jnp.max(s, axis=1, keepdims=True) for s in scores])
    weights = [jnp.exp(s - top) for s in scores]
    total = sum(jnp.sum(w, axis=1, keepdims=True) for w in weights)
    context[...] = sum(
        dot((w / total).astype(bf16), pair[tok : 2 * tok], (1, 0))
        for w, pair in zip(weights, pairs, strict=True)
    ).astype(bf16)
    log_total[...] = jnp.broadcast_to(top + jnp.log(total), log_total.shape)


def attend(place, queries, pairs):
    tok, head_dim = queries.shape
    vmem = pl.BlockSpec(memory_space=pltpu.VMEM)
    return pl.pallas_call(
        attend_kernel,
        out_shape=[
            jax.ShapeDtypeStruct((tok, head_dim), bf16),
            jax.ShapeDtypeStruct((tok, 128), f32),
        ],
        in_specs=[pl.BlockSpec(memory_space=pltpu.SMEM)] + [vmem] * 4,
        out_specs=[vmem] * 2,
        compiler_params=pltpu.CompilerParams(vmem_limit_bytes=SOME),
        cost_estimate=pl.CostEstimate(
            flops=12 * tok * tok * head_dim, bytes_accessed=1_500_000, transcendentals=3 * tok * tok
        ),
    )(place, queries, *pairs)


def attend_back_kernel(
    place, log_total, d_branch, weight, queries, far, near, own, d_queries, d_far, d_near, d_own
):
    pairs = (far, near, own)
    tok = queries.shape[0]
    d_context = dot(d_branch[...], weight[...], (1, 1)).astype(bf16)
    allowed = masks(place[2], pairs)
    lse = log_total[:, :1]
    probs, d_probs = [], []
    for ok, pair in zip(allowed, pairs, strict=True):
        scores = jnp.where(ok, dot(queries[...], pair[:tok], (1, 1)), -1e30)
        probs.append(jnp.exp(scores - lse))
        d_probs.append(dot(d_context, pair[tok : 2 * tok], (1, 1)))
    mean = sum(
        jnp.sum(p * d, axis=1, keepdims=True) for p, d in zip(probs, d_probs, strict=True)
    )
    total = None
    for p, d, pair, out in zip(probs, d_probs, pairs, (d_far, d_near, d_own), strict=True):
        d_scores = (p * (d - mean)).astype(bf16)
        part = dot(d_scores, pair[:tok], (1, 0))
        total = part if total is None else total + part
        out[:tok] = dot(d_scores, queries[...], (0, 0)).astype(out.dtype)
        out[tok:] = dot(p.astype(bf16), d_context, (0, 0)).astype(out.dtype)
    d_queries[...] = total


def attend_back(place, log_total, d_branch, weight, queries, pairs):
    tok, head_dim = queries.shape
    vmem = pl.BlockSpec(memory_space=pltpu.VMEM)
    return pl.pallas_call(
        attend_back_kernel,
        out_shape=[
            jax.ShapeDtypeStruct((tok, head_dim), f32),
            jax.ShapeDtypeStruct((2 * tok, head_dim), bf16),
            jax.ShapeDtypeStruct((2 * tok, head_dim), bf16),
            jax.ShapeDtypeStruct((2 * tok, head_dim), f32),
        ],
        in_specs=[pl.BlockSpec(memory_space=pltpu.SMEM)] + [vmem] * 7,
        out_specs=[vmem] * 4,
        compiler_params=pltpu.CompilerParams(vmem_limit_bytes=SOME),
        cost_estimate=pl.CostEstimate(
            flops=30 * tok * tok * head_dim, bytes_accessed=3_500_000, transcendentals=3 * tok * tok
        ),
    )(place, log_total, d_branch, weight, queries, *pairs)


def place_kernel(where_ref, *refs, turns, held):
    n = len(turns)
    parts, outs = refs[:n], refs[n + held : n + held + 3]
    stage, sems, tail_sems = refs[-3:]
    slots = stage.shape[0]
    core, first, second = where_ref[0], where_ref[1], where_ref[2]
    chunks = [
        (ref, i, base + i, other, flip)
        for ref, (other, flip, base) in zip(parts, turns, strict=True)
        for i in range(ref.shape[0])
    ]

    def place(index):
        _, _, across, other, flip = chunks[index]
        which = 1 - core if other else core
        along = (second if other else first) ^ flip
        y = jnp.where(which == 0, along, across)
        z = jnp.where(which == 0, across, along)
        odd = lax.rem(y, 2)
        row = 216 * (2 * z + y // 2) + 104 * odd + 48 * which + 8 * which * odd
        return pl.multiple_of(row, 8), (which == 1) | (odd == 1)

    def copies(index):
        slot = index % slots
        row, whole = place(index)
        for mat, out in enumerate(outs):
            yield (
                pltpu.make_async_copy(
                    stage.at[slot, mat, pl.ds(0, 48)],
                    out.at[pl.ds(row, 48)],
                    sems.at[slot, mat],
                ),
                pltpu.make_async_copy(
                    stage.at[slot, mat, pl.ds(48, 8)],
                    out.at[pl.ds(pl.multiple_of(row + 48, 8), 8)],
                    tail_sems.at[slot, mat],
                ),
                whole,
            )

    def finish(index):
        for most, tail, whole in copies(index):
            most.wait()
            pl.when(whole)(tail.wait)

    for index, (ref, i, *_) in enumerate(chunks):
        if index >= slots:
            finish(index - slots)
        stage[index % slots] = ref[i].astype(f32)
        for most, tail, whole in copies(index):
            most.start()
            pl.when(whole)(tail.start)
    for index in range(max(0, len(chunks) - slots), len(chunks)):
        finish(index)


def placed(where, parts, outs, units):
    arrays = [p[0].reshape(-1, 3, 56, p[0].shape[-1]) for p in parts]
    width = arrays[0].shape[-1]
    slots = 4
    return pl.pallas_call(
        functools.partial(
            place_kernel, turns=tuple(p[1:] for p in parts), held=len(outs)
        ),
        out_shape=[jax.ShapeDtypeStruct((units, width), f32)] * 3,
        in_specs=[pl.BlockSpec(memory_space=pltpu.SMEM)]
        + [pl.BlockSpec(memory_space=pltpu.VMEM)] * len(arrays)
        + [pl.BlockSpec(memory_space=pl.ANY)] * len(outs),
        out_specs=[pl.BlockSpec(memory_space=pl.ANY)] * 3,
        scratch_shapes=[
            pltpu.VMEM((slots, 3, 56, width), f32),
            pltpu.SemaphoreType.DMA((slots, 3)),
            pltpu.SemaphoreType.DMA((slots, 3)),
        ],
        input_output_aliases={1 + len(arrays) + i: i for i in range(len(outs))},
        compiler_params=pltpu.CompilerParams(vmem_limit_bytes=SOME),
        cost_estimate=pl.CostEstimate(
            flops=0, bytes_accessed=sum(p.size for p in arrays) * 6, transcendentals=0
        ),
    )(where, *arrays, *outs)


def sorted_rows(core, own, got, rows, kinds):
    for pieces, other in ((own, 0), (got, 1)):
        even = core == other
        for along in range(4):
            for across in range(4):
                row = jnp.where(even, 8 * across + 2 * along, 8 * along + 2 * across + 1) * 8
                row = pl.ds(pl.multiple_of(row, 8), 8)
                for kind in range(kinds):
                    rows[kind, row] = pieces(kind, along, across).astype(f32)


def square_kernel(where, own, got, out_grad, query_grad, rows):
    sorted_rows(
        where[0],
        lambda kind, along, across: own[along, kind, across],
        lambda kind, along, across: got[along, kind, across],
        rows,
        2,
    )
    out_grad[...] = rows[0]
    query_grad[...] = rows[1].T


def finish_kernel(
    where, own, got, key_grad, value_grad, attn, post, ffw, final, query, key, rows
):
    sorted_rows(
        where[0],
        lambda lane, along, across: own[lane, along, across],
        lambda lane, along, across: got[lane, along, across],
        rows,
        4,
    )
    for lane in range(4):
        key_grad[:, 64 * lane : 64 * lane + 64] = rows[lane, :64].T
        value_grad[:, 64 * lane : 64 * lane + 64] = rows[lane, 64:128].T
    gains = sum(rows[lane, 128:136] for lane in range(4))
    for at, out in enumerate((attn, post, ffw, final)):
        out[...] = gains[at]
    size = query.shape[0]
    query[...] = gains[4, :size]
    key[...] = gains[4, size : 2 * size]


def local(
    layer_input,
    segment_ids,
    out_cotangent,
    attn_norm_gain,
    query_weight,
    key_weight,
    value_weight,
    query_gain,
    key_gain,
    output_weight,
    attn_post_gain,
    ffw_norm_gain,
    gate_weight,
    up_weight,
    down_weight,
    ffw_post_gain,
):
    tok, width = layer_input.shape
    head_dim = key_weight.shape[1]
    units = down_weight.shape[0]
    block = lax.axis_index("seq")
    lane = lax.axis_index("tensor")
    core = lax.rem(block, 2)
    row = lax.rem(lax.div(block, 2), 4)
    plane = lax.div(block, 8)
    first = lax.select(core == 0, row, plane)
    second = lax.select(core == 0, plane, row)
    place = jnp.stack([lane, core, block])
    where = jnp.stack([core, first, second])
    afters = [lax.rem(at + by, 4) for at in (lane, first, second) for by in range(4)]
    flips = [first ^ flip for flip in range(1, 4)]
    place, where, core, other_core, even, *places_at = tied(
        place, where, core, 1 - core, core == 0, *afters, *flips
    )
    lanes, firsts, seconds = places_at[:4], places_at[4:8], places_at[8:12]
    flips = [firsts[0], *places_at[12:]]
    quarter_tok = tok // 4

    freq = rope_base ** (-2.0 * np.arange(head_dim // 2) / head_dim)
    start = (np.arange(lax.axis_size("seq")) * tok)[:, None] * freq[None, :]
    inner = np.arange(tok)[:, None] * freq[None, :]
    tables = [jnp.asarray(f(angle), f32) for angle in (start, inner) for f in (np.cos, np.sin)]

    square = (tok, head_dim)
    normed, own_pair, k_raw, q_raw, queries, cosine, sine = call(
        prepare_kernel,
        [
            ((tok, width), bf16),
            ((2 * tok + 16, head_dim), bf16),
            (square, f32),
            (square, f32),
            (square, bf16),
            ((tok, head_dim // 2), f32),
            ((tok, head_dim // 2), f32),
        ],
        place,
        layer_input,
        attn_norm_gain,
        key_weight,
        value_weight,
        query_weight,
        key_gain,
        query_gain,
        *tables,
        segment_ids,
        scalars=1,
        flops=6 * tok * width * head_dim,
        room=MOST,
    )
    left_one = shifted(own_pair, 1)
    left_two = shifted(own_pair, 2)

    weight_half = tok // 2
    halved, left_one = tied(output_weight, left_one)
    own_weight = pick(halved.reshape(2, weight_half, width), core)
    got_weight = [send(own_weight, round_x(by)) for by in (1, 2, 3)]

    pairs = (left_two, left_one, own_pair)
    context, log_total = attend(place, queries, pairs)

    got_context = [send(context, round_x(by)) for by in (1, 2, 3)]
    *got_context, got_weight[0], got_weight[1], got_weight[2] = tied(*got_context, *got_weight)
    other_weight = [send(part, swap_cores()) for part in got_weight]
    branch, middle, normed_two = call(
        project_kernel,
        [((tok, width), f32), ((tok, width), f32), ((tok, width), bf16)],
        place,
        layer_input,
        attn_post_gain,
        ffw_norm_gain,
        context,
        *got_context,
        output_weight,
        *got_weight,
        *other_weight,
        scalars=1,
        flops=8 * tok * tok * width,
    )
    gate = dot(gate_weight, normed_two, (0, 1))
    up_val = dot(up_weight, normed_two, (0, 1))
    active, gelu_back = jax.vjp(lambda val: jax.nn.gelu(val, approximate=True), gate)
    hidden = (active * up_val).astype(bf16)
    down_part = dot(hidden, down_weight, (0, 0)).astype(bf16)

    def halves(values):
        groups = values.reshape(8, units // 8, tok)
        groups = jnp.concatenate([groups[:, :56], groups[:, 48:]], axis=1)
        pieces = groups.reshape(4, 4, 2, 56, tok)
        return pick(pieces, core, 2), pick(pieces, other_core, 2)

    def arranged(values):
        values = jnp.where(even, values.swapaxes(0, 1), values)
        by_first = tied(*(pick(values, flip) for flip in flips))
        groups = [
            jnp.stack([by_first[i][2 * stream : 2 * stream + 2] for i in order])
            for stream, order in ((0, (0, 3)), (0, (1, 2)), (1, (0, 1)), (1, (3, 2)))
        ]
        return jnp.stack(groups).reshape(4, 224, tok)

    hidden_own, hidden_give = halves(hidden)
    hidden_got = send(hidden_give, swap_cores())
    normed_two_got = send(normed_two, swap_cores())

    def quarters(parts):
        parts = parts.reshape(4, quarter_tok, parts.shape[-1])
        given = [pick(parts, at) for at in lanes[1:]]
        return [pick(parts, lanes[0])] + [
            send(part, round_x(by)) for by, part in zip((1, 2, 3), given, strict=True)
        ]

    piece = (quarter_tok, width)
    out_own, d_branch_two, final_part = call(
        final_kernel,
        [(piece, bf16), (piece, bf16), ((1, width), f32)],
        place,
        *quarters(down_part),
        middle,
        out_cotangent,
        ffw_post_gain,
        scalars=1,
    )
    d_branch_two = gather(d_branch_two, lanes, round_x).reshape(tok, width)
    d_branch_two_got = send(d_branch_two, swap_cores())

    d_hidden = dot(down_weight, d_branch_two, (1, 1))
    d_gate = gelu_back(d_hidden * up_val)[0].astype(bf16)
    d_up = (d_hidden * active).astype(bf16)
    d_normed_two = (dot(d_gate, gate_weight, (0, 1)) + dot(d_up, up_weight, (0, 1))).astype(bf16)
    d_gate_own, d_gate_give = halves(d_gate)
    d_up_own, d_up_give = halves(d_up)
    d_pair_got = send(jnp.stack([d_gate_give, d_up_give]), swap_cores())

    keep_a, give_a, keep_b, give_b = weight_parts(
        *(
            arranged(v)
            for v in (hidden_own, hidden_got, d_gate_own, d_pair_got[0], d_up_own, d_pair_got[1])
        ),
        d_branch_two,
        d_branch_two_got,
        normed_two,
        normed_two_got,
    )
    got_a = send(give_a, along_first(1))
    got_b = send(give_b, along_first(3))

    *got_normed, keep_a, keep_b = tied(*quarters(d_normed_two), keep_a, keep_b)
    d_middle, d_branch, ffw_part, post_part = call(
        between_kernel,
        [(piece, f32), (piece, bf16), ((1, width), f32), ((1, width), f32)],
        place,
        *got_normed,
        middle,
        branch,
        out_cotangent,
        ffw_norm_gain,
        attn_post_gain,
        scalars=1,
    )
    d_branch = gather(d_branch, lanes, round_x).reshape(tok, width)
    d_queries, left_far, left_near, summed = attend_back(
        place, log_total, d_branch, output_weight, queries, pairs
    )
    got_near = shifted(left_near, -1)
    got_far = shifted(left_far, -2)
    got_near, got_far, got_a, got_b = tied(got_near, got_far, got_a, got_b)
    keep_a, give_a, keep_b, give_b = call(
        halve_kernel, [((336, width), bf16)] * 4, keep_a, got_a, keep_b, got_b
    )
    got_a = send(give_a, along_first(3))
    got_b = send(give_b, along_first(1))
    d_query, payload, query_part, key_part = call(
        key_kernel,
        [
            (square, bf16),
            ((tok, width + 2 * tok), bf16),
            ((1, head_dim), f32),
            ((1, head_dim), f32),
        ],
        q_raw,
        k_raw,
        d_queries,
        summed,
        got_near,
        got_far,
        cosine,
        sine,
        query_gain,
        key_gain,
        query_weight,
        key_weight,
        value_weight,
        flops=6 * tok * width * head_dim,
    )
    got_both = quarters(payload)
    (products,) = call(
        products_kernel,
        [((2 * head_dim, width), f32)],
        context,
        d_branch,
        d_query,
        normed,
        flops=4 * tok * width * head_dim,
    )
    *got_both, got_a, got_b = tied(*got_both, got_a, got_b)
    chunk = (3, 56, width)
    mine, *given = call(
        deal_kernel,
        [(chunk, f32)] + [(chunk, bf16)] * 3,
        where,
        keep_a,
        got_a,
        keep_b,
        got_b,
        scalars=1,
        scratch=[pltpu.VMEM((2, 336, width), f32)],
    )
    got = [send(part, round_second(by)) for by, part in zip((1, 2, 3), given, strict=True)]
    input_own, keep, give = pl.pallas_call(
        entry_kernel,
        out_shape=[
            jax.ShapeDtypeStruct(piece, bf16),
            jax.ShapeDtypeStruct((3, 16, 8, width), f32),
            jax.ShapeDtypeStruct((3, 16, 8, width), bf16),
        ],
        in_specs=[pl.BlockSpec(memory_space=pltpu.SMEM)]
        + [pl.BlockSpec(memory_space=pltpu.VMEM)] * 14,
        out_specs=[pl.BlockSpec(memory_space=pltpu.VMEM)] * 3,
        scratch_shapes=[pltpu.VMEM((tok, width), f32)],
        compiler_params=pltpu.CompilerParams(vmem_limit_bytes=SOME),
        cost_estimate=pl.CostEstimate(
            flops=256 * tok * width, bytes_accessed=12_000_000, transcendentals=0
        ),
    )(
        place,
        *got_both,
        layer_input,
        d_middle,
        attn_norm_gain,
        normed,
        post_part,
        ffw_part,
        final_part,
        query_part,
        key_part,
        products,
    )
    pack_got = send(give, swap_cores())
    part = (3, 4, 8, width)
    pack, *given = call(
        merge_kernel, [(part, f32)] + [(part, bf16)] * 3, where, keep, pack_got, scalars=1
    )
    given = [send(part, round_first(by)) for by, part in zip((1, 2, 3), given, strict=True)]
    *given, got[0], got[1], got[2] = tied(*given, *got)
    mine = mine + got[0].astype(f32) + (got[1].astype(f32) + got[2].astype(f32))
    mine = mine.astype(bf16).reshape(168, width)
    for part in given:
        pack = pack + part.astype(f32)
    pack = pack.astype(bf16).reshape(96, width)
    both = lax.optimization_barrier(jnp.concatenate([mine, pack]))
    given = [send(both, round_second(by)) for by in (1, 2, 3)]
    ends = jnp.concatenate([out_own, input_own])
    got_ends = [send(ends, round_x(by)) for by in (1, 2, 3)]
    given[0], given[1], given[2], *got_ends = tied(*given, *got_ends)
    ends = joined(ends, got_ends, lanes)
    layer_output = ends[:, :64].reshape(tok, width)
    input_grad = ends[:, 64:].reshape(tok, width)
    quarter = joined(both[:168], [part[:168] for part in given], seconds)
    pack, *given = (part[168:].astype(f32) for part in (both, *given))
    pack = (pack + given[1] + (given[0] + given[2])).astype(bf16).reshape(3, 4, 8, width)
    given = [send(pack, round_first(by)) for by in (1, 2, 3)]
    given[0], quarter = tied(given[0], quarter)
    near_a = send(quarter, along_first(1))
    near_b = send(quarter, along_first(3))
    other_own = send(quarter, swap_cores())
    pack = joined(pack, given, firsts)
    pack_got = send(pack, swap_cores())
    rest = pack[:, 2]
    given = [send(rest, round_x(by)) for by in (1, 2, 3)]
    out_grad, query_grad = call(
        square_kernel,
        [((256, width), f32), ((width, 256), f32)],
        where,
        pack,
        pack_got,
        scalars=1,
        scratch=[pltpu.VMEM((2, 256, width), f32)],
    )
    *given, near_a, near_b, out_grad, layer_output, input_grad = tied(
        *given, near_a, near_b, out_grad, layer_output, input_grad
    )
    far_a = send(near_b[:2], along_first(1))
    far_b = send(near_a[2:], along_first(3))
    other_a = send(near_a, swap_cores())
    other_b = send(near_b, swap_cores())
    rest = joined(rest, given, lanes)
    rest_got = send(rest, swap_cores())
    grads = placed(
        where,
        [
            (quarter, False, 0, 0),
            (near_a, False, 1, 0),
            (near_b, False, 3, 0),
            (other_own, True, 0, 0),
            (other_a, True, 1, 0),
            (other_b, True, 3, 0),
        ],
        [],
        units,
    )
    key_grad, value_grad, *gains = call(
        finish_kernel,
        [((width, 256), f32)] * 2 + [((width,), f32)] * 4 + [((256,), f32)] * 2,
        where,
        rest,
        rest_got,
        scalars=1,
        scratch=[pltpu.VMEM((4, 256, width), f32)],
    )
    far_a, far_b, *grads = tied(far_a, far_b, *grads)
    other_far_a = send(far_a, swap_cores())
    other_far_b = send(far_b, swap_cores())
    down_grad, gate_grad, up_grad = placed(
        where,
        [
            (far_a, False, 2, 0),
            (far_b, False, 2, 2),
            (other_far_a, True, 2, 0),
            (other_far_b, True, 2, 2),
        ],
        grads,
        units,
    )
    return (
        layer_output,
        input_grad,
        gains[0],
        query_grad,
        key_grad,
        value_grad,
        gains[4],
        gains[5],
        out_grad,
        gains[1],
        gains[2],
        gate_grad.T,
        up_grad.T,
        down_grad,
        gains[3],
    )


def solution(mesh):
    rows = P("seq", None)
    return jax.shard_map(
        local,
        mesh=mesh,
        in_specs=(
            rows,
            P("seq"),
            rows,
            P(),
            P(None, "tensor"),
            P(),
            P(),
            P(),
            P(),
            P("tensor", None),
            P(),
            P(),
            P(None, "tensor"),
            P(None, "tensor"),
            P("tensor", None),
            P(),
        ),
        out_specs=(
            rows,
            rows,
            P(),
            P(None, "tensor"),
            P(),
            P(),
            P(),
            P(),
            P("tensor", None),
            P(),
            P(),
            P(None, "tensor"),
            P(None, "tensor"),
            P("tensor", None),
            P(),
        ),
        check_vma=False,
    )
```

```python
import functools

import jax
import jax.numpy as jnp
import numpy as np
from jax import lax
from jax.experimental import pallas as pl
from jax.experimental.pallas import tpu as pltpu
from jax.sharding import PartitionSpec as P

WINDOW = 512
SOME = 24 * 1024 * 1024
MOST = 60 * 1024 * 1024

eps = 1e-06
rope_base = 10000.0
f32 = jnp.float32
bf16 = jnp.bfloat16
BOTH = ("seq", "tensor")


def places():
    return [(z, y, c, x) for z in range(4) for y in range(4) for c in range(2) for x in range(4)]


def number(z, y, c, x):
    return ((z * 4 + y) * 2 + c) * 4 + x


def route(move):
    return [(number(*p), number(*move(*p))) for p in places()]


def round_x(by):
    return route(lambda z, y, c, x: (z, y, c, (x + by) % 4))


def swap_cores():
    return route(lambda z, y, c, x: (z, y, 1 - c, x))


def along_first(flip):
    return route(lambda z, y, c, x: (z, y ^ flip, c, x) if c == 0 else (z ^ flip, y, c, x))


def round_first(by):
    return route(
        lambda z, y, c, x: (z, (y + by) % 4, c, x) if c == 0 else ((z + by) % 4, y, c, x)
    )


def round_second(by):
    return route(
        lambda z, y, c, x: ((z + by) % 4, y, c, x) if c == 0 else (z, (y + by) % 4, c, x)
    )


def send(value, pairs):
    return lax.ppermute(value, BOTH, pairs)


def shifted(value, by):
    pairs = [
        (i * 4 + x, (i + by) * 4 + x) for i in range(32) if 0 <= i + by < 32 for x in range(4)
    ]
    return send(value, pairs)


def pick(parts, index, axis=0):
    return lax.dynamic_index_in_dim(
        parts, index, axis, keepdims=False, allow_negative_indices=False
    )


def put(parts, part, index):
    return lax.dynamic_update_index_in_dim(parts, part, index, 0, allow_negative_indices=False)


def dot(first, second, over):
    return lax.dot_general(
        first, second, (((over[0],), (over[1],)), ((), ())), preferred_element_type=f32
    )


def joined(own, got, after):
    whole = put(jnp.zeros((4, *own.shape), own.dtype), own, after[0])
    for by, part in zip((1, 2, 3), got, strict=True):
        whole = put(whole, part, after[4 - by])
    return whole


def gather(part, after, turn):
    return joined(part, [send(part, turn(by)) for by in (1, 2, 3)], after)


def inv_scale(values):
    return lax.rsqrt(jnp.mean(values * values, axis=-1, keepdims=True) + eps)


def norm_back(values, scale, gain, grad):
    unit = values * scale
    weighted = grad * gain
    d_values = scale * (weighted - unit * jnp.mean(weighted * unit, axis=-1, keepdims=True))
    return (d_values, jnp.sum(grad * unit, axis=0))


def rotate(values, cosine, sine):
    half = values.shape[-1] // 2
    first = values[..., :half]
    second = values[..., half:]
    return jnp.concatenate(
        [first * cosine - second * sine, second * cosine + first * sine], axis=-1
    )


def padded(values, rows):
    return jnp.pad(values, ((0, rows - values.shape[0]), (0, 0)))


def added(first, second):
    return (first.astype(f32) + second.astype(f32)).astype(bf16)


def tied(*values):
    return lax.optimization_barrier(values)


def call(kernel, outs, *arrays, scalars=0, flops=0, room=SOME, scratch=()):
    vmem = pl.BlockSpec(memory_space=pltpu.VMEM)
    outs = [jax.ShapeDtypeStruct(*o) for o in outs]
    moved = sum(v.size * v.dtype.itemsize for v in (*arrays, *outs))
    return pl.pallas_call(
        kernel,
        out_shape=outs,
        in_specs=[pl.BlockSpec(memory_space=pltpu.SMEM)] * scalars
        + [vmem] * (len(arrays) - scalars),
        out_specs=[vmem] * len(outs),
        scratch_shapes=scratch,
        compiler_params=pltpu.CompilerParams(vmem_limit_bytes=room),
        cost_estimate=pl.CostEstimate(flops=flops, bytes_accessed=moved, transcendentals=0),
    )(*arrays)


def own_rows(ref, lane, rows):
    return ref[pl.ds(pl.multiple_of(lane * rows, rows), rows)].astype(f32)


def project_kernel(
    place, x, post_gain, ffw_gain, ctx0, ctx1, ctx2, ctx3, weight, own1, own2, own3, other1, other2, other3,
    branch, middle, normed
):
    even = place[1] == 0
    half = own1.shape[0]
    total = dot(ctx0[...], weight[...], (1, 0))
    for ctx, mine, theirs in ((ctx1, own1, other1), (ctx2, own2, other2), (ctx3, own3, other3)):
        low = jnp.where(even, mine[...], theirs[...])
        high = jnp.where(even, theirs[...], mine[...])
        total += dot(ctx[:, :half], low, (1, 0)) + dot(ctx[:, half:], high, (1, 0))
    branch[...] = total
    after = x[...].astype(f32) + total * inv_scale(total) * post_gain[...]
    middle[...] = after
    normed[...] = (after * inv_scale(after) * ffw_gain[...]).astype(bf16)


def final_kernel(place, p0, p1, p2, p3, middle, cotangent, gain, out, d_branch, part):
    lane = place[0]
    branch = p0[...].astype(f32) + p1[...].astype(f32) + p2[...].astype(f32) + p3[...].astype(f32)
    rows = branch.shape[0]
    scale = inv_scale(branch)
    cot = own_rows(cotangent, lane, rows)
    out[...] = (own_rows(middle, lane, rows) + branch * scale * gain[...]).astype(bf16)
    d_values, d_gain = norm_back(branch, scale, gain[...], cot)
    d_branch[...] = d_values.astype(bf16)
    part[...] = d_gain[None]


def between_kernel(
    place, p0, p1, p2, p3, middle, branch, cotangent, ffw_gain, post_gain,
    d_middle, d_branch, ffw_part, post_part
):
    lane = place[0]
    grad = p0[...].astype(f32) + p1[...].astype(f32) + p2[...].astype(f32) + p3[...].astype(f32)
    rows = grad.shape[0]
    after = own_rows(middle, lane, rows)
    before = own_rows(branch, lane, rows)
    d_values, d_gain = norm_back(after, inv_scale(after), ffw_gain[...], grad)
    ffw_part[...] = d_gain[None]
    d_values = own_rows(cotangent, lane, rows) + d_values
    d_middle[...] = d_values
    d_values, d_gain = norm_back(before, inv_scale(before), post_gain[...], d_values)
    d_branch[...] = d_values.astype(bf16)
    post_part[...] = d_gain[None]


def key_kernel(
    q_raw, k_raw, d_queries, d_own, d_near, d_far, cosine, sine, query_gain, key_gain, query_weight, key_weight,
    value_weight, d_query, payload, query_part, key_part
):
    tok, head_dim = q_raw.shape
    width = query_weight.shape[0]
    cos, sin = cosine[...], -sine[...]
    raw = q_raw[...]
    d_raw, d_gain = norm_back(
        raw, inv_scale(raw), query_gain[...], rotate(d_queries[...] * head_dim**-0.5, cos, sin)
    )
    query_part[...] = d_gain[None]
    d_low = d_raw.astype(bf16)
    d_query[...] = d_low
    total = dot(d_low, query_weight[...], (1, 1))
    summed = d_own[...] + d_near[...].astype(f32) + d_far[...].astype(f32)
    raw = k_raw[...]
    d_raw, d_gain = norm_back(raw, inv_scale(raw), key_gain[...], rotate(summed[:tok], cos, sin))
    key_part[...] = d_gain[None]
    total += dot(d_raw.astype(bf16), key_weight[...], (1, 1))
    total += dot(summed[tok:].astype(bf16), value_weight[...], (1, 1))
    payload[:, :width] = total.astype(bf16)
    payload[:, width : width + tok] = d_raw.T.astype(bf16)
    payload[:, width + tok :] = summed[tok:].T.astype(bf16)


def products_kernel(context, d_branch, d_query, normed, out):
    half = context.shape[1]
    out[:half] = dot(context[...], d_branch[...], (0, 0))
    out[half:] = dot(d_query[...], normed[...], (0, 0))


def entry_kernel(
    place, p0, p1, p2, p3, x, d_middle, gain, normed, post_part, ffw_part, final_part, query_part, key_part,
    products, input_grad, keep, give, rest
):
    lane, core = place[0], place[1]
    both = p0[...].astype(f32) + p1[...].astype(f32) + p2[...].astype(f32) + p3[...].astype(f32)
    rows = both.shape[0]
    width = normed.shape[1]
    tok = normed.shape[0]
    full = own_rows(x, lane, rows)
    d_values, d_gain = norm_back(full, inv_scale(full), gain[...], both[:, :width])
    input_grad[...] = (d_middle[...] + d_values).astype(bf16)
    d_keys = both[:, width : width + tok].astype(bf16)
    d_values = both[:, width + tok :].astype(bf16)
    rest[:rows] = dot(d_keys, normed[...], (1, 0))
    rest[rows : 2 * rows] = dot(d_values, normed[...], (1, 0))
    heads = jnp.concatenate(
        [query_part[...], key_part[...], jnp.zeros((1, width - 2 * query_part.shape[1]), f32)], axis=1
    )
    index = lax.broadcasted_iota(jnp.int32, (8, width), 0)
    gains = jnp.zeros((8, width), f32)
    for at, part in enumerate((d_gain[None], post_part[...], ffw_part[...], final_part[...], heads)):
        gains = jnp.where(index == at, part, gains)
    rest[2 * rows : 2 * rows + 8] = gains
    rest[2 * rows + 8 :] = jnp.zeros((rest.shape[0] - 2 * rows - 8, width), f32)
    for kind in range(3):
        source = rest if kind == 2 else products
        base = 256 if kind == 1 else 0
        for chip in range(16):
            at = base + 16 * chip
            keep[kind, chip] = source[pl.ds(pl.multiple_of(at + 8 * core, 8), 8)]
            give[kind, chip] = source[pl.ds(pl.multiple_of(at + 8 - 8 * core, 8), 8)].astype(bf16)


def merge_kernel(where, keep, got, *outs):
    core, first = where[0], where[1]
    for by, out in enumerate(outs):
        along = lax.rem(first + by, 4)
        for across in range(4):
            chip = jnp.where(core == 0, 4 * across + along, 4 * along + across)
            for kind in range(3):
                total = keep[kind, chip] + got[kind, chip].astype(f32)
                out[kind, across] = total.astype(out.dtype)


def weight_kernel(
    hid_own, hid_got, gate_own, gate_got, up_own, up_got, dy_own, dy_got, xn_own, xn_got, *outs
):
    mats = (
        (hid_own, hid_got, dy_own, dy_got),
        (gate_own, gate_got, xn_own, xn_got),
        (up_own, up_got, xn_own, xn_got),
    )
    for group, out in enumerate(outs):
        for index, (left_own, left_got, right_own, right_got) in enumerate(mats):
            total = jnp.dot(left_own[group], right_own[...], preferred_element_type=f32)
            total += jnp.dot(left_got[group], right_got[...], preferred_element_type=f32)
            total = total.astype(bf16)
            out[112 * index : 112 * index + 112] = total[:112]
            out[336 + 112 * index : 448 + 112 * index] = total[112:]


def weight_parts(*arrays):
    width = arrays[-1].shape[1]
    return pl.pallas_call(
        weight_kernel,
        out_shape=[jax.ShapeDtypeStruct((672, width), bf16)] * 4,
        in_specs=[pl.BlockSpec(memory_space=pltpu.VMEM)] * len(arrays),
        out_specs=[pl.BlockSpec(memory_space=pltpu.VMEM)] * 4,
        compiler_params=pltpu.CompilerParams(vmem_limit_bytes=SOME),
        cost_estimate=pl.CostEstimate(
            flops=2 * 2688 * 512 * width, bytes_accessed=12_000_000, transcendentals=0
        ),
    )(*arrays)


def halve_kernel(keep_a, got_a, keep_b, got_b, *outs):
    for keep, got, half in ((keep_a, got_a, outs[:2]), (keep_b, got_b, outs[2:])):
        for index, out in enumerate(half):
            rows = pl.ds(336 * index, 336)
            out[...] = (keep[rows].astype(f32) + got[rows].astype(f32)).astype(bf16)


def deal_kernel(where, keep_a, got_a, keep_b, got_b, *refs):
    outs, total = refs[:-1], refs[-1]
    total[0] = keep_a[...].astype(f32) + got_a[...].astype(f32)
    total[1] = keep_b[...].astype(f32) + got_b[...].astype(f32)
    for by, out in enumerate(outs):
        across = lax.rem(where[2] + by, 4)
        for mat in range(3):
            row = pl.multiple_of(112 * mat + 56 * lax.rem(across, 2), 8)
            out[mat] = total[across // 2, pl.ds(row, 56)].astype(out.dtype)


def masks(block, pairs):
    tok = pairs[0].shape[1]
    query = lax.broadcasted_iota(jnp.int32, (tok, tok), 0)
    key = lax.broadcasted_iota(jnp.int32, (tok, tok), 1)
    rows = [pair[2 * tok : 2 * tok + 16].astype(f32)[:1] for pair in pairs]
    segment = jnp.broadcast_to(rows[2], (tok, tok)).T
    same = [segment == row for row in rows]
    return (
        same[0] & (key > query) & (block >= 2),
        same[1] & (block >= 1),
        same[2] & (key <= query),
    )


def prepare_kernel(
    place, x, gain, key_weight, value_weight, query_weight, key_gain, query_gain, start_cos, start_sin, inner_cos,
    inner_sin, marks, xn, pair, k_raw, q_raw, queries, cosine, sine
):
    tok, head_dim = k_raw.shape
    full = x[...].astype(f32)
    low = (full * inv_scale(full) * gain[...]).astype(bf16)
    xn[...] = low
    at = pl.ds(place[2], 1)
    cos = start_cos[at] * inner_cos[...] - start_sin[at] * inner_sin[...]
    sin = start_sin[at] * inner_cos[...] + start_cos[at] * inner_sin[...]
    cosine[...] = cos
    sine[...] = sin
    raw = dot(low, key_weight[...], (1, 0))
    k_raw[...] = raw
    pair[:tok] = rotate(raw * inv_scale(raw) * key_gain[...], cos, sin).astype(bf16)
    pair[tok : 2 * tok] = dot(low, value_weight[...], (1, 0)).astype(bf16)
    pair[2 * tok :] = jnp.broadcast_to(marks[...].astype(f32)[None], (16, tok)).astype(bf16)
    raw = dot(low, query_weight[...], (1, 0))
    q_raw[...] = raw
    turned = rotate(raw * inv_scale(raw) * query_gain[...], cos, sin)
    queries[...] = (turned * head_dim**-0.5).astype(bf16)


def attend_kernel(place, queries, far, near, own, context, log_total):
    pairs = (far, near, own)
    tok = queries.shape[0]
    allowed = masks(place[2], pairs)
    scores = [
        jnp.where(ok, dot(queries[...], pair[:tok], (1, 1)), -1e30)
        for ok, pair in zip(allowed, pairs, strict=True)
    ]
    top = functools.reduce(jnp.maximum, [jnp.max(s, axis=1, keepdims=True) for s in scores])
    weights = [jnp.exp(s - top) for s in scores]
    total = sum(jnp.sum(w, axis=1, keepdims=True) for w in weights)
    context[...] = sum(
        dot((w / total).astype(bf16), pair[tok : 2 * tok], (1, 0))
        for w, pair in zip(weights, pairs, strict=True)
    ).astype(bf16)
    log_total[...] = jnp.broadcast_to(top + jnp.log(total), log_total.shape)


def attend(place, queries, pairs):
    tok, head_dim = queries.shape
    vmem = pl.BlockSpec(memory_space=pltpu.VMEM)
    return pl.pallas_call(
        attend_kernel,
        out_shape=[
            jax.ShapeDtypeStruct((tok, head_dim), bf16),
            jax.ShapeDtypeStruct((tok, 128), f32),
        ],
        in_specs=[pl.BlockSpec(memory_space=pltpu.SMEM)] + [vmem] * 4,
        out_specs=[vmem] * 2,
        compiler_params=pltpu.CompilerParams(vmem_limit_bytes=SOME),
        cost_estimate=pl.CostEstimate(
            flops=12 * tok * tok * head_dim, bytes_accessed=1_500_000, transcendentals=3 * tok * tok
        ),
    )(place, queries, *pairs)


def attend_back_kernel(
    place, log_total, d_branch, weight, queries, far, near, own, d_queries, d_far, d_near, d_own
):
    pairs = (far, near, own)
    tok = queries.shape[0]
    d_context = dot(d_branch[...], weight[...], (1, 1)).astype(bf16)
    allowed = masks(place[2], pairs)
    lse = log_total[:, :1]
    probs, d_probs = [], []
    for ok, pair in zip(allowed, pairs, strict=True):
        scores = jnp.where(ok, dot(queries[...], pair[:tok], (1, 1)), -1e30)
        probs.append(jnp.exp(scores - lse))
        d_probs.append(dot(d_context, pair[tok : 2 * tok], (1, 1)))
    mean = sum(
        jnp.sum(p * d, axis=1, keepdims=True) for p, d in zip(probs, d_probs, strict=True)
    )
    total = None
    for p, d, pair, out in zip(probs, d_probs, pairs, (d_far, d_near, d_own), strict=True):
        d_scores = (p * (d - mean)).astype(bf16)
        part = dot(d_scores, pair[:tok], (1, 0))
        total = part if total is None else total + part
        out[:tok] = dot(d_scores, queries[...], (0, 0)).astype(out.dtype)
        out[tok:] = dot(p.astype(bf16), d_context, (0, 0)).astype(out.dtype)
    d_queries[...] = total


def attend_back(place, log_total, d_branch, weight, queries, pairs):
    tok, head_dim = queries.shape
    vmem = pl.BlockSpec(memory_space=pltpu.VMEM)
    return pl.pallas_call(
        attend_back_kernel,
        out_shape=[
            jax.ShapeDtypeStruct((tok, head_dim), f32),
            jax.ShapeDtypeStruct((2 * tok, head_dim), bf16),
            jax.ShapeDtypeStruct((2 * tok, head_dim), bf16),
            jax.ShapeDtypeStruct((2 * tok, head_dim), f32),
        ],
        in_specs=[pl.BlockSpec(memory_space=pltpu.SMEM)] + [vmem] * 7,
        out_specs=[vmem] * 4,
        compiler_params=pltpu.CompilerParams(vmem_limit_bytes=SOME),
        cost_estimate=pl.CostEstimate(
            flops=30 * tok * tok * head_dim, bytes_accessed=3_500_000, transcendentals=3 * tok * tok
        ),
    )(place, log_total, d_branch, weight, queries, *pairs)


def place_kernel(where_ref, *refs, turns, held):
    n = len(turns)
    parts, outs = refs[:n], refs[n + held : n + held + 3]
    stage, sems, tail_sems = refs[-3:]
    slots = stage.shape[0]
    core, first, second = where_ref[0], where_ref[1], where_ref[2]
    chunks = [
        (ref, i, base + i, other, flip)
        for ref, (other, flip, base) in zip(parts, turns, strict=True)
        for i in range(ref.shape[0])
    ]

    def place(index):
        _, _, across, other, flip = chunks[index]
        which = 1 - core if other else core
        along = (second if other else first) ^ flip
        y = jnp.where(which == 0, along, across)
        z = jnp.where(which == 0, across, along)
        odd = lax.rem(y, 2)
        row = 216 * (2 * z + y // 2) + 104 * odd + 48 * which + 8 * which * odd
        return pl.multiple_of(row, 8), (which == 1) | (odd == 1)

    def copies(index):
        slot = index % slots
        row, whole = place(index)
        for mat, out in enumerate(outs):
            yield (
                pltpu.make_async_copy(
                    stage.at[slot, mat, pl.ds(0, 48)],
                    out.at[pl.ds(row, 48)],
                    sems.at[slot, mat],
                ),
                pltpu.make_async_copy(
                    stage.at[slot, mat, pl.ds(48, 8)],
                    out.at[pl.ds(pl.multiple_of(row + 48, 8), 8)],
                    tail_sems.at[slot, mat],
                ),
                whole,
            )

    def finish(index):
        for most, tail, whole in copies(index):
            most.wait()
            pl.when(whole)(tail.wait)

    for index, (ref, i, *_) in enumerate(chunks):
        if index >= slots:
            finish(index - slots)
        stage[index % slots] = ref[i].astype(f32)
        for most, tail, whole in copies(index):
            most.start()
            pl.when(whole)(tail.start)
    for index in range(max(0, len(chunks) - slots), len(chunks)):
        finish(index)


def placed(where, parts, outs, units):
    arrays = [p[0].reshape(-1, 3, 56, p[0].shape[-1]) for p in parts]
    width = arrays[0].shape[-1]
    slots = 4
    return pl.pallas_call(
        functools.partial(
            place_kernel, turns=tuple(p[1:] for p in parts), held=len(outs)
        ),
        out_shape=[jax.ShapeDtypeStruct((units, width), f32)] * 3,
        in_specs=[pl.BlockSpec(memory_space=pltpu.SMEM)]
        + [pl.BlockSpec(memory_space=pltpu.VMEM)] * len(arrays)
        + [pl.BlockSpec(memory_space=pl.ANY)] * len(outs),
        out_specs=[pl.BlockSpec(memory_space=pl.ANY)] * 3,
        scratch_shapes=[
            pltpu.VMEM((slots, 3, 56, width), f32),
            pltpu.SemaphoreType.DMA((slots, 3)),
            pltpu.SemaphoreType.DMA((slots, 3)),
        ],
        input_output_aliases={1 + len(arrays) + i: i for i in range(len(outs))},
        compiler_params=pltpu.CompilerParams(vmem_limit_bytes=SOME),
        cost_estimate=pl.CostEstimate(
            flops=0, bytes_accessed=sum(p.size for p in arrays) * 6, transcendentals=0
        ),
    )(where, *arrays, *outs)


def sorted_rows(core, own, got, rows, kinds):
    for pieces, other in ((own, 0), (got, 1)):
        even = core == other
        for along in range(4):
            for across in range(4):
                row = jnp.where(even, 8 * across + 2 * along, 8 * along + 2 * across + 1) * 8
                row = pl.ds(pl.multiple_of(row, 8), 8)
                for kind in range(kinds):
                    rows[kind, row] = pieces(kind, along, across).astype(f32)


def square_kernel(where, own, got, out_grad, query_grad, rows):
    sorted_rows(
        where[0],
        lambda kind, along, across: own[along, kind, across],
        lambda kind, along, across: got[along, kind, across],
        rows,
        2,
    )
    out_grad[...] = rows[0]
    query_grad[...] = rows[1].T


def finish_kernel(
    where, own, got, key_grad, value_grad, attn, post, ffw, final, query, key, rows
):
    sorted_rows(
        where[0],
        lambda lane, along, across: own[lane, along, across],
        lambda lane, along, across: got[lane, along, across],
        rows,
        4,
    )
    for lane in range(4):
        key_grad[:, 64 * lane : 64 * lane + 64] = rows[lane, :64].T
        value_grad[:, 64 * lane : 64 * lane + 64] = rows[lane, 64:128].T
    gains = sum(rows[lane, 128:136] for lane in range(4))
    for at, out in enumerate((attn, post, ffw, final)):
        out[...] = gains[at]
    size = query.shape[0]
    query[...] = gains[4, :size]
    key[...] = gains[4, size : 2 * size]


def local(
    layer_input,
    segment_ids,
    out_cotangent,
    attn_norm_gain,
    query_weight,
    key_weight,
    value_weight,
    query_gain,
    key_gain,
    output_weight,
    attn_post_gain,
    ffw_norm_gain,
    gate_weight,
    up_weight,
    down_weight,
    ffw_post_gain,
):
    tok, width = layer_input.shape
    head_dim = key_weight.shape[1]
    units = down_weight.shape[0]
    block = lax.axis_index("seq")
    lane = lax.axis_index("tensor")
    core = lax.rem(block, 2)
    row = lax.rem(lax.div(block, 2), 4)
    plane = lax.div(block, 8)
    first = lax.select(core == 0, row, plane)
    second = lax.select(core == 0, plane, row)
    place = jnp.stack([lane, core, block])
    where = jnp.stack([core, first, second])
    afters = [lax.rem(at + by, 4) for at in (lane, first, second) for by in range(4)]
    flips = [first ^ flip for flip in range(1, 4)]
    place, where, core, other_core, even, *places_at = tied(
        place, where, core, 1 - core, core == 0, *afters, *flips
    )
    lanes, firsts, seconds = places_at[:4], places_at[4:8], places_at[8:12]
    flips = [firsts[0], *places_at[12:]]
    quarter_tok = tok // 4

    freq = rope_base ** (-2.0 * np.arange(head_dim // 2) / head_dim)
    start = (np.arange(lax.axis_size("seq")) * tok)[:, None] * freq[None, :]
    inner = np.arange(tok)[:, None] * freq[None, :]
    tables = [jnp.asarray(f(angle), f32) for angle in (start, inner) for f in (np.cos, np.sin)]

    square = (tok, head_dim)
    normed, own_pair, k_raw, q_raw, queries, cosine, sine = call(
        prepare_kernel,
        [
            ((tok, width), bf16),
            ((2 * tok + 16, head_dim), bf16),
            (square, f32),
            (square, f32),
            (square, bf16),
            ((tok, head_dim // 2), f32),
            ((tok, head_dim // 2), f32),
        ],
        place,
        layer_input,
        attn_norm_gain,
        key_weight,
        value_weight,
        query_weight,
        key_gain,
        query_gain,
        *tables,
        segment_ids,
        scalars=1,
        flops=6 * tok * width * head_dim,
        room=MOST,
    )
    left_one = shifted(own_pair, 1)
    left_two = shifted(own_pair, 2)

    weight_half = tok // 2
    halved, left_one = tied(output_weight, left_one)
    own_weight = pick(halved.reshape(2, weight_half, width), core)
    got_weight = [send(own_weight, round_x(by)) for by in (1, 2, 3)]

    pairs = (left_two, left_one, own_pair)
    context, log_total = attend(place, queries, pairs)

    got_context = [send(context, round_x(by)) for by in (1, 2, 3)]
    *got_context, got_weight[0], got_weight[1], got_weight[2] = tied(*got_context, *got_weight)
    other_weight = [send(part, swap_cores()) for part in got_weight]
    branch, middle, normed_two = call(
        project_kernel,
        [((tok, width), f32), ((tok, width), f32), ((tok, width), bf16)],
        place,
        layer_input,
        attn_post_gain,
        ffw_norm_gain,
        context,
        *got_context,
        output_weight,
        *got_weight,
        *other_weight,
        scalars=1,
        flops=8 * tok * tok * width,
    )
    gate = dot(gate_weight, normed_two, (0, 1))
    up_val = dot(up_weight, normed_two, (0, 1))
    active, gelu_back = jax.vjp(lambda val: jax.nn.gelu(val, approximate=True), gate)
    hidden = (active * up_val).astype(bf16)
    down_part = dot(hidden, down_weight, (0, 0)).astype(bf16)

    def halves(values):
        groups = values.reshape(8, units // 8, tok)
        groups = jnp.concatenate([groups[:, :56], groups[:, 48:]], axis=1)
        pieces = groups.reshape(4, 4, 2, 56, tok)
        return pick(pieces, core, 2), pick(pieces, other_core, 2)

    def arranged(values):
        values = jnp.where(even, values.swapaxes(0, 1), values)
        by_first = tied(*(pick(values, flip) for flip in flips))
        groups = [
            jnp.stack([by_first[i][2 * stream : 2 * stream + 2] for i in order])
            for stream, order in ((0, (0, 3)), (0, (1, 2)), (1, (0, 1)), (1, (3, 2)))
        ]
        return jnp.stack(groups).reshape(4, 224, tok)

    hidden_own, hidden_give = halves(hidden)
    hidden_got = send(hidden_give, swap_cores())
    normed_two_got = send(normed_two, swap_cores())

    def quarters(parts):
        parts = parts.reshape(4, quarter_tok, parts.shape[-1])
        given = [pick(parts, at) for at in lanes[1:]]
        return [pick(parts, lanes[0])] + [
            send(part, round_x(by)) for by, part in zip((1, 2, 3), given, strict=True)
        ]

    piece = (quarter_tok, width)
    out_own, d_branch_two, final_part = call(
        final_kernel,
        [(piece, bf16), (piece, bf16), ((1, width), f32)],
        place,
        *quarters(down_part),
        middle,
        out_cotangent,
        ffw_post_gain,
        scalars=1,
    )
    d_branch_two = gather(d_branch_two, lanes, round_x).reshape(tok, width)
    d_branch_two_got = send(d_branch_two, swap_cores())

    d_hidden = dot(down_weight, d_branch_two, (1, 1))
    d_gate = gelu_back(d_hidden * up_val)[0].astype(bf16)
    d_up = (d_hidden * active).astype(bf16)
    d_normed_two = (dot(d_gate, gate_weight, (0, 1)) + dot(d_up, up_weight, (0, 1))).astype(bf16)
    d_gate_own, d_gate_give = halves(d_gate)
    d_up_own, d_up_give = halves(d_up)
    d_pair_got = send(jnp.stack([d_gate_give, d_up_give]), swap_cores())

    keep_a, give_a, keep_b, give_b = weight_parts(
        *(
            arranged(v)
            for v in (hidden_own, hidden_got, d_gate_own, d_pair_got[0], d_up_own, d_pair_got[1])
        ),
        d_branch_two,
        d_branch_two_got,
        normed_two,
        normed_two_got,
    )
    got_a = send(give_a, along_first(1))
    got_b = send(give_b, along_first(3))

    *got_normed, keep_a, keep_b = tied(*quarters(d_normed_two), keep_a, keep_b)
    d_middle, d_branch, ffw_part, post_part = call(
        between_kernel,
        [(piece, f32), (piece, bf16), ((1, width), f32), ((1, width), f32)],
        place,
        *got_normed,
        middle,
        branch,
        out_cotangent,
        ffw_norm_gain,
        attn_post_gain,
        scalars=1,
    )
    d_branch = gather(d_branch, lanes, round_x).reshape(tok, width)
    d_queries, left_far, left_near, summed = attend_back(
        place, log_total, d_branch, output_weight, queries, pairs
    )
    got_near = shifted(left_near, -1)
    got_far = shifted(left_far, -2)
    got_near, got_far, got_a, got_b = tied(got_near, got_far, got_a, got_b)
    keep_a, give_a, keep_b, give_b = call(
        halve_kernel, [((336, width), bf16)] * 4, keep_a, got_a, keep_b, got_b
    )
    got_a = send(give_a, along_first(3))
    got_b = send(give_b, along_first(1))
    d_query, payload, query_part, key_part = call(
        key_kernel,
        [
            (square, bf16),
            ((tok, width + 2 * tok), bf16),
            ((1, head_dim), f32),
            ((1, head_dim), f32),
        ],
        q_raw,
        k_raw,
        d_queries,
        summed,
        got_near,
        got_far,
        cosine,
        sine,
        query_gain,
        key_gain,
        query_weight,
        key_weight,
        value_weight,
        flops=6 * tok * width * head_dim,
    )
    got_both = quarters(payload)
    (products,) = call(
        products_kernel,
        [((2 * head_dim, width), f32)],
        context,
        d_branch,
        d_query,
        normed,
        flops=4 * tok * width * head_dim,
    )
    *got_both, got_a, got_b = tied(*got_both, got_a, got_b)
    chunk = (3, 56, width)
    mine, *given = call(
        deal_kernel,
        [(chunk, f32)] + [(chunk, bf16)] * 3,
        where,
        keep_a,
        got_a,
        keep_b,
        got_b,
        scalars=1,
        scratch=[pltpu.VMEM((2, 336, width), f32)],
    )
    got = [send(part, round_second(by)) for by, part in zip((1, 2, 3), given, strict=True)]
    input_own, keep, give = pl.pallas_call(
        entry_kernel,
        out_shape=[
            jax.ShapeDtypeStruct(piece, bf16),
            jax.ShapeDtypeStruct((3, 16, 8, width), f32),
            jax.ShapeDtypeStruct((3, 16, 8, width), bf16),
        ],
        in_specs=[pl.BlockSpec(memory_space=pltpu.SMEM)]
        + [pl.BlockSpec(memory_space=pltpu.VMEM)] * 14,
        out_specs=[pl.BlockSpec(memory_space=pltpu.VMEM)] * 3,
        scratch_shapes=[pltpu.VMEM((tok, width), f32)],
        compiler_params=pltpu.CompilerParams(vmem_limit_bytes=SOME),
        cost_estimate=pl.CostEstimate(
            flops=256 * tok * width, bytes_accessed=12_000_000, transcendentals=0
        ),
    )(
        place,
        *got_both,
        layer_input,
        d_middle,
        attn_norm_gain,
        normed,
        post_part,
        ffw_part,
        final_part,
        query_part,
        key_part,
        products,
    )
    pack_got = send(give, swap_cores())
    part = (3, 4, 8, width)
    pack, *given = call(
        merge_kernel, [(part, f32)] + [(part, bf16)] * 3, where, keep, pack_got, scalars=1
    )
    given = [send(part, round_first(by)) for by, part in zip((1, 2, 3), given, strict=True)]
    *given, got[0], got[1], got[2] = tied(*given, *got)
    mine = mine + got[0].astype(f32) + (got[1].astype(f32) + got[2].astype(f32))
    mine = mine.astype(bf16).reshape(168, width)
    for part in given:
        pack = pack + part.astype(f32)
    pack = pack.astype(bf16).reshape(96, width)
    both = lax.optimization_barrier(jnp.concatenate([mine, pack]))
    given = [send(both, round_second(by)) for by in (1, 2, 3)]
    ends = jnp.concatenate([out_own, input_own])
    got_ends = [send(ends, round_x(by)) for by in (1, 2, 3)]
    given[0], given[1], given[2], *got_ends = tied(*given, *got_ends)
    ends = joined(ends, got_ends, lanes)
    layer_output = ends[:, :64].reshape(tok, width)
    input_grad = ends[:, 64:].reshape(tok, width)
    quarter = joined(both[:168], [part[:168] for part in given], seconds)
    pack, *given = (part[168:].astype(f32) for part in (both, *given))
    pack = (pack + given[1] + (given[0] + given[2])).astype(bf16).reshape(3, 4, 8, width)
    given = [send(pack, round_first(by)) for by in (1, 2, 3)]
    other_own = send(quarter, swap_cores())
    given[0], quarter, other_own, layer_output, input_grad = tied(
        given[0], quarter, other_own, layer_output, input_grad
    )
    near_a = send(quarter, along_first(1))
    near_b = send(quarter, along_first(3))
    pack = joined(pack, given, firsts)
    pack_got = send(pack, swap_cores())
    rest = pack[:, 2]
    given = [send(rest, round_x(by)) for by in (1, 2, 3)]
    out_grad, query_grad = call(
        square_kernel,
        [((256, width), f32), ((width, 256), f32)],
        where,
        pack,
        pack_got,
        scalars=1,
        scratch=[pltpu.VMEM((2, 256, width), f32)],
    )
    grads = placed(where, [(quarter, False, 0, 0), (other_own, True, 0, 0)], [], units)
    grads = list(grads)
    *given, near_a, near_b, grads[0] = tied(*given, near_a, near_b, grads[0])
    far_a = send(near_b[:2], along_first(1))
    far_b = send(near_a[2:], along_first(3))
    other_a = send(near_a, swap_cores())
    other_b = send(near_b, swap_cores())
    rest = joined(rest, given, lanes)
    rest_got = send(rest, swap_cores())
    key_grad, value_grad, *gains = call(
        finish_kernel,
        [((width, 256), f32)] * 2 + [((width,), f32)] * 4 + [((256,), f32)] * 2,
        where,
        rest,
        rest_got,
        scalars=1,
        scratch=[pltpu.VMEM((4, 256, width), f32)],
    )
    other_a, out_grad, key_grad = tied(other_a, out_grad, key_grad)
    grads = placed(
        where,
        [
            (near_a, False, 1, 0),
            (near_b, False, 3, 0),
            (other_a, True, 1, 0),
            (other_b, True, 3, 0),
        ],
        grads,
        units,
    )
    far_a, far_b, *grads = tied(far_a, far_b, *grads)
    other_far_a = send(far_a, swap_cores())
    other_far_b = send(far_b, swap_cores())
    down_grad, gate_grad, up_grad = placed(
        where,
        [
            (far_a, False, 2, 0),
            (far_b, False, 2, 2),
            (other_far_a, True, 2, 0),
            (other_far_b, True, 2, 2),
        ],
        grads,
        units,
    )
    return (
        layer_output,
        input_grad,
        gains[0],
        query_grad,
        key_grad,
        value_grad,
        gains[4],
        gains[5],
        out_grad,
        gains[1],
        gains[2],
        gate_grad.T,
        up_grad.T,
        down_grad,
        gains[3],
    )


def solution(mesh):
    rows = P("seq", None)
    return jax.shard_map(
        local,
        mesh=mesh,
        in_specs=(
            rows,
            P("seq"),
            rows,
            P(),
            P(None, "tensor"),
            P(),
            P(),
            P(),
            P(),
            P("tensor", None),
            P(),
            P(),
            P(None, "tensor"),
            P(None, "tensor"),
            P("tensor", None),
            P(),
        ),
        out_specs=(
            rows,
            rows,
            P(),
            P(None, "tensor"),
            P(),
            P(),
            P(),
            P(),
            P("tensor", None),
            P(),
            P(),
            P(None, "tensor"),
            P(None, "tensor"),
            P("tensor", None),
            P(),
        ),
        check_vma=False,
    )
```

```python
import functools

import jax
import jax.numpy as jnp
import numpy as np
from jax import lax
from jax.experimental import pallas as pl
from jax.experimental.pallas import tpu as pltpu
from jax.sharding import PartitionSpec as P

WINDOW = 512
SOME = 24 * 1024 * 1024
MOST = 60 * 1024 * 1024

eps = 1e-06
rope_base = 10000.0
f32 = jnp.float32
bf16 = jnp.bfloat16
BOTH = ("seq", "tensor")


def places():
    return [(z, y, c, x) for z in range(4) for y in range(4) for c in range(2) for x in range(4)]


def number(z, y, c, x):
    return ((z * 4 + y) * 2 + c) * 4 + x


def route(move):
    return [(number(*p), number(*move(*p))) for p in places()]


def round_x(by):
    return route(lambda z, y, c, x: (z, y, c, (x + by) % 4))


def swap_cores():
    return route(lambda z, y, c, x: (z, y, 1 - c, x))


def along_first(flip):
    return route(lambda z, y, c, x: (z, y ^ flip, c, x) if c == 0 else (z ^ flip, y, c, x))


def round_first(by):
    return route(
        lambda z, y, c, x: (z, (y + by) % 4, c, x) if c == 0 else ((z + by) % 4, y, c, x)
    )


def round_second(by):
    return route(
        lambda z, y, c, x: ((z + by) % 4, y, c, x) if c == 0 else (z, (y + by) % 4, c, x)
    )


def send(value, pairs):
    return lax.ppermute(value, BOTH, pairs)


def shifted(value, by):
    pairs = [
        (i * 4 + x, (i + by) * 4 + x) for i in range(32) if 0 <= i + by < 32 for x in range(4)
    ]
    return send(value, pairs)


def pick(parts, index, axis=0):
    return lax.dynamic_index_in_dim(
        parts, index, axis, keepdims=False, allow_negative_indices=False
    )


def put(parts, part, index):
    return lax.dynamic_update_index_in_dim(parts, part, index, 0, allow_negative_indices=False)


def dot(first, second, over):
    return lax.dot_general(
        first, second, (((over[0],), (over[1],)), ((), ())), preferred_element_type=f32
    )


def joined(own, got, after):
    whole = put(jnp.zeros((4, *own.shape), own.dtype), own, after[0])
    for by, part in zip((1, 2, 3), got, strict=True):
        whole = put(whole, part, after[4 - by])
    return whole


def gather(part, after, turn):
    return joined(part, [send(part, turn(by)) for by in (1, 2, 3)], after)


def inv_scale(values):
    return lax.rsqrt(jnp.mean(values * values, axis=-1, keepdims=True) + eps)


def norm_back(values, scale, gain, grad):
    unit = values * scale
    weighted = grad * gain
    d_values = scale * (weighted - unit * jnp.mean(weighted * unit, axis=-1, keepdims=True))
    return (d_values, jnp.sum(grad * unit, axis=0))


def rotate(values, cosine, sine):
    half = values.shape[-1] // 2
    first = values[..., :half]
    second = values[..., half:]
    return jnp.concatenate(
        [first * cosine - second * sine, second * cosine + first * sine], axis=-1
    )


def padded(values, rows):
    return jnp.pad(values, ((0, rows - values.shape[0]), (0, 0)))


def added(first, second):
    return (first.astype(f32) + second.astype(f32)).astype(bf16)


def tied(*values):
    return lax.optimization_barrier(values)


def call(kernel, outs, *arrays, scalars=0, flops=0, room=SOME, scratch=()):
    vmem = pl.BlockSpec(memory_space=pltpu.VMEM)
    outs = [jax.ShapeDtypeStruct(*o) for o in outs]
    moved = sum(v.size * v.dtype.itemsize for v in (*arrays, *outs))
    return pl.pallas_call(
        kernel,
        out_shape=outs,
        in_specs=[pl.BlockSpec(memory_space=pltpu.SMEM)] * scalars
        + [vmem] * (len(arrays) - scalars),
        out_specs=[vmem] * len(outs),
        scratch_shapes=scratch,
        compiler_params=pltpu.CompilerParams(vmem_limit_bytes=room),
        cost_estimate=pl.CostEstimate(flops=flops, bytes_accessed=moved, transcendentals=0),
    )(*arrays)


def own_rows(ref, lane, rows):
    return ref[pl.ds(pl.multiple_of(lane * rows, rows), rows)].astype(f32)


def project_kernel(
    place, x, post_gain, ffw_gain, ctx0, ctx1, ctx2, ctx3, weight, own1, own2, own3, other1, other2, other3,
    branch, middle, normed
):
    even = place[1] == 0
    half = own1.shape[0]
    total = dot(ctx0[...], weight[...], (1, 0))
    for ctx, mine, theirs in ((ctx1, own1, other1), (ctx2, own2, other2), (ctx3, own3, other3)):
        low = jnp.where(even, mine[...], theirs[...])
        high = jnp.where(even, theirs[...], mine[...])
        total += dot(ctx[:, :half], low, (1, 0)) + dot(ctx[:, half:], high, (1, 0))
    branch[...] = total
    after = x[...].astype(f32) + total * inv_scale(total) * post_gain[...]
    middle[...] = after
    normed[...] = (after * inv_scale(after) * ffw_gain[...]).astype(bf16)


def final_kernel(place, p0, p1, p2, p3, middle, cotangent, gain, out, d_branch, part):
    lane = place[0]
    branch = p0[...].astype(f32) + p1[...].astype(f32) + p2[...].astype(f32) + p3[...].astype(f32)
    rows = branch.shape[0]
    scale = inv_scale(branch)
    cot = own_rows(cotangent, lane, rows)
    out[...] = (own_rows(middle, lane, rows) + branch * scale * gain[...]).astype(bf16)
    d_values, d_gain = norm_back(branch, scale, gain[...], cot)
    d_branch[...] = d_values.astype(bf16)
    part[...] = d_gain[None]


def between_kernel(
    place, p0, p1, p2, p3, middle, branch, cotangent, ffw_gain, post_gain,
    d_middle, d_branch, ffw_part, post_part
):
    lane = place[0]
    grad = p0[...].astype(f32) + p1[...].astype(f32) + p2[...].astype(f32) + p3[...].astype(f32)
    rows = grad.shape[0]
    after = own_rows(middle, lane, rows)
    before = own_rows(branch, lane, rows)
    d_values, d_gain = norm_back(after, inv_scale(after), ffw_gain[...], grad)
    ffw_part[...] = d_gain[None]
    d_values = own_rows(cotangent, lane, rows) + d_values
    d_middle[...] = d_values
    d_values, d_gain = norm_back(before, inv_scale(before), post_gain[...], d_values)
    d_branch[...] = d_values.astype(bf16)
    post_part[...] = d_gain[None]


def key_kernel(
    q_raw, k_raw, d_queries, d_own, d_near, d_far, cosine, sine, query_gain, key_gain, query_weight, key_weight,
    value_weight, d_query, payload, query_part, key_part
):
    tok, head_dim = q_raw.shape
    width = query_weight.shape[0]
    cos, sin = cosine[...], -sine[...]
    raw = q_raw[...]
    d_raw, d_gain = norm_back(
        raw, inv_scale(raw), query_gain[...], rotate(d_queries[...] * head_dim**-0.5, cos, sin)
    )
    query_part[...] = d_gain[None]
    d_low = d_raw.astype(bf16)
    d_query[...] = d_low
    total = dot(d_low, query_weight[...], (1, 1))
    summed = d_own[...] + d_near[...].astype(f32) + d_far[...].astype(f32)
    raw = k_raw[...]
    d_raw, d_gain = norm_back(raw, inv_scale(raw), key_gain[...], rotate(summed[:tok], cos, sin))
    key_part[...] = d_gain[None]
    total += dot(d_raw.astype(bf16), key_weight[...], (1, 1))
    total += dot(summed[tok:].astype(bf16), value_weight[...], (1, 1))
    payload[:, :width] = total.astype(bf16)
    payload[:, width : width + tok] = d_raw.T.astype(bf16)
    payload[:, width + tok :] = summed[tok:].T.astype(bf16)


def products_kernel(context, d_branch, d_query, normed, out):
    half = context.shape[1]
    out[:half] = dot(context[...], d_branch[...], (0, 0))
    out[half:] = dot(d_query[...], normed[...], (0, 0))


def entry_kernel(
    place, p0, p1, p2, p3, x, d_middle, gain, normed, post_part, ffw_part, final_part, query_part, key_part,
    products, input_grad, keep, give, rest
):
    lane, core = place[0], place[1]
    both = p0[...].astype(f32) + p1[...].astype(f32) + p2[...].astype(f32) + p3[...].astype(f32)
    rows = both.shape[0]
    width = normed.shape[1]
    tok = normed.shape[0]
    full = own_rows(x, lane, rows)
    d_values, d_gain = norm_back(full, inv_scale(full), gain[...], both[:, :width])
    input_grad[...] = (d_middle[...] + d_values).astype(bf16)
    d_keys = both[:, width : width + tok].astype(bf16)
    d_values = both[:, width + tok :].astype(bf16)
    rest[:rows] = dot(d_keys, normed[...], (1, 0))
    rest[rows : 2 * rows] = dot(d_values, normed[...], (1, 0))
    heads = jnp.concatenate(
        [query_part[...], key_part[...], jnp.zeros((1, width - 2 * query_part.shape[1]), f32)], axis=1
    )
    index = lax.broadcasted_iota(jnp.int32, (8, width), 0)
    gains = jnp.zeros((8, width), f32)
    for at, part in enumerate((d_gain[None], post_part[...], ffw_part[...], final_part[...], heads)):
        gains = jnp.where(index == at, part, gains)
    rest[2 * rows : 2 * rows + 8] = gains
    rest[2 * rows + 8 :] = jnp.zeros((rest.shape[0] - 2 * rows - 8, width), f32)
    for kind in range(3):
        source = rest if kind == 2 else products
        base = 256 if kind == 1 else 0
        for chip in range(16):
            at = base + 16 * chip
            keep[kind, chip] = source[pl.ds(pl.multiple_of(at + 8 * core, 8), 8)]
            give[kind, chip] = source[pl.ds(pl.multiple_of(at + 8 - 8 * core, 8), 8)].astype(bf16)


def merge_kernel(where, keep, got, *outs):
    core, first = where[0], where[1]
    for by, out in enumerate(outs):
        along = lax.rem(first + by, 4)
        for across in range(4):
            chip = jnp.where(core == 0, 4 * across + along, 4 * along + across)
            for kind in range(3):
                total = keep[kind, chip] + got[kind, chip].astype(f32)
                out[kind, across] = total.astype(out.dtype)


def weight_kernel(
    hid_own, hid_got, gate_own, gate_got, up_own, up_got, dy_own, dy_got, xn_own, xn_got, *outs
):
    mats = (
        (hid_own, hid_got, dy_own, dy_got),
        (gate_own, gate_got, xn_own, xn_got),
        (up_own, up_got, xn_own, xn_got),
    )
    for group, out in enumerate(outs):
        for index, (left_own, left_got, right_own, right_got) in enumerate(mats):
            total = jnp.dot(left_own[group], right_own[...], preferred_element_type=f32)
            total += jnp.dot(left_got[group], right_got[...], preferred_element_type=f32)
            total = total.astype(bf16)
            out[112 * index : 112 * index + 112] = total[:112]
            out[336 + 112 * index : 448 + 112 * index] = total[112:]


def weight_parts(*arrays):
    width = arrays[-1].shape[1]
    return pl.pallas_call(
        weight_kernel,
        out_shape=[jax.ShapeDtypeStruct((672, width), bf16)] * 4,
        in_specs=[pl.BlockSpec(memory_space=pltpu.VMEM)] * len(arrays),
        out_specs=[pl.BlockSpec(memory_space=pltpu.VMEM)] * 4,
        compiler_params=pltpu.CompilerParams(vmem_limit_bytes=SOME),
        cost_estimate=pl.CostEstimate(
            flops=2 * 2688 * 512 * width, bytes_accessed=12_000_000, transcendentals=0
        ),
    )(*arrays)


def halve_kernel(keep_a, got_a, keep_b, got_b, *outs):
    for keep, got, half in ((keep_a, got_a, outs[:2]), (keep_b, got_b, outs[2:])):
        for index, out in enumerate(half):
            rows = pl.ds(336 * index, 336)
            out[...] = (keep[rows].astype(f32) + got[rows].astype(f32)).astype(bf16)


def deal_kernel(where, keep_a, got_a, keep_b, got_b, *refs):
    outs, total = refs[:-1], refs[-1]
    total[0] = keep_a[...].astype(f32) + got_a[...].astype(f32)
    total[1] = keep_b[...].astype(f32) + got_b[...].astype(f32)
    for by, out in enumerate(outs):
        across = lax.rem(where[2] + by, 4)
        for mat in range(3):
            row = pl.multiple_of(112 * mat + 56 * lax.rem(across, 2), 8)
            out[mat] = total[across // 2, pl.ds(row, 56)].astype(out.dtype)


def masks(block, pairs):
    tok = pairs[0].shape[1]
    query = lax.broadcasted_iota(jnp.int32, (tok, tok), 0)
    key = lax.broadcasted_iota(jnp.int32, (tok, tok), 1)
    rows = [pair[2 * tok : 2 * tok + 16].astype(f32)[:1] for pair in pairs]
    segment = jnp.broadcast_to(rows[2], (tok, tok)).T
    same = [segment == row for row in rows]
    return (
        same[0] & (key > query) & (block >= 2),
        same[1] & (block >= 1),
        same[2] & (key <= query),
    )


def prepare_kernel(
    place, x, gain, key_weight, value_weight, query_weight, key_gain, query_gain, start_cos, start_sin, inner_cos,
    inner_sin, marks, xn, pair, k_raw, q_raw, queries, cosine, sine
):
    tok, head_dim = k_raw.shape
    full = x[...].astype(f32)
    low = (full * inv_scale(full) * gain[...]).astype(bf16)
    xn[...] = low
    at = pl.ds(place[2], 1)
    cos = start_cos[at] * inner_cos[...] - start_sin[at] * inner_sin[...]
    sin = start_sin[at] * inner_cos[...] + start_cos[at] * inner_sin[...]
    cosine[...] = cos
    sine[...] = sin
    raw = dot(low, key_weight[...], (1, 0))
    k_raw[...] = raw
    pair[:tok] = rotate(raw * inv_scale(raw) * key_gain[...], cos, sin).astype(bf16)
    pair[tok : 2 * tok] = dot(low, value_weight[...], (1, 0)).astype(bf16)
    pair[2 * tok :] = jnp.broadcast_to(marks[...].astype(f32)[None], (16, tok)).astype(bf16)
    raw = dot(low, query_weight[...], (1, 0))
    q_raw[...] = raw
    turned = rotate(raw * inv_scale(raw) * query_gain[...], cos, sin)
    queries[...] = (turned * head_dim**-0.5).astype(bf16)


def attend_kernel(place, queries, far, near, own, context, log_total):
    pairs = (far, near, own)
    tok = queries.shape[0]
    allowed = masks(place[2], pairs)
    scores = [
        jnp.where(ok, dot(queries[...], pair[:tok], (1, 1)), -1e30)
        for ok, pair in zip(allowed, pairs, strict=True)
    ]
    top = functools.reduce(jnp.maximum, [jnp.max(s, axis=1, keepdims=True) for s in scores])
    weights = [jnp.exp(s - top) for s in scores]
    total = sum(jnp.sum(w, axis=1, keepdims=True) for w in weights)
    context[...] = sum(
        dot((w / total).astype(bf16), pair[tok : 2 * tok], (1, 0))
        for w, pair in zip(weights, pairs, strict=True)
    ).astype(bf16)
    log_total[...] = jnp.broadcast_to(top + jnp.log(total), log_total.shape)


def attend(place, queries, pairs):
    tok, head_dim = queries.shape
    vmem = pl.BlockSpec(memory_space=pltpu.VMEM)
    return pl.pallas_call(
        attend_kernel,
        out_shape=[
            jax.ShapeDtypeStruct((tok, head_dim), bf16),
            jax.ShapeDtypeStruct((tok, 128), f32),
        ],
        in_specs=[pl.BlockSpec(memory_space=pltpu.SMEM)] + [vmem] * 4,
        out_specs=[vmem] * 2,
        compiler_params=pltpu.CompilerParams(vmem_limit_bytes=SOME),
        cost_estimate=pl.CostEstimate(
            flops=12 * tok * tok * head_dim, bytes_accessed=1_500_000, transcendentals=3 * tok * tok
        ),
    )(place, queries, *pairs)


def attend_back_kernel(
    place, log_total, d_branch, weight, queries, far, near, own, d_queries, d_far, d_near, d_own
):
    pairs = (far, near, own)
    tok = queries.shape[0]
    d_context = dot(d_branch[...], weight[...], (1, 1)).astype(bf16)
    allowed = masks(place[2], pairs)
    lse = log_total[:, :1]
    probs, d_probs = [], []
    for ok, pair in zip(allowed, pairs, strict=True):
        scores = jnp.where(ok, dot(queries[...], pair[:tok], (1, 1)), -1e30)
        probs.append(jnp.exp(scores - lse))
        d_probs.append(dot(d_context, pair[tok : 2 * tok], (1, 1)))
    mean = sum(
        jnp.sum(p * d, axis=1, keepdims=True) for p, d in zip(probs, d_probs, strict=True)
    )
    total = None
    for p, d, pair, out in zip(probs, d_probs, pairs, (d_far, d_near, d_own), strict=True):
        d_scores = (p * (d - mean)).astype(bf16)
        part = dot(d_scores, pair[:tok], (1, 0))
        total = part if total is None else total + part
        out[:tok] = dot(d_scores, queries[...], (0, 0)).astype(out.dtype)
        out[tok:] = dot(p.astype(bf16), d_context, (0, 0)).astype(out.dtype)
    d_queries[...] = total


def attend_back(place, log_total, d_branch, weight, queries, pairs):
    tok, head_dim = queries.shape
    vmem = pl.BlockSpec(memory_space=pltpu.VMEM)
    return pl.pallas_call(
        attend_back_kernel,
        out_shape=[
            jax.ShapeDtypeStruct((tok, head_dim), f32),
            jax.ShapeDtypeStruct((2 * tok, head_dim), bf16),
            jax.ShapeDtypeStruct((2 * tok, head_dim), bf16),
            jax.ShapeDtypeStruct((2 * tok, head_dim), f32),
        ],
        in_specs=[pl.BlockSpec(memory_space=pltpu.SMEM)] + [vmem] * 7,
        out_specs=[vmem] * 4,
        compiler_params=pltpu.CompilerParams(vmem_limit_bytes=SOME),
        cost_estimate=pl.CostEstimate(
            flops=30 * tok * tok * head_dim, bytes_accessed=3_500_000, transcendentals=3 * tok * tok
        ),
    )(place, log_total, d_branch, weight, queries, *pairs)


def place_kernel(where_ref, *refs, turns, held):
    n = len(turns)
    parts, outs = refs[:n], refs[n + held : n + held + 3]
    stage, sems, tail_sems = refs[-3:]
    slots = stage.shape[0]
    core, first, second = where_ref[0], where_ref[1], where_ref[2]
    chunks = [
        (ref, i, base + i, other, flip)
        for ref, (other, flip, base) in zip(parts, turns, strict=True)
        for i in range(ref.shape[0])
    ]

    def place(index):
        _, _, across, other, flip = chunks[index]
        which = 1 - core if other else core
        along = (second if other else first) ^ flip
        y = jnp.where(which == 0, along, across)
        z = jnp.where(which == 0, across, along)
        odd = lax.rem(y, 2)
        row = 216 * (2 * z + y // 2) + 104 * odd + 48 * which + 8 * which * odd
        return pl.multiple_of(row, 8), (which == 1) | (odd == 1)

    def copies(index):
        slot = index % slots
        row, whole = place(index)
        for mat, out in enumerate(outs):
            yield (
                pltpu.make_async_copy(
                    stage.at[slot, mat, pl.ds(0, 48)],
                    out.at[pl.ds(row, 48)],
                    sems.at[slot, mat],
                ),
                pltpu.make_async_copy(
                    stage.at[slot, mat, pl.ds(48, 8)],
                    out.at[pl.ds(pl.multiple_of(row + 48, 8), 8)],
                    tail_sems.at[slot, mat],
                ),
                whole,
            )

    def finish(index):
        for most, tail, whole in copies(index):
            most.wait()
            pl.when(whole)(tail.wait)

    for index, (ref, i, *_) in enumerate(chunks):
        if index >= slots:
            finish(index - slots)
        stage[index % slots] = ref[i].astype(f32)
        for most, tail, whole in copies(index):
            most.start()
            pl.when(whole)(tail.start)
    for index in range(max(0, len(chunks) - slots), len(chunks)):
        finish(index)


def placed(where, parts, outs, units):
    arrays = [p[0].reshape(-1, 3, 56, p[0].shape[-1]) for p in parts]
    width = arrays[0].shape[-1]
    slots = 4
    return pl.pallas_call(
        functools.partial(
            place_kernel, turns=tuple(p[1:] for p in parts), held=len(outs)
        ),
        out_shape=[jax.ShapeDtypeStruct((units, width), f32)] * 3,
        in_specs=[pl.BlockSpec(memory_space=pltpu.SMEM)]
        + [pl.BlockSpec(memory_space=pltpu.VMEM)] * len(arrays)
        + [pl.BlockSpec(memory_space=pl.ANY)] * len(outs),
        out_specs=[pl.BlockSpec(memory_space=pl.ANY)] * 3,
        scratch_shapes=[
            pltpu.VMEM((slots, 3, 56, width), f32),
            pltpu.SemaphoreType.DMA((slots, 3)),
            pltpu.SemaphoreType.DMA((slots, 3)),
        ],
        input_output_aliases={1 + len(arrays) + i: i for i in range(len(outs))},
        compiler_params=pltpu.CompilerParams(vmem_limit_bytes=SOME),
        cost_estimate=pl.CostEstimate(
            flops=0, bytes_accessed=sum(p.size for p in arrays) * 6, transcendentals=0
        ),
    )(where, *arrays, *outs)


def sorted_rows(core, own, got, rows, kinds):
    for pieces, other in ((own, 0), (got, 1)):
        even = core == other
        for along in range(4):
            for across in range(4):
                row = jnp.where(even, 8 * across + 2 * along, 8 * along + 2 * across + 1) * 8
                row = pl.ds(pl.multiple_of(row, 8), 8)
                for kind in range(kinds):
                    rows[kind, row] = pieces(kind, along, across).astype(f32)


def square_kernel(where, own, got, out_grad, query_grad, rows):
    sorted_rows(
        where[0],
        lambda kind, along, across: own[along, kind, across],
        lambda kind, along, across: got[along, kind, across],
        rows,
        2,
    )
    out_grad[...] = rows[0]
    query_grad[...] = rows[1].T


def finish_kernel(
    where, own, got, key_grad, value_grad, attn, post, ffw, final, query, key, rows
):
    sorted_rows(
        where[0],
        lambda lane, along, across: own[lane, along, across],
        lambda lane, along, across: got[lane, along, across],
        rows,
        4,
    )
    for lane in range(4):
        key_grad[:, 64 * lane : 64 * lane + 64] = rows[lane, :64].T
        value_grad[:, 64 * lane : 64 * lane + 64] = rows[lane, 64:128].T
    gains = sum(rows[lane, 128:136] for lane in range(4))
    for at, out in enumerate((attn, post, ffw, final)):
        out[...] = gains[at]
    size = query.shape[0]
    query[...] = gains[4, :size]
    key[...] = gains[4, size : 2 * size]


def local(
    layer_input,
    segment_ids,
    out_cotangent,
    attn_norm_gain,
    query_weight,
    key_weight,
    value_weight,
    query_gain,
    key_gain,
    output_weight,
    attn_post_gain,
    ffw_norm_gain,
    gate_weight,
    up_weight,
    down_weight,
    ffw_post_gain,
):
    tok, width = layer_input.shape
    head_dim = key_weight.shape[1]
    units = down_weight.shape[0]
    block = lax.axis_index("seq")
    lane = lax.axis_index("tensor")
    core = lax.rem(block, 2)
    row = lax.rem(lax.div(block, 2), 4)
    plane = lax.div(block, 8)
    first = lax.select(core == 0, row, plane)
    second = lax.select(core == 0, plane, row)
    place = jnp.stack([lane, core, block])
    where = jnp.stack([core, first, second])
    afters = [lax.rem(at + by, 4) for at in (lane, first, second) for by in range(4)]
    flips = [first ^ flip for flip in range(1, 4)]
    place, where, core, other_core, even, *places_at = tied(
        place, where, core, 1 - core, core == 0, *afters, *flips
    )
    lanes, firsts, seconds = places_at[:4], places_at[4:8], places_at[8:12]
    flips = [firsts[0], *places_at[12:]]
    quarter_tok = tok // 4

    freq = rope_base ** (-2.0 * np.arange(head_dim // 2) / head_dim)
    start = (np.arange(lax.axis_size("seq")) * tok)[:, None] * freq[None, :]
    inner = np.arange(tok)[:, None] * freq[None, :]
    tables = [jnp.asarray(f(angle), f32) for angle in (start, inner) for f in (np.cos, np.sin)]

    square = (tok, head_dim)
    normed, own_pair, k_raw, q_raw, queries, cosine, sine = call(
        prepare_kernel,
        [
            ((tok, width), bf16),
            ((2 * tok + 16, head_dim), bf16),
            (square, f32),
            (square, f32),
            (square, bf16),
            ((tok, head_dim // 2), f32),
            ((tok, head_dim // 2), f32),
        ],
        place,
        layer_input,
        attn_norm_gain,
        key_weight,
        value_weight,
        query_weight,
        key_gain,
        query_gain,
        *tables,
        segment_ids,
        scalars=1,
        flops=6 * tok * width * head_dim,
        room=MOST,
    )
    left_one = shifted(own_pair, 1)
    left_two = shifted(own_pair, 2)

    weight_half = tok // 2
    halved, left_one = tied(output_weight, left_one)
    own_weight = pick(halved.reshape(2, weight_half, width), core)
    got_weight = [send(own_weight, round_x(by)) for by in (1, 2, 3)]

    pairs = (left_two, left_one, own_pair)
    context, log_total = attend(place, queries, pairs)

    got_context = [send(context, round_x(by)) for by in (1, 2, 3)]
    *got_context, got_weight[0], got_weight[1], got_weight[2] = tied(*got_context, *got_weight)
    other_weight = [send(part, swap_cores()) for part in got_weight]
    branch, middle, normed_two = call(
        project_kernel,
        [((tok, width), f32), ((tok, width), f32), ((tok, width), bf16)],
        place,
        layer_input,
        attn_post_gain,
        ffw_norm_gain,
        context,
        *got_context,
        output_weight,
        *got_weight,
        *other_weight,
        scalars=1,
        flops=8 * tok * tok * width,
    )
    gate = dot(gate_weight, normed_two, (0, 1))
    up_val = dot(up_weight, normed_two, (0, 1))
    active, gelu_back = jax.vjp(lambda val: jax.nn.gelu(val, approximate=True), gate)
    hidden = (active * up_val).astype(bf16)
    down_part = dot(hidden, down_weight, (0, 0)).astype(bf16)

    def halves(values):
        groups = values.reshape(8, units // 8, tok)
        groups = jnp.concatenate([groups[:, :56], groups[:, 48:]], axis=1)
        pieces = groups.reshape(4, 4, 2, 56, tok)
        return pick(pieces, core, 2), pick(pieces, other_core, 2)

    def arranged(values):
        values = jnp.where(even, values.swapaxes(0, 1), values)
        by_first = tied(*(pick(values, flip) for flip in flips))
        groups = [
            jnp.stack([by_first[i][2 * stream : 2 * stream + 2] for i in order])
            for stream, order in ((0, (0, 3)), (0, (1, 2)), (1, (0, 1)), (1, (3, 2)))
        ]
        return jnp.stack(groups).reshape(4, 224, tok)

    hidden_own, hidden_give = halves(hidden)
    hidden_got = send(hidden_give, swap_cores())
    normed_two_got = send(normed_two, swap_cores())

    def quarters(parts):
        parts = parts.reshape(4, quarter_tok, parts.shape[-1])
        given = [pick(parts, at) for at in lanes[1:]]
        return [pick(parts, lanes[0])] + [
            send(part, round_x(by)) for by, part in zip((1, 2, 3), given, strict=True)
        ]

    piece = (quarter_tok, width)
    out_own, d_branch_two, final_part = call(
        final_kernel,
        [(piece, bf16), (piece, bf16), ((1, width), f32)],
        place,
        *quarters(down_part),
        middle,
        out_cotangent,
        ffw_post_gain,
        scalars=1,
    )
    d_branch_two = gather(d_branch_two, lanes, round_x).reshape(tok, width)
    d_branch_two_got = send(d_branch_two, swap_cores())

    d_hidden = dot(down_weight, d_branch_two, (1, 1))
    d_gate = gelu_back(d_hidden * up_val)[0].astype(bf16)
    d_up = (d_hidden * active).astype(bf16)
    d_normed_two = (dot(d_gate, gate_weight, (0, 1)) + dot(d_up, up_weight, (0, 1))).astype(bf16)
    d_gate_own, d_gate_give = halves(d_gate)
    d_up_own, d_up_give = halves(d_up)
    d_pair_got = send(jnp.stack([d_gate_give, d_up_give]), swap_cores())

    keep_a, give_a, keep_b, give_b = weight_parts(
        *(
            arranged(v)
            for v in (hidden_own, hidden_got, d_gate_own, d_pair_got[0], d_up_own, d_pair_got[1])
        ),
        d_branch_two,
        d_branch_two_got,
        normed_two,
        normed_two_got,
    )
    got_a = send(give_a, along_first(1))
    got_b = send(give_b, along_first(3))

    *got_normed, keep_a, keep_b = tied(*quarters(d_normed_two), keep_a, keep_b)
    d_middle, d_branch, ffw_part, post_part = call(
        between_kernel,
        [(piece, f32), (piece, bf16), ((1, width), f32), ((1, width), f32)],
        place,
        *got_normed,
        middle,
        branch,
        out_cotangent,
        ffw_norm_gain,
        attn_post_gain,
        scalars=1,
    )
    d_branch = gather(d_branch, lanes, round_x).reshape(tok, width)
    d_queries, left_far, left_near, summed = attend_back(
        place, log_total, d_branch, output_weight, queries, pairs
    )
    got_near = shifted(left_near, -1)
    got_far = shifted(left_far, -2)
    got_near, got_far, got_a, got_b = tied(got_near, got_far, got_a, got_b)
    keep_a, give_a, keep_b, give_b = call(
        halve_kernel, [((336, width), bf16)] * 4, keep_a, got_a, keep_b, got_b
    )
    got_a = send(give_a, along_first(3))
    got_b = send(give_b, along_first(1))
    d_query, payload, query_part, key_part = call(
        key_kernel,
        [
            (square, bf16),
            ((tok, width + 2 * tok), bf16),
            ((1, head_dim), f32),
            ((1, head_dim), f32),
        ],
        q_raw,
        k_raw,
        d_queries,
        summed,
        got_near,
        got_far,
        cosine,
        sine,
        query_gain,
        key_gain,
        query_weight,
        key_weight,
        value_weight,
        flops=6 * tok * width * head_dim,
    )
    got_both = quarters(payload)
    (products,) = call(
        products_kernel,
        [((2 * head_dim, width), f32)],
        context,
        d_branch,
        d_query,
        normed,
        flops=4 * tok * width * head_dim,
    )
    *got_both, got_a, got_b = tied(*got_both, got_a, got_b)
    chunk = (3, 56, width)
    mine, *given = call(
        deal_kernel,
        [(chunk, f32)] + [(chunk, bf16)] * 3,
        where,
        keep_a,
        got_a,
        keep_b,
        got_b,
        scalars=1,
        scratch=[pltpu.VMEM((2, 336, width), f32)],
    )
    got = [send(part, round_second(by)) for by, part in zip((1, 2, 3), given, strict=True)]
    input_own, keep, give = pl.pallas_call(
        entry_kernel,
        out_shape=[
            jax.ShapeDtypeStruct(piece, bf16),
            jax.ShapeDtypeStruct((3, 16, 8, width), f32),
            jax.ShapeDtypeStruct((3, 16, 8, width), bf16),
        ],
        in_specs=[pl.BlockSpec(memory_space=pltpu.SMEM)]
        + [pl.BlockSpec(memory_space=pltpu.VMEM)] * 14,
        out_specs=[pl.BlockSpec(memory_space=pltpu.VMEM)] * 3,
        scratch_shapes=[pltpu.VMEM((tok, width), f32)],
        compiler_params=pltpu.CompilerParams(vmem_limit_bytes=SOME),
        cost_estimate=pl.CostEstimate(
            flops=256 * tok * width, bytes_accessed=12_000_000, transcendentals=0
        ),
    )(
        place,
        *got_both,
        layer_input,
        d_middle,
        attn_norm_gain,
        normed,
        post_part,
        ffw_part,
        final_part,
        query_part,
        key_part,
        products,
    )
    pack_got = send(give, swap_cores())
    part = (3, 4, 8, width)
    pack, *given = call(
        merge_kernel, [(part, f32)] + [(part, bf16)] * 3, where, keep, pack_got, scalars=1
    )
    got[0], *given = tied(got[0], *given)
    given = [send(part, round_first(by)) for by, part in zip((1, 2, 3), given, strict=True)]
    *given, got[0], got[1], got[2] = tied(*given, *got)
    mine = mine + got[0].astype(f32) + (got[1].astype(f32) + got[2].astype(f32))
    mine = mine.astype(bf16).reshape(168, width)
    for part in given:
        pack = pack + part.astype(f32)
    pack = pack.astype(bf16).reshape(96, width)
    both = lax.optimization_barrier(jnp.concatenate([mine, pack]))
    given = [send(both, round_second(by)) for by in (1, 2, 3)]
    ends = jnp.concatenate([out_own, input_own])
    got_ends = [send(ends, round_x(by)) for by in (1, 2, 3)]
    given[0], given[1], given[2], *got_ends = tied(*given, *got_ends)
    ends = joined(ends, got_ends, lanes)
    layer_output = ends[:, :64].reshape(tok, width)
    input_grad = ends[:, 64:].reshape(tok, width)
    quarter = joined(both[:168], [part[:168] for part in given], seconds)
    pack, *given = (part[168:].astype(f32) for part in (both, *given))
    pack = (pack + given[1] + (given[0] + given[2])).astype(bf16).reshape(3, 4, 8, width)
    given = [send(pack, round_first(by)) for by in (1, 2, 3)]
    other_own = send(quarter, swap_cores())
    given[0], quarter, other_own, layer_output, input_grad = tied(
        given[0], quarter, other_own, layer_output, input_grad
    )
    near_a = send(quarter, along_first(1))
    near_b = send(quarter, along_first(3))
    pack = joined(pack, given, firsts)
    pack_got = send(pack, swap_cores())
    rest = pack[:, 2]
    given = [send(rest, round_x(by)) for by in (1, 2, 3)]
    out_grad, query_grad = call(
        square_kernel,
        [((256, width), f32), ((width, 256), f32)],
        where,
        pack,
        pack_got,
        scalars=1,
        scratch=[pltpu.VMEM((2, 256, width), f32)],
    )
    grads = placed(where, [(quarter, False, 0, 0), (other_own, True, 0, 0)], [], units)
    grads = list(grads)
    *given, near_a, near_b, grads[0] = tied(*given, near_a, near_b, grads[0])
    far_a = send(near_b[:2], along_first(1))
    far_b = send(near_a[2:], along_first(3))
    other_a = send(near_a, swap_cores())
    other_b = send(near_b, swap_cores())
    rest = joined(rest, given, lanes)
    rest_got = send(rest, swap_cores())
    key_grad, value_grad, *gains = call(
        finish_kernel,
        [((width, 256), f32)] * 2 + [((width,), f32)] * 4 + [((256,), f32)] * 2,
        where,
        rest,
        rest_got,
        scalars=1,
        scratch=[pltpu.VMEM((4, 256, width), f32)],
    )
    other_a, out_grad, key_grad = tied(other_a, out_grad, key_grad)
    grads = placed(
        where,
        [
            (near_a, False, 1, 0),
            (near_b, False, 3, 0),
            (other_a, True, 1, 0),
            (other_b, True, 3, 0),
        ],
        grads,
        units,
    )
    far_a, far_b, *grads = tied(far_a, far_b, *grads)
    other_far_a = send(far_a, swap_cores())
    other_far_b = send(far_b, swap_cores())
    down_grad, gate_grad, up_grad = placed(
        where,
        [
            (far_a, False, 2, 0),
            (far_b, False, 2, 2),
            (other_far_a, True, 2, 0),
            (other_far_b, True, 2, 2),
        ],
        grads,
        units,
    )
    return (
        layer_output,
        input_grad,
        gains[0],
        query_grad,
        key_grad,
        value_grad,
        gains[4],
        gains[5],
        out_grad,
        gains[1],
        gains[2],
        gate_grad.T,
        up_grad.T,
        down_grad,
        gains[3],
    )


def solution(mesh):
    rows = P("seq", None)
    return jax.shard_map(
        local,
        mesh=mesh,
        in_specs=(
            rows,
            P("seq"),
            rows,
            P(),
            P(None, "tensor"),
            P(),
            P(),
            P(),
            P(),
            P("tensor", None),
            P(),
            P(),
            P(None, "tensor"),
            P(None, "tensor"),
            P("tensor", None),
            P(),
        ),
        out_specs=(
            rows,
            rows,
            P(),
            P(None, "tensor"),
            P(),
            P(),
            P(),
            P(),
            P("tensor", None),
            P(),
            P(),
            P(None, "tensor"),
            P(None, "tensor"),
            P("tensor", None),
            P(),
        ),
        check_vma=False,
    )
```

```python
import functools

import jax
import jax.numpy as jnp
import numpy as np
from jax import lax
from jax.experimental import pallas as pl
from jax.experimental.pallas import tpu as pltpu
from jax.sharding import PartitionSpec as P

WINDOW = 512
SOME = 24 * 1024 * 1024
MOST = 60 * 1024 * 1024

eps = 1e-06
rope_base = 10000.0
f32 = jnp.float32
bf16 = jnp.bfloat16
BOTH = ("seq", "tensor")


def places():
    return [(z, y, c, x) for z in range(4) for y in range(4) for c in range(2) for x in range(4)]


def number(z, y, c, x):
    return ((z * 4 + y) * 2 + c) * 4 + x


def route(move):
    return [(number(*p), number(*move(*p))) for p in places()]


def round_x(by):
    return route(lambda z, y, c, x: (z, y, c, (x + by) % 4))


def swap_cores():
    return route(lambda z, y, c, x: (z, y, 1 - c, x))


def along_first(flip):
    return route(lambda z, y, c, x: (z, y ^ flip, c, x) if c == 0 else (z ^ flip, y, c, x))


def round_first(by):
    return route(
        lambda z, y, c, x: (z, (y + by) % 4, c, x) if c == 0 else ((z + by) % 4, y, c, x)
    )


def round_second(by):
    return route(
        lambda z, y, c, x: ((z + by) % 4, y, c, x) if c == 0 else (z, (y + by) % 4, c, x)
    )


def send(value, pairs):
    return lax.ppermute(value, BOTH, pairs)


def shifted(value, by):
    pairs = [
        (i * 4 + x, (i + by) * 4 + x) for i in range(32) if 0 <= i + by < 32 for x in range(4)
    ]
    return send(value, pairs)


def pick(parts, index, axis=0):
    return lax.dynamic_index_in_dim(
        parts, index, axis, keepdims=False, allow_negative_indices=False
    )


def put(parts, part, index):
    return lax.dynamic_update_index_in_dim(parts, part, index, 0, allow_negative_indices=False)


def dot(first, second, over):
    return lax.dot_general(
        first, second, (((over[0],), (over[1],)), ((), ())), preferred_element_type=f32
    )


def joined(own, got, after):
    whole = put(jnp.zeros((4, *own.shape), own.dtype), own, after[0])
    for by, part in zip((1, 2, 3), got, strict=True):
        whole = put(whole, part, after[4 - by])
    return whole


def gather(part, after, turn):
    return joined(part, [send(part, turn(by)) for by in (1, 2, 3)], after)


def inv_scale(values):
    return lax.rsqrt(jnp.mean(values * values, axis=-1, keepdims=True) + eps)


def norm_back(values, scale, gain, grad):
    unit = values * scale
    weighted = grad * gain
    d_values = scale * (weighted - unit * jnp.mean(weighted * unit, axis=-1, keepdims=True))
    return (d_values, jnp.sum(grad * unit, axis=0))


def rotate(values, cosine, sine):
    half = values.shape[-1] // 2
    first = values[..., :half]
    second = values[..., half:]
    return jnp.concatenate(
        [first * cosine - second * sine, second * cosine + first * sine], axis=-1
    )


def padded(values, rows):
    return jnp.pad(values, ((0, rows - values.shape[0]), (0, 0)))


def added(first, second):
    return (first.astype(f32) + second.astype(f32)).astype(bf16)


def tied(*values):
    return lax.optimization_barrier(values)


def call(kernel, outs, *arrays, scalars=0, flops=0, room=SOME, scratch=()):
    vmem = pl.BlockSpec(memory_space=pltpu.VMEM)
    outs = [jax.ShapeDtypeStruct(*o) for o in outs]
    moved = sum(v.size * v.dtype.itemsize for v in (*arrays, *outs))
    return pl.pallas_call(
        kernel,
        out_shape=outs,
        in_specs=[pl.BlockSpec(memory_space=pltpu.SMEM)] * scalars
        + [vmem] * (len(arrays) - scalars),
        out_specs=[vmem] * len(outs),
        scratch_shapes=scratch,
        compiler_params=pltpu.CompilerParams(vmem_limit_bytes=room),
        cost_estimate=pl.CostEstimate(flops=flops, bytes_accessed=moved, transcendentals=0),
    )(*arrays)


def own_rows(ref, lane, rows):
    return ref[pl.ds(pl.multiple_of(lane * rows, rows), rows)].astype(f32)


def project_kernel(
    place, x, post_gain, ffw_gain, ctx0, ctx1, ctx2, ctx3, weight, own1, own2, own3, other1, other2, other3,
    branch, middle, normed
):
    even = place[1] == 0
    half = own1.shape[0]
    total = dot(ctx0[...], weight[...], (1, 0))
    for ctx, mine, theirs in ((ctx1, own1, other1), (ctx2, own2, other2), (ctx3, own3, other3)):
        low = jnp.where(even, mine[...], theirs[...])
        high = jnp.where(even, theirs[...], mine[...])
        total += dot(ctx[:, :half], low, (1, 0)) + dot(ctx[:, half:], high, (1, 0))
    branch[...] = total
    after = x[...].astype(f32) + total * inv_scale(total) * post_gain[...]
    middle[...] = after
    normed[...] = (after * inv_scale(after) * ffw_gain[...]).astype(bf16)


def final_kernel(place, p0, p1, p2, p3, middle, cotangent, gain, out, d_branch, part):
    lane = place[0]
    branch = p0[...].astype(f32) + p1[...].astype(f32) + p2[...].astype(f32) + p3[...].astype(f32)
    rows = branch.shape[0]
    scale = inv_scale(branch)
    cot = own_rows(cotangent, lane, rows)
    out[...] = (own_rows(middle, lane, rows) + branch * scale * gain[...]).astype(bf16)
    d_values, d_gain = norm_back(branch, scale, gain[...], cot)
    d_branch[...] = d_values.astype(bf16)
    part[...] = d_gain[None]


def between_kernel(
    place, p0, p1, p2, p3, middle, branch, cotangent, ffw_gain, post_gain,
    d_middle, d_branch, ffw_part, post_part
):
    lane = place[0]
    grad = p0[...].astype(f32) + p1[...].astype(f32) + p2[...].astype(f32) + p3[...].astype(f32)
    rows = grad.shape[0]
    after = own_rows(middle, lane, rows)
    before = own_rows(branch, lane, rows)
    d_values, d_gain = norm_back(after, inv_scale(after), ffw_gain[...], grad)
    ffw_part[...] = d_gain[None]
    d_values = own_rows(cotangent, lane, rows) + d_values
    d_middle[...] = d_values
    d_values, d_gain = norm_back(before, inv_scale(before), post_gain[...], d_values)
    d_branch[...] = d_values.astype(bf16)
    post_part[...] = d_gain[None]


def key_kernel(
    q_raw, k_raw, d_queries, d_own, d_near, d_far, cosine, sine, query_gain, key_gain, query_weight, key_weight,
    value_weight, d_query, payload, query_part, key_part
):
    tok, head_dim = q_raw.shape
    width = query_weight.shape[0]
    cos, sin = cosine[...], -sine[...]
    raw = q_raw[...]
    d_raw, d_gain = norm_back(
        raw, inv_scale(raw), query_gain[...], rotate(d_queries[...] * head_dim**-0.5, cos, sin)
    )
    query_part[...] = d_gain[None]
    d_low = d_raw.astype(bf16)
    d_query[...] = d_low
    total = dot(d_low, query_weight[...], (1, 1))
    summed = d_own[...] + d_near[...].astype(f32) + d_far[...].astype(f32)
    raw = k_raw[...]
    d_raw, d_gain = norm_back(raw, inv_scale(raw), key_gain[...], rotate(summed[:tok], cos, sin))
    key_part[...] = d_gain[None]
    total += dot(d_raw.astype(bf16), key_weight[...], (1, 1))
    total += dot(summed[tok:].astype(bf16), value_weight[...], (1, 1))
    payload[:, :width] = total.astype(bf16)
    payload[:, width : width + tok] = d_raw.T.astype(bf16)
    payload[:, width + tok :] = summed[tok:].T.astype(bf16)


def products_kernel(context, d_branch, d_query, normed, out):
    half = context.shape[1]
    out[:half] = dot(context[...], d_branch[...], (0, 0))
    out[half:] = dot(d_query[...], normed[...], (0, 0))


def entry_kernel(
    place, p0, p1, p2, p3, x, d_middle, gain, normed, post_part, ffw_part, final_part, query_part, key_part,
    products, input_grad, keep, give, rest
):
    lane, core = place[0], place[1]
    both = p0[...].astype(f32) + p1[...].astype(f32) + p2[...].astype(f32) + p3[...].astype(f32)
    rows = both.shape[0]
    width = normed.shape[1]
    tok = normed.shape[0]
    full = own_rows(x, lane, rows)
    d_values, d_gain = norm_back(full, inv_scale(full), gain[...], both[:, :width])
    input_grad[...] = (d_middle[...] + d_values).astype(bf16)
    d_keys = both[:, width : width + tok].astype(bf16)
    d_values = both[:, width + tok :].astype(bf16)
    rest[:rows] = dot(d_keys, normed[...], (1, 0))
    rest[rows : 2 * rows] = dot(d_values, normed[...], (1, 0))
    heads = jnp.concatenate(
        [query_part[...], key_part[...], jnp.zeros((1, width - 2 * query_part.shape[1]), f32)], axis=1
    )
    index = lax.broadcasted_iota(jnp.int32, (8, width), 0)
    gains = jnp.zeros((8, width), f32)
    for at, part in enumerate((d_gain[None], post_part[...], ffw_part[...], final_part[...], heads)):
        gains = jnp.where(index == at, part, gains)
    rest[2 * rows : 2 * rows + 8] = gains
    rest[2 * rows + 8 :] = jnp.zeros((rest.shape[0] - 2 * rows - 8, width), f32)
    for kind in range(3):
        source = rest if kind == 2 else products
        base = 256 if kind == 1 else 0
        for chip in range(16):
            at = base + 16 * chip
            keep[kind, chip] = source[pl.ds(pl.multiple_of(at + 8 * core, 8), 8)]
            give[kind, chip] = source[pl.ds(pl.multiple_of(at + 8 - 8 * core, 8), 8)].astype(bf16)


def merge_kernel(where, keep, got, *outs):
    core, first = where[0], where[1]
    for by, out in enumerate(outs):
        along = lax.rem(first + by, 4)
        for across in range(4):
            chip = jnp.where(core == 0, 4 * across + along, 4 * along + across)
            for kind in range(3):
                total = keep[kind, chip] + got[kind, chip].astype(f32)
                out[kind, across] = total.astype(out.dtype)


def weight_kernel(
    hid_own, hid_got, gate_own, gate_got, up_own, up_got, dy_own, dy_got, xn_own, xn_got, *outs
):
    mats = (
        (hid_own, hid_got, dy_own, dy_got),
        (gate_own, gate_got, xn_own, xn_got),
        (up_own, up_got, xn_own, xn_got),
    )
    for group, out in enumerate(outs):
        for index, (left_own, left_got, right_own, right_got) in enumerate(mats):
            total = jnp.dot(left_own[group], right_own[...], preferred_element_type=f32)
            total += jnp.dot(left_got[group], right_got[...], preferred_element_type=f32)
            total = total.astype(bf16)
            out[112 * index : 112 * index + 112] = total[:112]
            out[336 + 112 * index : 448 + 112 * index] = total[112:]


def weight_parts(*arrays):
    width = arrays[-1].shape[1]
    return pl.pallas_call(
        weight_kernel,
        out_shape=[jax.ShapeDtypeStruct((672, width), bf16)] * 4,
        in_specs=[pl.BlockSpec(memory_space=pltpu.VMEM)] * len(arrays),
        out_specs=[pl.BlockSpec(memory_space=pltpu.VMEM)] * 4,
        compiler_params=pltpu.CompilerParams(vmem_limit_bytes=SOME),
        cost_estimate=pl.CostEstimate(
            flops=2 * 2688 * 512 * width, bytes_accessed=12_000_000, transcendentals=0
        ),
    )(*arrays)


def halve_kernel(keep_a, got_a, keep_b, got_b, *outs):
    for keep, got, half in ((keep_a, got_a, outs[:2]), (keep_b, got_b, outs[2:])):
        for index, out in enumerate(half):
            rows = pl.ds(336 * index, 336)
            out[...] = (keep[rows].astype(f32) + got[rows].astype(f32)).astype(bf16)


def deal_kernel(where, keep_a, got_a, keep_b, got_b, *refs):
    outs, total = refs[:-1], refs[-1]
    total[0] = keep_a[...].astype(f32) + got_a[...].astype(f32)
    total[1] = keep_b[...].astype(f32) + got_b[...].astype(f32)
    for by, out in enumerate(outs):
        across = lax.rem(where[2] + by, 4)
        for mat in range(3):
            row = pl.multiple_of(112 * mat + 56 * lax.rem(across, 2), 8)
            out[mat] = total[across // 2, pl.ds(row, 56)].astype(out.dtype)


def masks(block, pairs):
    tok = pairs[0].shape[1]
    query = lax.broadcasted_iota(jnp.int32, (tok, tok), 0)
    key = lax.broadcasted_iota(jnp.int32, (tok, tok), 1)
    rows = [pair[2 * tok : 2 * tok + 16].astype(f32)[:1] for pair in pairs]
    segment = jnp.broadcast_to(rows[2], (tok, tok)).T
    same = [segment == row for row in rows]
    return (
        same[0] & (key > query) & (block >= 2),
        same[1] & (block >= 1),
        same[2] & (key <= query),
    )


def prepare_kernel(
    place, x, gain, key_weight, value_weight, query_weight, key_gain, query_gain, start_cos, start_sin, inner_cos,
    inner_sin, marks, xn, pair, k_raw, q_raw, queries, cosine, sine
):
    tok, head_dim = k_raw.shape
    full = x[...].astype(f32)
    low = (full * inv_scale(full) * gain[...]).astype(bf16)
    xn[...] = low
    at = pl.ds(place[2], 1)
    cos = start_cos[at] * inner_cos[...] - start_sin[at] * inner_sin[...]
    sin = start_sin[at] * inner_cos[...] + start_cos[at] * inner_sin[...]
    cosine[...] = cos
    sine[...] = sin
    raw = dot(low, key_weight[...], (1, 0))
    k_raw[...] = raw
    pair[:tok] = rotate(raw * inv_scale(raw) * key_gain[...], cos, sin).astype(bf16)
    pair[tok : 2 * tok] = dot(low, value_weight[...], (1, 0)).astype(bf16)
    pair[2 * tok :] = jnp.broadcast_to(marks[...].astype(f32)[None], (16, tok)).astype(bf16)
    raw = dot(low, query_weight[...], (1, 0))
    q_raw[...] = raw
    turned = rotate(raw * inv_scale(raw) * query_gain[...], cos, sin)
    queries[...] = (turned * head_dim**-0.5).astype(bf16)


def attend_kernel(place, queries, far, near, own, context, log_total):
    pairs = (far, near, own)
    tok = queries.shape[0]
    allowed = masks(place[2], pairs)
    scores = [
        jnp.where(ok, dot(queries[...], pair[:tok], (1, 1)), -1e30)
        for ok, pair in zip(allowed, pairs, strict=True)
    ]
    top = functools.reduce(jnp.maximum, [jnp.max(s, axis=1, keepdims=True) for s in scores])
    weights = [jnp.exp(s - top) for s in scores]
    total = sum(jnp.sum(w, axis=1, keepdims=True) for w in weights)
    context[...] = sum(
        dot((w / total).astype(bf16), pair[tok : 2 * tok], (1, 0))
        for w, pair in zip(weights, pairs, strict=True)
    ).astype(bf16)
    log_total[...] = jnp.broadcast_to(top + jnp.log(total), log_total.shape)


def attend(place, queries, pairs):
    tok, head_dim = queries.shape
    vmem = pl.BlockSpec(memory_space=pltpu.VMEM)
    return pl.pallas_call(
        attend_kernel,
        out_shape=[
            jax.ShapeDtypeStruct((tok, head_dim), bf16),
            jax.ShapeDtypeStruct((tok, 128), f32),
        ],
        in_specs=[pl.BlockSpec(memory_space=pltpu.SMEM)] + [vmem] * 4,
        out_specs=[vmem] * 2,
        compiler_params=pltpu.CompilerParams(vmem_limit_bytes=SOME),
        cost_estimate=pl.CostEstimate(
            flops=12 * tok * tok * head_dim, bytes_accessed=1_500_000, transcendentals=3 * tok * tok
        ),
    )(place, queries, *pairs)


def attend_back_kernel(
    place, log_total, d_branch, weight, queries, far, near, own, d_queries, d_far, d_near, d_own
):
    pairs = (far, near, own)
    tok = queries.shape[0]
    d_context = dot(d_branch[...], weight[...], (1, 1)).astype(bf16)
    allowed = masks(place[2], pairs)
    lse = log_total[:, :1]
    probs, d_probs = [], []
    for ok, pair in zip(allowed, pairs, strict=True):
        scores = jnp.where(ok, dot(queries[...], pair[:tok], (1, 1)), -1e30)
        probs.append(jnp.exp(scores - lse))
        d_probs.append(dot(d_context, pair[tok : 2 * tok], (1, 1)))
    mean = sum(
        jnp.sum(p * d, axis=1, keepdims=True) for p, d in zip(probs, d_probs, strict=True)
    )
    total = None
    for p, d, pair, out in zip(probs, d_probs, pairs, (d_far, d_near, d_own), strict=True):
        d_scores = (p * (d - mean)).astype(bf16)
        part = dot(d_scores, pair[:tok], (1, 0))
        total = part if total is None else total + part
        out[:tok] = dot(d_scores, queries[...], (0, 0)).astype(out.dtype)
        out[tok:] = dot(p.astype(bf16), d_context, (0, 0)).astype(out.dtype)
    d_queries[...] = total


def attend_back(place, log_total, d_branch, weight, queries, pairs):
    tok, head_dim = queries.shape
    vmem = pl.BlockSpec(memory_space=pltpu.VMEM)
    return pl.pallas_call(
        attend_back_kernel,
        out_shape=[
            jax.ShapeDtypeStruct((tok, head_dim), f32),
            jax.ShapeDtypeStruct((2 * tok, head_dim), bf16),
            jax.ShapeDtypeStruct((2 * tok, head_dim), bf16),
            jax.ShapeDtypeStruct((2 * tok, head_dim), f32),
        ],
        in_specs=[pl.BlockSpec(memory_space=pltpu.SMEM)] + [vmem] * 7,
        out_specs=[vmem] * 4,
        compiler_params=pltpu.CompilerParams(vmem_limit_bytes=SOME),
        cost_estimate=pl.CostEstimate(
            flops=30 * tok * tok * head_dim, bytes_accessed=3_500_000, transcendentals=3 * tok * tok
        ),
    )(place, log_total, d_branch, weight, queries, *pairs)


def place_kernel(where_ref, *refs, turns, held):
    n = len(turns)
    parts, outs = refs[:n], refs[n + held : n + held + 3]
    stage, sems, tail_sems = refs[-3:]
    slots = stage.shape[0]
    core, first, second = where_ref[0], where_ref[1], where_ref[2]
    chunks = [
        (ref, i, base + i, other, flip)
        for ref, (other, flip, base) in zip(parts, turns, strict=True)
        for i in range(ref.shape[0])
    ]

    def place(index):
        _, _, across, other, flip = chunks[index]
        which = 1 - core if other else core
        along = (second if other else first) ^ flip
        y = jnp.where(which == 0, along, across)
        z = jnp.where(which == 0, across, along)
        odd = lax.rem(y, 2)
        row = 216 * (2 * z + y // 2) + 104 * odd + 48 * which + 8 * which * odd
        return pl.multiple_of(row, 8), (which == 1) | (odd == 1)

    def copies(index):
        slot = index % slots
        row, whole = place(index)
        for mat, out in enumerate(outs):
            yield (
                pltpu.make_async_copy(
                    stage.at[slot, mat, pl.ds(0, 48)],
                    out.at[pl.ds(row, 48)],
                    sems.at[slot, mat],
                ),
                pltpu.make_async_copy(
                    stage.at[slot, mat, pl.ds(48, 8)],
                    out.at[pl.ds(pl.multiple_of(row + 48, 8), 8)],
                    tail_sems.at[slot, mat],
                ),
                whole,
            )

    def finish(index):
        for most, tail, whole in copies(index):
            most.wait()
            pl.when(whole)(tail.wait)

    for index, (ref, i, *_) in enumerate(chunks):
        if index >= slots:
            finish(index - slots)
        stage[index % slots] = ref[i].astype(f32)
        for most, tail, whole in copies(index):
            most.start()
            pl.when(whole)(tail.start)
    for index in range(max(0, len(chunks) - slots), len(chunks)):
        finish(index)


def placed(where, parts, outs, units):
    arrays = [p[0].reshape(-1, 3, 56, p[0].shape[-1]) for p in parts]
    width = arrays[0].shape[-1]
    slots = 4
    return pl.pallas_call(
        functools.partial(
            place_kernel, turns=tuple(p[1:] for p in parts), held=len(outs)
        ),
        out_shape=[jax.ShapeDtypeStruct((units, width), f32)] * 3,
        in_specs=[pl.BlockSpec(memory_space=pltpu.SMEM)]
        + [pl.BlockSpec(memory_space=pltpu.VMEM)] * len(arrays)
        + [pl.BlockSpec(memory_space=pl.ANY)] * len(outs),
        out_specs=[pl.BlockSpec(memory_space=pl.ANY)] * 3,
        scratch_shapes=[
            pltpu.VMEM((slots, 3, 56, width), f32),
            pltpu.SemaphoreType.DMA((slots, 3)),
            pltpu.SemaphoreType.DMA((slots, 3)),
        ],
        input_output_aliases={1 + len(arrays) + i: i for i in range(len(outs))},
        compiler_params=pltpu.CompilerParams(vmem_limit_bytes=SOME),
        cost_estimate=pl.CostEstimate(
            flops=0, bytes_accessed=sum(p.size for p in arrays) * 6, transcendentals=0
        ),
    )(where, *arrays, *outs)


def sorted_rows(core, own, got, rows, kinds):
    for pieces, other in ((own, 0), (got, 1)):
        even = core == other
        for along in range(4):
            for across in range(4):
                row = jnp.where(even, 8 * across + 2 * along, 8 * along + 2 * across + 1) * 8
                row = pl.ds(pl.multiple_of(row, 8), 8)
                for kind in range(kinds):
                    rows[kind, row] = pieces(kind, along, across).astype(f32)


def square_kernel(where, own, got, out_grad, query_grad, rows):
    sorted_rows(
        where[0],
        lambda kind, along, across: own[along, kind, across],
        lambda kind, along, across: got[along, kind, across],
        rows,
        2,
    )
    out_grad[...] = rows[0]
    query_grad[...] = rows[1].T


def finish_kernel(
    where, own, got, key_grad, value_grad, attn, post, ffw, final, query, key, rows
):
    sorted_rows(
        where[0],
        lambda lane, along, across: own[lane, along, across],
        lambda lane, along, across: got[lane, along, across],
        rows,
        4,
    )
    for lane in range(4):
        key_grad[:, 64 * lane : 64 * lane + 64] = rows[lane, :64].T
        value_grad[:, 64 * lane : 64 * lane + 64] = rows[lane, 64:128].T
    gains = sum(rows[lane, 128:136] for lane in range(4))
    for at, out in enumerate((attn, post, ffw, final)):
        out[...] = gains[at]
    size = query.shape[0]
    query[...] = gains[4, :size]
    key[...] = gains[4, size : 2 * size]


def local(
    layer_input,
    segment_ids,
    out_cotangent,
    attn_norm_gain,
    query_weight,
    key_weight,
    value_weight,
    query_gain,
    key_gain,
    output_weight,
    attn_post_gain,
    ffw_norm_gain,
    gate_weight,
    up_weight,
    down_weight,
    ffw_post_gain,
):
    tok, width = layer_input.shape
    head_dim = key_weight.shape[1]
    units = down_weight.shape[0]
    block = lax.axis_index("seq")
    lane = lax.axis_index("tensor")
    core = lax.rem(block, 2)
    row = lax.rem(lax.div(block, 2), 4)
    plane = lax.div(block, 8)
    first = lax.select(core == 0, row, plane)
    second = lax.select(core == 0, plane, row)
    place = jnp.stack([lane, core, block])
    where = jnp.stack([core, first, second])
    afters = [lax.rem(at + by, 4) for at in (lane, first, second) for by in range(4)]
    flips = [first ^ flip for flip in range(1, 4)]
    place, where, core, other_core, even, *places_at = tied(
        place, where, core, 1 - core, core == 0, *afters, *flips
    )
    lanes, firsts, seconds = places_at[:4], places_at[4:8], places_at[8:12]
    flips = [firsts[0], *places_at[12:]]
    quarter_tok = tok // 4

    freq = rope_base ** (-2.0 * np.arange(head_dim // 2) / head_dim)
    start = (np.arange(lax.axis_size("seq")) * tok)[:, None] * freq[None, :]
    inner = np.arange(tok)[:, None] * freq[None, :]
    tables = [jnp.asarray(f(angle), f32) for angle in (start, inner) for f in (np.cos, np.sin)]

    square = (tok, head_dim)
    normed, own_pair, k_raw, q_raw, queries, cosine, sine = call(
        prepare_kernel,
        [
            ((tok, width), bf16),
            ((2 * tok + 16, head_dim), bf16),
            (square, f32),
            (square, f32),
            (square, bf16),
            ((tok, head_dim // 2), f32),
            ((tok, head_dim // 2), f32),
        ],
        place,
        layer_input,
        attn_norm_gain,
        key_weight,
        value_weight,
        query_weight,
        key_gain,
        query_gain,
        *tables,
        segment_ids,
        scalars=1,
        flops=6 * tok * width * head_dim,
        room=MOST,
    )
    left_one = shifted(own_pair, 1)
    left_two = shifted(own_pair, 2)

    weight_half = tok // 2
    halved, left_one = tied(output_weight, left_one)
    own_weight = pick(halved.reshape(2, weight_half, width), core)
    got_weight = [send(own_weight, round_x(by)) for by in (1, 2, 3)]

    pairs = (left_two, left_one, own_pair)
    context, log_total = attend(place, queries, pairs)

    got_context = [send(context, round_x(by)) for by in (1, 2, 3)]
    *got_context, got_weight[0], got_weight[1], got_weight[2] = tied(*got_context, *got_weight)
    other_weight = [send(part, swap_cores()) for part in got_weight]
    branch, middle, normed_two = call(
        project_kernel,
        [((tok, width), f32), ((tok, width), f32), ((tok, width), bf16)],
        place,
        layer_input,
        attn_post_gain,
        ffw_norm_gain,
        context,
        *got_context,
        output_weight,
        *got_weight,
        *other_weight,
        scalars=1,
        flops=8 * tok * tok * width,
    )
    gate = dot(gate_weight, normed_two, (0, 1))
    up_val = dot(up_weight, normed_two, (0, 1))
    active, gelu_back = jax.vjp(lambda val: jax.nn.gelu(val, approximate=True), gate)
    hidden = (active * up_val).astype(bf16)
    down_part = dot(hidden, down_weight, (0, 0)).astype(bf16)

    def halves(values):
        groups = values.reshape(8, units // 8, tok)
        groups = jnp.concatenate([groups[:, :56], groups[:, 48:]], axis=1)
        pieces = groups.reshape(4, 4, 2, 56, tok)
        return pick(pieces, core, 2), pick(pieces, other_core, 2)

    def arranged(values):
        values = jnp.where(even, values.swapaxes(0, 1), values)
        by_first = tied(*(pick(values, flip) for flip in flips))
        groups = [
            jnp.stack([by_first[i][2 * stream : 2 * stream + 2] for i in order])
            for stream, order in ((0, (0, 3)), (0, (1, 2)), (1, (0, 1)), (1, (3, 2)))
        ]
        return jnp.stack(groups).reshape(4, 224, tok)

    hidden_own, hidden_give = halves(hidden)
    hidden_got = send(hidden_give, swap_cores())
    normed_two_got = send(normed_two, swap_cores())

    def quarters(parts):
        parts = parts.reshape(4, quarter_tok, parts.shape[-1])
        given = [pick(parts, at) for at in lanes[1:]]
        return [pick(parts, lanes[0])] + [
            send(part, round_x(by)) for by, part in zip((1, 2, 3), given, strict=True)
        ]

    piece = (quarter_tok, width)
    out_own, d_branch_two, final_part = call(
        final_kernel,
        [(piece, bf16), (piece, bf16), ((1, width), f32)],
        place,
        *quarters(down_part),
        middle,
        out_cotangent,
        ffw_post_gain,
        scalars=1,
    )
    d_branch_two = gather(d_branch_two, lanes, round_x).reshape(tok, width)
    d_branch_two_got = send(d_branch_two, swap_cores())

    d_hidden = dot(down_weight, d_branch_two, (1, 1))
    d_gate = gelu_back(d_hidden * up_val)[0].astype(bf16)
    d_up = (d_hidden * active).astype(bf16)
    d_normed_two = (dot(d_gate, gate_weight, (0, 1)) + dot(d_up, up_weight, (0, 1))).astype(bf16)
    d_gate_own, d_gate_give = halves(d_gate)
    d_up_own, d_up_give = halves(d_up)
    d_pair_got = send(jnp.stack([d_gate_give, d_up_give]), swap_cores())

    keep_a, give_a, keep_b, give_b = weight_parts(
        *(
            arranged(v)
            for v in (hidden_own, hidden_got, d_gate_own, d_pair_got[0], d_up_own, d_pair_got[1])
        ),
        d_branch_two,
        d_branch_two_got,
        normed_two,
        normed_two_got,
    )
    *got_normed, keep_a, keep_b = tied(*quarters(d_normed_two), keep_a, keep_b)
    d_middle, d_branch, ffw_part, post_part = call(
        between_kernel,
        [(piece, f32), (piece, bf16), ((1, width), f32), ((1, width), f32)],
        place,
        *got_normed,
        middle,
        branch,
        out_cotangent,
        ffw_norm_gain,
        attn_post_gain,
        scalars=1,
    )
    d_branch = gather(d_branch, lanes, round_x).reshape(tok, width)
    d_queries, left_far, left_near, summed = attend_back(
        place, log_total, d_branch, output_weight, queries, pairs
    )
    got_near = shifted(left_near, -1)
    got_far = shifted(left_far, -2)
    got_near, got_far, give_a, give_b = tied(got_near, got_far, give_a, give_b)
    got_a = send(give_a, along_first(1))
    got_b = send(give_b, along_first(3))
    d_query, payload, query_part, key_part = call(
        key_kernel,
        [
            (square, bf16),
            ((tok, width + 2 * tok), bf16),
            ((1, head_dim), f32),
            ((1, head_dim), f32),
        ],
        q_raw,
        k_raw,
        d_queries,
        summed,
        got_near,
        got_far,
        cosine,
        sine,
        query_gain,
        key_gain,
        query_weight,
        key_weight,
        value_weight,
        flops=6 * tok * width * head_dim,
    )
    got_both = quarters(payload)
    (products,) = call(
        products_kernel,
        [((2 * head_dim, width), f32)],
        context,
        d_branch,
        d_query,
        normed,
        flops=4 * tok * width * head_dim,
    )
    *got_both, got_a, got_b = tied(*got_both, got_a, got_b)
    keep_a, give_a, keep_b, give_b = call(
        halve_kernel, [((336, width), bf16)] * 4, keep_a, got_a, keep_b, got_b
    )
    got_a = send(give_a, along_first(3))
    got_b = send(give_b, along_first(1))
    input_own, keep, give = pl.pallas_call(
        entry_kernel,
        out_shape=[
            jax.ShapeDtypeStruct(piece, bf16),
            jax.ShapeDtypeStruct((3, 16, 8, width), f32),
            jax.ShapeDtypeStruct((3, 16, 8, width), bf16),
        ],
        in_specs=[pl.BlockSpec(memory_space=pltpu.SMEM)]
        + [pl.BlockSpec(memory_space=pltpu.VMEM)] * 14,
        out_specs=[pl.BlockSpec(memory_space=pltpu.VMEM)] * 3,
        scratch_shapes=[pltpu.VMEM((tok, width), f32)],
        compiler_params=pltpu.CompilerParams(vmem_limit_bytes=SOME),
        cost_estimate=pl.CostEstimate(
            flops=256 * tok * width, bytes_accessed=12_000_000, transcendentals=0
        ),
    )(
        place,
        *got_both,
        layer_input,
        d_middle,
        attn_norm_gain,
        normed,
        post_part,
        ffw_part,
        final_part,
        query_part,
        key_part,
        products,
    )
    pack_got = send(give, swap_cores())
    part = (3, 4, 8, width)
    pack, *given = call(
        merge_kernel, [(part, f32)] + [(part, bf16)] * 3, where, keep, pack_got, scalars=1
    )
    given = [send(part, round_first(by)) for by, part in zip((1, 2, 3), given, strict=True)]
    *given, got_a, got_b = tied(*given, got_a, got_b)
    chunk = (3, 56, width)
    mine, *dealt = call(
        deal_kernel,
        [(chunk, f32)] + [(chunk, bf16)] * 3,
        where,
        keep_a,
        got_a,
        keep_b,
        got_b,
        scalars=1,
        scratch=[pltpu.VMEM((2, 336, width), f32)],
    )
    got = [send(part, round_second(by)) for by, part in zip((1, 2, 3), dealt, strict=True)]
    for part in given:
        pack = pack + part.astype(f32)
    got[0], pack = tied(got[0], pack.astype(bf16))
    given = [send(pack, round_second(by)) for by in (1, 2, 3)]
    *given, got[0], got[1], got[2] = tied(*given, *got)
    mine = mine + got[0].astype(f32) + (got[1].astype(f32) + got[2].astype(f32))
    mine = mine.astype(bf16).reshape(168, width)
    got = [send(mine, round_second(by)) for by in (1, 2, 3)]
    pack, *given = (part.astype(f32) for part in (pack, *given))
    pack = (pack + given[1] + (given[0] + given[2])).astype(bf16)
    got[0], pack = tied(got[0], pack)
    given = [send(pack, round_first(by)) for by in (1, 2, 3)]
    quarter = joined(mine, got, seconds)
    near_a = send(quarter, along_first(1))
    near_b = send(quarter, along_first(3))
    other_own = send(quarter, swap_cores())
    pack = joined(pack, given, firsts)
    pack_got = send(pack, swap_cores())
    rest, pack_got = tied(pack[:, 2], pack_got)
    given = [send(rest, round_x(by)) for by in (1, 2, 3)]
    out_grad, query_grad = call(
        square_kernel,
        [((256, width), f32), ((width, 256), f32)],
        where,
        pack,
        pack_got,
        scalars=1,
        scratch=[pltpu.VMEM((2, 256, width), f32)],
    )
    grads = placed(where, [(quarter, False, 0, 0), (other_own, True, 0, 0)], [], units)
    grads = list(grads)
    given[0], given[1], given[2], out_own, input_own, out_grad = tied(
        *given, out_own, input_own, out_grad
    )
    ends = jnp.concatenate([out_own, input_own])
    got_ends = [send(ends, round_x(by)) for by in (1, 2, 3)]
    near_a, near_b, grads[0] = tied(near_a, near_b, grads[0])
    far_a = send(near_b[:2], along_first(1))
    far_b = send(near_a[2:], along_first(3))
    other_a = send(near_a, swap_cores())
    other_b = send(near_b, swap_cores())
    rest = joined(rest, given, lanes)
    rest_got = send(rest, swap_cores())
    key_grad, value_grad, *gains = call(
        finish_kernel,
        [((width, 256), f32)] * 2 + [((width,), f32)] * 4 + [((256,), f32)] * 2,
        where,
        rest,
        rest_got,
        scalars=1,
        scratch=[pltpu.VMEM((4, 256, width), f32)],
    )
    other_a, key_grad = tied(other_a, key_grad)
    ends = joined(ends, got_ends, lanes)
    layer_output = ends[:, :64].reshape(tok, width)
    input_grad = ends[:, 64:].reshape(tok, width)
    grads = placed(
        where,
        [
            (near_a, False, 1, 0),
            (near_b, False, 3, 0),
            (other_a, True, 1, 0),
            (other_b, True, 3, 0),
        ],
        grads,
        units,
    )
    far_a, far_b, *grads = tied(far_a, far_b, *grads)
    other_far_a = send(far_a, swap_cores())
    other_far_b = send(far_b, swap_cores())
    down_grad, gate_grad, up_grad = placed(
        where,
        [
            (far_a, False, 2, 0),
            (far_b, False, 2, 2),
            (other_far_a, True, 2, 0),
            (other_far_b, True, 2, 2),
        ],
        grads,
        units,
    )
    return (
        layer_output,
        input_grad,
        gains[0],
        query_grad,
        key_grad,
        value_grad,
        gains[4],
        gains[5],
        out_grad,
        gains[1],
        gains[2],
        gate_grad.T,
        up_grad.T,
        down_grad,
        gains[3],
    )


def solution(mesh):
    rows = P("seq", None)
    return jax.shard_map(
        local,
        mesh=mesh,
        in_specs=(
            rows,
            P("seq"),
            rows,
            P(),
            P(None, "tensor"),
            P(),
            P(),
            P(),
            P(),
            P("tensor", None),
            P(),
            P(),
            P(None, "tensor"),
            P(None, "tensor"),
            P("tensor", None),
            P(),
        ),
        out_specs=(
            rows,
            rows,
            P(),
            P(None, "tensor"),
            P(),
            P(),
            P(),
            P(),
            P("tensor", None),
            P(),
            P(),
            P(None, "tensor"),
            P(None, "tensor"),
            P("tensor", None),
            P(),
        ),
        check_vma=False,
    )
```

```python
import functools

import jax
import jax.numpy as jnp
import numpy as np
from jax import lax
from jax.experimental import pallas as pl
from jax.experimental.pallas import tpu as pltpu
from jax.sharding import PartitionSpec as P

WINDOW = 512
SOME = 24 * 1024 * 1024
MOST = 60 * 1024 * 1024

eps = 1e-06
rope_base = 10000.0
f32 = jnp.float32
bf16 = jnp.bfloat16
BOTH = ("seq", "tensor")


def places():
    return [(z, y, c, x) for z in range(4) for y in range(4) for c in range(2) for x in range(4)]


def number(z, y, c, x):
    return ((z * 4 + y) * 2 + c) * 4 + x


def route(move):
    return [(number(*p), number(*move(*p))) for p in places()]


def round_x(by):
    return route(lambda z, y, c, x: (z, y, c, (x + by) % 4))


def swap_cores():
    return route(lambda z, y, c, x: (z, y, 1 - c, x))


def along_first(flip):
    return route(lambda z, y, c, x: (z, y ^ flip, c, x) if c == 0 else (z ^ flip, y, c, x))


def round_first(by):
    return route(
        lambda z, y, c, x: (z, (y + by) % 4, c, x) if c == 0 else ((z + by) % 4, y, c, x)
    )


def round_second(by):
    return route(
        lambda z, y, c, x: ((z + by) % 4, y, c, x) if c == 0 else (z, (y + by) % 4, c, x)
    )


def send(value, pairs):
    return lax.ppermute(value, BOTH, pairs)


def shifted(value, by):
    pairs = [
        (i * 4 + x, (i + by) * 4 + x) for i in range(32) if 0 <= i + by < 32 for x in range(4)
    ]
    return send(value, pairs)


def pick(parts, index, axis=0):
    return lax.dynamic_index_in_dim(
        parts, index, axis, keepdims=False, allow_negative_indices=False
    )


def put(parts, part, index):
    return lax.dynamic_update_index_in_dim(parts, part, index, 0, allow_negative_indices=False)


def dot(first, second, over):
    return lax.dot_general(
        first, second, (((over[0],), (over[1],)), ((), ())), preferred_element_type=f32
    )


def joined(own, got, after):
    whole = put(jnp.zeros((4, *own.shape), own.dtype), own, after[0])
    for by, part in zip((1, 2, 3), got, strict=True):
        whole = put(whole, part, after[4 - by])
    return whole


def gather(part, after, turn):
    return joined(part, [send(part, turn(by)) for by in (1, 2, 3)], after)


def inv_scale(values):
    return lax.rsqrt(jnp.mean(values * values, axis=-1, keepdims=True) + eps)


def norm_back(values, scale, gain, grad):
    unit = values * scale
    weighted = grad * gain
    d_values = scale * (weighted - unit * jnp.mean(weighted * unit, axis=-1, keepdims=True))
    return (d_values, jnp.sum(grad * unit, axis=0))


def rotate(values, cosine, sine):
    half = values.shape[-1] // 2
    first = values[..., :half]
    second = values[..., half:]
    return jnp.concatenate(
        [first * cosine - second * sine, second * cosine + first * sine], axis=-1
    )


def padded(values, rows):
    return jnp.pad(values, ((0, rows - values.shape[0]), (0, 0)))


def added(first, second):
    return (first.astype(f32) + second.astype(f32)).astype(bf16)


def tied(*values):
    return lax.optimization_barrier(values)


def call(kernel, outs, *arrays, scalars=0, flops=0, room=SOME, scratch=()):
    vmem = pl.BlockSpec(memory_space=pltpu.VMEM)
    outs = [jax.ShapeDtypeStruct(*o) for o in outs]
    moved = sum(v.size * v.dtype.itemsize for v in (*arrays, *outs))
    return pl.pallas_call(
        kernel,
        out_shape=outs,
        in_specs=[pl.BlockSpec(memory_space=pltpu.SMEM)] * scalars
        + [vmem] * (len(arrays) - scalars),
        out_specs=[vmem] * len(outs),
        scratch_shapes=scratch,
        compiler_params=pltpu.CompilerParams(vmem_limit_bytes=room),
        cost_estimate=pl.CostEstimate(flops=flops, bytes_accessed=moved, transcendentals=0),
    )(*arrays)


def own_rows(ref, lane, rows):
    return ref[pl.ds(pl.multiple_of(lane * rows, rows), rows)].astype(f32)


def project_kernel(
    place, x, post_gain, ffw_gain, ctx0, ctx1, ctx2, ctx3, weight, own1, own2, own3, other1, other2, other3,
    branch, middle, normed
):
    even = place[1] == 0
    half = own1.shape[0]
    total = dot(ctx0[...], weight[...], (1, 0))
    for ctx, mine, theirs in ((ctx1, own1, other1), (ctx2, own2, other2), (ctx3, own3, other3)):
        low = jnp.where(even, mine[...], theirs[...])
        high = jnp.where(even, theirs[...], mine[...])
        total += dot(ctx[:, :half], low, (1, 0)) + dot(ctx[:, half:], high, (1, 0))
    branch[...] = total
    after = x[...].astype(f32) + total * inv_scale(total) * post_gain[...]
    middle[...] = after
    normed[...] = (after * inv_scale(after) * ffw_gain[...]).astype(bf16)


def final_kernel(place, p0, p1, p2, p3, middle, cotangent, gain, out, d_branch, part):
    lane = place[0]
    branch = p0[...].astype(f32) + p1[...].astype(f32) + p2[...].astype(f32) + p3[...].astype(f32)
    rows = branch.shape[0]
    scale = inv_scale(branch)
    cot = own_rows(cotangent, lane, rows)
    out[...] = (own_rows(middle, lane, rows) + branch * scale * gain[...]).astype(bf16)
    d_values, d_gain = norm_back(branch, scale, gain[...], cot)
    d_branch[...] = d_values.astype(bf16)
    part[...] = d_gain[None]


def between_kernel(
    place, p0, p1, p2, p3, middle, branch, cotangent, ffw_gain, post_gain,
    d_middle, d_branch, ffw_part, post_part
):
    lane = place[0]
    grad = p0[...].astype(f32) + p1[...].astype(f32) + p2[...].astype(f32) + p3[...].astype(f32)
    rows = grad.shape[0]
    after = own_rows(middle, lane, rows)
    before = own_rows(branch, lane, rows)
    d_values, d_gain = norm_back(after, inv_scale(after), ffw_gain[...], grad)
    ffw_part[...] = d_gain[None]
    d_values = own_rows(cotangent, lane, rows) + d_values
    d_middle[...] = d_values
    d_values, d_gain = norm_back(before, inv_scale(before), post_gain[...], d_values)
    d_branch[...] = d_values.astype(bf16)
    post_part[...] = d_gain[None]


def key_kernel(
    q_raw, k_raw, d_queries, d_own, d_near, d_far, cosine, sine, query_gain, key_gain, query_weight, key_weight,
    value_weight, d_query, payload, query_part, key_part
):
    tok, head_dim = q_raw.shape
    width = query_weight.shape[0]
    cos, sin = cosine[...], -sine[...]
    raw = q_raw[...]
    d_raw, d_gain = norm_back(
        raw, inv_scale(raw), query_gain[...], rotate(d_queries[...] * head_dim**-0.5, cos, sin)
    )
    query_part[...] = d_gain[None]
    d_low = d_raw.astype(bf16)
    d_query[...] = d_low
    total = dot(d_low, query_weight[...], (1, 1))
    summed = d_own[...] + d_near[...].astype(f32) + d_far[...].astype(f32)
    raw = k_raw[...]
    d_raw, d_gain = norm_back(raw, inv_scale(raw), key_gain[...], rotate(summed[:tok], cos, sin))
    key_part[...] = d_gain[None]
    total += dot(d_raw.astype(bf16), key_weight[...], (1, 1))
    total += dot(summed[tok:].astype(bf16), value_weight[...], (1, 1))
    payload[:, :width] = total.astype(bf16)
    payload[:, width : width + tok] = d_raw.T.astype(bf16)
    payload[:, width + tok :] = summed[tok:].T.astype(bf16)


def products_kernel(context, d_branch, d_query, normed, out):
    half = context.shape[1]
    out[:half] = dot(context[...], d_branch[...], (0, 0))
    out[half:] = dot(d_query[...], normed[...], (0, 0))


def entry_kernel(
    place, p0, p1, p2, p3, x, d_middle, gain, normed, post_part, ffw_part, final_part, query_part, key_part,
    products, input_grad, keep, give, rest
):
    lane, core = place[0], place[1]
    both = p0[...].astype(f32) + p1[...].astype(f32) + p2[...].astype(f32) + p3[...].astype(f32)
    rows = both.shape[0]
    width = normed.shape[1]
    tok = normed.shape[0]
    full = own_rows(x, lane, rows)
    d_values, d_gain = norm_back(full, inv_scale(full), gain[...], both[:, :width])
    input_grad[...] = (d_middle[...] + d_values).astype(bf16)
    d_keys = both[:, width : width + tok].astype(bf16)
    d_values = both[:, width + tok :].astype(bf16)
    rest[:rows] = dot(d_keys, normed[...], (1, 0))
    rest[rows : 2 * rows] = dot(d_values, normed[...], (1, 0))
    heads = jnp.concatenate(
        [query_part[...], key_part[...], jnp.zeros((1, width - 2 * query_part.shape[1]), f32)], axis=1
    )
    index = lax.broadcasted_iota(jnp.int32, (8, width), 0)
    gains = jnp.zeros((8, width), f32)
    for at, part in enumerate((d_gain[None], post_part[...], ffw_part[...], final_part[...], heads)):
        gains = jnp.where(index == at, part, gains)
    rest[2 * rows : 2 * rows + 8] = gains
    rest[2 * rows + 8 :] = jnp.zeros((rest.shape[0] - 2 * rows - 8, width), f32)
    for kind in range(3):
        source = rest if kind == 2 else products
        base = 256 if kind == 1 else 0
        for chip in range(16):
            at = base + 16 * chip
            keep[kind, chip] = source[pl.ds(pl.multiple_of(at + 8 * core, 8), 8)]
            give[kind, chip] = source[pl.ds(pl.multiple_of(at + 8 - 8 * core, 8), 8)].astype(bf16)


def merge_kernel(where, keep, got, *outs):
    core, first = where[0], where[1]
    for by, out in enumerate(outs):
        along = lax.rem(first + by, 4)
        for across in range(4):
            chip = jnp.where(core == 0, 4 * across + along, 4 * along + across)
            for kind in range(3):
                total = keep[kind, chip] + got[kind, chip].astype(f32)
                out[kind, across] = total.astype(out.dtype)


def weight_kernel(
    hid_own, hid_got, gate_own, gate_got, up_own, up_got, dy_own, dy_got, xn_own, xn_got, *outs
):
    mats = (
        (hid_own, hid_got, dy_own, dy_got),
        (gate_own, gate_got, xn_own, xn_got),
        (up_own, up_got, xn_own, xn_got),
    )
    for group, out in enumerate(outs):
        for index, (left_own, left_got, right_own, right_got) in enumerate(mats):
            total = jnp.dot(left_own[group], right_own[...], preferred_element_type=f32)
            total += jnp.dot(left_got[group], right_got[...], preferred_element_type=f32)
            total = total.astype(bf16)
            out[112 * index : 112 * index + 112] = total[:112]
            out[336 + 112 * index : 448 + 112 * index] = total[112:]


def weight_parts(*arrays):
    width = arrays[-1].shape[1]
    return pl.pallas_call(
        weight_kernel,
        out_shape=[jax.ShapeDtypeStruct((672, width), bf16)] * 4,
        in_specs=[pl.BlockSpec(memory_space=pltpu.VMEM)] * len(arrays),
        out_specs=[pl.BlockSpec(memory_space=pltpu.VMEM)] * 4,
        compiler_params=pltpu.CompilerParams(vmem_limit_bytes=SOME),
        cost_estimate=pl.CostEstimate(
            flops=2 * 2688 * 512 * width, bytes_accessed=12_000_000, transcendentals=0
        ),
    )(*arrays)


def halve_kernel(keep_a, got_a, keep_b, got_b, *outs):
    for keep, got, half in ((keep_a, got_a, outs[:2]), (keep_b, got_b, outs[2:])):
        for index, out in enumerate(half):
            rows = pl.ds(336 * index, 336)
            out[...] = (keep[rows].astype(f32) + got[rows].astype(f32)).astype(bf16)


def deal_kernel(where, keep_a, got_a, keep_b, got_b, *refs):
    outs, total = refs[:-1], refs[-1]
    total[0] = keep_a[...].astype(f32) + got_a[...].astype(f32)
    total[1] = keep_b[...].astype(f32) + got_b[...].astype(f32)
    for by, out in enumerate(outs):
        across = lax.rem(where[2] + by, 4)
        for mat in range(3):
            row = pl.multiple_of(112 * mat + 56 * lax.rem(across, 2), 8)
            out[mat] = total[across // 2, pl.ds(row, 56)].astype(out.dtype)


def masks(block, pairs):
    tok = pairs[0].shape[1]
    query = lax.broadcasted_iota(jnp.int32, (tok, tok), 0)
    key = lax.broadcasted_iota(jnp.int32, (tok, tok), 1)
    rows = [pair[2 * tok : 2 * tok + 16].astype(f32)[:1] for pair in pairs]
    segment = jnp.broadcast_to(rows[2], (tok, tok)).T
    same = [segment == row for row in rows]
    return (
        same[0] & (key > query) & (block >= 2),
        same[1] & (block >= 1),
        same[2] & (key <= query),
    )


def prepare_kernel(
    place, x, gain, key_weight, value_weight, query_weight, key_gain, query_gain, start_cos, start_sin, inner_cos,
    inner_sin, marks, xn, pair, k_raw, q_raw, queries, cosine, sine
):
    tok, head_dim = k_raw.shape
    full = x[...].astype(f32)
    low = (full * inv_scale(full) * gain[...]).astype(bf16)
    xn[...] = low
    at = pl.ds(place[2], 1)
    cos = start_cos[at] * inner_cos[...] - start_sin[at] * inner_sin[...]
    sin = start_sin[at] * inner_cos[...] + start_cos[at] * inner_sin[...]
    cosine[...] = cos
    sine[...] = sin
    raw = dot(low, key_weight[...], (1, 0))
    k_raw[...] = raw
    pair[:tok] = rotate(raw * inv_scale(raw) * key_gain[...], cos, sin).astype(bf16)
    pair[tok : 2 * tok] = dot(low, value_weight[...], (1, 0)).astype(bf16)
    pair[2 * tok :] = jnp.broadcast_to(marks[...].astype(f32)[None], (16, tok)).astype(bf16)
    raw = dot(low, query_weight[...], (1, 0))
    q_raw[...] = raw
    turned = rotate(raw * inv_scale(raw) * query_gain[...], cos, sin)
    queries[...] = (turned * head_dim**-0.5).astype(bf16)


def attend_kernel(place, queries, far, near, own, context, log_total):
    pairs = (far, near, own)
    tok = queries.shape[0]
    allowed = masks(place[2], pairs)
    scores = [
        jnp.where(ok, dot(queries[...], pair[:tok], (1, 1)), -1e30)
        for ok, pair in zip(allowed, pairs, strict=True)
    ]
    top = functools.reduce(jnp.maximum, [jnp.max(s, axis=1, keepdims=True) for s in scores])
    weights = [jnp.exp(s - top) for s in scores]
    total = sum(jnp.sum(w, axis=1, keepdims=True) for w in weights)
    context[...] = sum(
        dot((w / total).astype(bf16), pair[tok : 2 * tok], (1, 0))
        for w, pair in zip(weights, pairs, strict=True)
    ).astype(bf16)
    log_total[...] = jnp.broadcast_to(top + jnp.log(total), log_total.shape)


def attend(place, queries, pairs):
    tok, head_dim = queries.shape
    vmem = pl.BlockSpec(memory_space=pltpu.VMEM)
    return pl.pallas_call(
        attend_kernel,
        out_shape=[
            jax.ShapeDtypeStruct((tok, head_dim), bf16),
            jax.ShapeDtypeStruct((tok, 128), f32),
        ],
        in_specs=[pl.BlockSpec(memory_space=pltpu.SMEM)] + [vmem] * 4,
        out_specs=[vmem] * 2,
        compiler_params=pltpu.CompilerParams(vmem_limit_bytes=SOME),
        cost_estimate=pl.CostEstimate(
            flops=12 * tok * tok * head_dim, bytes_accessed=1_500_000, transcendentals=3 * tok * tok
        ),
    )(place, queries, *pairs)


def attend_back_kernel(
    place, log_total, d_branch, weight, queries, far, near, own, d_queries, d_far, d_near, d_own
):
    pairs = (far, near, own)
    tok = queries.shape[0]
    d_context = dot(d_branch[...], weight[...], (1, 1)).astype(bf16)
    allowed = masks(place[2], pairs)
    lse = log_total[:, :1]
    probs, d_probs = [], []
    for ok, pair in zip(allowed, pairs, strict=True):
        scores = jnp.where(ok, dot(queries[...], pair[:tok], (1, 1)), -1e30)
        probs.append(jnp.exp(scores - lse))
        d_probs.append(dot(d_context, pair[tok : 2 * tok], (1, 1)))
    mean = sum(
        jnp.sum(p * d, axis=1, keepdims=True) for p, d in zip(probs, d_probs, strict=True)
    )
    total = None
    for p, d, pair, out in zip(probs, d_probs, pairs, (d_far, d_near, d_own), strict=True):
        d_scores = (p * (d - mean)).astype(bf16)
        part = dot(d_scores, pair[:tok], (1, 0))
        total = part if total is None else total + part
        out[:tok] = dot(d_scores, queries[...], (0, 0)).astype(out.dtype)
        out[tok:] = dot(p.astype(bf16), d_context, (0, 0)).astype(out.dtype)
    d_queries[...] = total


def attend_back(place, log_total, d_branch, weight, queries, pairs):
    tok, head_dim = queries.shape
    vmem = pl.BlockSpec(memory_space=pltpu.VMEM)
    return pl.pallas_call(
        attend_back_kernel,
        out_shape=[
            jax.ShapeDtypeStruct((tok, head_dim), f32),
            jax.ShapeDtypeStruct((2 * tok, head_dim), bf16),
            jax.ShapeDtypeStruct((2 * tok, head_dim), bf16),
            jax.ShapeDtypeStruct((2 * tok, head_dim), f32),
        ],
        in_specs=[pl.BlockSpec(memory_space=pltpu.SMEM)] + [vmem] * 7,
        out_specs=[vmem] * 4,
        compiler_params=pltpu.CompilerParams(vmem_limit_bytes=SOME),
        cost_estimate=pl.CostEstimate(
            flops=30 * tok * tok * head_dim, bytes_accessed=3_500_000, transcendentals=3 * tok * tok
        ),
    )(place, log_total, d_branch, weight, queries, *pairs)


def place_kernel(where_ref, *refs, turns, held):
    n = len(turns)
    parts, outs = refs[:n], refs[n + held : n + held + 3]
    stage, sems, tail_sems = refs[-3:]
    slots = stage.shape[0]
    core, first, second = where_ref[0], where_ref[1], where_ref[2]
    chunks = [
        (ref, i, base + i, other, flip)
        for ref, (other, flip, base) in zip(parts, turns, strict=True)
        for i in range(ref.shape[0])
    ]

    def place(index):
        _, _, across, other, flip = chunks[index]
        which = 1 - core if other else core
        along = (second if other else first) ^ flip
        y = jnp.where(which == 0, along, across)
        z = jnp.where(which == 0, across, along)
        odd = lax.rem(y, 2)
        row = 216 * (2 * z + y // 2) + 104 * odd + 48 * which + 8 * which * odd
        return pl.multiple_of(row, 8), (which == 1) | (odd == 1)

    def copies(index):
        slot = index % slots
        row, whole = place(index)
        for mat, out in enumerate(outs):
            yield (
                pltpu.make_async_copy(
                    stage.at[slot, mat, pl.ds(0, 48)],
                    out.at[pl.ds(row, 48)],
                    sems.at[slot, mat],
                ),
                pltpu.make_async_copy(
                    stage.at[slot, mat, pl.ds(48, 8)],
                    out.at[pl.ds(pl.multiple_of(row + 48, 8), 8)],
                    tail_sems.at[slot, mat],
                ),
                whole,
            )

    def finish(index):
        for most, tail, whole in copies(index):
            most.wait()
            pl.when(whole)(tail.wait)

    for index, (ref, i, *_) in enumerate(chunks):
        if index >= slots:
            finish(index - slots)
        stage[index % slots] = ref[i].astype(f32)
        for most, tail, whole in copies(index):
            most.start()
            pl.when(whole)(tail.start)
    for index in range(max(0, len(chunks) - slots), len(chunks)):
        finish(index)


def placed(where, parts, outs, units):
    arrays = [p[0].reshape(-1, 3, 56, p[0].shape[-1]) for p in parts]
    width = arrays[0].shape[-1]
    slots = 4
    return pl.pallas_call(
        functools.partial(
            place_kernel, turns=tuple(p[1:] for p in parts), held=len(outs)
        ),
        out_shape=[jax.ShapeDtypeStruct((units, width), f32)] * 3,
        in_specs=[pl.BlockSpec(memory_space=pltpu.SMEM)]
        + [pl.BlockSpec(memory_space=pltpu.VMEM)] * len(arrays)
        + [pl.BlockSpec(memory_space=pl.ANY)] * len(outs),
        out_specs=[pl.BlockSpec(memory_space=pl.ANY)] * 3,
        scratch_shapes=[
            pltpu.VMEM((slots, 3, 56, width), f32),
            pltpu.SemaphoreType.DMA((slots, 3)),
            pltpu.SemaphoreType.DMA((slots, 3)),
        ],
        input_output_aliases={1 + len(arrays) + i: i for i in range(len(outs))},
        compiler_params=pltpu.CompilerParams(vmem_limit_bytes=SOME),
        cost_estimate=pl.CostEstimate(
            flops=0, bytes_accessed=sum(p.size for p in arrays) * 6, transcendentals=0
        ),
    )(where, *arrays, *outs)


def sorted_rows(core, own, got, rows, kinds):
    for pieces, other in ((own, 0), (got, 1)):
        even = core == other
        for along in range(4):
            for across in range(4):
                row = jnp.where(even, 8 * across + 2 * along, 8 * along + 2 * across + 1) * 8
                row = pl.ds(pl.multiple_of(row, 8), 8)
                for kind in range(kinds):
                    rows[kind, row] = pieces(kind, along, across).astype(f32)


def square_kernel(where, own, got, out_grad, query_grad, rows):
    sorted_rows(
        where[0],
        lambda kind, along, across: own[along, kind, across],
        lambda kind, along, across: got[along, kind, across],
        rows,
        2,
    )
    out_grad[...] = rows[0]
    query_grad[...] = rows[1].T


def finish_kernel(
    where, own, got, key_grad, value_grad, attn, post, ffw, final, query, key, rows
):
    sorted_rows(
        where[0],
        lambda lane, along, across: own[lane, along, across],
        lambda lane, along, across: got[lane, along, across],
        rows,
        4,
    )
    for lane in range(4):
        key_grad[:, 64 * lane : 64 * lane + 64] = rows[lane, :64].T
        value_grad[:, 64 * lane : 64 * lane + 64] = rows[lane, 64:128].T
    gains = sum(rows[lane, 128:136] for lane in range(4))
    for at, out in enumerate((attn, post, ffw, final)):
        out[...] = gains[at]
    size = query.shape[0]
    query[...] = gains[4, :size]
    key[...] = gains[4, size : 2 * size]


def local(
    layer_input,
    segment_ids,
    out_cotangent,
    attn_norm_gain,
    query_weight,
    key_weight,
    value_weight,
    query_gain,
    key_gain,
    output_weight,
    attn_post_gain,
    ffw_norm_gain,
    gate_weight,
    up_weight,
    down_weight,
    ffw_post_gain,
):
    tok, width = layer_input.shape
    head_dim = key_weight.shape[1]
    units = down_weight.shape[0]
    block = lax.axis_index("seq")
    lane = lax.axis_index("tensor")
    core = lax.rem(block, 2)
    row = lax.rem(lax.div(block, 2), 4)
    plane = lax.div(block, 8)
    first = lax.select(core == 0, row, plane)
    second = lax.select(core == 0, plane, row)
    place = jnp.stack([lane, core, block])
    where = jnp.stack([core, first, second])
    afters = [lax.rem(at + by, 4) for at in (lane, first, second) for by in range(4)]
    flips = [first ^ flip for flip in range(1, 4)]
    place, where, core, other_core, even, *places_at = tied(
        place, where, core, 1 - core, core == 0, *afters, *flips
    )
    lanes, firsts, seconds = places_at[:4], places_at[4:8], places_at[8:12]
    flips = [firsts[0], *places_at[12:]]
    quarter_tok = tok // 4

    freq = rope_base ** (-2.0 * np.arange(head_dim // 2) / head_dim)
    start = (np.arange(lax.axis_size("seq")) * tok)[:, None] * freq[None, :]
    inner = np.arange(tok)[:, None] * freq[None, :]
    tables = [jnp.asarray(f(angle), f32) for angle in (start, inner) for f in (np.cos, np.sin)]

    square = (tok, head_dim)
    normed, own_pair, k_raw, q_raw, queries, cosine, sine = call(
        prepare_kernel,
        [
            ((tok, width), bf16),
            ((2 * tok + 16, head_dim), bf16),
            (square, f32),
            (square, f32),
            (square, bf16),
            ((tok, head_dim // 2), f32),
            ((tok, head_dim // 2), f32),
        ],
        place,
        layer_input,
        attn_norm_gain,
        key_weight,
        value_weight,
        query_weight,
        key_gain,
        query_gain,
        *tables,
        segment_ids,
        scalars=1,
        flops=6 * tok * width * head_dim,
        room=MOST,
    )
    left_one = shifted(own_pair, 1)
    left_two = shifted(own_pair, 2)

    weight_half = tok // 2
    halved, left_one = tied(output_weight, left_one)
    own_weight = pick(halved.reshape(2, weight_half, width), core)
    got_weight = [send(own_weight, round_x(by)) for by in (1, 2, 3)]

    pairs = (left_two, left_one, own_pair)
    context, log_total = attend(place, queries, pairs)

    got_context = [send(context, round_x(by)) for by in (1, 2, 3)]
    *got_context, got_weight[0], got_weight[1], got_weight[2] = tied(*got_context, *got_weight)
    other_weight = [send(part, swap_cores()) for part in got_weight]
    branch, middle, normed_two = call(
        project_kernel,
        [((tok, width), f32), ((tok, width), f32), ((tok, width), bf16)],
        place,
        layer_input,
        attn_post_gain,
        ffw_norm_gain,
        context,
        *got_context,
        output_weight,
        *got_weight,
        *other_weight,
        scalars=1,
        flops=8 * tok * tok * width,
    )
    gate = dot(gate_weight, normed_two, (0, 1))
    up_val = dot(up_weight, normed_two, (0, 1))
    active, gelu_back = jax.vjp(lambda val: jax.nn.gelu(val, approximate=True), gate)
    hidden = (active * up_val).astype(bf16)
    down_part = dot(hidden, down_weight, (0, 0)).astype(bf16)

    def halves(values):
        groups = values.reshape(8, units // 8, tok)
        groups = jnp.concatenate([groups[:, :56], groups[:, 48:]], axis=1)
        pieces = groups.reshape(4, 4, 2, 56, tok)
        return pick(pieces, core, 2), pick(pieces, other_core, 2)

    def arranged(values):
        values = jnp.where(even, values.swapaxes(0, 1), values)
        by_first = tied(*(pick(values, flip) for flip in flips))
        groups = [
            jnp.stack([by_first[i][2 * stream : 2 * stream + 2] for i in order])
            for stream, order in ((0, (0, 3)), (0, (1, 2)), (1, (0, 1)), (1, (3, 2)))
        ]
        return jnp.stack(groups).reshape(4, 224, tok)

    hidden_own, hidden_give = halves(hidden)
    hidden_got = send(hidden_give, swap_cores())
    normed_two_got = send(normed_two, swap_cores())

    def quarters(parts):
        parts = parts.reshape(4, quarter_tok, parts.shape[-1])
        given = [pick(parts, at) for at in lanes[1:]]
        return [pick(parts, lanes[0])] + [
            send(part, round_x(by)) for by, part in zip((1, 2, 3), given, strict=True)
        ]

    piece = (quarter_tok, width)
    out_own, d_branch_two, final_part = call(
        final_kernel,
        [(piece, bf16), (piece, bf16), ((1, width), f32)],
        place,
        *quarters(down_part),
        middle,
        out_cotangent,
        ffw_post_gain,
        scalars=1,
    )
    d_branch_two = gather(d_branch_two, lanes, round_x).reshape(tok, width)
    d_branch_two_got = send(d_branch_two, swap_cores())

    d_hidden = dot(down_weight, d_branch_two, (1, 1))
    d_gate = gelu_back(d_hidden * up_val)[0].astype(bf16)
    d_up = (d_hidden * active).astype(bf16)
    d_normed_two = (dot(d_gate, gate_weight, (0, 1)) + dot(d_up, up_weight, (0, 1))).astype(bf16)
    d_gate_own, d_gate_give = halves(d_gate)
    d_up_own, d_up_give = halves(d_up)
    d_pair_got = send(jnp.stack([d_gate_give, d_up_give]), swap_cores())

    keep_a, give_a, keep_b, give_b = weight_parts(
        *(
            arranged(v)
            for v in (hidden_own, hidden_got, d_gate_own, d_pair_got[0], d_up_own, d_pair_got[1])
        ),
        d_branch_two,
        d_branch_two_got,
        normed_two,
        normed_two_got,
    )
    got_a = send(give_a, along_first(1))
    got_b = send(give_b, along_first(3))

    *got_normed, keep_a, keep_b = tied(*quarters(d_normed_two), keep_a, keep_b)
    d_middle, d_branch, ffw_part, post_part = call(
        between_kernel,
        [(piece, f32), (piece, bf16), ((1, width), f32), ((1, width), f32)],
        place,
        *got_normed,
        middle,
        branch,
        out_cotangent,
        ffw_norm_gain,
        attn_post_gain,
        scalars=1,
    )
    d_branch = gather(d_branch, lanes, round_x).reshape(tok, width)
    d_queries, left_far, left_near, summed = attend_back(
        place, log_total, d_branch, output_weight, queries, pairs
    )
    got_near = shifted(left_near, -1)
    got_far = shifted(left_far, -2)
    got_near, got_far, got_a, got_b = tied(got_near, got_far, got_a, got_b)
    keep_a, give_a, keep_b, give_b = call(
        halve_kernel, [((336, width), bf16)] * 4, keep_a, got_a, keep_b, got_b
    )
    got_a = send(give_a, along_first(3))
    got_b = send(give_b, along_first(1))
    d_query, payload, query_part, key_part = call(
        key_kernel,
        [
            (square, bf16),
            ((tok, width + 2 * tok), bf16),
            ((1, head_dim), f32),
            ((1, head_dim), f32),
        ],
        q_raw,
        k_raw,
        d_queries,
        summed,
        got_near,
        got_far,
        cosine,
        sine,
        query_gain,
        key_gain,
        query_weight,
        key_weight,
        value_weight,
        flops=6 * tok * width * head_dim,
    )
    got_both = quarters(payload)
    (products,) = call(
        products_kernel,
        [((2 * head_dim, width), f32)],
        context,
        d_branch,
        d_query,
        normed,
        flops=4 * tok * width * head_dim,
    )
    *got_both, got_a, got_b = tied(*got_both, got_a, got_b)
    chunk = (3, 56, width)
    mine, *given = call(
        deal_kernel,
        [(chunk, f32)] + [(chunk, bf16)] * 3,
        where,
        keep_a,
        got_a,
        keep_b,
        got_b,
        scalars=1,
        scratch=[pltpu.VMEM((2, 336, width), f32)],
    )
    got = [send(part, round_second(by)) for by, part in zip((1, 2, 3), given, strict=True)]
    input_own, keep, give = pl.pallas_call(
        entry_kernel,
        out_shape=[
            jax.ShapeDtypeStruct(piece, bf16),
            jax.ShapeDtypeStruct((3, 16, 8, width), f32),
            jax.ShapeDtypeStruct((3, 16, 8, width), bf16),
        ],
        in_specs=[pl.BlockSpec(memory_space=pltpu.SMEM)]
        + [pl.BlockSpec(memory_space=pltpu.VMEM)] * 14,
        out_specs=[pl.BlockSpec(memory_space=pltpu.VMEM)] * 3,
        scratch_shapes=[pltpu.VMEM((tok, width), f32)],
        compiler_params=pltpu.CompilerParams(vmem_limit_bytes=SOME),
        cost_estimate=pl.CostEstimate(
            flops=256 * tok * width, bytes_accessed=12_000_000, transcendentals=0
        ),
    )(
        place,
        *got_both,
        layer_input,
        d_middle,
        attn_norm_gain,
        normed,
        post_part,
        ffw_part,
        final_part,
        query_part,
        key_part,
        products,
    )
    pack_got = send(give, swap_cores())
    part = (3, 4, 8, width)
    pack, *given = call(
        merge_kernel, [(part, f32)] + [(part, bf16)] * 3, where, keep, pack_got, scalars=1
    )
    got[0], *given = tied(got[0], *given)
    given = [send(part, round_first(by)) for by, part in zip((1, 2, 3), given, strict=True)]
    *given, got[0], got[1], got[2] = tied(*given, *got)
    mine = mine + got[0].astype(f32) + (got[1].astype(f32) + got[2].astype(f32))
    mine = mine.astype(bf16).reshape(168, width)
    for part in given:
        pack = pack + part.astype(f32)
    pack = pack.astype(bf16).reshape(96, width)
    both = lax.optimization_barrier(jnp.concatenate([mine, pack]))
    given = [send(both, round_second(by)) for by in (1, 2, 3)]
    ends = jnp.concatenate([out_own, input_own])
    got_ends = [send(ends, round_x(by)) for by in (1, 2, 3)]
    given[0], given[1], given[2], *got_ends = tied(*given, *got_ends)
    ends = joined(ends, got_ends, lanes)
    layer_output = ends[:, :64].reshape(tok, width)
    input_grad = ends[:, 64:].reshape(tok, width)
    quarter = joined(both[:168], [part[:168] for part in given], seconds)
    pack, *given = (part[168:].astype(f32) for part in (both, *given))
    pack = (pack + given[1] + (given[0] + given[2])).astype(bf16).reshape(3, 4, 8, width)
    given = [send(pack, round_first(by)) for by in (1, 2, 3)]
    other_own = send(quarter, swap_cores())
    given[0], quarter, other_own, layer_output, input_grad = tied(
        given[0], quarter, other_own, layer_output, input_grad
    )
    near_a = send(quarter, along_first(1))
    near_b = send(quarter, along_first(3))
    pack = joined(pack, given, firsts)
    pack_got = send(pack, swap_cores())
    rest, pack_got, own_quarter = tied(pack[:, 2], pack_got, quarter)
    given = [send(rest, round_x(by)) for by in (1, 2, 3)]
    out_grad, query_grad = call(
        square_kernel,
        [((256, width), f32), ((width, 256), f32)],
        where,
        pack,
        pack_got,
        scalars=1,
        scratch=[pltpu.VMEM((2, 256, width), f32)],
    )
    grads = placed(where, [(own_quarter, False, 0, 0), (other_own, True, 0, 0)], [], units)
    grads = list(grads)
    *given, near_a, near_b, grads[0], out_grad = tied(
        *given, near_a, near_b, grads[0], out_grad
    )
    far_a = send(near_b[:2], along_first(1))
    far_b = send(near_a[2:], along_first(3))
    other_a = send(near_a, swap_cores())
    other_b = send(near_b, swap_cores())
    rest = joined(rest, given, lanes)
    rest_got = send(rest, swap_cores())
    key_grad, value_grad, *gains = call(
        finish_kernel,
        [((width, 256), f32)] * 2 + [((width,), f32)] * 4 + [((256,), f32)] * 2,
        where,
        rest,
        rest_got,
        scalars=1,
        scratch=[pltpu.VMEM((4, 256, width), f32)],
    )
    other_a, key_grad = tied(other_a, key_grad)
    grads = placed(
        where,
        [
            (near_a, False, 1, 0),
            (near_b, False, 3, 0),
            (other_a, True, 1, 0),
            (other_b, True, 3, 0),
        ],
        grads,
        units,
    )
    far_a, far_b, *grads = tied(far_a, far_b, *grads)
    other_far_a = send(far_a, swap_cores())
    other_far_b = send(far_b, swap_cores())
    down_grad, gate_grad, up_grad = placed(
        where,
        [
            (far_a, False, 2, 0),
            (far_b, False, 2, 2),
            (other_far_a, True, 2, 0),
            (other_far_b, True, 2, 2),
        ],
        grads,
        units,
    )
    return (
        layer_output,
        input_grad,
        gains[0],
        query_grad,
        key_grad,
        value_grad,
        gains[4],
        gains[5],
        out_grad,
        gains[1],
        gains[2],
        gate_grad.T,
        up_grad.T,
        down_grad,
        gains[3],
    )


def solution(mesh):
    rows = P("seq", None)
    return jax.shard_map(
        local,
        mesh=mesh,
        in_specs=(
            rows,
            P("seq"),
            rows,
            P(),
            P(None, "tensor"),
            P(),
            P(),
            P(),
            P(),
            P("tensor", None),
            P(),
            P(),
            P(None, "tensor"),
            P(None, "tensor"),
            P("tensor", None),
            P(),
        ),
        out_specs=(
            rows,
            rows,
            P(),
            P(None, "tensor"),
            P(),
            P(),
            P(),
            P(),
            P("tensor", None),
            P(),
            P(),
            P(None, "tensor"),
            P(None, "tensor"),
            P("tensor", None),
            P(),
        ),
        check_vma=False,
    )
```

```python
import functools

import jax
import jax.numpy as jnp
import numpy as np
from jax import lax
from jax.experimental import pallas as pl
from jax.experimental.pallas import tpu as pltpu
from jax.sharding import PartitionSpec as P

WINDOW = 512
SOME = 24 * 1024 * 1024
MOST = 60 * 1024 * 1024

eps = 1e-06
rope_base = 10000.0
f32 = jnp.float32
bf16 = jnp.bfloat16
BOTH = ("seq", "tensor")


def places():
    return [(z, y, c, x) for z in range(4) for y in range(4) for c in range(2) for x in range(4)]


def number(z, y, c, x):
    return ((z * 4 + y) * 2 + c) * 4 + x


def route(move):
    return [(number(*p), number(*move(*p))) for p in places()]


def round_x(by):
    return route(lambda z, y, c, x: (z, y, c, (x + by) % 4))


def swap_cores():
    return route(lambda z, y, c, x: (z, y, 1 - c, x))


def along_first(flip):
    return route(lambda z, y, c, x: (z, y ^ flip, c, x) if c == 0 else (z ^ flip, y, c, x))


def round_first(by):
    return route(
        lambda z, y, c, x: (z, (y + by) % 4, c, x) if c == 0 else ((z + by) % 4, y, c, x)
    )


def round_second(by):
    return route(
        lambda z, y, c, x: ((z + by) % 4, y, c, x) if c == 0 else (z, (y + by) % 4, c, x)
    )


def send(value, pairs):
    return lax.ppermute(value, BOTH, pairs)


def shifted(value, by):
    pairs = [
        (i * 4 + x, (i + by) * 4 + x) for i in range(32) if 0 <= i + by < 32 for x in range(4)
    ]
    return send(value, pairs)


def pick(parts, index, axis=0):
    return lax.dynamic_index_in_dim(
        parts, index, axis, keepdims=False, allow_negative_indices=False
    )


def put(parts, part, index):
    return lax.dynamic_update_index_in_dim(parts, part, index, 0, allow_negative_indices=False)


def dot(first, second, over):
    return lax.dot_general(
        first, second, (((over[0],), (over[1],)), ((), ())), preferred_element_type=f32
    )


def joined(own, got, after):
    whole = put(jnp.zeros((4, *own.shape), own.dtype), own, after[0])
    for by, part in zip((1, 2, 3), got, strict=True):
        whole = put(whole, part, after[4 - by])
    return whole


def gather(part, after, turn):
    return joined(part, [send(part, turn(by)) for by in (1, 2, 3)], after)


def inv_scale(values):
    return lax.rsqrt(jnp.mean(values * values, axis=-1, keepdims=True) + eps)


def norm_back(values, scale, gain, grad):
    unit = values * scale
    weighted = grad * gain
    d_values = scale * (weighted - unit * jnp.mean(weighted * unit, axis=-1, keepdims=True))
    return (d_values, jnp.sum(grad * unit, axis=0))


def rotate(values, cosine, sine):
    half = values.shape[-1] // 2
    first = values[..., :half]
    second = values[..., half:]
    return jnp.concatenate(
        [first * cosine - second * sine, second * cosine + first * sine], axis=-1
    )


def padded(values, rows):
    return jnp.pad(values, ((0, rows - values.shape[0]), (0, 0)))


def added(first, second):
    return (first.astype(f32) + second.astype(f32)).astype(bf16)


def tied(*values):
    return lax.optimization_barrier(values)


def call(kernel, outs, *arrays, scalars=0, flops=0, room=SOME, scratch=()):
    vmem = pl.BlockSpec(memory_space=pltpu.VMEM)
    outs = [jax.ShapeDtypeStruct(*o) for o in outs]
    moved = sum(v.size * v.dtype.itemsize for v in (*arrays, *outs))
    return pl.pallas_call(
        kernel,
        out_shape=outs,
        in_specs=[pl.BlockSpec(memory_space=pltpu.SMEM)] * scalars
        + [vmem] * (len(arrays) - scalars),
        out_specs=[vmem] * len(outs),
        scratch_shapes=scratch,
        compiler_params=pltpu.CompilerParams(vmem_limit_bytes=room),
        cost_estimate=pl.CostEstimate(flops=flops, bytes_accessed=moved, transcendentals=0),
    )(*arrays)


def own_rows(ref, lane, rows):
    return ref[pl.ds(pl.multiple_of(lane * rows, rows), rows)].astype(f32)


def project_kernel(
    place, x, post_gain, ffw_gain, ctx0, ctx1, ctx2, ctx3, weight, own1, own2, own3, other1, other2, other3,
    branch, middle, normed
):
    even = place[1] == 0
    half = own1.shape[0]
    total = dot(ctx0[...], weight[...], (1, 0))
    for ctx, mine, theirs in ((ctx1, own1, other1), (ctx2, own2, other2), (ctx3, own3, other3)):
        low = jnp.where(even, mine[...], theirs[...])
        high = jnp.where(even, theirs[...], mine[...])
        total += dot(ctx[:, :half], low, (1, 0)) + dot(ctx[:, half:], high, (1, 0))
    branch[...] = total
    after = x[...].astype(f32) + total * inv_scale(total) * post_gain[...]
    middle[...] = after
    normed[...] = (after * inv_scale(after) * ffw_gain[...]).astype(bf16)


def final_kernel(place, p0, p1, p2, p3, middle, cotangent, gain, out, d_branch, part):
    lane = place[0]
    branch = p0[...].astype(f32) + p1[...].astype(f32) + p2[...].astype(f32) + p3[...].astype(f32)
    rows = branch.shape[0]
    scale = inv_scale(branch)
    cot = own_rows(cotangent, lane, rows)
    out[...] = (own_rows(middle, lane, rows) + branch * scale * gain[...]).astype(bf16)
    d_values, d_gain = norm_back(branch, scale, gain[...], cot)
    d_branch[...] = d_values.astype(bf16)
    part[...] = d_gain[None]


def between_kernel(
    place, p0, p1, p2, p3, middle, branch, cotangent, ffw_gain, post_gain,
    d_middle, d_branch, ffw_part, post_part
):
    lane = place[0]
    grad = p0[...].astype(f32) + p1[...].astype(f32) + p2[...].astype(f32) + p3[...].astype(f32)
    rows = grad.shape[0]
    after = own_rows(middle, lane, rows)
    before = own_rows(branch, lane, rows)
    d_values, d_gain = norm_back(after, inv_scale(after), ffw_gain[...], grad)
    ffw_part[...] = d_gain[None]
    d_values = own_rows(cotangent, lane, rows) + d_values
    d_middle[...] = d_values
    d_values, d_gain = norm_back(before, inv_scale(before), post_gain[...], d_values)
    d_branch[...] = d_values.astype(bf16)
    post_part[...] = d_gain[None]


def key_kernel(
    q_raw, k_raw, d_queries, d_own, d_near, d_far, cosine, sine, query_gain, key_gain, query_weight, key_weight,
    value_weight, d_query, payload, query_part, key_part
):
    tok, head_dim = q_raw.shape
    width = query_weight.shape[0]
    cos, sin = cosine[...], -sine[...]
    raw = q_raw[...]
    d_raw, d_gain = norm_back(
        raw, inv_scale(raw), query_gain[...], rotate(d_queries[...] * head_dim**-0.5, cos, sin)
    )
    query_part[...] = d_gain[None]
    d_low = d_raw.astype(bf16)
    d_query[...] = d_low
    total = dot(d_low, query_weight[...], (1, 1))
    summed = d_own[...] + d_near[...].astype(f32) + d_far[...].astype(f32)
    raw = k_raw[...]
    d_raw, d_gain = norm_back(raw, inv_scale(raw), key_gain[...], rotate(summed[:tok], cos, sin))
    key_part[...] = d_gain[None]
    total += dot(d_raw.astype(bf16), key_weight[...], (1, 1))
    total += dot(summed[tok:].astype(bf16), value_weight[...], (1, 1))
    payload[:, :width] = total.astype(bf16)
    payload[:, width : width + tok] = d_raw.T.astype(bf16)
    payload[:, width + tok :] = summed[tok:].T.astype(bf16)


def products_kernel(context, d_branch, d_query, normed, out):
    half = context.shape[1]
    out[:half] = dot(context[...], d_branch[...], (0, 0))
    out[half:] = dot(d_query[...], normed[...], (0, 0))


def entry_kernel(
    place, p0, p1, p2, p3, x, d_middle, gain, normed, post_part, ffw_part, final_part, query_part, key_part,
    products, input_grad, keep, give, rest
):
    lane, core = place[0], place[1]
    both = p0[...].astype(f32) + p1[...].astype(f32) + p2[...].astype(f32) + p3[...].astype(f32)
    rows = both.shape[0]
    width = normed.shape[1]
    tok = normed.shape[0]
    full = own_rows(x, lane, rows)
    d_values, d_gain = norm_back(full, inv_scale(full), gain[...], both[:, :width])
    input_grad[...] = (d_middle[...] + d_values).astype(bf16)
    d_keys = both[:, width : width + tok].astype(bf16)
    d_values = both[:, width + tok :].astype(bf16)
    rest[:rows] = dot(d_keys, normed[...], (1, 0))
    rest[rows : 2 * rows] = dot(d_values, normed[...], (1, 0))
    heads = jnp.concatenate(
        [query_part[...], key_part[...], jnp.zeros((1, width - 2 * query_part.shape[1]), f32)], axis=1
    )
    index = lax.broadcasted_iota(jnp.int32, (8, width), 0)
    gains = jnp.zeros((8, width), f32)
    for at, part in enumerate((d_gain[None], post_part[...], ffw_part[...], final_part[...], heads)):
        gains = jnp.where(index == at, part, gains)
    rest[2 * rows : 2 * rows + 8] = gains
    rest[2 * rows + 8 :] = jnp.zeros((rest.shape[0] - 2 * rows - 8, width), f32)
    for kind in range(3):
        source = rest if kind == 2 else products
        base = 256 if kind == 1 else 0
        for chip in range(16):
            at = base + 16 * chip
            keep[kind, chip] = source[pl.ds(pl.multiple_of(at + 8 * core, 8), 8)]
            give[kind, chip] = source[pl.ds(pl.multiple_of(at + 8 - 8 * core, 8), 8)].astype(bf16)


def merge_kernel(where, keep, got, *outs):
    core, first = where[0], where[1]
    for by, out in enumerate(outs):
        along = lax.rem(first + by, 4)
        for across in range(4):
            chip = jnp.where(core == 0, 4 * across + along, 4 * along + across)
            for kind in range(3):
                total = keep[kind, chip] + got[kind, chip].astype(f32)
                out[kind, across] = total.astype(out.dtype)


def weight_kernel(
    hid_own, hid_got, gate_own, gate_got, up_own, up_got, dy_own, dy_got, xn_own, xn_got, *outs
):
    mats = (
        (hid_own, hid_got, dy_own, dy_got),
        (gate_own, gate_got, xn_own, xn_got),
        (up_own, up_got, xn_own, xn_got),
    )
    for group, out in enumerate(outs):
        for index, (left_own, left_got, right_own, right_got) in enumerate(mats):
            total = jnp.dot(left_own[group], right_own[...], preferred_element_type=f32)
            total += jnp.dot(left_got[group], right_got[...], preferred_element_type=f32)
            total = total.astype(bf16)
            out[112 * index : 112 * index + 112] = total[:112]
            out[336 + 112 * index : 448 + 112 * index] = total[112:]


def weight_parts(*arrays):
    width = arrays[-1].shape[1]
    return pl.pallas_call(
        weight_kernel,
        out_shape=[jax.ShapeDtypeStruct((672, width), bf16)] * 4,
        in_specs=[pl.BlockSpec(memory_space=pltpu.VMEM)] * len(arrays),
        out_specs=[pl.BlockSpec(memory_space=pltpu.VMEM)] * 4,
        compiler_params=pltpu.CompilerParams(vmem_limit_bytes=SOME),
        cost_estimate=pl.CostEstimate(
            flops=2 * 2688 * 512 * width, bytes_accessed=12_000_000, transcendentals=0
        ),
    )(*arrays)


def halve_kernel(keep_a, got_a, keep_b, got_b, *outs):
    for keep, got, half in ((keep_a, got_a, outs[:2]), (keep_b, got_b, outs[2:])):
        for index, out in enumerate(half):
            rows = pl.ds(336 * index, 336)
            out[...] = (keep[rows].astype(f32) + got[rows].astype(f32)).astype(bf16)


def deal_kernel(where, keep_a, got_a, keep_b, got_b, *refs):
    outs, total = refs[:-1], refs[-1]
    total[0] = keep_a[...].astype(f32) + got_a[...].astype(f32)
    total[1] = keep_b[...].astype(f32) + got_b[...].astype(f32)
    for by, out in enumerate(outs):
        across = lax.rem(where[2] + by, 4)
        for mat in range(3):
            row = pl.multiple_of(112 * mat + 56 * lax.rem(across, 2), 8)
            out[mat] = total[across // 2, pl.ds(row, 56)].astype(out.dtype)


def masks(block, pairs):
    tok = pairs[0].shape[1]
    query = lax.broadcasted_iota(jnp.int32, (tok, tok), 0)
    key = lax.broadcasted_iota(jnp.int32, (tok, tok), 1)
    rows = [pair[2 * tok : 2 * tok + 16].astype(f32)[:1] for pair in pairs]
    segment = jnp.broadcast_to(rows[2], (tok, tok)).T
    same = [segment == row for row in rows]
    return (
        same[0] & (key > query) & (block >= 2),
        same[1] & (block >= 1),
        same[2] & (key <= query),
    )


def prepare_kernel(
    place, x, gain, key_weight, value_weight, query_weight, key_gain, query_gain, start_cos, start_sin, inner_cos,
    inner_sin, marks, xn, pair, k_raw, q_raw, queries, cosine, sine
):
    tok, head_dim = k_raw.shape
    full = x[...].astype(f32)
    low = (full * inv_scale(full) * gain[...]).astype(bf16)
    xn[...] = low
    at = pl.ds(place[2], 1)
    cos = start_cos[at] * inner_cos[...] - start_sin[at] * inner_sin[...]
    sin = start_sin[at] * inner_cos[...] + start_cos[at] * inner_sin[...]
    cosine[...] = cos
    sine[...] = sin
    raw = dot(low, key_weight[...], (1, 0))
    k_raw[...] = raw
    pair[:tok] = rotate(raw * inv_scale(raw) * key_gain[...], cos, sin).astype(bf16)
    pair[tok : 2 * tok] = dot(low, value_weight[...], (1, 0)).astype(bf16)
    pair[2 * tok :] = jnp.broadcast_to(marks[...].astype(f32)[None], (16, tok)).astype(bf16)
    raw = dot(low, query_weight[...], (1, 0))
    q_raw[...] = raw
    turned = rotate(raw * inv_scale(raw) * query_gain[...], cos, sin)
    queries[...] = (turned * head_dim**-0.5).astype(bf16)


def attend_kernel(place, queries, far, near, own, context, log_total):
    pairs = (far, near, own)
    tok = queries.shape[0]
    allowed = masks(place[2], pairs)
    scores = [
        jnp.where(ok, dot(queries[...], pair[:tok], (1, 1)), -1e30)
        for ok, pair in zip(allowed, pairs, strict=True)
    ]
    top = functools.reduce(jnp.maximum, [jnp.max(s, axis=1, keepdims=True) for s in scores])
    weights = [jnp.exp(s - top) for s in scores]
    total = sum(jnp.sum(w, axis=1, keepdims=True) for w in weights)
    context[...] = sum(
        dot((w / total).astype(bf16), pair[tok : 2 * tok], (1, 0))
        for w, pair in zip(weights, pairs, strict=True)
    ).astype(bf16)
    log_total[...] = jnp.broadcast_to(top + jnp.log(total), log_total.shape)


def attend(place, queries, pairs):
    tok, head_dim = queries.shape
    vmem = pl.BlockSpec(memory_space=pltpu.VMEM)
    return pl.pallas_call(
        attend_kernel,
        out_shape=[
            jax.ShapeDtypeStruct((tok, head_dim), bf16),
            jax.ShapeDtypeStruct((tok, 128), f32),
        ],
        in_specs=[pl.BlockSpec(memory_space=pltpu.SMEM)] + [vmem] * 4,
        out_specs=[vmem] * 2,
        compiler_params=pltpu.CompilerParams(vmem_limit_bytes=SOME),
        cost_estimate=pl.CostEstimate(
            flops=12 * tok * tok * head_dim, bytes_accessed=1_500_000, transcendentals=3 * tok * tok
        ),
    )(place, queries, *pairs)


def attend_back_kernel(
    place, log_total, d_branch, weight, queries, far, near, own, d_queries, d_far, d_near, d_own
):
    pairs = (far, near, own)
    tok = queries.shape[0]
    d_context = dot(d_branch[...], weight[...], (1, 1)).astype(bf16)
    allowed = masks(place[2], pairs)
    lse = log_total[:, :1]
    probs, d_probs = [], []
    for ok, pair in zip(allowed, pairs, strict=True):
        scores = jnp.where(ok, dot(queries[...], pair[:tok], (1, 1)), -1e30)
        probs.append(jnp.exp(scores - lse))
        d_probs.append(dot(d_context, pair[tok : 2 * tok], (1, 1)))
    mean = sum(
        jnp.sum(p * d, axis=1, keepdims=True) for p, d in zip(probs, d_probs, strict=True)
    )
    total = None
    for p, d, pair, out in zip(probs, d_probs, pairs, (d_far, d_near, d_own), strict=True):
        d_scores = (p * (d - mean)).astype(bf16)
        part = dot(d_scores, pair[:tok], (1, 0))
        total = part if total is None else total + part
        out[:tok] = dot(d_scores, queries[...], (0, 0)).astype(out.dtype)
        out[tok:] = dot(p.astype(bf16), d_context, (0, 0)).astype(out.dtype)
    d_queries[...] = total


def attend_back(place, log_total, d_branch, weight, queries, pairs):
    tok, head_dim = queries.shape
    vmem = pl.BlockSpec(memory_space=pltpu.VMEM)
    return pl.pallas_call(
        attend_back_kernel,
        out_shape=[
            jax.ShapeDtypeStruct((tok, head_dim), f32),
            jax.ShapeDtypeStruct((2 * tok, head_dim), bf16),
            jax.ShapeDtypeStruct((2 * tok, head_dim), bf16),
            jax.ShapeDtypeStruct((2 * tok, head_dim), f32),
        ],
        in_specs=[pl.BlockSpec(memory_space=pltpu.SMEM)] + [vmem] * 7,
        out_specs=[vmem] * 4,
        compiler_params=pltpu.CompilerParams(vmem_limit_bytes=SOME),
        cost_estimate=pl.CostEstimate(
            flops=30 * tok * tok * head_dim, bytes_accessed=3_500_000, transcendentals=3 * tok * tok
        ),
    )(place, log_total, d_branch, weight, queries, *pairs)


def place_kernel(where_ref, *refs, turns, held):
    n = len(turns)
    parts, outs = refs[:n], refs[n + held : n + held + 3]
    stage, sems, tail_sems = refs[-3:]
    slots = stage.shape[0]
    core, first, second = where_ref[0], where_ref[1], where_ref[2]
    chunks = [
        (ref, i, base + i, other, flip)
        for ref, (other, flip, base) in zip(parts, turns, strict=True)
        for i in range(ref.shape[0])
    ]

    def place(index):
        _, _, across, other, flip = chunks[index]
        which = 1 - core if other else core
        along = (second if other else first) ^ flip
        y = jnp.where(which == 0, along, across)
        z = jnp.where(which == 0, across, along)
        odd = lax.rem(y, 2)
        row = 216 * (2 * z + y // 2) + 104 * odd + 48 * which + 8 * which * odd
        return pl.multiple_of(row, 8), (which == 1) | (odd == 1)

    def copies(index):
        slot = index % slots
        row, whole = place(index)
        for mat, out in enumerate(outs):
            yield (
                pltpu.make_async_copy(
                    stage.at[slot, mat, pl.ds(0, 48)],
                    out.at[pl.ds(row, 48)],
                    sems.at[slot, mat],
                ),
                pltpu.make_async_copy(
                    stage.at[slot, mat, pl.ds(48, 8)],
                    out.at[pl.ds(pl.multiple_of(row + 48, 8), 8)],
                    tail_sems.at[slot, mat],
                ),
                whole,
            )

    def finish(index):
        for most, tail, whole in copies(index):
            most.wait()
            pl.when(whole)(tail.wait)

    for index, (ref, i, *_) in enumerate(chunks):
        if index >= slots:
            finish(index - slots)
        stage[index % slots] = ref[i].astype(f32)
        for most, tail, whole in copies(index):
            most.start()
            pl.when(whole)(tail.start)
    for index in range(max(0, len(chunks) - slots), len(chunks)):
        finish(index)


def placed(where, parts, outs, units):
    arrays = [p[0].reshape(-1, 3, 56, p[0].shape[-1]) for p in parts]
    width = arrays[0].shape[-1]
    slots = 4
    return pl.pallas_call(
        functools.partial(
            place_kernel, turns=tuple(p[1:] for p in parts), held=len(outs)
        ),
        out_shape=[jax.ShapeDtypeStruct((units, width), f32)] * 3,
        in_specs=[pl.BlockSpec(memory_space=pltpu.SMEM)]
        + [pl.BlockSpec(memory_space=pltpu.VMEM)] * len(arrays)
        + [pl.BlockSpec(memory_space=pl.ANY)] * len(outs),
        out_specs=[pl.BlockSpec(memory_space=pl.ANY)] * 3,
        scratch_shapes=[
            pltpu.VMEM((slots, 3, 56, width), f32),
            pltpu.SemaphoreType.DMA((slots, 3)),
            pltpu.SemaphoreType.DMA((slots, 3)),
        ],
        input_output_aliases={1 + len(arrays) + i: i for i in range(len(outs))},
        compiler_params=pltpu.CompilerParams(vmem_limit_bytes=SOME),
        cost_estimate=pl.CostEstimate(
            flops=0, bytes_accessed=sum(p.size for p in arrays) * 6, transcendentals=0
        ),
    )(where, *arrays, *outs)


def sorted_rows(core, own, got, rows, kinds):
    for pieces, other in ((own, 0), (got, 1)):
        even = core == other
        for along in range(4):
            for across in range(4):
                row = jnp.where(even, 8 * across + 2 * along, 8 * along + 2 * across + 1) * 8
                row = pl.ds(pl.multiple_of(row, 8), 8)
                for kind in range(kinds):
                    rows[kind, row] = pieces(kind, along, across).astype(f32)


def square_kernel(where, own, got, out_grad, query_grad, rows):
    sorted_rows(
        where[0],
        lambda kind, along, across: own[along, kind, across],
        lambda kind, along, across: got[along, kind, across],
        rows,
        2,
    )
    out_grad[...] = rows[0]
    query_grad[...] = rows[1].T


def finish_kernel(
    where, own, got, key_grad, value_grad, attn, post, ffw, final, query, key, rows
):
    sorted_rows(
        where[0],
        lambda lane, along, across: own[lane, along, across],
        lambda lane, along, across: got[lane, along, across],
        rows,
        4,
    )
    for lane in range(4):
        key_grad[:, 64 * lane : 64 * lane + 64] = rows[lane, :64].T
        value_grad[:, 64 * lane : 64 * lane + 64] = rows[lane, 64:128].T
    gains = sum(rows[lane, 128:136] for lane in range(4))
    for at, out in enumerate((attn, post, ffw, final)):
        out[...] = gains[at]
    size = query.shape[0]
    query[...] = gains[4, :size]
    key[...] = gains[4, size : 2 * size]


def local(
    layer_input,
    segment_ids,
    out_cotangent,
    attn_norm_gain,
    query_weight,
    key_weight,
    value_weight,
    query_gain,
    key_gain,
    output_weight,
    attn_post_gain,
    ffw_norm_gain,
    gate_weight,
    up_weight,
    down_weight,
    ffw_post_gain,
):
    tok, width = layer_input.shape
    head_dim = key_weight.shape[1]
    units = down_weight.shape[0]
    block = lax.axis_index("seq")
    lane = lax.axis_index("tensor")
    core = lax.rem(block, 2)
    row = lax.rem(lax.div(block, 2), 4)
    plane = lax.div(block, 8)
    first = lax.select(core == 0, row, plane)
    second = lax.select(core == 0, plane, row)
    place = jnp.stack([lane, core, block])
    where = jnp.stack([core, first, second])
    afters = [lax.rem(at + by, 4) for at in (lane, first, second) for by in range(4)]
    flips = [first ^ flip for flip in range(1, 4)]
    place, where, core, other_core, even, *places_at = tied(
        place, where, core, 1 - core, core == 0, *afters, *flips
    )
    lanes, firsts, seconds = places_at[:4], places_at[4:8], places_at[8:12]
    flips = [firsts[0], *places_at[12:]]
    quarter_tok = tok // 4

    freq = rope_base ** (-2.0 * np.arange(head_dim // 2) / head_dim)
    start = (np.arange(lax.axis_size("seq")) * tok)[:, None] * freq[None, :]
    inner = np.arange(tok)[:, None] * freq[None, :]
    tables = [jnp.asarray(f(angle), f32) for angle in (start, inner) for f in (np.cos, np.sin)]

    square = (tok, head_dim)
    normed, own_pair, k_raw, q_raw, queries, cosine, sine = call(
        prepare_kernel,
        [
            ((tok, width), bf16),
            ((2 * tok + 16, head_dim), bf16),
            (square, f32),
            (square, f32),
            (square, bf16),
            ((tok, head_dim // 2), f32),
            ((tok, head_dim // 2), f32),
        ],
        place,
        layer_input,
        attn_norm_gain,
        key_weight,
        value_weight,
        query_weight,
        key_gain,
        query_gain,
        *tables,
        segment_ids,
        scalars=1,
        flops=6 * tok * width * head_dim,
        room=MOST,
    )
    left_one = shifted(own_pair, 1)
    left_two = shifted(own_pair, 2)

    weight_half = tok // 2
    halved, _ = tied(output_weight, own_pair)
    own_weight = pick(halved.reshape(2, weight_half, width), core)
    got_weight = [send(own_weight, round_x(by)) for by in (1, 2, 3)]

    pairs = (left_two, left_one, own_pair)
    context, log_total = attend(place, queries, pairs)

    got_context = [send(context, round_x(by)) for by in (1, 2, 3)]
    *got_context, got_weight[0], got_weight[1], got_weight[2] = tied(*got_context, *got_weight)
    other_weight = [send(part, swap_cores()) for part in got_weight]
    branch, middle, normed_two = call(
        project_kernel,
        [((tok, width), f32), ((tok, width), f32), ((tok, width), bf16)],
        place,
        layer_input,
        attn_post_gain,
        ffw_norm_gain,
        context,
        *got_context,
        output_weight,
        *got_weight,
        *other_weight,
        scalars=1,
        flops=8 * tok * tok * width,
    )
    gate = dot(gate_weight, normed_two, (0, 1))
    up_val = dot(up_weight, normed_two, (0, 1))
    active, gelu_back = jax.vjp(lambda val: jax.nn.gelu(val, approximate=True), gate)
    hidden = (active * up_val).astype(bf16)
    down_part = dot(hidden, down_weight, (0, 0)).astype(bf16)

    def halves(values):
        groups = values.reshape(8, units // 8, tok)
        groups = jnp.concatenate([groups[:, :56], groups[:, 48:]], axis=1)
        pieces = groups.reshape(4, 4, 2, 56, tok)
        return pick(pieces, core, 2), pick(pieces, other_core, 2)

    def arranged(values):
        values = jnp.where(even, values.swapaxes(0, 1), values)
        by_first = [pick(values, flip) for flip in flips]
        groups = [
            jnp.stack([by_first[i][2 * stream : 2 * stream + 2] for i in order])
            for stream, order in ((0, (0, 3)), (0, (1, 2)), (1, (0, 1)), (1, (3, 2)))
        ]
        return jnp.stack(groups).reshape(4, 224, tok)

    hidden_own, hidden_give = halves(hidden)
    hidden_got = send(hidden_give, swap_cores())
    normed_two_got = send(normed_two, swap_cores())

    def quarters(parts):
        parts = parts.reshape(4, quarter_tok, parts.shape[-1])
        given = [pick(parts, at) for at in lanes[1:]]
        return [pick(parts, lanes[0])] + [
            send(part, round_x(by)) for by, part in zip((1, 2, 3), given, strict=True)
        ]

    piece = (quarter_tok, width)
    out_own, d_branch_two, final_part = call(
        final_kernel,
        [(piece, bf16), (piece, bf16), ((1, width), f32)],
        place,
        *quarters(down_part),
        middle,
        out_cotangent,
        ffw_post_gain,
        scalars=1,
    )
    d_branch_two = gather(d_branch_two, lanes, round_x).reshape(tok, width)
    d_branch_two_got = send(d_branch_two, swap_cores())

    d_hidden = dot(down_weight, d_branch_two, (1, 1))
    d_gate = gelu_back(d_hidden * up_val)[0].astype(bf16)
    d_up = (d_hidden * active).astype(bf16)
    d_normed_two = (dot(d_gate, gate_weight, (0, 1)) + dot(d_up, up_weight, (0, 1))).astype(bf16)
    d_gate_own, d_gate_give = halves(d_gate)
    d_up_own, d_up_give = halves(d_up)
    d_pair_got = send(jnp.stack([d_gate_give, d_up_give]), swap_cores())

    keep_a, give_a, keep_b, give_b = weight_parts(
        *(
            arranged(v)
            for v in (hidden_own, hidden_got, d_gate_own, d_pair_got[0], d_up_own, d_pair_got[1])
        ),
        d_branch_two,
        d_branch_two_got,
        normed_two,
        normed_two_got,
    )
    got_a = send(give_a, along_first(1))
    got_b = send(give_b, along_first(3))

    *got_normed, keep_a, keep_b = tied(*quarters(d_normed_two), keep_a, keep_b)
    d_middle, d_branch, ffw_part, post_part = call(
        between_kernel,
        [(piece, f32), (piece, bf16), ((1, width), f32), ((1, width), f32)],
        place,
        *got_normed,
        middle,
        branch,
        out_cotangent,
        ffw_norm_gain,
        attn_post_gain,
        scalars=1,
    )
    d_branch = gather(d_branch, lanes, round_x).reshape(tok, width)
    d_queries, left_far, left_near, summed = attend_back(
        place, log_total, d_branch, output_weight, queries, pairs
    )
    got_near = shifted(left_near, -1)
    got_far = shifted(left_far, -2)
    got_near, got_far, got_a, got_b = tied(got_near, got_far, got_a, got_b)
    keep_a, give_a, keep_b, give_b = call(
        halve_kernel, [((336, width), bf16)] * 4, keep_a, got_a, keep_b, got_b
    )
    got_a = send(give_a, along_first(3))
    got_b = send(give_b, along_first(1))
    d_query, payload, query_part, key_part = call(
        key_kernel,
        [
            (square, bf16),
            ((tok, width + 2 * tok), bf16),
            ((1, head_dim), f32),
            ((1, head_dim), f32),
        ],
        q_raw,
        k_raw,
        d_queries,
        summed,
        got_near,
        got_far,
        cosine,
        sine,
        query_gain,
        key_gain,
        query_weight,
        key_weight,
        value_weight,
        flops=6 * tok * width * head_dim,
    )
    got_both = quarters(payload)
    (products,) = call(
        products_kernel,
        [((2 * head_dim, width), f32)],
        context,
        d_branch,
        d_query,
        normed,
        flops=4 * tok * width * head_dim,
    )
    *got_both, got_a, got_b = tied(*got_both, got_a, got_b)
    chunk = (3, 56, width)
    mine, *given = call(
        deal_kernel,
        [(chunk, f32)] + [(chunk, bf16)] * 3,
        where,
        keep_a,
        got_a,
        keep_b,
        got_b,
        scalars=1,
        scratch=[pltpu.VMEM((2, 336, width), f32)],
    )
    got = [send(part, round_second(by)) for by, part in zip((1, 2, 3), given, strict=True)]
    input_own, keep, give = pl.pallas_call(
        entry_kernel,
        out_shape=[
            jax.ShapeDtypeStruct(piece, bf16),
            jax.ShapeDtypeStruct((3, 16, 8, width), f32),
            jax.ShapeDtypeStruct((3, 16, 8, width), bf16),
        ],
        in_specs=[pl.BlockSpec(memory_space=pltpu.SMEM)]
        + [pl.BlockSpec(memory_space=pltpu.VMEM)] * 14,
        out_specs=[pl.BlockSpec(memory_space=pltpu.VMEM)] * 3,
        scratch_shapes=[pltpu.VMEM((tok, width), f32)],
        compiler_params=pltpu.CompilerParams(vmem_limit_bytes=SOME),
        cost_estimate=pl.CostEstimate(
            flops=256 * tok * width, bytes_accessed=12_000_000, transcendentals=0
        ),
    )(
        place,
        *got_both,
        layer_input,
        d_middle,
        attn_norm_gain,
        normed,
        post_part,
        ffw_part,
        final_part,
        query_part,
        key_part,
        products,
    )
    pack_got = send(give, swap_cores())
    part = (3, 4, 8, width)
    pack, *given = call(
        merge_kernel, [(part, f32)] + [(part, bf16)] * 3, where, keep, pack_got, scalars=1
    )
    given = [send(part, round_first(by)) for by, part in zip((1, 2, 3), given, strict=True)]
    *given, got[0], got[1], got[2] = tied(*given, *got)
    mine = mine + got[0].astype(f32) + (got[1].astype(f32) + got[2].astype(f32))
    mine = mine.astype(bf16).reshape(168, width)
    for part in given:
        pack = pack + part.astype(f32)
    pack = pack.astype(bf16).reshape(96, width)
    both = lax.optimization_barrier(jnp.concatenate([mine, pack]))
    given = [send(both, round_second(by)) for by in (1, 2, 3)]
    ends = jnp.concatenate([out_own, input_own])
    got_ends = [send(ends, round_x(by)) for by in (1, 2, 3)]
    given[0], given[1], given[2], *got_ends = tied(*given, *got_ends)
    ends = joined(ends, got_ends, lanes)
    layer_output = ends[:, :64].reshape(tok, width)
    input_grad = ends[:, 64:].reshape(tok, width)
    quarter = joined(both[:168], [part[:168] for part in given], seconds)
    pack, *given = (part[168:].astype(f32) for part in (both, *given))
    pack = (pack + given[1] + (given[0] + given[2])).astype(bf16).reshape(3, 4, 8, width)
    given = [send(pack, round_first(by)) for by in (1, 2, 3)]
    other_own = send(quarter, swap_cores())
    given[0], quarter, other_own, layer_output, input_grad = tied(
        given[0], quarter, other_own, layer_output, input_grad
    )
    near_a = send(quarter, along_first(1))
    near_b = send(quarter, along_first(3))
    pack = joined(pack, given, firsts)
    pack_got = send(pack, swap_cores())
    rest, pack_got, own_quarter = tied(pack[:, 2], pack_got, quarter)
    given = [send(rest, round_x(by)) for by in (1, 2, 3)]
    out_grad, query_grad = call(
        square_kernel,
        [((256, width), f32), ((width, 256), f32)],
        where,
        pack,
        pack_got,
        scalars=1,
        scratch=[pltpu.VMEM((2, 256, width), f32)],
    )
    grads = placed(where, [(own_quarter, False, 0, 0), (other_own, True, 0, 0)], [], units)
    grads = list(grads)
    *given, near_a, near_b, grads[0], out_grad = tied(
        *given, near_a, near_b, grads[0], out_grad
    )
    far_a = send(near_b[:2], along_first(1))
    far_b = send(near_a[2:], along_first(3))
    other_a = send(near_a, swap_cores())
    other_b = send(near_b, swap_cores())
    rest = joined(rest, given, lanes)
    rest_got = send(rest, swap_cores())
    key_grad, value_grad, *gains = call(
        finish_kernel,
        [((width, 256), f32)] * 2 + [((width,), f32)] * 4 + [((256,), f32)] * 2,
        where,
        rest,
        rest_got,
        scalars=1,
        scratch=[pltpu.VMEM((4, 256, width), f32)],
    )
    grads = placed(
        where,
        [
            (near_a, False, 1, 0),
            (near_b, False, 3, 0),
            (other_a, True, 1, 0),
            (other_b, True, 3, 0),
        ],
        grads,
        units,
    )
    far_a, far_b, *grads = tied(far_a, far_b, *grads)
    other_far_a = send(far_a, swap_cores())
    other_far_b = send(far_b, swap_cores())
    down_grad, gate_grad, up_grad = placed(
        where,
        [
            (far_a, False, 2, 0),
            (far_b, False, 2, 2),
            (other_far_a, True, 2, 0),
            (other_far_b, True, 2, 2),
        ],
        grads,
        units,
    )
    return (
        layer_output,
        input_grad,
        gains[0],
        query_grad,
        key_grad,
        value_grad,
        gains[4],
        gains[5],
        out_grad,
        gains[1],
        gains[2],
        gate_grad.T,
        up_grad.T,
        down_grad,
        gains[3],
    )


def solution(mesh):
    rows = P("seq", None)
    return jax.shard_map(
        local,
        mesh=mesh,
        in_specs=(
            rows,
            P("seq"),
            rows,
            P(),
            P(None, "tensor"),
            P(),
            P(),
            P(),
            P(),
            P("tensor", None),
            P(),
            P(),
            P(None, "tensor"),
            P(None, "tensor"),
            P("tensor", None),
            P(),
        ),
        out_specs=(
            rows,
            rows,
            P(),
            P(None, "tensor"),
            P(),
            P(),
            P(),
            P(),
            P("tensor", None),
            P(),
            P(),
            P(None, "tensor"),
            P(None, "tensor"),
            P("tensor", None),
            P(),
        ),
        check_vma=False,
    )
```
